32 devices in a mesh: section: 2 (over y), tensor: 2 (over core), dp: 8 (over z, x).
Axes of the slice: x: 2, y: 2, z: 4, core: 2. Of those that a mesh axis runs over, the one named last changes fastest.
Arguments:
- inputs: bfloat16 [2, 8, 768, 1024], P(None, 'dp', None, 'tensor'), may hold values from -6 to 6
- cotangent: bfloat16 [2, 8, 768, 1024], P(None, 'dp', None, 'tensor'), may hold values from -6 to 6
- ln1_gain: bfloat16 [2, 1024], P('section', 'tensor'), may hold values from 0.25 to 1.75
- ln1_bias: bfloat16 [2, 1024], P('section', 'tensor'), may hold values from -1.75 to 1.75
- qkv_weight: bfloat16 [2, 1024, 3, 1024], P('section', None, None, 'tensor'), may hold values from -0.1875 to 0.1875
- qv_bias: bfloat16 [2, 2, 1024], P('section', None, 'tensor'), may hold values from -0.625 to 0.625
- out_weight: bfloat16 [2, 1024, 1024], P('section', 'tensor'), may hold values from -3 to 3
- out_bias: bfloat16 [2, 1024], P('section', 'tensor'), may hold values from -1.75 to 1.75
- scale_attn: bfloat16 [2, 1024], P('section', 'tensor'), may hold values from 0.29882812 to 1
- ln2_gain: bfloat16 [2, 1024], P('section', 'tensor'), may hold values from 0.25 to 1.75
- ln2_bias: bfloat16 [2, 1024], P('section', 'tensor'), may hold values from -1.75 to 1.75
- fc1_weight: bfloat16 [2, 1024, 4096], P('section', None, 'tensor'), may hold values from -0.1875 to 0.1875
- fc1_bias: bfloat16 [2, 4096], P('section', 'tensor'), may hold values from -3 to 3
- fc2_weight: bfloat16 [2, 4096, 1024], P('section', 'tensor'), may hold values from -0.09375 to 0.09375
- fc2_bias: bfloat16 [2, 1024], P('section', 'tensor'), may hold values from -1.75 to 1.75
- scale_mlp: bfloat16 [2, 1024], P('section', 'tensor'), may hold values from 0.29882812 to 1
Outputs:
- block_outputs: bfloat16 [2, 2, 8, 768, 1024], P('section', None, 'dp', None, 'tensor')
- input_grads: bfloat16 [2, 2, 8, 768, 1024], P('section', None, 'dp', None, 'tensor')
- grad_ln1_gain: float32 [2, 1024], P('section', 'tensor')
- grad_ln1_bias: float32 [2, 1024], P('section', 'tensor')
- grad_qkv_weight: float32 [2, 1024, 3, 1024], P('section', None, None, 'tensor')
- grad_qv_bias: float32 [2, 2, 1024], P('section', None, 'tensor')
- grad_out_weight: float32 [2, 1024, 1024], P('section', 'tensor')
- grad_out_bias: float32 [2, 1024], P('section', 'tensor')
- grad_scale_attn: float32 [2, 1024], P('section', 'tensor')
- grad_ln2_gain: float32 [2, 1024], P('section', 'tensor')
- grad_ln2_bias: float32 [2, 1024], P('section', 'tensor')
- grad_fc1_weight: float32 [2, 1024, 4096], P('section', None, 'tensor')
- grad_fc1_bias: float32 [2, 4096], P('section', 'tensor')
- grad_fc2_weight: float32 [2, 4096, 1024], P('section', 'tensor')
- grad_fc2_bias: float32 [2, 1024], P('section', 'tensor')
- grad_scale_mlp: float32 [2, 1024], P('section', 'tensor')
The draws below stay inside these ranges and needn't reach their ends.
All inputs are finite; a program needn't handle non-finite values.
Results may differ from the reference program's by a relative error of at most 0.017.
Values may be sent and summed in bfloat16 or wider, within the bound.
No kernel may reach another device: no remote copies, remote signals or barrier semaphores. Data moves between devices by JAX's collectives and lax.ppermute only.
A program may use at most 512 MiB of HBM per device.

```python
import jax
import jax.numpy as jnp
from jax import lax

D = 1024
HEADS = 16
HEAD_DIM = 64
FF = 4096
SEQ = 768
MICRO = 2
LAYERS = 2
IMAGES = 8


def levels(rng, dims, shards, smallest, top_value):
    def one(dim, blocks):
        heights = jax.random.uniform(jax.random.fold_in(jax.random.fold_in(rng, 6), dim), (blocks,), jnp.float32, smallest / len(shards), top_value / len(shards))
        return jnp.repeat(jnp.exp(heights), dims[dim] // blocks).reshape((-1,) + (1,) * (len(dims) - dim - 1))

    loudness = one(*shards[0])
    for cut in shards[1:]:
        loudness = loudness * one(*cut)
    return loudness


def scatter_about(own_key, dims, scale, bound, shards=(), dtype=jnp.bfloat16):
    array = scale * jax.random.normal(own_key, dims, jnp.float32)
    if shards:
        array = array * levels(own_key, dims, shards, -0.22, 0.18)
    return jnp.clip(array, -bound, bound).astype(dtype)


def setup_inputs(seed: int = 0) -> dict:
    streams_of = jax.random.split(jax.random.key(seed), 17)
    inputs = scatter_about(streams_of[0], (MICRO, IMAGES, SEQ, D), 1.0, 6.0, ((1, 8), (3, 2)))
    cotangent = scatter_about(streams_of[1], (MICRO, IMAGES, SEQ, D), 1.0, 6.0, ((1, 8), (3, 2)))
    ln1_gain = jnp.clip(1.0 + 0.15 * jax.random.normal(streams_of[2], (LAYERS, D), jnp.float32), 0.25, 1.75).astype(jnp.bfloat16)
    ln1_bias = scatter_about(streams_of[3], (LAYERS, D), 0.3, 1.75, ((0, 2), (1, 2)))
    qkv_weight = scatter_about(streams_of[4], (LAYERS, D, 3, D), D ** -0.5, 0.1875, ((0, 2), (3, 2)))
    qv_bias = scatter_about(streams_of[5], (LAYERS, 2, D), 0.1, 0.625, ((0, 2), (2, 2)))
    out_weight = scatter_about(streams_of[6], (LAYERS, D, D), (max(3 * D // SEQ, 1)) ** -0.5, 3.0, ((0, 2), (1, 2)))
    out_bias = scatter_about(streams_of[7], (LAYERS, D), 0.3, 1.75, ((0, 2), (1, 2)))
    scale_attn = jnp.clip(0.29882812 + 0.7011719 * jax.random.uniform(streams_of[8], (LAYERS, D), jnp.float32) ** levels(streams_of[8], (LAYERS, D), ((0, 2), (1, 2)), -0.2, 0.2), 0.29882812, 1.0).astype(jnp.bfloat16)
    ln2_gain = jnp.clip(1.0 + 0.15 * jax.random.normal(streams_of[9], (LAYERS, D), jnp.float32), 0.25, 1.75).astype(jnp.bfloat16)
    ln2_bias = scatter_about(streams_of[10], (LAYERS, D), 0.3, 1.75, ((0, 2), (1, 2)))
    fc1_weight = scatter_about(streams_of[11], (LAYERS, D, FF), D ** -0.5, 0.1875, ((0, 2), (2, 2)))
    fc1_bias = scatter_about(streams_of[12], (LAYERS, FF), 0.5, 3.0, ((0, 2), (1, 2)))
    fc2_weight = scatter_about(streams_of[13], (LAYERS, FF, D), FF ** -0.5, 0.09375, ((0, 2), (1, 2)))
    fc2_bias = scatter_about(streams_of[14], (LAYERS, D), 0.3, 1.75, ((0, 2), (1, 2)))
    scale_mlp = jnp.clip(0.29882812 + 0.7011719 * jax.random.uniform(streams_of[15], (LAYERS, D), jnp.float32) ** levels(streams_of[15], (LAYERS, D), ((0, 2), (1, 2)), -0.2, 0.2), 0.29882812, 1.0).astype(jnp.bfloat16)
    return dict(inputs=inputs, cotangent=cotangent, ln1_gain=ln1_gain, ln1_bias=ln1_bias, qkv_weight=qkv_weight, qv_bias=qv_bias, out_weight=out_weight, out_bias=out_bias, scale_attn=scale_attn, ln2_gain=ln2_gain, ln2_bias=ln2_bias, fc1_weight=fc1_weight, fc1_bias=fc1_bias, fc2_weight=fc2_weight, fc2_bias=fc2_bias, scale_mlp=scale_mlp)


EPSILON = 1e-06

@jax.custom_vjp
def low(v):
    return lax.optimization_barrier(v.astype(jnp.bfloat16)).astype(jnp.float32)

@jax.custom_vjp
def low_back(v):
    return v

def low_keep(v):
    return (low(v), None)

def low_pass(kept, grad):
    return (grad,)

def back_keep(v):
    return (v, None)

def back_low(kept, grad):
    return (low(grad),)
low.defvjp(low_keep, low_pass)
low_back.defvjp(back_keep, back_low)

def product(left, right):
    return jnp.dot(left, right, precision=lax.Precision.HIGHEST, preferred_element_type=jnp.float32)

def norm_rows(values, gain, shift):
    centre = lax.optimization_barrier(jnp.mean(values, axis=-1, keepdims=True))
    centred = values - centre
    spread = lax.optimization_barrier(jnp.mean(centred * centred, axis=-1, keepdims=True))
    return centred * lax.rsqrt(spread + EPSILON) * gain + shift

def heads_view(flat):
    return flat.reshape(flat.shape[0], HEADS, HEAD_DIM)

def encoder_layer(tokens_in, params):
    gain_one, shift_one, w_qkv, qv_shift, w_out, out_shift, attn_scale, gain_two, shift_two, w_up, up_shift, w_down, down_shift, mlp_scale = params
    normed_one = low(norm_rows(tokens_in, gain_one, shift_one))
    queries = low(low_back(product(normed_one, w_qkv[:, 0, :]) + qv_shift[0]))
    key_rows = low(low_back(product(normed_one, w_qkv[:, 1, :])))
    value_rows = low(low_back(product(normed_one, w_qkv[:, 2, :]) + qv_shift[1]))
    scores = jnp.einsum('qhd,khd->hqk', heads_view(queries), heads_view(key_rows), precision=lax.Precision.HIGHEST) * HEAD_DIM ** (-0.5)
    scores = low_back(scores)
    probs = low(jax.nn.softmax(scores, axis=-1))
    mixed = jnp.einsum('hqk,khd->qhd', probs, heads_view(value_rows), precision=lax.Precision.HIGHEST).reshape(tokens_in.shape)
    mixed = low(low_back(mixed))
    attended = low_back(product(mixed, w_out) + out_shift)
    residual = tokens_in + attn_scale * attended
    normed_two = low(norm_rows(residual, gain_two, shift_two))
    before = low_back(product(normed_two, w_up) + up_shift)
    active = low(jax.nn.gelu(before, approximate=False))
    branch = low_back(product(active, w_down) + down_shift)
    return residual + mlp_scale * branch

def reference(inputs, cotangent, ln1_gain, ln1_bias, qkv_weight, qv_bias, out_weight, out_bias, scale_attn, ln2_gain, ln2_bias, fc1_weight, fc1_bias, fc2_weight, fc2_bias, scale_mlp):
    stacked = (ln1_gain, ln1_bias, qkv_weight, qv_bias, out_weight, out_bias, scale_attn, ln2_gain, ln2_bias, fc1_weight, fc1_bias, fc2_weight, fc2_bias, scale_mlp)
    first_part = tuple((stacked_arg[0].astype(jnp.float32) for stacked_arg in stacked))
    second_part = tuple((stacked_arg[1].astype(jnp.float32) for stacked_arg in stacked))
    flat_in = inputs.reshape(MICRO * IMAGES, SEQ, D)
    flat_cot = cotangent.reshape(MICRO * IMAGES, SEQ, D)

    def one_image(running, image_pair):
        tokens_img, cot_img = image_pair
        first_in = tokens_img.astype(jnp.float32)
        first_out, first_pull = jax.vjp(encoder_layer, first_in, first_part)
        first_sent = first_out.astype(jnp.bfloat16)
        second_in = lax.optimization_barrier(first_sent).astype(jnp.float32)
        second_out, second_pull = jax.vjp(encoder_layer, second_in, second_part)
        grad_second_in, grad_second = second_pull(cot_img.astype(jnp.float32))
        grad_sent = grad_second_in.astype(jnp.bfloat16)
        grad_first_in, grad_first = first_pull(lax.optimization_barrier(grad_sent).astype(jnp.float32))
        running = jax.tree.map(lambda total, extra: total + extra, running, (grad_first, grad_second))
        return (running, (first_sent, second_out.astype(jnp.bfloat16), grad_first_in.astype(jnp.bfloat16), grad_sent))
    zeros = jax.tree.map(jnp.zeros_like, (first_part, second_part))
    totals, (outs_first, outs_second, grads_first, grads_second) = lax.scan(one_image, zeros, (flat_in, flat_cot))
    block_outputs = jnp.stack([outs_first.reshape(MICRO, IMAGES, SEQ, D), outs_second.reshape(MICRO, IMAGES, SEQ, D)])
    input_grads = jnp.stack([grads_first.reshape(MICRO, IMAGES, SEQ, D), grads_second.reshape(MICRO, IMAGES, SEQ, D)])
    grad_list = [jnp.stack([totals[0][position], totals[1][position]]) for position in range(14)]
    return (block_outputs, input_grads, grad_list[0], grad_list[1], grad_list[2], grad_list[3], grad_list[4], grad_list[5], grad_list[6], grad_list[7], grad_list[8], grad_list[9], grad_list[10], grad_list[11], grad_list[12], grad_list[13])
```

```python
import math

import jax
import jax.numpy as jnp
from jax import lax
from jax.experimental import pallas as pl
from jax.experimental.pallas import tpu as pltpu
from jax.sharding import PartitionSpec as P

HEAD_DIM = 64
EPSILON = 1e-06
F32 = jnp.float32
BF16 = jnp.bfloat16
MIB = 1 << 20
VMEM_MIB = 60
SLOTS = 3
LN1G, LN1B, OUTB, SATT, LN2G, LN2B, FC2B, SMLP = range(8)


def dot(left, right):
    return jnp.dot(left, right, preferred_element_type=F32)


def dot_nt(left, right):
    return lax.dot_general(left, right, (((1,), (1,)), ((), ())), preferred_element_type=F32)


def dot_tn(left, right):
    return lax.dot_general(left, right, (((0,), (0,)), ((), ())), preferred_element_type=F32)


def norm_stats(values):
    centre = jnp.mean(values, axis=-1, keepdims=True)
    centred = values - centre
    spread = jnp.mean(centred * centred, axis=-1, keepdims=True)
    scale = lax.rsqrt(spread + EPSILON)
    return centred * scale, scale


def norm_backward(hat, scale, gain, error):
    weighted = error * gain
    mean_one = jnp.mean(weighted, axis=-1, keepdims=True)
    mean_two = jnp.mean(weighted * hat, axis=-1, keepdims=True)
    return scale * (weighted - mean_one - hat * mean_two)


def col_sum(values):
    return jnp.sum(values, axis=0, keepdims=True)


def call(kernel, scalars, grid, ins, outs, scratch=(), flops=0, moved=0):
    arrays = [a for a, _, _ in ins]
    in_specs = [pl.BlockSpec(b, m) for _, b, m in ins]
    aliases = {}
    for number, out in enumerate(outs):
        if out[4] is not None:
            aliases[1 + len(arrays)] = number
            arrays.append(out[4])
            in_specs.append(pl.BlockSpec(memory_space=pl.ANY))
    extra = len(aliases)
    in_count = len(ins)

    def body(*refs):
        kernel(*refs[: 1 + in_count], *refs[1 + in_count + extra :])

    return pl.pallas_call(
        body,
        out_shape=[jax.ShapeDtypeStruct(s, d) for s, d, _, _, _ in outs],
        grid_spec=pltpu.PrefetchScalarGridSpec(
            num_scalar_prefetch=1,
            grid=grid,
            in_specs=in_specs,
            out_specs=[pl.BlockSpec(b, m) for _, _, b, m, _ in outs],
            scratch_shapes=list(scratch),
        ),
        input_output_aliases=aliases,
        compiler_params=pltpu.CompilerParams(
            dimension_semantics=("arbitrary",) * len(grid), vmem_limit_bytes=VMEM_MIB * MIB
        ),
        cost_estimate=pl.CostEstimate(
            flops=int(flops), bytes_accessed=int(moved), transcendentals=0
        ),
    )(scalars, *arrays)


def manual(kernel, scalars, ins, outs, scratch, flops=0, moved=0):
    any_space = pl.BlockSpec(memory_space=pl.ANY)
    vmem_space = pl.BlockSpec(memory_space=pltpu.VMEM)
    arrays = [a for a, _ in ins]
    in_specs = [vmem_space if inside else any_space for _, inside in ins]
    aliases = {}
    for number, out in enumerate(outs):
        if out[3] is not None:
            aliases[1 + len(arrays)] = number
            arrays.append(out[3])
            in_specs.append(any_space)
    extra = len(aliases)
    in_count = len(ins)

    def body(*refs):
        kernel(*refs[: 1 + in_count], *refs[1 + in_count + extra :])

    return pl.pallas_call(
        body,
        out_shape=[jax.ShapeDtypeStruct(s, d) for s, d, _, _ in outs],
        in_specs=[pl.BlockSpec(memory_space=pltpu.SMEM)] + in_specs,
        out_specs=[vmem_space if inside else any_space for _, _, inside, _ in outs],
        scratch_shapes=list(scratch),
        input_output_aliases=aliases,
        compiler_params=pltpu.CompilerParams(vmem_limit_bytes=VMEM_MIB * MIB),
        cost_estimate=pl.CostEstimate(
            flops=int(flops), bytes_accessed=int(moved), transcendentals=0
        ),
    )(scalars, *arrays)


def begin(src, dst, sem):
    copy = pltpu.make_async_copy(src, dst, sem)
    copy.start()
    return copy


def dma_sems(count):
    return pltpu.SemaphoreType.DMA((count,))


def whole2(i, s):
    return (0, 0)


def slot3(i, s):
    return (s[0], 0, 0)


def fill_tokens(s, sources, target, sems):
    whole, number, other, relay, section = sources
    rows, width = target.shape
    half = width // 2
    rank = s[3]

    @pl.when(s[1] == section)
    def _():
        first = pl.multiple_of(rank * half, half)
        second = pl.multiple_of((1 - rank) * half, half)
        begin(
            whole.at[number, 0, pl.ds(pl.multiple_of(rank * rows, rows), rows)],
            target.at[:, pl.ds(first, half)],
            sems.at[0],
        )
        begin(other, target.at[:, pl.ds(second, half)], sems.at[1])

    @pl.when(s[1] != section)
    def _():
        begin(relay.at[:, pl.ds(0, half)], target.at[:, pl.ds(0, half)], sems.at[0])
        begin(relay.at[:, pl.ds(half, half)], target.at[:, pl.ds(half, half)], sems.at[1])


def await_tokens(relay, target, sems):
    half = target.shape[1] // 2
    for number in range(2):
        columns = pl.ds(number * half, half)
        pltpu.make_async_copy(
            relay.at[:, columns], target.at[:, columns], sems.at[number]
        ).wait()


def norm_kv(scalars, inputs, number, other, relay, vec, w_own, w_oth, bias_v, kept):
    rows, width = relay.shape
    half = width // 2

    def kernel(s, whole, oth_ref, relay_ref, v, own, oth, bv, x_out, n_out, kv_out,
               x_v, n_v, w_v, kv_v, tok_sems, w_sems, out_sems):
        @pl.when(s[2] == 1)
        def _():
            fill_tokens(s, (whole, number, oth_ref, relay_ref, 0), x_v, tok_sems)
            loads = []
            for part in range(4):
                ref = own if part < 2 else oth
                loads.append(begin(ref.at[1 + part % 2], w_v.at[part], w_sems.at[part]))
            await_tokens(relay_ref, x_v, tok_sems)
            outs = [begin(x_v, x_out.at[s[0]], out_sems.at[0])]
            hat, _ = norm_stats(x_v[...].astype(F32))
            n_v[...] = (hat * v[LN1G : LN1G + 1] + v[LN1B : LN1B + 1]).astype(BF16)
            outs.append(begin(n_v, n_out.at[s[0]], out_sems.at[1]))
            for part in range(4):
                loads[part].wait()
                result = dot(n_v[...], w_v[part])
                kind, side = part % 2, part // 2
                columns = slice(side * half, (side + 1) * half)
                if kind == 1:
                    result = result + bv[:, columns]
                kv_v[part] = result.astype(BF16)
                outs.append(
                    begin(
                        kv_v.at[part],
                        kv_out.at[kind, :, pl.ds(side * half, half)],
                        out_sems.at[2 + part],
                    )
                )
            for copy in outs:
                copy.wait()

    stack = (SLOTS, rows, width)
    return manual(
        kernel,
        scalars,
        [
            (inputs, False),
            (other, False),
            (relay, False),
            (vec, True),
            (w_own, False),
            (w_oth, False),
            (bias_v, True),
        ],
        [
            (stack, BF16, False, kept.get("x")),
            (stack, BF16, False, kept.get("normed1")),
            ((2, rows, width), BF16, False, None),
        ],
        [
            pltpu.VMEM((rows, width), BF16),
            pltpu.VMEM((rows, width), BF16),
            pltpu.VMEM((4, width, half), BF16),
            pltpu.VMEM((4, rows, half), BF16),
            dma_sems(2),
            dma_sems(4),
            dma_sems(6),
        ],
        flops=2 * rows * width * 2 * width,
        moved=4 * width * width + 10 * rows * width,
    )


def project_q(scalars, normed, w_own, w_oth, bias_q, kept):
    _, rows, width = normed.shape
    half = width // 2

    def kernel(s, n, own, oth, bq, q_out, n_v, w_v, q_v, in_sems, out_sems):
        @pl.when(s[2] == 1)
        def _():
            load = begin(n.at[s[0]], n_v, in_sems.at[0])
            loads = [
                begin(own.at[0], w_v.at[0], in_sems.at[1]),
                begin(oth.at[0], w_v.at[1], in_sems.at[2]),
            ]
            load.wait()
            outs = []
            for side in range(2):
                loads[side].wait()
                columns = slice(side * half, (side + 1) * half)
                q_v[side] = (dot(n_v[...], w_v[side]) + bq[:, columns]).astype(BF16)
                outs.append(
                    begin(
                        q_v.at[side],
                        q_out.at[s[0], :, pl.ds(side * half, half)],
                        out_sems.at[side],
                    )
                )
            for copy in outs:
                copy.wait()

    return manual(
        kernel,
        scalars,
        [(normed, False), (w_own, False), (w_oth, False), (bias_q, True)],
        [((SLOTS, rows, width), BF16, False, kept.get("q"))],
        [
            pltpu.VMEM((rows, width), BF16),
            pltpu.VMEM((2, width, half), BF16),
            pltpu.VMEM((2, rows, half), BF16),
            dma_sems(3),
            dma_sems(2),
        ],
        flops=2 * rows * width * width,
        moved=2 * width * width + 4 * rows * width,
    )[0]


def attend(scalars, q, kv_here, kv_there, kept):
    _, rows, width = q.shape
    pairs = width // (2 * HEAD_DIM)
    factor = HEAD_DIM**-0.5 * math.log2(math.e)
    lanes = 2 * HEAD_DIM

    def kernel(s, *refs):
        @pl.when(s[2] == 1)
        def _():
            compute(*refs)

    def compute(q_ref, here, there, e_out, o_out, mixed_out, inv_out, kv_out):
        qs = q_ref[0]
        kv_out[0, :, :rows] = here[...]
        kv_out[0, :, rows:] = there[...]
        keys = jnp.concatenate([here[0], there[0]], axis=0)
        values = jnp.concatenate([here[1], there[1]], axis=0)
        first_q = lax.broadcasted_iota(jnp.int32, (rows, lanes), 1) < HEAD_DIM
        first_k = lax.broadcasted_iota(jnp.int32, (2 * rows, lanes), 1) < HEAD_DIM
        results = []
        for head in range(2):
            mine_q = first_q if head == 0 else ~first_q
            mine_k = first_k if head == 0 else ~first_k
            scores = dot_nt(jnp.where(mine_q, qs, 0), keys) * factor
            top = jnp.max(scores, axis=-1, keepdims=True)
            grown = jnp.exp2(scores - top).astype(BF16)
            e_out[0, head] = grown
            results.append(dot(grown, jnp.where(mine_k, values, 1)))
        total = jnp.where(
            first_q,
            pltpu.roll(results[0], HEAD_DIM, 1),
            pltpu.roll(results[1], HEAD_DIM, 1),
        )
        inverse = 1.0 / total
        mixed = jnp.where(first_q, results[0], results[1]) * inverse
        o_out[0] = mixed
        mixed_out[0] = mixed.astype(BF16)
        inv_out[0] = inverse

    heads = 2 * pairs
    column = lambda i, s: (s[0], 0, i)
    return call(
        kernel,
        scalars,
        (pairs,),
        [
            (q, (1, rows, lanes), column),
            (kv_here, (2, rows, lanes), lambda i, s: (0, 0, i)),
            (kv_there, (2, rows, lanes), lambda i, s: (0, 0, (i + pairs // 2) % pairs)),
        ],
        [
            (
                (SLOTS, heads, rows, 2 * rows),
                BF16,
                (1, 2, rows, 2 * rows),
                lambda i, s: (s[0], i, 0, 0),
                kept.get("grown"),
            ),
            ((SLOTS, rows, width), F32, (1, rows, lanes), column, kept.get("mixed_full")),
            ((SLOTS, rows, width), BF16, (1, rows, lanes), column, kept.get("mixed")),
            ((SLOTS, rows, width), F32, (1, rows, lanes), column, kept.get("inverse")),
            (
                (SLOTS, 2, 2 * rows, width),
                BF16,
                (1, 2, 2 * rows, lanes),
                lambda i, s: (s[0], 0, 0, i),
                kept.get("kv"),
            ),
        ],
        flops=8 * rows * rows * width,
        moved=4 * heads * rows * rows + 30 * rows * width,
    )


def gelu_parts(x):
    size = jnp.abs(x)
    base = 1.0 + (0.3275911 * math.sqrt(0.5)) * size
    t = pl.reciprocal(base, approx=True)
    t = t * (2.0 - base * t)
    grown = jnp.exp2(x * x * (-0.5 * math.log2(math.e)))
    poly = 0.5 * 1.061405429
    for factor in (-1.453152027, 1.421413741, -0.284496736, 0.254829592):
        poly = poly * t + 0.5 * factor
    tail = poly * t * grown
    below = jnp.where(x < 0.0, tail, 1.0 - tail)
    return x * below, below + x * grown * (1.0 / math.sqrt(2.0 * math.pi))


CHUNK = 512


def mlp_forward(scalars, mixed, x, vec, wo_own, wo_oth, wu_own, wu_oth, wd_own, wd_oth, b_up, kept):
    _, rows, width = x.shape
    side_hidden = wu_own.shape[1]
    hidden = 2 * side_hidden
    half = width // 2
    steps = hidden // CHUNK
    split = steps // 2

    def kernel(
        s, m, x_ref, v, woo, wot, wuo, wut, wdo, wdt, bu,
        att_out, res_out, n_out, act_out, slope_out, branch_out, y_out, relay_out,
        m_v, x_v, wo_v, wu_v, wd_v, att_v, res_v, n_v, h_v, act_v, slope_v, branch_v, y_v, acc,
        in_sems, wu_sems, wd_sems, out_sems, act_sems, slope_sems,
    ):
        @pl.when(s[2] == 1)
        def _():
            slot = s[0]
            first = [
                begin(m.at[slot], m_v, in_sems.at[0]),
                begin(woo, wo_v.at[0], in_sems.at[1]),
                begin(wot, wo_v.at[1], in_sems.at[2]),
                begin(x_ref.at[slot], x_v, in_sems.at[3]),
            ]
            ups, downs = [], []
            for i in range(steps):
                part = pl.ds((i % split) * CHUNK, CHUNK)
                up, down = (wuo, wdo) if i < split else (wut, wdt)
                ups.append(begin(up.at[:, part], wu_v.at[i], wu_sems.at[i]))
                downs.append(begin(down.at[part], wd_v.at[i], wd_sems.at[i]))
            for copy in first:
                copy.wait()
            attended = dot(m_v[:, :half], wo_v[0]) + dot(m_v[:, half:], wo_v[1])
            attended = attended + v[OUTB : OUTB + 1]
            att_v[...] = attended.astype(BF16)
            residual = x_v[...].astype(F32) + v[SATT : SATT + 1] * attended
            res_v[...] = residual
            hat, _ = norm_stats(residual)
            n_v[...] = (hat * v[LN2G : LN2G + 1] + v[LN2B : LN2B + 1]).astype(BF16)
            outs = [
                begin(att_v, att_out.at[slot], out_sems.at[0]),
                begin(res_v, res_out.at[slot], out_sems.at[1]),
                begin(n_v, n_out.at[slot], out_sems.at[2]),
            ]

            def up_product(i):
                ups[i].wait()
                h_v[i % 2] = dot(n_v[...], wu_v[i]) + bu[i : i + 1]

            up_product(0)
            for i in range(steps):
                downs[i].wait()
                if i + 1 < steps:
                    up_product(i + 1)
                active, slope = gelu_parts(h_v[i % 2])
                act_v[i] = active.astype(BF16)
                slope_v[i] = slope.astype(BF16)
                part = pl.ds(i * CHUNK, CHUNK)
                outs.append(begin(act_v.at[i], act_out.at[slot, :, part], act_sems.at[i]))
                outs.append(begin(slope_v.at[i], slope_out.at[slot, :, part], slope_sems.at[i]))
                product = dot(act_v[i], wd_v[i])
                acc[...] = product if i == 0 else acc[...] + product
            branch = acc[...] + v[FC2B : FC2B + 1]
            y_v[...] = (res_v[...] + v[SMLP : SMLP + 1] * branch).astype(BF16)
            branch_v[...] = branch.astype(BF16)
            outs.append(begin(y_v, relay_out, out_sems.at[3]))
            outs.append(begin(y_v, y_out.at[slot], out_sems.at[4]))
            outs.append(begin(branch_v, branch_out.at[slot], out_sems.at[5]))
            for copy in outs:
                copy.wait()

    stack = (SLOTS, rows, width)
    tall = (SLOTS, rows, hidden)
    plain = pltpu.VMEM((rows, width), BF16)
    full = pltpu.VMEM((rows, width), F32)
    chunks = pltpu.VMEM((steps, rows, CHUNK), BF16)
    return manual(
        kernel,
        scalars,
        [
            (mixed, False),
            (x, False),
            (vec, True),
            (wo_own, False),
            (wo_oth, False),
            (wu_own, False),
            (wu_oth, False),
            (wd_own, False),
            (wd_oth, False),
            (b_up, True),
        ],
        [
            (stack, BF16, False, kept.get("attended")),
            (stack, F32, False, kept.get("residual")),
            (stack, BF16, False, kept.get("normed2")),
            (tall, BF16, False, kept.get("active")),
            (tall, BF16, False, kept.get("slope")),
            (stack, BF16, False, kept.get("branch")),
            (stack, BF16, False, kept.get("output")),
            ((rows, width), BF16, False, None),
        ],
        [
            plain,
            plain,
            pltpu.VMEM((2, half, width), BF16),
            pltpu.VMEM((steps, width, CHUNK), BF16),
            pltpu.VMEM((steps, CHUNK, width), BF16),
            plain,
            full,
            plain,
            pltpu.VMEM((2, rows, CHUNK), F32),
            chunks,
            chunks,
            plain,
            plain,
            full,
            dma_sems(4),
            dma_sems(steps),
            dma_sems(steps),
            dma_sems(6),
            dma_sems(steps),
            dma_sems(steps),
        ],
        flops=4 * rows * width * hidden + 2 * rows * width * width,
        moved=4 * width * hidden + 2 * width * width + 8 * rows * hidden,
    )


def mlp_backward(scalars, cotangent, number, other, relay, vec, wo_own, wo_oth, wu_own, wu_oth, wd_own, wd_oth, kept, grads):
    _, rows, width = kept["x"].shape
    side_hidden = wu_own.shape[1]
    hidden = 2 * side_hidden
    half = width // 2
    steps = hidden // CHUNK
    split = steps // 2

    def kernel(
        s, whole, oth_ref, relay_ref, branch, slope, res, att, v, woo, wot, wuo, wut, wdo, wdt,
        gb_out, before_out, ga_out, gm_out, gr_out, small_out, shift_out,
        g_v, branch_v, slope_v, res_v, att_v, wo_v, wu_v, wd_v, gb_v, d_v, before_v, ga_v, gm_v,
        gr_v, acc, tok_sems, in_sems, slope_sems, wu_sems, wd_sems, out_sems, before_sems,
    ):
        @pl.when(s[2] == 0)
        def _():
            small_out[...] = jnp.zeros_like(small_out)
            shift_out[...] = jnp.zeros_like(shift_out)

        @pl.when(s[2] == 1)
        def _():
            slot = s[0]
            fill_tokens(s, (whole, number, oth_ref, relay_ref, 1), g_v, tok_sems)
            branch_in = begin(branch.at[slot], branch_v, in_sems.at[0])
            ups, downs, slopes = [], [], []
            for i in range(steps):
                part = pl.ds((i % split) * CHUNK, CHUNK)
                up, down = (wuo, wdo) if i < split else (wut, wdt)
                downs.append(begin(down.at[part], wd_v.at[i], wd_sems.at[i]))
                slopes.append(
                    begin(
                        slope.at[slot, :, pl.ds(i * CHUNK, CHUNK)], slope_v.at[i], slope_sems.at[i]
                    )
                )
                ups.append(begin(up.at[:, part], wu_v.at[i], wu_sems.at[i]))
            last = [
                begin(res.at[slot], res_v, in_sems.at[1]),
                begin(att.at[slot], att_v, in_sems.at[2]),
                begin(woo, wo_v.at[0], in_sems.at[3]),
                begin(wot, wo_v.at[1], in_sems.at[4]),
            ]
            await_tokens(relay_ref, g_v, tok_sems)
            g = g_v[...].astype(F32)
            gb = (v[SMLP : SMLP + 1] * g).astype(BF16)
            gb_v[...] = gb
            outs = [begin(gb_v, gb_out.at[slot], out_sems.at[0])]

            def down_product(i):
                downs[i].wait()
                d_v[i % 2] = dot_nt(gb_v[...], wd_v[i])

            down_product(0)
            branch_in.wait()
            small_out[...] = jnp.zeros_like(small_out)
            small_out[0:1] = col_sum(g * branch_v[...].astype(F32))
            small_out[1:2] = col_sum(gb.astype(F32))
            for i in range(steps):
                slopes[i].wait()
                ups[i].wait()
                if i + 1 < steps:
                    down_product(i + 1)
                grad_before = (d_v[i % 2] * slope_v[i].astype(F32)).astype(BF16)
                before_v[i] = grad_before
                part = pl.ds(i * CHUNK, CHUNK)
                outs.append(begin(before_v.at[i], before_out.at[slot, :, part], before_sems.at[i]))
                shift_out[i : i + 1] = col_sum(grad_before.astype(F32))
                product = dot_nt(before_v[i], wu_v[i])
                acc[...] = product if i == 0 else acc[...] + product
            for copy in last:
                copy.wait()
            hat, scale = norm_stats(res_v[...])
            error = acc[...]
            grad = g_v[...].astype(F32) + norm_backward(hat, scale, v[LN2G : LN2G + 1], error)
            ga = (v[SATT : SATT + 1] * grad).astype(BF16)
            ga_v[...] = ga
            outs.append(begin(ga_v, ga_out.at[slot], out_sems.at[1]))
            gm_v[:, :half] = dot_nt(ga, wo_v[0]).astype(BF16)
            gm_v[:, half:] = dot_nt(ga, wo_v[1]).astype(BF16)
            outs.append(begin(gm_v, gm_out, out_sems.at[2]))
            gr_v[...] = grad
            outs.append(begin(gr_v, gr_out, out_sems.at[3]))
            small_out[2:3] = col_sum(error * hat)
            small_out[3:4] = col_sum(error)
            small_out[4:5] = col_sum(grad * att_v[...].astype(F32))
            small_out[5:6] = col_sum(ga.astype(F32))
            for copy in outs:
                copy.wait()

    stack = (SLOTS, rows, width)
    plain = pltpu.VMEM((rows, width), BF16)
    full = pltpu.VMEM((rows, width), F32)
    chunks = pltpu.VMEM((steps, rows, CHUNK), BF16)
    return manual(
        kernel,
        scalars,
        [
            (cotangent, False),
            (other, False),
            (relay, False),
            (kept["branch"], False),
            (kept["slope"], False),
            (kept["residual"], False),
            (kept["attended"], False),
            (vec, True),
            (wo_own, False),
            (wo_oth, False),
            (wu_own, False),
            (wu_oth, False),
            (wd_own, False),
            (wd_oth, False),
        ],
        [
            (stack, BF16, False, grads.get("branch")),
            ((SLOTS, rows, hidden), BF16, False, grads.get("before")),
            (stack, BF16, False, grads.get("attended")),
            ((rows, width), BF16, False, None),
            ((rows, width), F32, False, None),
            ((8, width), F32, True, None),
            ((steps, CHUNK), F32, True, None),
        ],
        [
            plain,
            plain,
            chunks,
            full,
            plain,
            pltpu.VMEM((2, half, width), BF16),
            pltpu.VMEM((steps, width, CHUNK), BF16),
            pltpu.VMEM((steps, CHUNK, width), BF16),
            plain,
            pltpu.VMEM((2, rows, CHUNK), F32),
            chunks,
            plain,
            plain,
            full,
            full,
            dma_sems(2),
            dma_sems(5),
            dma_sems(steps),
            dma_sems(steps),
            dma_sems(steps),
            dma_sems(4),
            dma_sems(steps),
        ],
        flops=4 * rows * width * hidden + 2 * rows * width * width,
        moved=4 * width * hidden + 2 * width * width + 8 * rows * hidden,
    )


def attend_backward(scalars, grad_mixed, kept):
    _, rows, width = kept["q"].shape
    pairs = width // (2 * HEAD_DIM)
    lanes = 2 * HEAD_DIM
    score_scale = HEAD_DIM**-0.5

    def kernel(s, *refs):
        @pl.when(s[2] == 1)
        def _():
            compute(*refs)

    def compute(gm, q_ref, kv, grown, full, inv, dq_out, here_out, there_out):
        qs = q_ref[0]
        keys = kv[0, 0]
        values = kv[0, 1]
        first_q = lax.broadcasted_iota(jnp.int32, (rows, lanes), 1) < HEAD_DIM
        scaled = (gm[...].astype(F32) * inv[0]).astype(BF16)
        product = scaled.astype(F32) * full[0]
        grad_q = []
        grad_k = None
        grad_v = None
        for head in range(2):
            mine = first_q if head == 0 else ~first_q
            own = jnp.where(mine, scaled, 0)
            centre = jnp.sum(jnp.where(mine, product, 0.0), axis=-1, keepdims=True)
            grad_probs = dot_nt(own, values)
            weight = grown[0, head]
            grad_scores = (weight.astype(F32) * (grad_probs - centre)).astype(BF16)
            grad_q.append(dot(grad_scores, keys))
            k_part = dot_tn(grad_scores, jnp.where(mine, qs, 0))
            v_part = dot_tn(weight, own)
            grad_k = k_part if head == 0 else grad_k + k_part
            grad_v = v_part if head == 0 else grad_v + v_part
        dq_out[...] = (jnp.where(first_q, grad_q[0], grad_q[1]) * score_scale).astype(BF16)
        grad_k = (grad_k * score_scale).astype(BF16)
        grad_v = grad_v.astype(BF16)
        here_out[0] = grad_k[:rows]
        here_out[1] = grad_v[:rows]
        there_out[0] = grad_k[rows:]
        there_out[1] = grad_v[rows:]

    column = lambda i, s: (s[0], 0, i)
    plain = lambda i, s: (0, i)
    return call(
        kernel,
        scalars,
        (pairs,),
        [
            (grad_mixed, (rows, lanes), plain),
            (kept["q"], (1, rows, lanes), column),
            (kept["kv"], (1, 2, 2 * rows, lanes), lambda i, s: (s[0], 0, 0, i)),
            (kept["grown"], (1, 2, rows, 2 * rows), lambda i, s: (s[0], i, 0, 0)),
            (kept["mixed_full"], (1, rows, lanes), column),
            (kept["inverse"], (1, rows, lanes), column),
        ],
        [
            ((rows, width), BF16, (rows, lanes), plain, None),
            ((2, rows, width), BF16, (2, rows, lanes), lambda i, s: (0, 0, i), None),
            ((2, rows, width), BF16, (2, rows, lanes), lambda i, s: (0, 0, i), None),
        ],
        flops=16 * rows * rows * width,
        moved=4 * 2 * pairs * rows * rows + 30 * rows * width,
    )


def qkv_backward(scalars, dq, dkv_here, dkv_there, w_own, w_oth, grad_res, vec, kept, grads):
    _, rows, width = kept["x"].shape
    half = width // 2

    def kernel(s, dq_ref, here, there, own, oth, gr, x_ref, v, packed_out, gx_out, relay_out,
               small_out, shift_out, a_v, b_v, p_v, w_v, gr_v, x_v, gx_v, acc,
               a_sems, b_sems, w_sems, in_sems, packed_sems, out_sems):
        @pl.when(s[2] == 0)
        def _():
            small_out[...] = jnp.zeros_like(small_out)
            shift_out[...] = jnp.zeros_like(shift_out)

        @pl.when(s[2] == 1)
        def _():
            slot = s[0]
            loads = []
            for part in range(6):
                kind, side = part % 3, part // 3
                columns = pl.ds(side * half, half)
                if kind == 0:
                    copies = [begin(dq_ref.at[:, columns], a_v.at[part], a_sems.at[part])]
                else:
                    turned = pl.ds((1 - side) * half, half)
                    copies = [
                        begin(here.at[kind - 1, :, columns], a_v.at[part], a_sems.at[part]),
                        begin(there.at[kind - 1, :, turned], b_v.at[part], b_sems.at[part]),
                    ]
                weight = own if side == 0 else oth
                copies.append(begin(weight.at[kind], w_v.at[part], w_sems.at[part]))
                loads.append(copies)
            last = [
                begin(x_ref.at[slot], x_v, in_sems.at[0]),
                begin(gr, gr_v, in_sems.at[1]),
            ]
            outs = []
            for part in range(6):
                for copy in loads[part]:
                    copy.wait()
                if part % 3 == 0:
                    packed = a_v[part]
                else:
                    packed = (a_v[part].astype(F32) + b_v[part].astype(F32)).astype(BF16)
                p_v[part] = packed
                outs.append(
                    begin(
                        p_v.at[part],
                        packed_out.at[slot, :, pl.ds(part * half, half)],
                        packed_sems.at[part],
                    )
                )
                shift_out[part : part + 1] = col_sum(packed.astype(F32))
                product = dot_nt(packed, w_v[part])
                acc[...] = product if part == 0 else acc[...] + product
            for copy in last:
                copy.wait()
            hat, scale = norm_stats(x_v[...].astype(F32))
            error = acc[...]
            grad = gr_v[...] + norm_backward(hat, scale, v[LN1G : LN1G + 1], error)
            gx_v[...] = grad.astype(BF16)
            outs.append(begin(gx_v, relay_out, out_sems.at[0]))
            outs.append(begin(gx_v, gx_out.at[slot], out_sems.at[1]))
            small_out[...] = jnp.zeros_like(small_out)
            small_out[0:1] = col_sum(error * hat)
            small_out[1:2] = col_sum(error)
            for copy in outs:
                copy.wait()

    stack = (SLOTS, rows, width)
    parts = pltpu.VMEM((6, rows, half), BF16)
    return manual(
        kernel,
        scalars,
        [
            (dq, False),
            (dkv_here, False),
            (dkv_there, False),
            (w_own, False),
            (w_oth, False),
            (grad_res, False),
            (kept["x"], False),
            (vec, True),
        ],
        [
            ((SLOTS, rows, 3 * width), BF16, False, grads.get("packed")),
            (stack, BF16, False, grads.get("input")),
            ((rows, width), BF16, False, None),
            ((8, width), F32, True, None),
            ((8, half), F32, True, None),
        ],
        [
            parts,
            parts,
            parts,
            pltpu.VMEM((6, width, half), BF16),
            pltpu.VMEM((rows, width), F32),
            pltpu.VMEM((rows, width), BF16),
            pltpu.VMEM((rows, width), BF16),
            pltpu.VMEM((rows, width), F32),
            dma_sems(6),
            dma_sems(6),
            dma_sems(6),
            dma_sems(2),
            dma_sems(6),
            dma_sems(2),
        ],
        flops=6 * rows * width * width,
        moved=6 * width * width + 16 * rows * width,
    )


def swap(block):
    return lax.ppermute(block, "tensor", [(0, 1), (1, 0)])


def ring_order(count):
    return list(range(0, count, 2)) + list(range(count - 1, 0, -2))


def ring_sum(parts):
    count = lax.axis_size("dp")
    order = ring_order(count)
    place = jnp.asarray([order.index(i) for i in range(count)], jnp.int32)[lax.axis_index("dp")]
    chunks = [part.shape[0] // (2 * count) for part in parts]
    signs = (1, -1)
    routes = [[(order[i], order[(i + s) % count]) for i in range(count)] for s in signs]

    def start(way, owner, chunk):
        return (way * count + owner % count) * chunk

    def own(way, owner):
        blocks = [
            lax.dynamic_slice_in_dim(part, start(way, owner, chunk), chunk, 0)
            for part, chunk in zip(parts, chunks)
        ]
        return blocks[0] if len(blocks) == 1 else jnp.concatenate(blocks, axis=0)

    moving = [own(w, place) for w in range(2)]
    for step in range(count - 1):
        arrived = [lax.ppermute(moving[w], "dp", routes[w]) for w in range(2)]
        moving = [
            (
                arrived[w].astype(F32) + own(w, place - signs[w] * (step + 1)).astype(F32)
            ).astype(BF16)
            for w in range(2)
        ]
    totals = [jnp.zeros(part.shape, F32) for part in parts]

    def put(totals, way, owner, block):
        done = []
        base = 0
        for total, chunk in zip(totals, chunks):
            piece = block[base : base + chunk].astype(F32)
            done.append(
                lax.dynamic_update_slice_in_dim(total, piece, start(way, owner, chunk), 0)
            )
            base += chunk
        return done

    for w in range(2):
        totals = put(totals, w, place + signs[w], moving[w])
    for step in range(count - 1):
        moving = [lax.ppermute(moving[w], "dp", routes[w]) for w in range(2)]
        for w in range(2):
            totals = put(totals, w, place - signs[w] * step, moving[w])
    return totals


def shards(
    inputs,
    cotangent,
    ln1_gain,
    ln1_bias,
    qkv_weight,
    qv_bias,
    out_weight,
    out_bias,
    scale_attn,
    ln2_gain,
    ln2_bias,
    fc1_weight,
    fc1_bias,
    fc2_weight,
    fc2_bias,
    scale_mlp,
):
    section = lax.axis_index("section")
    rank = lax.axis_index("tensor")
    micro, images, seq_len, half = inputs.shape
    assert micro == 2 and images == 1
    width = 2 * half
    rows = seq_len // 2
    hidden_half = fc1_weight.shape[2]
    low = rank == 0

    def whole_width(own, oth):
        return jnp.where(
            low, jnp.concatenate([own, oth], axis=-1), jnp.concatenate([oth, own], axis=-1)
        )

    def partner_tokens(block):
        return lax.dynamic_slice_in_dim(block, (1 - rank) * rows, rows, block.ndim - 2)

    def by_features(block):
        def part(index):
            return lax.dynamic_slice_in_dim(block, index * half, half, 2)

        own, oth = part(rank), swap(part(1 - rank))
        return jnp.where(
            low, jnp.concatenate([own, oth], axis=1), jnp.concatenate([oth, own], axis=1)
        )

    vectors = jnp.concatenate(
        [
            ln1_gain,
            ln1_bias,
            out_bias,
            scale_attn,
            ln2_gain,
            ln2_bias,
            fc2_bias,
            scale_mlp,
            qv_bias[0],
            fc1_bias.reshape(hidden_half // half, half),
        ],
        axis=0,
    )
    first_oth = swap(partner_tokens(inputs[0, 0]))
    vectors_oth = swap(vectors)
    wq_own = jnp.transpose(qkv_weight[0], (1, 0, 2))
    wq_oth = swap(wq_own)
    wo_own, wu_own, wd_own = out_weight[0], fc1_weight[0], fc2_weight[0]
    wo_late, wu_late, wd_late, first_oth = lax.optimization_barrier(
        (wo_own, wu_own, wd_own, first_oth)
    )
    wo_oth = swap(wo_late)
    wu_oth = swap(wu_late)
    wd_oth = swap(wd_late)
    later = jnp.stack([inputs[1, 0], cotangent[0, 0], cotangent[1, 0]])
    later_oth = swap(partner_tokens(later))
    in_oth = [first_oth, later_oth[0], later_oth[0]]
    cot_oth = [later_oth[1], later_oth[2], later_oth[2]]
    vec = whole_width(vectors[:8], vectors_oth[:8]).astype(F32)
    bias_q = jnp.concatenate([vectors[8:9], vectors_oth[8:9]], axis=1).astype(F32)
    bias_v = jnp.concatenate([vectors[9:10], vectors_oth[9:10]], axis=1).astype(F32)
    b_up = jnp.concatenate([vectors[10:], vectors_oth[10:]], axis=0).astype(F32)
    b_up = b_up.reshape(2 * hidden_half // CHUNK, CHUNK)

    def tick_scalars(number):
        active = (number >= 0) & (number < micro)
        slot = jnp.where(active, number, micro)
        return jnp.stack([slot, section, active.astype(jnp.int32), rank]).astype(jnp.int32)

    kept = {}
    received = jnp.zeros((rows, width), BF16)
    for tick in range(micro + 1):
        scalars = tick_scalars(tick - section)
        number = min(tick, micro - 1)
        kept["x"], kept["normed1"], kv_here = norm_kv(
            scalars, inputs, number, in_oth[tick], received, vec, wq_own, wq_oth, bias_v, kept
        )
        kv_there = swap(kv_here)
        kept["q"] = project_q(scalars, kept["normed1"], wq_own, wq_oth, bias_q, kept)
        kept["grown"], kept["mixed_full"], kept["mixed"], kept["inverse"], kept["kv"] = attend(
            scalars, kept["q"], kv_here, kv_there, kept
        )
        (
            kept["attended"],
            kept["residual"],
            kept["normed2"],
            kept["active"],
            kept["slope"],
            kept["branch"],
            kept["output"],
            relayed,
        ) = mlp_forward(
            scalars, kept["mixed"], kept["x"], vec, wo_own, wo_oth, wu_own, wu_oth, wd_own,
            wd_oth, b_up, kept,
        )
        if tick < micro:
            received = lax.ppermute(relayed, "section", [(0, 1)])

    block_outputs = by_features(kept["output"][:micro])

    def weight_grad(left, right):
        return lax.dot_general(
            left, right, (((0, 1), (0, 1)), ((), ())), preferred_element_type=F32
        ).astype(BF16)

    def paired(own, oth):
        return (own.astype(F32) + swap(oth).astype(F32)).astype(BF16)

    def both(name, part):
        return part[name][:micro]

    grads = {}
    received = jnp.zeros((rows, width), BF16)
    small_two = small_one = shift_up = shift_qkv = None
    for tick in range(micro + 1):
        scalars = tick_scalars(tick - 1 + section)
        number = min(tick, micro - 1)
        (
            grads["branch"],
            grads["before"],
            grads["attended"],
            grad_mixed,
            grad_res,
            small_b,
            shift_b,
        ) = mlp_backward(
            scalars, cotangent, number, cot_oth[tick], received, vec, wo_own, wo_oth, wu_own,
            wu_oth, wd_own, wd_oth, kept, grads,
        )
        if tick == micro:
            active = both("active", kept)
            g_branch = both("branch", grads)
            grad_down = paired(
                weight_grad(active[:, :, :hidden_half], g_branch),
                weight_grad(active[:, :, hidden_half:], g_branch),
            )
            normed2 = both("normed2", kept)
            before = both("before", grads)
            grad_up = paired(
                weight_grad(normed2, before[:, :, :hidden_half]),
                weight_grad(normed2, before[:, :, hidden_half:]),
            )
            grad_down, grad_up, grad_mixed = lax.optimization_barrier(
                (grad_down, grad_up, grad_mixed)
            )
        dq, dkv_here, dkv_send = attend_backward(scalars, grad_mixed, kept)
        dkv_there = swap(dkv_send)
        grads["packed"], grads["input"], relayed, small_a, shift_a = qkv_backward(
            scalars, dq, dkv_here, dkv_there, wq_own, wq_oth, grad_res, vec, kept, grads
        )
        if tick == 0:
            small_two, small_one, shift_up, shift_qkv = small_b, small_a, shift_b, shift_a
        else:
            small_two += small_b
            small_one += small_a
            shift_up += shift_b
            shift_qkv += shift_a
        if tick < micro:
            received = lax.ppermute(relayed, "section", [(1, 0)])

    total_down = lax.psum(grad_down, "dp").astype(F32)
    (total_up,) = ring_sum([grad_up])
    mixed = both("mixed", kept)
    g_att = both("attended", grads)
    grad_out = paired(
        weight_grad(mixed[:, :, :half], g_att), weight_grad(mixed[:, :, half:], g_att)
    )
    normed1 = both("normed1", kept)
    packed = both("packed", grads)

    def qkv_grad(base):
        return jnp.concatenate(
            [
                weight_grad(normed1, packed[:, :, (base + j) * half : (base + j + 1) * half])
                for j in range(3)
            ],
            axis=0,
        )

    grad_qkv = paired(qkv_grad(0), qkv_grad(3))

    feature_sums = jnp.concatenate([small_one[:2], small_two[:6]], axis=0)

    def feature_part(index):
        return lax.dynamic_slice_in_dim(feature_sums, index * half, half, 1)

    up_rows = shift_up.reshape(2, hidden_half // half, half)
    small_own = jnp.concatenate([feature_part(rank), shift_qkv[0:3], up_rows[0]], axis=0)
    small_oth = jnp.concatenate([feature_part(1 - rank), shift_qkv[3:6], up_rows[1]], axis=0)
    small = paired(small_own.astype(BF16), small_oth.astype(BF16))
    unit = 16 * lax.axis_size("dp")
    small = jnp.concatenate([small, jnp.zeros((-small.shape[0] % unit, half), BF16)], axis=0)
    total_qkv, out_left, out_right, sums = ring_sum(
        [grad_qkv, grad_out[:, :half], grad_out[:, half:], small]
    )
    total_qkv = total_qkv.reshape(3, width, half)
    total_out = jnp.concatenate([out_left, out_right], axis=1)
    input_grads = by_features(grads["input"][:micro])

    def row(number):
        return sums[number][None]

    return (
        block_outputs.reshape(1, micro, images, seq_len, half),
        input_grads.reshape(1, micro, images, seq_len, half),
        row(0),
        row(1),
        jnp.transpose(total_qkv, (1, 0, 2))[None],
        jnp.stack([sums[8], sums[10]])[None],
        total_out[None],
        row(7),
        row(6),
        row(4),
        row(5),
        total_up[None],
        sums[11 : 11 + hidden_half // half].reshape(1, hidden_half),
        total_down[None],
        row(3),
        row(2),
    )


def solution(mesh):
    placed = (
        P(None, "dp", None, "tensor"),
        P(None, "dp", None, "tensor"),
        P("section", "tensor"),
        P("section", "tensor"),
        P("section", None, None, "tensor"),
        P("section", None, "tensor"),
        P("section", "tensor", None),
        P("section", "tensor"),
        P("section", "tensor"),
        P("section", "tensor"),
        P("section", "tensor"),
        P("section", None, "tensor"),
        P("section", "tensor"),
        P("section", "tensor", None),
        P("section", "tensor"),
        P("section", "tensor"),
    )
    return jax.shard_map(
        shards,
        mesh=mesh,
        in_specs=placed,
        out_specs=(
            P("section", None, "dp", None, "tensor"),
            P("section", None, "dp", None, "tensor"),
            P("section", "tensor"),
            P("section", "tensor"),
            P("section", None, None, "tensor"),
            P("section", None, "tensor"),
            P("section", "tensor", None),
            P("section", "tensor"),
            P("section", "tensor"),
            P("section", "tensor"),
            P("section", "tensor"),
            P("section", None, "tensor"),
            P("section", "tensor"),
            P("section", "tensor", None),
            P("section", "tensor"),
            P("section", "tensor"),
        ),
        check_vma=False,
    )
```

```python
import math

import jax
import jax.numpy as jnp
from jax import lax
from jax.experimental import pallas as pl
from jax.experimental.pallas import tpu as pltpu
from jax.sharding import PartitionSpec as P

HEAD_DIM = 64
EPSILON = 1e-06
F32 = jnp.float32
BF16 = jnp.bfloat16
MIB = 1 << 20
VMEM_MIB = 62
TILE = 16
MICRO = 2
SPARE = MICRO
RANK, ACTIVE, UNITS = 0, 1, 3
LN1G, LN1B, OUTB, SATT, LN2G, LN2B, FC2B, SMLP = range(8)


def dot(left, right):
    return jnp.dot(left, right, preferred_element_type=F32)


def dot_nt(left, right):
    return lax.dot_general(left, right, (((1,), (1,)), ((), ())), preferred_element_type=F32)


def dot_tn(left, right):
    return lax.dot_general(left, right, (((0,), (0,)), ((), ())), preferred_element_type=F32)


def norm_stats(values):
    centre = jnp.mean(values, axis=-1, keepdims=True)
    centred = values - centre
    spread = jnp.mean(centred * centred, axis=-1, keepdims=True)
    scale = lax.rsqrt(spread + EPSILON)
    return centred * scale, scale


def tiles(rows):
    return [slice(r, r + TILE) for r in range(0, rows, TILE)]


def eights(values):
    total = values[:8]
    for r in range(8, values.shape[0], 8):
        total = total + values[r : r + 8]
    return total


def norm_backward(hat, scale, gain, error):
    weighted = error * gain
    mean_one = jnp.mean(weighted, axis=-1, keepdims=True)
    mean_two = jnp.mean(weighted * hat, axis=-1, keepdims=True)
    return scale * (weighted - mean_one - hat * mean_two)


def col_sum(values):
    return jnp.sum(values, axis=0, keepdims=True)


def call(kernel, scalars, grid, ins, outs, scratch=(), flops=0, moved=0):
    arrays = [a for a, _, _ in ins]
    in_specs = [pl.BlockSpec(b, m) for _, b, m in ins]
    aliases = {}
    for number, out in enumerate(outs):
        if out[4] is not None:
            aliases[1 + len(arrays)] = number
            arrays.append(out[4])
            in_specs.append(pl.BlockSpec(memory_space=pl.ANY))
    extra = len(aliases)
    in_count = len(ins)

    def body(*refs):
        kernel(*refs[: 1 + in_count], *refs[1 + in_count + extra :])

    return pl.pallas_call(
        body,
        out_shape=[jax.ShapeDtypeStruct(s, d) for s, d, _, _, _ in outs],
        grid_spec=pltpu.PrefetchScalarGridSpec(
            num_scalar_prefetch=1,
            grid=grid,
            in_specs=in_specs,
            out_specs=[pl.BlockSpec(b, m) for _, _, b, m, _ in outs],
            scratch_shapes=list(scratch),
        ),
        input_output_aliases=aliases,
        compiler_params=pltpu.CompilerParams(
            dimension_semantics=("arbitrary",) * len(grid), vmem_limit_bytes=VMEM_MIB * MIB
        ),
        cost_estimate=pl.CostEstimate(
            flops=int(flops), bytes_accessed=int(moved), transcendentals=0
        ),
    )(scalars, *arrays)


def manual(kernel, scalars, ins, outs, scratch, flops=0, moved=0, vmem=VMEM_MIB):
    any_space = pl.BlockSpec(memory_space=pl.ANY)
    vmem_space = pl.BlockSpec(memory_space=pltpu.VMEM)
    arrays = [a for a, _ in ins]
    in_specs = [vmem_space if inside else any_space for _, inside in ins]
    aliases = {}
    for number, out in enumerate(outs):
        if out[3] is not None:
            aliases[1 + len(arrays)] = number
            arrays.append(out[3])
            in_specs.append(any_space)
    extra = len(aliases)
    in_count = len(ins)

    def body(*refs):
        kernel(*refs[: 1 + in_count], *refs[1 + in_count + extra :])

    return pl.pallas_call(
        body,
        out_shape=[jax.ShapeDtypeStruct(s, d) for s, d, _, _ in outs],
        in_specs=[pl.BlockSpec(memory_space=pltpu.SMEM)] + in_specs,
        out_specs=[vmem_space if inside else any_space for _, _, inside, _ in outs],
        scratch_shapes=list(scratch),
        input_output_aliases=aliases,
        compiler_params=pltpu.CompilerParams(vmem_limit_bytes=vmem * MIB),
        cost_estimate=pl.CostEstimate(
            flops=int(flops), bytes_accessed=int(moved), transcendentals=0
        ),
    )(scalars, *arrays)


def begin(src, dst, sem):
    copy = pltpu.make_async_copy(src, dst, sem)
    copy.start()
    return copy


def dma_sems(count):
    return pltpu.SemaphoreType.DMA((count,))


def whole2(i, s):
    return (0, 0)


def slot3(i, s):
    return (s[0], 0, 0)


def token_copies(s, source, number, refs, target, sems):
    rows, width = target.shape
    half = width // 2
    rank = s[RANK]
    if source == "relay":
        return [begin(refs[0], target, sems.at[0])]
    first = pl.multiple_of(rank * half, half)
    second = pl.multiple_of((1 - rank) * half, half)
    whole, other = refs
    return [
        begin(
            whole.at[number, 0, pl.ds(pl.multiple_of(rank * rows, rows), rows)],
            target.at[:, pl.ds(first, half)],
            sems.at[0],
        ),
        begin(other, target.at[:, pl.ds(second, half)], sems.at[1]),
    ]


def norm_kv(info, owner, number, source, tokens, vec, w_own, w_oth, bias_v, kept):
    rows, width = tokens[-1].shape[0], vec.shape[1]
    half = width // 2
    count = len(tokens)

    def kernel(s, *refs):
        token_refs = refs[:count]
        (v, own, oth, bv, x_out, n_out, kv_out, x_v, n_v, w_v, kv_v, tok_sems, w_sems,
         out_sems) = refs[count:]

        @pl.when(s[ACTIVE + owner] == 1)
        def _():
            arriving = token_copies(s, source, number, token_refs, x_v, tok_sems)
            loads = []
            for part in range(4):
                ref = own if part < 2 else oth
                loads.append(begin(ref.at[1 + part % 2], w_v.at[part], w_sems.at[part]))
            for copy in arriving:
                copy.wait()
            outs = [begin(x_v, x_out.at[number], out_sems.at[0])]
            for t in tiles(rows):
                hat, _ = norm_stats(x_v[t].astype(F32))
                n_v[t] = (hat * v[LN1G : LN1G + 1] + v[LN1B : LN1B + 1]).astype(BF16)
            outs.append(begin(n_v, n_out.at[number], out_sems.at[1]))
            for part in range(4):
                loads[part].wait()
                result = dot(n_v[...], w_v[part])
                kind, side = part % 2, part // 2
                columns = slice(side * half, (side + 1) * half)
                if kind == 1:
                    result = result + bv[:, columns]
                kv_v[part] = result.astype(BF16)
                outs.append(
                    begin(
                        kv_v.at[part],
                        kv_out.at[kind, :, pl.ds(side * half, half)],
                        out_sems.at[2 + part],
                    )
                )
            for copy in outs:
                copy.wait()

    stack = (MICRO, rows, width)
    return manual(
        kernel,
        info,
        [(array, False) for array in tokens]
        + [(vec, True), (w_own, False), (w_oth, False), (bias_v, True)],
        [
            (stack, BF16, False, kept.get("x")),
            (stack, BF16, False, kept.get("normed1")),
            ((2, rows, width), BF16, False, None),
        ],
        [
            pltpu.VMEM((rows, width), BF16),
            pltpu.VMEM((rows, width), BF16),
            pltpu.VMEM((4, width, half), BF16),
            pltpu.VMEM((4, rows, half), BF16),
            dma_sems(2),
            dma_sems(4),
            dma_sems(6),
        ],
        flops=2 * rows * width * 2 * width,
        moved=4 * width * width + 10 * rows * width,
    )


def project_q(info, owner, number, normed, w_own, w_oth, bias_q, kept):
    _, rows, width = normed.shape
    half = width // 2

    def kernel(s, n, own, oth, bq, q_out, n_v, w_v, q_v, in_sems, out_sems):
        @pl.when(s[ACTIVE + owner] == 1)
        def _():
            load = begin(n.at[number], n_v, in_sems.at[0])
            loads = [
                begin(own.at[0], w_v.at[0], in_sems.at[1]),
                begin(oth.at[0], w_v.at[1], in_sems.at[2]),
            ]
            load.wait()
            outs = []
            for side in range(2):
                loads[side].wait()
                columns = slice(side * half, (side + 1) * half)
                q_v[side] = (dot(n_v[...], w_v[side]) + bq[:, columns]).astype(BF16)
                outs.append(
                    begin(
                        q_v.at[side],
                        q_out.at[number, :, pl.ds(side * half, half)],
                        out_sems.at[side],
                    )
                )
            for copy in outs:
                copy.wait()

    return manual(
        kernel,
        info,
        [(normed, False), (w_own, False), (w_oth, False), (bias_q, True)],
        [((MICRO, rows, width), BF16, False, kept.get("q"))],
        [
            pltpu.VMEM((rows, width), BF16),
            pltpu.VMEM((2, width, half), BF16),
            pltpu.VMEM((2, rows, half), BF16),
            dma_sems(3),
            dma_sems(2),
        ],
        flops=2 * rows * width * width,
        moved=2 * width * width + 4 * rows * width,
    )[0]


def attend(info, owner, number, q, kv_here, kv_there, kept):
    _, rows, width = q.shape
    heads = width // HEAD_DIM
    factor = HEAD_DIM**-0.5 * math.log2(math.e)
    lanes = 2 * HEAD_DIM
    block = 2 * lanes
    steps = width // block

    def kernel(s, *refs):
        @pl.when(s[ACTIVE + owner] == 1)
        def _():
            compute(*refs)

    def compute(q_ref, here, there, e_out, o_out, mixed_out, inv_out, kv_out, *scratch):
        scores, results = scratch[:4], scratch[4:]
        kv_out[0, :, :rows] = here[...]
        kv_out[0, :, rows:] = there[...]
        first_q = lax.broadcasted_iota(jnp.int32, (rows, lanes), 1) < HEAD_DIM
        first_k = lax.broadcasted_iota(jnp.int32, (2 * rows, lanes), 1) < HEAD_DIM
        first_t = lax.broadcasted_iota(jnp.int32, (TILE, lanes), 1) < HEAD_DIM

        def columns(head):
            return slice(head // 2 * lanes, (head // 2 + 1) * lanes)

        def score(head):
            mine = first_q if head % 2 == 0 else ~first_q
            masked = jnp.where(mine, q_ref[0, :, columns(head)], 0)
            scores[head][...] = dot_nt(masked, kv_out[0, 0, :, columns(head)])

        score(0)
        for head in range(4):
            if head < 3:
                score(head + 1)
            for t in tiles(rows):
                tile = scores[head][t]
                top = jnp.max(tile, axis=-1, keepdims=True)
                e_out[0, head, t] = jnp.exp2((tile - top) * factor).astype(BF16)
            mine = first_k if head % 2 == 0 else ~first_k
            values = jnp.where(mine, kv_out[0, 1, :, columns(head)], 1)
            results[head][...] = dot(e_out[0, head], values)
        for pair in range(2):
            place = slice(pair * lanes, (pair + 1) * lanes)
            for t in tiles(rows):
                one, two = results[2 * pair][t], results[2 * pair + 1][t]
                total = jnp.where(
                    first_t, pltpu.roll(one, HEAD_DIM, 1), pltpu.roll(two, HEAD_DIM, 1)
                )
                inverse = 1.0 / total
                mixed = jnp.where(first_t, one, two) * inverse
                o_out[0, t, place] = mixed
                mixed_out[t, place] = mixed.astype(BF16)
                inv_out[0, t, place] = inverse

    def on(s):
        return s[ACTIVE + owner]

    def slot(s):
        return jnp.where(on(s) == 1, number, SPARE)

    column = lambda i, s: (slot(s), 0, i * on(s))
    spare = MICRO + 1
    return call(
        kernel,
        info,
        (steps,),
        [
            (q, (1, rows, block), lambda i, s: (number, 0, i * on(s))),
            (kv_here, (2, rows, block), lambda i, s: (0, 0, i * on(s))),
            (
                kv_there,
                (2, rows, block),
                lambda i, s: (0, 0, lax.rem(i + steps // 2, steps) * on(s)),
            ),
        ],
        [
            (
                (spare, heads, rows, 2 * rows),
                BF16,
                (1, 4, rows, 2 * rows),
                lambda i, s: (slot(s), i * on(s), 0, 0),
                kept.get("grown"),
            ),
            ((spare, rows, width), F32, (1, rows, block), column, kept.get("mixed_full")),
            ((rows, width), BF16, (rows, block), lambda i, s: (0, i * on(s)), None),
            ((spare, rows, width), F32, (1, rows, block), column, kept.get("inverse")),
            (
                (spare, 2, 2 * rows, width),
                BF16,
                (1, 2, 2 * rows, block),
                lambda i, s: (slot(s), 0, 0, i * on(s)),
                kept.get("kv"),
            ),
        ],
        [pltpu.VMEM((rows, 2 * rows), F32)] * 4 + [pltpu.VMEM((rows, lanes), F32)] * 4,
        flops=8 * rows * rows * width,
        moved=4 * heads * rows * rows + 30 * rows * width,
    )


def gelu_parts(x):
    size = jnp.abs(x)
    base = 1.0 + (0.3275911 * math.sqrt(0.5)) * size
    t = pl.reciprocal(base, approx=True)
    t = t * (2.0 - base * t)
    grown = jnp.exp2(x * x * (-0.5 * math.log2(math.e)))
    poly = 0.5 * 1.061405429
    for factor in (-1.453152027, 1.421413741, -0.284496736, 0.254829592):
        poly = poly * t + 0.5 * factor
    tail = poly * t * grown
    below = jnp.where(x < 0.0, tail, 1.0 - tail)
    return x * below, below + x * grown * (1.0 / math.sqrt(2.0 * math.pi))


CHUNK = 512


def mlp_forward(info, owner, number, mixed, x, vec, wo_own, wo_oth, wu_own, wu_oth, wd_own, wd_oth, b_up, kept):
    _, rows, width = x.shape
    side_hidden = wu_own.shape[1]
    hidden = 2 * side_hidden
    half = width // 2
    steps = hidden // CHUNK
    split = steps // 2

    def kernel(
        s, m, x_ref, v, woo, wot, wuo, wut, wdo, wdt, bu,
        att_out, res_out, n_out, act_out, slope_out, branch_out, y_out, relay_out, m_out,
        m_v, x_v, wo_v, wu_v, wd_v, att_v, res_v, n_v, h_v, act_v, slope_v, branch_v, y_v, acc,
        in_sems, wu_sems, wd_sems, out_sems, act_sems, slope_sems,
    ):
        @pl.when(s[ACTIVE + owner] == 1)
        def _():
            slot = number
            first = [
                begin(m, m_v, in_sems.at[0]),
                begin(woo, wo_v.at[0], in_sems.at[1]),
                begin(wot, wo_v.at[1], in_sems.at[2]),
                begin(x_ref.at[slot], x_v, in_sems.at[3]),
            ]
            ups, downs = [], []

            def prefetch(i):
                if i < steps:
                    part = pl.ds((i % split) * CHUNK, CHUNK)
                    up, down = (wuo, wdo) if i < split else (wut, wdt)
                    ups.append(begin(up.at[:, part], wu_v.at[i], wu_sems.at[i]))
                    downs.append(begin(down.at[part], wd_v.at[i], wd_sems.at[i]))

            prefetch(0)
            prefetch(1)
            for copy in first:
                copy.wait()
            acc[...] = dot(m_v[:, :half], wo_v[0]) + dot(m_v[:, half:], wo_v[1])
            for t in tiles(rows):
                attended = acc[t] + v[OUTB : OUTB + 1]
                att_v[t] = attended.astype(BF16)
                residual = x_v[t].astype(F32) + v[SATT : SATT + 1] * attended
                res_v[t] = residual
                hat, _ = norm_stats(residual)
                n_v[t] = (hat * v[LN2G : LN2G + 1] + v[LN2B : LN2B + 1]).astype(BF16)
            outs = [
                begin(att_v, att_out.at[slot], out_sems.at[0]),
                begin(res_v, res_out.at[slot], out_sems.at[1]),
                begin(n_v, n_out.at[slot], out_sems.at[2]),
                begin(m_v, m_out.at[slot], out_sems.at[6]),
            ]

            def up_product(i):
                ups[i].wait()
                h_v[i % 2] = dot(n_v[...], wu_v[i])

            def down_product(i):
                downs[i].wait()
                part = pl.ds(i * CHUNK, CHUNK)
                outs.append(begin(act_v.at[i], act_out.at[slot, :, part], act_sems.at[i]))
                outs.append(begin(slope_v.at[i], slope_out.at[slot, :, part], slope_sems.at[i]))
                product = dot(act_v[i], wd_v[i])
                acc[...] = product if i == 0 else acc[...] + product

            up_product(0)
            for i in range(steps):
                prefetch(i + 2)
                if i > 0:
                    down_product(i - 1)
                if i + 1 < steps:
                    up_product(i + 1)
                for t in tiles(rows):
                    active, slope = gelu_parts(h_v[i % 2, t] + bu[i : i + 1])
                    act_v[i, t] = active.astype(BF16)
                    slope_v[i, t] = slope.astype(BF16)
            down_product(steps - 1)
            for t in tiles(rows):
                branch = acc[t] + v[FC2B : FC2B + 1]
                y_v[t] = (res_v[t] + v[SMLP : SMLP + 1] * branch).astype(BF16)
                branch_v[t] = branch.astype(BF16)
            outs.append(begin(y_v, relay_out, out_sems.at[3]))
            outs.append(begin(y_v, y_out.at[slot], out_sems.at[4]))
            outs.append(begin(branch_v, branch_out.at[slot], out_sems.at[5]))
            for copy in outs:
                copy.wait()

    stack = (MICRO, rows, width)
    tall = (MICRO, rows, hidden)
    plain = pltpu.VMEM((rows, width), BF16)
    full = pltpu.VMEM((rows, width), F32)
    chunks = pltpu.VMEM((steps, rows, CHUNK), BF16)
    return manual(
        kernel,
        info,
        [
            (mixed, False),
            (x, False),
            (vec, True),
            (wo_own, False),
            (wo_oth, False),
            (wu_own, False),
            (wu_oth, False),
            (wd_own, False),
            (wd_oth, False),
            (b_up, True),
        ],
        [
            (stack, BF16, False, kept.get("attended")),
            (stack, F32, False, kept.get("residual")),
            (stack, BF16, False, kept.get("normed2")),
            (tall, BF16, False, kept.get("active")),
            (tall, BF16, False, kept.get("slope")),
            (stack, BF16, False, kept.get("branch")),
            (stack, BF16, False, kept.get("output")),
            ((rows, width), BF16, False, None),
            (stack, BF16, False, kept.get("mixed")),
        ],
        [
            plain,
            plain,
            pltpu.VMEM((2, half, width), BF16),
            pltpu.VMEM((steps, width, CHUNK), BF16),
            pltpu.VMEM((steps, CHUNK, width), BF16),
            plain,
            full,
            plain,
            pltpu.VMEM((2, rows, CHUNK), F32),
            chunks,
            chunks,
            plain,
            plain,
            full,
            dma_sems(4),
            dma_sems(steps),
            dma_sems(steps),
            dma_sems(7),
            dma_sems(steps),
            dma_sems(steps),
        ],
        flops=4 * rows * width * hidden + 2 * rows * width * width,
        moved=4 * width * hidden + 2 * width * width + 8 * rows * hidden,
    )


def scale_branch(info, owner, number, relay, vec, earlier):
    rows, width = relay.shape

    def kernel(s, g, v, gb_out, g_v, gb_v, sems):
        @pl.when(s[ACTIVE + owner] == 1)
        def _():
            begin(g, g_v, sems.at[0]).wait()
            gb_v[...] = (v[SMLP : SMLP + 1] * g_v[...].astype(F32)).astype(BF16)
            begin(gb_v, gb_out.at[number], sems.at[1]).wait()

    return manual(
        kernel,
        info,
        [(relay, False), (vec, True)],
        [((MICRO, rows, width), BF16, False, earlier)],
        [pltpu.VMEM((rows, width), BF16), pltpu.VMEM((rows, width), BF16), dma_sems(2)],
        moved=4 * rows * width,
    )[0]


def mlp_backward(info, owner, number, source, tokens, vec, wo_own, wo_oth, wu_own, wu_oth, wd_own, wd_oth, kept, grads, scaled):
    count = len(tokens)
    _, rows, width = kept["x"].shape
    side_hidden = wu_own.shape[1]
    hidden = 2 * side_hidden
    half = width // 2
    steps = hidden // CHUNK
    split = steps // 2

    def kernel(s, *refs):
        work(s, refs[:count], *refs[count:])

    def work(
        s, token_refs, branch, slope, res, att, v, woo, wot, wuo, wut, wdo, wdt,
        gb_out, before_out, ga_out, gm_out, gr_out, small_out, shift_out,
        g_v, branch_v, slope_v, res_v, att_v, wo_v, wu_v, wd_v, gb_v, d_v, before_v, ga_v, gm_v,
        gr_v, acc, sums, tok_sems, in_sems, slope_sems, wu_sems, wd_sems, out_sems, before_sems,
    ):
        @pl.when(s[ACTIVE + owner] == 0)
        def _():
            small_out[...] = jnp.zeros_like(small_out)
            shift_out[...] = jnp.zeros_like(shift_out)

        @pl.when(s[ACTIVE + owner] == 1)
        def _():
            slot = number
            arriving = token_copies(s, source, number, token_refs, g_v, tok_sems)
            ups, downs, slopes = [], [], []

            def prefetch(i):
                if i < steps:
                    part = pl.ds((i % split) * CHUNK, CHUNK)
                    up, down = (wuo, wdo) if i < split else (wut, wdt)
                    here = pl.ds(i * CHUNK, CHUNK)
                    downs.append(begin(down.at[part], wd_v.at[i], wd_sems.at[i]))
                    slopes.append(begin(slope.at[slot, :, here], slope_v.at[i], slope_sems.at[i]))
                    ups.append(begin(up.at[:, part], wu_v.at[i], wu_sems.at[i]))

            prefetch(0)
            branch_in = begin(branch.at[slot], branch_v, in_sems.at[0])
            prefetch(1)
            last = []
            for copy in arriving:
                copy.wait()
            for t in tiles(rows):
                gb_v[t] = (v[SMLP : SMLP + 1] * g_v[t].astype(F32)).astype(BF16)
            outs = []
            if not scaled:
                outs.append(begin(gb_v, gb_out.at[slot], out_sems.at[0]))

            def down_product(i):
                downs[i].wait()
                d_v[i % 2] = dot_nt(gb_v[...], wd_v[i])

            down_product(0)
            branch_in.wait()
            sums[...] = jnp.zeros_like(sums)
            for t in tiles(rows):
                sums[0] += eights(g_v[t].astype(F32) * branch_v[t].astype(F32))
                sums[1] += eights(gb_v[t].astype(F32))

            def up_product(i):
                ups[i].wait()
                part = pl.ds(i * CHUNK, CHUNK)
                outs.append(begin(before_v.at[i], before_out.at[slot, :, part], before_sems.at[i]))
                product = dot_nt(before_v[i], wu_v[i])
                acc[...] = product if i == 0 else acc[...] + product

            for i in range(steps):
                prefetch(i + 2)
                if i == steps - 2:
                    last = [
                        begin(res.at[slot], res_v, in_sems.at[1]),
                        begin(att.at[slot], att_v, in_sems.at[2]),
                        begin(woo, wo_v.at[0], in_sems.at[3]),
                        begin(wot, wo_v.at[1], in_sems.at[4]),
                    ]
                slopes[i].wait()
                if i > 0:
                    up_product(i - 1)
                if i + 1 < steps:
                    down_product(i + 1)
                total = jnp.zeros((8, CHUNK), F32)
                for t in tiles(rows):
                    grad_before = (d_v[i % 2, t] * slope_v[i, t].astype(F32)).astype(BF16)
                    before_v[i, t] = grad_before
                    total = total + eights(grad_before.astype(F32))
                shift_out[i : i + 1] = col_sum(total)
            up_product(steps - 1)
            for copy in last:
                copy.wait()
            for t in tiles(rows):
                hat, scale = norm_stats(res_v[t])
                error = acc[t]
                sums[2] += eights(error * hat)
                sums[3] += eights(error)
                grad = g_v[t].astype(F32) + norm_backward(hat, scale, v[LN2G : LN2G + 1], error)
                gr_v[t] = grad
                sums[4] += eights(grad * att_v[t].astype(F32))
                ga = (v[SATT : SATT + 1] * grad).astype(BF16)
                ga_v[t] = ga
                sums[5] += eights(ga.astype(F32))
            outs.append(begin(ga_v, ga_out.at[slot], out_sems.at[1]))
            outs.append(begin(gr_v, gr_out, out_sems.at[3]))
            gm_v[:, :half] = dot_nt(ga_v[...], wo_v[0]).astype(BF16)
            gm_v[:, half:] = dot_nt(ga_v[...], wo_v[1]).astype(BF16)
            outs.append(begin(gm_v, gm_out, out_sems.at[2]))
            small_out[...] = jnp.zeros_like(small_out)
            for row in range(6):
                small_out[row : row + 1] = col_sum(sums[row])
            for copy in outs:
                copy.wait()

    stack = (MICRO, rows, width)
    plain = pltpu.VMEM((rows, width), BF16)
    full = pltpu.VMEM((rows, width), F32)
    chunks = pltpu.VMEM((steps, rows, CHUNK), BF16)
    return manual(
        kernel,
        info,
        [(array, False) for array in tokens]
        + [
            (kept["branch"], False),
            (kept["slope"], False),
            (kept["residual"], False),
            (kept["attended"], False),
            (vec, True),
            (wo_own, False),
            (wo_oth, False),
            (wu_own, False),
            (wu_oth, False),
            (wd_own, False),
            (wd_oth, False),
        ],
        [
            (stack, BF16, False, None if scaled else grads.get("branch")),
            ((MICRO, rows, hidden), BF16, False, grads.get("before")),
            (stack, BF16, False, grads.get("attended")),
            ((rows, width), BF16, False, None),
            ((rows, width), F32, False, None),
            ((8, width), F32, True, None),
            ((steps, CHUNK), F32, True, None),
        ],
        [
            plain,
            plain,
            chunks,
            full,
            plain,
            pltpu.VMEM((2, half, width), BF16),
            pltpu.VMEM((steps, width, CHUNK), BF16),
            pltpu.VMEM((steps, CHUNK, width), BF16),
            plain,
            pltpu.VMEM((2, rows, CHUNK), F32),
            chunks,
            plain,
            plain,
            full,
            full,
            pltpu.VMEM((6, 8, width), F32),
            dma_sems(2),
            dma_sems(5),
            dma_sems(steps),
            dma_sems(steps),
            dma_sems(steps),
            dma_sems(4),
            dma_sems(steps),
        ],
        flops=4 * rows * width * hidden + 2 * rows * width * width,
        moved=4 * width * hidden + 2 * width * width + 8 * rows * hidden,
    )


def attend_backward(info, owner, number, grad_mixed, kept):
    _, rows, width = kept["q"].shape
    heads = width // HEAD_DIM
    lanes = 2 * HEAD_DIM
    block = 2 * lanes
    steps = width // block
    score_scale = HEAD_DIM**-0.5

    def kernel(s, *refs):
        @pl.when(s[ACTIVE + owner] == 1)
        def _():
            compute(*refs)

    def compute(gm, q_ref, kv, grown, full, inv, dq_out, here_out, there_out, *scratch):
        probs, scores = scratch[:4], scratch[4:8]
        own_v, centre_v = scratch[8:]
        first_q = lax.broadcasted_iota(jnp.int32, (rows, lanes), 1) < HEAD_DIM
        first_t = lax.broadcasted_iota(jnp.int32, (TILE, lanes), 1) < HEAD_DIM

        def columns(head):
            return slice(head // 2 * lanes, (head // 2 + 1) * lanes)

        for pair in range(2):
            place = columns(2 * pair)
            for t in tiles(rows):
                scaled = (gm[t, place].astype(F32) * inv[0, t, place]).astype(BF16)
                product = scaled.astype(F32) * full[0, t, place]
                for side in range(2):
                    mine = first_t if side == 0 else ~first_t
                    own_v[2 * pair + side, t] = jnp.where(mine, scaled, 0)
                    centre_v[2 * pair + side, t] = jnp.sum(
                        jnp.where(mine, product, 0.0), axis=-1, keepdims=True
                    )

        def prob(head):
            probs[head][...] = dot_nt(own_v[head], kv[0, 1, :, columns(head)])

        prob(0)
        grad_q, grad_k, grad_v = [], [], []
        for head in range(4):
            if head < 3:
                prob(head + 1)
            for t in tiles(rows):
                weight = grown[0, head, t].astype(F32)
                scores[head][t] = (weight * (probs[head][t] - centre_v[head, t])).astype(BF16)
            mine = first_q if head % 2 == 0 else ~first_q
            grad_v.append(dot_tn(grown[0, head], own_v[head]))
            grad_q.append(dot(scores[head][...], kv[0, 0, :, columns(head)]))
            masked = jnp.where(mine, q_ref[0, :, columns(head)], 0)
            grad_k.append(dot_tn(scores[head][...], masked))
            if head % 2 == 1:
                place = columns(head)
                dq = jnp.where(first_q, grad_q[head - 1], grad_q[head]) * score_scale
                dq_out[:, place] = dq.astype(BF16)
                dk = ((grad_k[head - 1] + grad_k[head]) * score_scale).astype(BF16)
                dv = (grad_v[head - 1] + grad_v[head]).astype(BF16)
                here_out[0, :, place] = dk[:rows]
                here_out[1, :, place] = dv[:rows]
                there_out[0, :, place] = dk[rows:]
                there_out[1, :, place] = dv[rows:]

    def on(s):
        return s[ACTIVE + owner]

    def slot(s):
        return jnp.where(on(s) == 1, number, SPARE)

    column = lambda i, s: (slot(s), 0, i * on(s))
    plain = lambda i, s: (0, i * on(s))
    return call(
        kernel,
        info,
        (steps,),
        [
            (grad_mixed, (rows, block), plain),
            (kept["q"], (1, rows, block), lambda i, s: (number, 0, i * on(s))),
            (kept["kv"], (1, 2, 2 * rows, block), lambda i, s: (slot(s), 0, 0, i * on(s))),
            (kept["grown"], (1, 4, rows, 2 * rows), lambda i, s: (slot(s), i * on(s), 0, 0)),
            (kept["mixed_full"], (1, rows, block), column),
            (kept["inverse"], (1, rows, block), column),
        ],
        [
            ((rows, width), BF16, (rows, block), plain, None),
            ((2, rows, width), BF16, (2, rows, block), lambda i, s: (0, 0, i * on(s)), None),
            ((2, rows, width), BF16, (2, rows, block), lambda i, s: (0, 0, i * on(s)), None),
        ],
        [pltpu.VMEM((rows, 2 * rows), F32)] * 4
        + [pltpu.VMEM((rows, 2 * rows), BF16)] * 4
        + [pltpu.VMEM((4, rows, lanes), BF16), pltpu.VMEM((4, rows, 1), F32)],
        flops=16 * rows * rows * width,
        moved=4 * heads * rows * rows + 30 * rows * width,
    )


def qkv_backward(info, owner, number, dq, dkv_here, dkv_there, w_own, w_oth, grad_res, vec, kept, grads):
    _, rows, width = kept["x"].shape
    half = width // 2

    def kernel(s, dq_ref, here, there, own, oth, gr, x_ref, v, packed_out, gx_out, relay_out,
               small_out, shift_out, a_v, b_v, p_v, w_v, gr_v, x_v, gx_v, acc, sums,
               a_sems, b_sems, w_sems, in_sems, packed_sems, out_sems):
        @pl.when(s[ACTIVE + owner] == 0)
        def _():
            small_out[...] = jnp.zeros_like(small_out)
            shift_out[...] = jnp.zeros_like(shift_out)

        @pl.when(s[ACTIVE + owner] == 1)
        def _():
            slot = number
            loads = []
            for part in range(6):
                kind, side = part % 3, part // 3
                columns = pl.ds(side * half, half)
                if kind == 0:
                    copies = [begin(dq_ref.at[:, columns], a_v.at[part], a_sems.at[part])]
                else:
                    turned = pl.ds((1 - side) * half, half)
                    copies = [
                        begin(here.at[kind - 1, :, columns], a_v.at[part], a_sems.at[part]),
                        begin(there.at[kind - 1, :, turned], b_v.at[part], b_sems.at[part]),
                    ]
                weight = own if side == 0 else oth
                copies.append(begin(weight.at[kind], w_v.at[part], w_sems.at[part]))
                loads.append(copies)
            last = [
                begin(x_ref.at[slot], x_v, in_sems.at[0]),
                begin(gr, gr_v, in_sems.at[1]),
            ]
            outs = []
            for part in range(6):
                for copy in loads[part]:
                    copy.wait()
                total = jnp.zeros((8, half), F32)
                for t in tiles(rows):
                    packed = a_v[part, t]
                    if part % 3 > 0:
                        packed = (packed.astype(F32) + b_v[part, t].astype(F32)).astype(BF16)
                    p_v[part, t] = packed
                    total = total + eights(packed.astype(F32))
                shift_out[part : part + 1] = col_sum(total)
                outs.append(
                    begin(
                        p_v.at[part],
                        packed_out.at[slot, :, pl.ds(part * half, half)],
                        packed_sems.at[part],
                    )
                )
                product = dot_nt(p_v[part], w_v[part])
                acc[...] = product if part == 0 else acc[...] + product
            for copy in last:
                copy.wait()
            sums[...] = jnp.zeros_like(sums)
            for t in tiles(rows):
                hat, scale = norm_stats(x_v[t].astype(F32))
                error = acc[t]
                grad = gr_v[t] + norm_backward(hat, scale, v[LN1G : LN1G + 1], error)
                gx_v[t] = grad.astype(BF16)
                sums[0] += eights(error * hat)
                sums[1] += eights(error)
            outs.append(begin(gx_v, relay_out, out_sems.at[0]))
            outs.append(begin(gx_v, gx_out.at[slot], out_sems.at[1]))
            small_out[...] = jnp.zeros_like(small_out)
            for row in range(2):
                small_out[row : row + 1] = col_sum(sums[row])
            for copy in outs:
                copy.wait()

    stack = (MICRO, rows, width)
    parts = pltpu.VMEM((6, rows, half), BF16)
    return manual(
        kernel,
        info,
        [
            (dq, False),
            (dkv_here, False),
            (dkv_there, False),
            (w_own, False),
            (w_oth, False),
            (grad_res, False),
            (kept["x"], False),
            (vec, True),
        ],
        [
            ((MICRO, rows, 3 * width), BF16, False, grads.get("packed")),
            (stack, BF16, False, grads.get("input")),
            ((rows, width), BF16, False, None),
            ((8, width), F32, True, None),
            ((8, half), F32, True, None),
        ],
        [
            parts,
            parts,
            parts,
            pltpu.VMEM((6, width, half), BF16),
            pltpu.VMEM((rows, width), F32),
            pltpu.VMEM((rows, width), BF16),
            pltpu.VMEM((rows, width), BF16),
            pltpu.VMEM((rows, width), F32),
            pltpu.VMEM((2, 8, width), F32),
            dma_sems(6),
            dma_sems(6),
            dma_sems(6),
            dma_sems(2),
            dma_sems(6),
            dma_sems(2),
        ],
        flops=6 * rows * width * width,
        moved=6 * width * width + 16 * rows * width,
    )


def swap(block):
    return lax.ppermute(block, "tensor", [(0, 1), (1, 0)])


def ring_order(count):
    return list(range(0, count, 2)) + list(range(count - 1, 0, -2))


def tied(value, *others):
    return lax.optimization_barrier((value, *others))[0]


class Ring:
    def __init__(self, info, parts, shapes, places):
        self.info, self.parts, self.shapes, self.places = info, parts, shapes, places
        self.count = lax.axis_size("dp")
        order = ring_order(self.count)
        n = self.count
        self.chunk = parts[0][0].shape[0] // (2 * n)
        self.widths = [pair[0].shape[1] for pair in parts]
        self.signs = (1, -1)
        self.routes = [[(order[i], order[(i + s) % n]) for i in range(n)] for s in self.signs]
        self.step = 0
        self.steps = 2 * (n - 1)
        self.totals = [None] * len(shapes)
        self.moving = self.add([0, 0], None)

    def unit(self, way, ahead):
        return UNITS + way * self.count + ahead % self.count

    def add(self, ahead, arrived):
        chunk, width, parts = self.chunk, sum(self.widths), len(self.parts)
        units = [self.unit(w, ahead[w]) for w in range(2)]
        terms = 2 if arrived is None else 3

        def kernel(s, *refs):
            halves = refs[: 2 * parts]
            refs = refs[2 * parts :]
            if terms == 3:
                arrivals, refs = refs[:2], refs[2:]
            outs, (held, sems) = refs[:2], refs[2:]
            copies = []
            for w in range(2):
                rows = pl.ds(pl.multiple_of(s[units[w]] * chunk, chunk), chunk)
                base = 0
                for number, columns in enumerate(self.widths):
                    for term in range(2):
                        copies.append(
                            begin(
                                halves[2 * number + term].at[rows],
                                held.at[w, term, :, pl.ds(base, columns)],
                                sems.at[w, term, number],
                            )
                        )
                    base += columns
                if terms == 3:
                    copies.append(begin(arrivals[w], held.at[w, 2], sems.at[w, 2, 0]))
            for copy in copies:
                copy.wait()
            for w in range(2):
                for t in tiles(chunk):
                    for first in range(0, width, 512):
                        c = slice(first, min(first + 512, width))
                        total = held[w, 0, t, c].astype(F32) + held[w, 1, t, c].astype(F32)
                        if terms == 3:
                            total = total + held[w, 2, t, c].astype(F32)
                        outs[w][t, c] = total.astype(BF16)

        arrays = [(term, False) for pair in self.parts for term in pair]
        if arrived is not None:
            arrays += [(block, False) for block in arrived]
        return manual(
            kernel,
            self.info,
            arrays,
            [((chunk, width), BF16, True, None)] * 2,
            [pltpu.VMEM((2, terms, chunk, width), BF16), pltpu.SemaphoreType.DMA((2, 3, parts))],
            moved=2 * (terms + 1) * 2 * chunk * width,
            vmem=16,
        )

    def put(self, ahead, blocks):
        chunk, width = self.chunk, sum(self.widths)
        units = [self.unit(w, ahead[w]) for w in range(2)]
        count = len(self.shapes)
        pieces = sum(len(self.places.columns(c)) for c in range(count))

        def kernel(s, *refs):
            sources, outs, (held, wide, in_sems, out_sems) = (
                refs[:2],
                refs[2 : 2 + count],
                refs[2 + count :],
            )
            loads = [begin(sources[w], held.at[w], in_sems.at[w]) for w in range(2)]
            copies = []
            for w in range(2):
                loads[w].wait()
                for t in tiles(chunk):
                    for first in range(0, width, 512):
                        c = slice(first, min(first + 512, width))
                        wide[w, t, c] = held[w, t, c].astype(F32)
                number = 0
                for target in range(count):
                    for first, columns in self.places.columns(target):
                        ref = self.places.ref(
                            outs[target], target, first, columns, s[units[w]], chunk
                        )
                        copies.append(
                            begin(
                                wide.at[w, :, pl.ds(first, columns)],
                                ref,
                                out_sems.at[w, number],
                            )
                        )
                        number += 1
            for copy in copies:
                copy.wait()

        self.totals = manual(
            kernel,
            self.info,
            [(block, False) for block in blocks],
            [(shape, F32, False, old) for shape, old in zip(self.shapes, self.totals)],
            [
                pltpu.VMEM((2, chunk, width), BF16),
                pltpu.VMEM((2, chunk, width), F32),
                dma_sems(2),
                pltpu.SemaphoreType.DMA((2, pieces)),
            ],
            moved=2 * 6 * chunk * width,
            vmem=16,
        )

    def advance(self, *after):
        arrived = [lax.ppermute(self.moving[w], "dp", self.routes[w]) for w in range(2)]
        if after:
            arrived = list(lax.optimization_barrier((*arrived, *after))[:2])
        step = self.step
        if step < self.count - 1:
            self.moving = self.add([-s * (step + 1) for s in self.signs], arrived)
        else:
            if step == self.count - 1:
                self.put(self.signs, self.moving)
            self.moving = arrived
            self.put([-s * (step - self.count + 1) for s in self.signs], arrived)
        self.step += 1

    def done(self):
        return self.step == self.steps

    def finish(self):
        while not self.done():
            self.advance()
        return self.totals


class WholeRows:
    def __init__(self, width):
        self.width = width

    def columns(self, target):
        return [(0, self.width)]

    def ref(self, out, target, first, columns, unit, chunk):
        return out.at[pl.ds(pl.multiple_of(unit * chunk, chunk), chunk)]


class TailPlaces:
    def __init__(self, half, lanes):
        self.half, self.lanes = half, lanes

    def columns(self, target):
        half = self.half
        if target == 0:
            return [(j * half, half) for j in range(3)]
        return [(3 * half, half)] if target == 1 else [(4 * half, self.lanes)]

    def ref(self, out, target, first, columns, unit, chunk):
        rows = pl.ds(pl.multiple_of(unit * chunk, chunk), chunk)
        if target == 0:
            return out.at[first // self.half, rows]
        if target == 2:
            return out.at[rows]
        each = self.half // chunk
        return out.at[
            pl.ds(pl.multiple_of(lax.rem(unit, each) * chunk, chunk), chunk),
            pl.ds(pl.multiple_of(lax.div(unit, each) * self.half, self.half), self.half),
        ]


def partner_tokens(info, block, numbers):
    _, _, seq, half = block.shape
    rows = seq // 2

    def kernel(s, ref, out, sems):
        start = pl.multiple_of((1 - s[RANK]) * rows, rows)
        copies = [
            begin(ref.at[number, 0, pl.ds(start, rows)], out.at[place], sems.at[place])
            for place, number in enumerate(numbers)
        ]
        for copy in copies:
            copy.wait()

    return manual(
        kernel,
        info,
        [(block, False)],
        [((len(numbers), rows, half), BF16, False, None)],
        [dma_sems(len(numbers))],
        vmem=4,
    )[0]


def partner_features(info, block):
    micro, rows, width = block.shape
    half = width // 2

    def kernel(s, ref, out, sems):
        start = pl.multiple_of((1 - s[RANK]) * half, half)
        copies = [
            begin(ref.at[m, :, pl.ds(start, half)], out.at[m], sems.at[m]) for m in range(micro)
        ]
        for copy in copies:
            copy.wait()

    return manual(
        kernel,
        info,
        [(block, False)],
        [((micro, rows, half), BF16, False, None)],
        [dma_sems(micro)],
        vmem=4,
    )[0]


def join_tokens(info, block, received):
    micro, rows, width = block.shape
    half = width // 2

    def kernel(s, ref, other, out, sems):
        rank = s[RANK]
        features = pl.ds(pl.multiple_of(rank * half, half), half)
        here = pl.ds(pl.multiple_of(rank * rows, rows), rows)
        there = pl.ds(pl.multiple_of((1 - rank) * rows, rows), rows)
        copies = []
        for m in range(micro):
            copies.append(begin(ref.at[m, :, features], out.at[0, m, 0, here], sems.at[0, m]))
            copies.append(begin(other.at[m], out.at[0, m, 0, there], sems.at[1, m]))
        for copy in copies:
            copy.wait()

    return manual(
        kernel,
        info,
        [(block, False), (received, False)],
        [((1, micro, 1, 2 * rows, half), BF16, False, None)],
        [pltpu.SemaphoreType.DMA((2, micro))],
        vmem=4,
    )[0]


LANES = 128


def gather_vectors(info, sums, rows_out):
    calls = len(sums)
    width = sums[0][0].shape[1]
    half = width // 2

    def kernel(s, *refs):
        own, oth = refs[4 * calls :]
        low = s[RANK] == 0

        def total(kind):
            blocks = [refs[4 * c + kind][...] for c in range(calls)]
            return sum(blocks[1:], blocks[0])

        two, up, one, qkv = [total(kind) for kind in range(4)]
        own[...] = jnp.zeros_like(own)
        oth[...] = jnp.zeros_like(oth)
        place = 0

        def write(first, second):
            nonlocal place
            for c in range(0, half, LANES):
                own[place : place + 1] = first[:, c : c + LANES].astype(BF16)
                oth[place : place + 1] = second[:, c : c + LANES].astype(BF16)
                place += 1

        for block, count in ((one, 2), (two, 6)):
            for row in range(count):
                line = block[row : row + 1]
                left, right = line[:, :half], line[:, half:]
                write(jnp.where(low, left, right), jnp.where(low, right, left))
        for row in range(3):
            write(qkv[row : row + 1], qkv[3 + row : 4 + row])
        hidden_rows = up.shape[0] // 2
        for row in range(hidden_rows):
            write(up[row : row + 1], up[hidden_rows + row : hidden_rows + row + 1])

    vmem = pl.BlockSpec(memory_space=pltpu.VMEM)
    return pl.pallas_call(
        kernel,
        in_specs=[pl.BlockSpec(memory_space=pltpu.SMEM)] + [vmem] * (4 * calls),
        out_specs=[vmem] * 2,
        out_shape=[jax.ShapeDtypeStruct((rows_out, LANES), BF16)] * 2,
    )(info, *[block for group in sums for block in group])


def spread_vectors(sums, half, hidden_half):
    def kernel(ref, *outs):
        def line(number, out, row=0, columns=half, first=0):
            for c in range(0, columns, LANES):
                place = (number * half + c) // LANES
                out[row : row + 1, first + c : first + c + LANES] = ref[place : place + 1]

        for number in range(8):
            line(number, outs[number])
        line(8, outs[8])
        line(10, outs[8], row=1)
        line(11, outs[9], columns=hidden_half)

    vmem = pl.BlockSpec(memory_space=pltpu.VMEM)
    shapes = [(1, half)] * 8 + [(2, half), (1, hidden_half)]
    return pl.pallas_call(
        kernel,
        in_specs=[vmem],
        out_specs=[vmem] * 10,
        out_shape=[jax.ShapeDtypeStruct(shape, F32) for shape in shapes],
    )(sums)


def pack_vectors(blocks, hidden_bias):
    half = blocks[0].shape[1]
    hidden_rows = hidden_bias.shape[1] // half
    filled = sum(b.shape[0] for b in blocks)

    def kernel(*refs):
        out = refs[-1]
        place = 0
        for ref in refs[: len(blocks)]:
            for row in range(ref.shape[0]):
                out[place : place + 1] = ref[row : row + 1].astype(F32)
                place += 1
        for row in range(hidden_rows):
            columns = slice(row * half, (row + 1) * half)
            out[place : place + 1] = refs[len(blocks)][:, columns].astype(F32)
            place += 1

    return pl.pallas_call(
        kernel, out_shape=jax.ShapeDtypeStruct((filled + hidden_rows, half), F32)
    )(*blocks, hidden_bias)


def join_vectors(scalars, own, oth, hidden_rows):
    half = own.shape[1]

    def kernel(s, own_ref, oth_ref, vec, bias_q, bias_v, bias_up):
        low = s[RANK] == 0
        vec[:, :half] = jnp.where(low, own_ref[:8], oth_ref[:8])
        vec[:, half:] = jnp.where(low, oth_ref[:8], own_ref[:8])
        for row, out in ((8, bias_q), (9, bias_v)):
            out[:, :half] = own_ref[row : row + 1]
            out[:, half:] = oth_ref[row : row + 1]
        bias_up[:hidden_rows] = own_ref[10 : 10 + hidden_rows]
        bias_up[hidden_rows:] = oth_ref[10 : 10 + hidden_rows]

    vmem = pl.BlockSpec(memory_space=pltpu.VMEM)
    return pl.pallas_call(
        kernel,
        in_specs=[pl.BlockSpec(memory_space=pltpu.SMEM), vmem, vmem],
        out_specs=[vmem] * 4,
        out_shape=[
            jax.ShapeDtypeStruct((8, 2 * half), F32),
            jax.ShapeDtypeStruct((1, 2 * half), F32),
            jax.ShapeDtypeStruct((1, 2 * half), F32),
            jax.ShapeDtypeStruct((2 * hidden_rows, half), F32),
        ],
    )(scalars, own, oth)


def shards(
    inputs,
    cotangent,
    ln1_gain,
    ln1_bias,
    qkv_weight,
    qv_bias,
    out_weight,
    out_bias,
    scale_attn,
    ln2_gain,
    ln2_bias,
    fc1_weight,
    fc1_bias,
    fc2_weight,
    fc2_bias,
    scale_mlp,
):
    micro, images, seq_len, half = inputs.shape
    assert micro == MICRO and images == 1
    width = 2 * half
    hidden_half = fc1_weight.shape[2]

    count = lax.axis_size("dp")
    order = ring_order(count)
    table = [
        [rank, int(section == 0), int(section == 1)]
        + [way * count + (order.index(i) + ahead) % count for way in range(2) for ahead in range(count)]
        for section in range(2)
        for rank in range(2)
        for i in range(count)
    ]
    info = lax.dynamic_slice(
        jnp.asarray(table, jnp.int32),
        (lax.axis_index(("section", "tensor", "dp")), 0),
        (1, len(table[0])),
        allow_negative_indices=False,
    ).reshape(-1)

    first_oth = swap(partner_tokens(info, inputs, (0,))[0])
    vectors = pack_vectors(
        [
            ln1_gain, ln1_bias, out_bias, scale_attn, ln2_gain, ln2_bias, fc2_bias, scale_mlp,
            qv_bias[0],
        ],
        fc1_bias,
    )
    vectors_oth = swap(vectors)
    wq_own = jnp.transpose(qkv_weight[0], (1, 0, 2))
    wq_oth = swap(tied(wq_own, vectors))
    vec, bias_q, bias_v, b_up = join_vectors(info, vectors, vectors_oth, hidden_half // half)
    b_up = b_up.reshape(2 * hidden_half // CHUNK, CHUNK)
    wo_own, wu_own, wd_own = out_weight[0], fc1_weight[0], fc2_weight[0]
    wo_oth = swap(tied(wo_own, first_oth, vectors_oth))
    wu_oth = swap(tied(wu_own, first_oth, vectors_oth))
    wd_oth = swap(tied(wd_own, first_oth, vectors_oth))
    second_oth = swap(partner_tokens(info, tied(inputs, wd_oth), (1,))[0])
    cot_oth = swap(partner_tokens(info, tied(cotangent, wd_oth), (0, 1)))

    kept = {}

    def forward(owner, number, source, tokens):
        kept["x"], kept["normed1"], kv_here = norm_kv(
            info, owner, number, source, tokens, vec, wq_own, wq_oth, bias_v, kept
        )
        kv_there = swap(kv_here)
        kept["q"] = project_q(info, owner, number, kept["normed1"], wq_own, wq_oth, bias_q, kept)
        kept["grown"], kept["mixed_full"], mixed, kept["inverse"], kept["kv"] = attend(
            info, owner, number, kept["q"], kv_here, kv_there, kept
        )
        (
            kept["attended"],
            kept["residual"],
            kept["normed2"],
            kept["active"],
            kept["slope"],
            kept["branch"],
            kept["output"],
            relayed,
            kept["mixed"],
        ) = mlp_forward(
            info, owner, number, mixed, kept["x"], vec, wo_own, wo_oth, wu_own, wu_oth, wd_own,
            wd_oth, b_up, kept,
        )
        return relayed

    relayed = forward(0, 0, "argument", (inputs, first_oth))
    first = lax.ppermute(relayed, "section", [(0, 1)])
    relayed = forward(0, 1, "argument", (inputs, second_oth))
    relayed, first = lax.optimization_barrier((relayed, first))
    second = lax.ppermute(relayed, "section", [(0, 1)])
    forward(1, 0, "relay", (first,))
    forward(1, 1, "relay", (second,))

    grads = {}
    sums = []

    def backward_mlp(owner, number, source, tokens, scaled=False):
        (
            branch,
            grads["before"],
            grads["attended"],
            grad_mixed,
            grad_res,
            small,
            shift,
        ) = mlp_backward(
            info, owner, number, source, tokens, vec, wo_own, wo_oth, wu_own, wu_oth, wd_own,
            wd_oth, kept, grads, scaled,
        )
        if not scaled:
            grads["branch"] = branch
        return grad_mixed, grad_res, small, shift

    def backward_attention(owner, number, grad_mixed):
        dq, dkv_here, dkv_send = attend_backward(info, owner, number, grad_mixed, kept)
        return dq, dkv_here, swap(dkv_send)

    def backward_qkv(owner, number, dq, dkv_here, dkv_there, grad_res, small, shift):
        grads["packed"], grads["input"], relayed, small_one, shift_qkv = qkv_backward(
            info, owner, number, dq, dkv_here, dkv_there, wq_own, wq_oth, grad_res, vec, kept,
            grads,
        )
        sums.append((small, shift, small_one, shift_qkv))
        return relayed

    def backward(owner, number, source, tokens):
        grad_mixed, grad_res, small, shift = backward_mlp(owner, number, source, tokens)
        flows = backward_attention(owner, number, grad_mixed)
        return backward_qkv(owner, number, *flows, grad_res, small, shift)

    relayed = backward(1, 0, "argument", (cotangent, cot_oth[0]))
    first = lax.ppermute(relayed, "section", [(1, 0)])
    relayed = backward(1, 1, "argument", (cotangent, cot_oth[1]))
    relayed, first = lax.optimization_barrier((relayed, first))
    second = lax.ppermute(relayed, "section", [(1, 0)])
    backward(0, 0, "relay", (first,))

    def weight_grad(left, right):
        return lax.dot_general(
            left, right, (((0, 1), (0, 1)), ((), ())), preferred_element_type=F32
        ).astype(BF16)

    grads["branch"] = scale_branch(info, 0, 1, second, vec, grads["branch"])
    active, g_branch = kept["active"], grads["branch"]
    down_oth = weight_grad(active[:, :, hidden_half:], g_branch)
    down_sent = swap(down_oth)
    down_own = weight_grad(active[:, :, :hidden_half], tied(g_branch, down_oth))
    ring_down = Ring(info, [(down_own, down_sent)], [down_own.shape], WholeRows(width))
    second = tied(second, *ring_down.moving)
    grad_mixed, grad_res, small, shift = backward_mlp(0, 1, "relay", (second,), scaled=True)
    ring_down.advance(grad_mixed)
    normed2 = tied(kept["normed2"], *ring_down.moving)
    before = grads["before"]
    up_oth = weight_grad(normed2, before[:, :, hidden_half:])
    up_sent = swap(up_oth)
    ring_down.advance(up_oth)
    normed2 = tied(normed2, *ring_down.moving)
    up_own = weight_grad(normed2, before[:, :, :hidden_half])
    ring_down.advance(up_own)
    ring_up = Ring(info, [(up_own, up_sent)], [up_own.shape], WholeRows(hidden_half))
    grad_mixed = tied(grad_mixed, *ring_down.moving, *ring_up.moving)
    flows = backward_attention(0, 1, grad_mixed)
    ring_down.advance(flows[0])
    ring_up.advance(flows[0])
    grad_res = tied(grad_res, *ring_down.moving, *ring_up.moving)
    backward_qkv(0, 1, *flows, grad_res, small, shift)
    packed = grads["packed"]
    ring_down.advance(packed)
    ring_up.advance(packed)
    normed1 = tied(kept["normed1"], *ring_down.moving, *ring_up.moving)
    vectors = gather_vectors(info, sums, width)

    def tail(index):
        columns = packed[:, :, index * 3 * half : (index + 1) * 3 * half]
        mixed = kept["mixed"][:, :, index * half : (index + 1) * half]
        g_att = grads["attended"]
        outs = [weight_grad(mixed, g_att[:, :, half * j : half * (j + 1)]) for j in range(2)]
        return [weight_grad(normed1, columns), jnp.concatenate(outs, axis=0), vectors[index]]

    tail_oth = tail(1)
    tail_sent = [swap(block) for block in tail_oth]
    ring_down.advance(tail_oth[0])
    ring_up.advance(tail_oth[0])
    normed1 = tied(normed1, *ring_down.moving, *ring_up.moving)
    tail_own = tail(0)
    ring_down.advance(tail_own[0])
    ring_up.advance(tail_own[0])
    ring_tail = Ring(
        info,
        list(zip(tail_own, tail_sent)),
        [(3, width, half), (half, width), (width, LANES)],
        TailPlaces(half, LANES),
    )
    rings = [ring_down, ring_up, ring_tail]
    before_it = ring_tail
    while not all(ring.done() for ring in rings):
        for ring in rings:
            if not ring.done():
                ring.advance(*before_it.moving)
                before_it = ring
    (total_down,) = ring_down.finish()
    (total_up,) = ring_up.finish()
    total_qkv, total_out, total_vectors = ring_tail.finish()
    block_outputs = join_tokens(info, kept["output"], swap(partner_features(info, kept["output"])))
    input_grads = join_tokens(info, grads["input"], swap(partner_features(info, grads["input"])))
    rows = spread_vectors(total_vectors, half, hidden_half)
    return (
        block_outputs,
        input_grads,
        rows[0],
        rows[1],
        jnp.transpose(total_qkv, (1, 0, 2))[None],
        rows[8][None],
        total_out[None],
        rows[7],
        rows[6],
        rows[4],
        rows[5],
        total_up[None],
        rows[9],
        total_down[None],
        rows[3],
        rows[2],
    )


def solution(mesh):
    placed = (
        P(None, "dp", None, "tensor"),
        P(None, "dp", None, "tensor"),
        P("section", "tensor"),
        P("section", "tensor"),
        P("section", None, None, "tensor"),
        P("section", None, "tensor"),
        P("section", "tensor", None),
        P("section", "tensor"),
        P("section", "tensor"),
        P("section", "tensor"),
        P("section", "tensor"),
        P("section", None, "tensor"),
        P("section", "tensor"),
        P("section", "tensor", None),
        P("section", "tensor"),
        P("section", "tensor"),
    )
    return jax.shard_map(
        shards,
        mesh=mesh,
        in_specs=placed,
        out_specs=(
            P("section", None, "dp", None, "tensor"),
            P("section", None, "dp", None, "tensor"),
            P("section", "tensor"),
            P("section", "tensor"),
            P("section", None, None, "tensor"),
            P("section", None, "tensor"),
            P("section", "tensor", None),
            P("section", "tensor"),
            P("section", "tensor"),
            P("section", "tensor"),
            P("section", "tensor"),
            P("section", None, "tensor"),
            P("section", "tensor"),
            P("section", "tensor", None),
            P("section", "tensor"),
            P("section", "tensor"),
        ),
        check_vma=False,
    )
```

```python
import math

import jax
import jax.numpy as jnp
from jax import lax
from jax.experimental import pallas as pl
from jax.experimental.pallas import tpu as pltpu
from jax.sharding import PartitionSpec as P

HEAD_DIM = 64
EPSILON = 1e-06
F32 = jnp.float32
BF16 = jnp.bfloat16
MIB = 1 << 20
VMEM_MIB = 62
RING_MIB = 61
TILE = 16
MICRO = 2
SPARE = MICRO
RANK, ACTIVE, UNITS = 0, 1, 3
LN1G, LN1B, OUTB, SATT, LN2G, LN2B, FC2B, SMLP = range(8)


def dot(left, right):
    return jnp.dot(left, right, preferred_element_type=F32)


def dot_nt(left, right):
    return lax.dot_general(left, right, (((1,), (1,)), ((), ())), preferred_element_type=F32)


def dot_tn(left, right):
    return lax.dot_general(left, right, (((0,), (0,)), ((), ())), preferred_element_type=F32)


def norm_stats(values):
    centre = jnp.mean(values, axis=-1, keepdims=True)
    centred = values - centre
    spread = jnp.mean(centred * centred, axis=-1, keepdims=True)
    scale = lax.rsqrt(spread + EPSILON)
    return centred * scale, scale


def tiles(rows):
    return [slice(r, r + TILE) for r in range(0, rows, TILE)]


def eights(values):
    total = values[:8]
    for r in range(8, values.shape[0], 8):
        total = total + values[r : r + 8]
    return total


def norm_backward(hat, scale, gain, error):
    weighted = error * gain
    mean_one = jnp.mean(weighted, axis=-1, keepdims=True)
    mean_two = jnp.mean(weighted * hat, axis=-1, keepdims=True)
    return scale * (weighted - mean_one - hat * mean_two)


def col_sum(values):
    return jnp.sum(values, axis=0, keepdims=True)


def call(kernel, scalars, grid, ins, outs, scratch=(), flops=0, moved=0, after=()):
    arrays = [a for a, _, _ in ins]
    in_specs = [pl.BlockSpec(b, m) for _, b, m in ins]
    aliases = {}
    for number, out in enumerate(outs):
        if out[4] is not None:
            aliases[1 + len(arrays)] = number
            arrays.append(out[4])
            in_specs.append(pl.BlockSpec(memory_space=pl.ANY))
    arrays += after
    in_specs += [pl.BlockSpec(memory_space=pl.ANY)] * len(after)
    extra = len(aliases) + len(after)
    in_count = len(ins)

    def body(*refs):
        kernel(*refs[: 1 + in_count], *refs[1 + in_count + extra :])

    return pl.pallas_call(
        body,
        out_shape=[jax.ShapeDtypeStruct(s, d) for s, d, _, _, _ in outs],
        grid_spec=pltpu.PrefetchScalarGridSpec(
            num_scalar_prefetch=1,
            grid=grid,
            in_specs=in_specs,
            out_specs=[pl.BlockSpec(b, m) for _, _, b, m, _ in outs],
            scratch_shapes=list(scratch),
        ),
        input_output_aliases=aliases,
        compiler_params=pltpu.CompilerParams(
            dimension_semantics=("arbitrary",) * len(grid), vmem_limit_bytes=VMEM_MIB * MIB
        ),
        cost_estimate=pl.CostEstimate(
            flops=int(flops), bytes_accessed=int(moved), transcendentals=0
        ),
    )(scalars, *arrays)


def manual(kernel, scalars, ins, outs, scratch, flops=0, moved=0, vmem=VMEM_MIB, after=(), same=None):
    any_space = pl.BlockSpec(memory_space=pl.ANY)
    vmem_space = pl.BlockSpec(memory_space=pltpu.VMEM)
    arrays = [a for a, _ in ins]
    in_specs = [vmem_space if inside else any_space for _, inside in ins]
    aliases = {1 + i: o for i, o in (same or {}).items()}
    before = len(arrays)
    for number, out in enumerate(outs):
        if out[3] is not None:
            aliases[1 + len(arrays)] = number
            arrays.append(out[3])
            in_specs.append(any_space)
    arrays += after
    in_specs += [any_space] * len(after)
    extra = len(arrays) - before
    in_count = len(ins)

    def body(*refs):
        kernel(*refs[: 1 + in_count], *refs[1 + in_count + extra :])

    return pl.pallas_call(
        body,
        out_shape=[jax.ShapeDtypeStruct(s, d) for s, d, _, _ in outs],
        in_specs=[pl.BlockSpec(memory_space=pltpu.SMEM)] + in_specs,
        out_specs=[vmem_space if inside else any_space for _, _, inside, _ in outs],
        scratch_shapes=list(scratch),
        input_output_aliases=aliases,
        compiler_params=pltpu.CompilerParams(vmem_limit_bytes=vmem * MIB),
        cost_estimate=pl.CostEstimate(
            flops=int(flops), bytes_accessed=int(moved), transcendentals=0
        ),
    )(scalars, *arrays)


def begin(src, dst, sem):
    copy = pltpu.make_async_copy(src, dst, sem)
    copy.start()
    return copy


def dma_sems(count):
    return pltpu.SemaphoreType.DMA((count,))


def whole2(i, s):
    return (0, 0)


def slot3(i, s):
    return (s[0], 0, 0)


def token_copies(s, source, number, refs, target, sems):
    rows, width = target.shape
    half = width // 2
    rank = s[RANK]
    if source == "relay":
        return [begin(refs[0], target, sems.at[0])]
    first = pl.multiple_of(rank * half, half)
    second = pl.multiple_of((1 - rank) * half, half)
    whole, other = refs
    return [
        begin(
            whole.at[number, 0, pl.ds(pl.multiple_of(rank * rows, rows), rows)],
            target.at[:, pl.ds(first, half)],
            sems.at[0],
        ),
        begin(other, target.at[:, pl.ds(second, half)], sems.at[1]),
    ]


def norm_kv(info, owner, number, source, tokens, vec, w_own, w_oth, bias_v, kept, after=()):
    rows, width = tokens[-1].shape[0], vec.shape[1]
    half = width // 2
    count = len(tokens)

    def kernel(s, *refs):
        token_refs = refs[:count]
        (v, own, oth, bv, x_out, n_out, kv_out, x_v, n_v, w_v, kv_v, tok_sems, w_sems,
         out_sems) = refs[count:]

        @pl.when(s[ACTIVE + owner] == 1)
        def _():
            arriving = token_copies(s, source, number, token_refs, x_v, tok_sems)
            loads = []
            for part in range(4):
                ref = own if part < 2 else oth
                loads.append(begin(ref.at[1 + part % 2], w_v.at[part], w_sems.at[part]))
            for copy in arriving:
                copy.wait()
            outs = [begin(x_v, x_out.at[number], out_sems.at[0])]
            for t in tiles(rows):
                hat, _ = norm_stats(x_v[t].astype(F32))
                n_v[t] = (hat * v[LN1G : LN1G + 1] + v[LN1B : LN1B + 1]).astype(BF16)
            outs.append(begin(n_v, n_out.at[number], out_sems.at[1]))
            for part in range(4):
                loads[part].wait()
                result = dot(n_v[...], w_v[part])
                kind, side = part % 2, part // 2
                columns = slice(side * half, (side + 1) * half)
                if kind == 1:
                    result = result + bv[:, columns]
                kv_v[part] = result.astype(BF16)
                outs.append(
                    begin(
                        kv_v.at[part],
                        kv_out.at[kind, :, pl.ds(side * half, half)],
                        out_sems.at[2 + part],
                    )
                )
            for copy in outs:
                copy.wait()

    stack = (MICRO, rows, width)
    return manual(
        kernel,
        info,
        [(array, False) for array in tokens]
        + [(vec, True), (w_own, False), (w_oth, False), (bias_v, True)],
        [
            (stack, BF16, False, kept.get("x")),
            (stack, BF16, False, kept.get("normed1")),
            ((2, rows, width), BF16, False, None),
        ],
        [
            pltpu.VMEM((rows, width), BF16),
            pltpu.VMEM((rows, width), BF16),
            pltpu.VMEM((4, width, half), BF16),
            pltpu.VMEM((4, rows, half), BF16),
            dma_sems(2),
            dma_sems(4),
            dma_sems(6),
        ],
        flops=2 * rows * width * 2 * width,
        moved=4 * width * width + 10 * rows * width,
        after=after,
    )


def project_q(info, owner, number, normed, w_own, w_oth, bias_q, kept):
    _, rows, width = normed.shape
    half = width // 2

    def kernel(s, n, own, oth, bq, q_out, n_v, w_v, q_v, in_sems, out_sems):
        @pl.when(s[ACTIVE + owner] == 1)
        def _():
            load = begin(n.at[number], n_v, in_sems.at[0])
            loads = [
                begin(own.at[0], w_v.at[0], in_sems.at[1]),
                begin(oth.at[0], w_v.at[1], in_sems.at[2]),
            ]
            load.wait()
            outs = []
            for side in range(2):
                loads[side].wait()
                columns = slice(side * half, (side + 1) * half)
                q_v[side] = (dot(n_v[...], w_v[side]) + bq[:, columns]).astype(BF16)
                outs.append(
                    begin(
                        q_v.at[side],
                        q_out.at[number, :, pl.ds(side * half, half)],
                        out_sems.at[side],
                    )
                )
            for copy in outs:
                copy.wait()

    return manual(
        kernel,
        info,
        [(normed, False), (w_own, False), (w_oth, False), (bias_q, True)],
        [((MICRO, rows, width), BF16, False, kept.get("q"))],
        [
            pltpu.VMEM((rows, width), BF16),
            pltpu.VMEM((2, width, half), BF16),
            pltpu.VMEM((2, rows, half), BF16),
            dma_sems(3),
            dma_sems(2),
        ],
        flops=2 * rows * width * width,
        moved=2 * width * width + 4 * rows * width,
    )[0]


def attend(info, owner, number, q, kv_here, kv_there, kept):
    _, rows, width = q.shape
    heads = width // HEAD_DIM
    factor = HEAD_DIM**-0.5 * math.log2(math.e)
    lanes = 2 * HEAD_DIM
    block = 2 * lanes
    steps = width // block

    def kernel(s, *refs):
        @pl.when(s[ACTIVE + owner] == 1)
        def _():
            compute(*refs)

    def compute(q_ref, here, there, e_out, o_out, mixed_out, inv_out, kv_out, *scratch):
        scores, results = scratch[:4], scratch[4:]
        kv_out[0, :, :rows] = here[...]
        kv_out[0, :, rows:] = there[...]
        first_q = lax.broadcasted_iota(jnp.int32, (rows, lanes), 1) < HEAD_DIM
        first_k = lax.broadcasted_iota(jnp.int32, (2 * rows, lanes), 1) < HEAD_DIM
        first_t = lax.broadcasted_iota(jnp.int32, (TILE, lanes), 1) < HEAD_DIM

        def columns(head):
            return slice(head // 2 * lanes, (head // 2 + 1) * lanes)

        def score(head):
            mine = first_q if head % 2 == 0 else ~first_q
            masked = jnp.where(mine, q_ref[0, :, columns(head)], 0)
            scores[head][...] = dot_nt(masked, kv_out[0, 0, :, columns(head)])

        score(0)
        for head in range(4):
            if head < 3:
                score(head + 1)
            for t in tiles(rows):
                tile = scores[head][t]
                top = jnp.max(tile, axis=-1, keepdims=True)
                e_out[0, head, t] = jnp.exp2((tile - top) * factor).astype(BF16)
            mine = first_k if head % 2 == 0 else ~first_k
            values = jnp.where(mine, kv_out[0, 1, :, columns(head)], 1)
            results[head][...] = dot(e_out[0, head], values)
        for pair in range(2):
            place = slice(pair * lanes, (pair + 1) * lanes)
            for t in tiles(rows):
                one, two = results[2 * pair][t], results[2 * pair + 1][t]
                total = jnp.where(
                    first_t, pltpu.roll(one, HEAD_DIM, 1), pltpu.roll(two, HEAD_DIM, 1)
                )
                inverse = 1.0 / total
                mixed = jnp.where(first_t, one, two) * inverse
                o_out[0, t, place] = mixed
                mixed_out[t, place] = mixed.astype(BF16)
                inv_out[0, t, place] = inverse

    def on(s):
        return s[ACTIVE + owner]

    def slot(s):
        return jnp.where(on(s) == 1, number, SPARE)

    column = lambda i, s: (slot(s), 0, i * on(s))
    spare = MICRO + 1
    return call(
        kernel,
        info,
        (steps,),
        [
            (q, (1, rows, block), lambda i, s: (number, 0, i * on(s))),
            (kv_here, (2, rows, block), lambda i, s: (0, 0, i * on(s))),
            (
                kv_there,
                (2, rows, block),
                lambda i, s: (0, 0, lax.rem(i + steps // 2, steps) * on(s)),
            ),
        ],
        [
            (
                (spare, heads, rows, 2 * rows),
                BF16,
                (1, 4, rows, 2 * rows),
                lambda i, s: (slot(s), i * on(s), 0, 0),
                kept.get("grown"),
            ),
            ((spare, rows, width), F32, (1, rows, block), column, kept.get("mixed_full")),
            ((rows, width), BF16, (rows, block), lambda i, s: (0, i * on(s)), None),
            ((spare, rows, width), F32, (1, rows, block), column, kept.get("inverse")),
            (
                (spare, 2, 2 * rows, width),
                BF16,
                (1, 2, 2 * rows, block),
                lambda i, s: (slot(s), 0, 0, i * on(s)),
                kept.get("kv"),
            ),
        ],
        [pltpu.VMEM((rows, 2 * rows), F32)] * 4 + [pltpu.VMEM((rows, lanes), F32)] * 4,
        flops=8 * rows * rows * width,
        moved=4 * heads * rows * rows + 30 * rows * width,
    )


def gelu_parts(x):
    size = jnp.abs(x)
    base = 1.0 + (0.3275911 * math.sqrt(0.5)) * size
    t = pl.reciprocal(base, approx=True)
    t = t * (2.0 - base * t)
    grown = jnp.exp2(x * x * (-0.5 * math.log2(math.e)))
    poly = 0.5 * 1.061405429
    for factor in (-1.453152027, 1.421413741, -0.284496736, 0.254829592):
        poly = poly * t + 0.5 * factor
    tail = poly * t * grown
    below = jnp.where(x < 0.0, tail, 1.0 - tail)
    return x * below, below + x * grown * (1.0 / math.sqrt(2.0 * math.pi))


CHUNK = 512


def mlp_forward(info, owner, number, mixed, x, vec, wo_own, wo_oth, wu_own, wu_oth, wd_own, wd_oth, b_up, kept, after=()):
    _, rows, width = x.shape
    side_hidden = wu_own.shape[1]
    hidden = 2 * side_hidden
    half = width // 2
    steps = hidden // CHUNK
    split = steps // 2

    def kernel(
        s, m, x_ref, v, woo, wot, wuo, wut, wdo, wdt, bu,
        att_out, res_out, n_out, act_out, slope_out, branch_out, y_out, relay_out, m_out,
        m_v, x_v, wo_v, wu_v, wd_v, att_v, res_v, n_v, h_v, act_v, slope_v, branch_v, y_v, acc,
        in_sems, wu_sems, wd_sems, out_sems, act_sems, slope_sems,
    ):
        @pl.when(s[ACTIVE + owner] == 1)
        def _():
            slot = number
            first = [
                begin(m, m_v, in_sems.at[0]),
                begin(woo, wo_v.at[0], in_sems.at[1]),
                begin(wot, wo_v.at[1], in_sems.at[2]),
                begin(x_ref.at[slot], x_v, in_sems.at[3]),
            ]
            ups, downs = [], []

            def prefetch(i):
                if i < steps:
                    part = pl.ds((i % split) * CHUNK, CHUNK)
                    up, down = (wuo, wdo) if i < split else (wut, wdt)
                    ups.append(begin(up.at[:, part], wu_v.at[i], wu_sems.at[i]))
                    downs.append(begin(down.at[part], wd_v.at[i], wd_sems.at[i]))

            prefetch(0)
            prefetch(1)
            for copy in first:
                copy.wait()
            acc[...] = dot(m_v[:, :half], wo_v[0]) + dot(m_v[:, half:], wo_v[1])
            for t in tiles(rows):
                attended = acc[t] + v[OUTB : OUTB + 1]
                att_v[t] = attended.astype(BF16)
                residual = x_v[t].astype(F32) + v[SATT : SATT + 1] * attended
                res_v[t] = residual
                hat, _ = norm_stats(residual)
                n_v[t] = (hat * v[LN2G : LN2G + 1] + v[LN2B : LN2B + 1]).astype(BF16)
            outs = [
                begin(att_v, att_out.at[slot], out_sems.at[0]),
                begin(res_v, res_out.at[slot], out_sems.at[1]),
                begin(n_v, n_out.at[slot], out_sems.at[2]),
                begin(m_v, m_out.at[slot], out_sems.at[6]),
            ]

            def up_product(i):
                ups[i].wait()
                h_v[i % 2] = dot(n_v[...], wu_v[i])

            def down_product(i):
                downs[i].wait()
                part = pl.ds(i * CHUNK, CHUNK)
                outs.append(begin(act_v.at[i], act_out.at[slot, :, part], act_sems.at[i]))
                outs.append(begin(slope_v.at[i], slope_out.at[slot, :, part], slope_sems.at[i]))
                product = dot(act_v[i], wd_v[i])
                acc[...] = product if i == 0 else acc[...] + product

            up_product(0)
            for i in range(steps):
                prefetch(i + 2)
                if i > 0:
                    down_product(i - 1)
                if i + 1 < steps:
                    up_product(i + 1)
                for t in tiles(rows):
                    active, slope = gelu_parts(h_v[i % 2, t] + bu[i : i + 1])
                    act_v[i, t] = active.astype(BF16)
                    slope_v[i, t] = slope.astype(BF16)
            down_product(steps - 1)
            for t in tiles(rows):
                branch = acc[t] + v[FC2B : FC2B + 1]
                y_v[t] = (res_v[t] + v[SMLP : SMLP + 1] * branch).astype(BF16)
                branch_v[t] = branch.astype(BF16)
            outs.append(begin(y_v, relay_out, out_sems.at[3]))
            outs.append(begin(y_v, y_out.at[slot], out_sems.at[4]))
            outs.append(begin(branch_v, branch_out.at[slot], out_sems.at[5]))
            for copy in outs:
                copy.wait()

    stack = (MICRO, rows, width)
    tall = (MICRO, rows, hidden)
    plain = pltpu.VMEM((rows, width), BF16)
    full = pltpu.VMEM((rows, width), F32)
    chunks = pltpu.VMEM((steps, rows, CHUNK), BF16)
    return manual(
        kernel,
        info,
        [
            (mixed, False),
            (x, False),
            (vec, True),
            (wo_own, False),
            (wo_oth, False),
            (wu_own, False),
            (wu_oth, False),
            (wd_own, False),
            (wd_oth, False),
            (b_up, True),
        ],
        [
            (stack, BF16, False, kept.get("attended")),
            (stack, F32, False, kept.get("residual")),
            (stack, BF16, False, kept.get("normed2")),
            (tall, BF16, False, kept.get("active")),
            (tall, BF16, False, kept.get("slope")),
            (stack, BF16, False, kept.get("branch")),
            (stack, BF16, False, kept.get("output")),
            ((rows, width), BF16, False, None),
            (stack, BF16, False, kept.get("mixed")),
        ],
        [
            plain,
            plain,
            pltpu.VMEM((2, half, width), BF16),
            pltpu.VMEM((steps, width, CHUNK), BF16),
            pltpu.VMEM((steps, CHUNK, width), BF16),
            plain,
            full,
            plain,
            pltpu.VMEM((2, rows, CHUNK), F32),
            chunks,
            chunks,
            plain,
            plain,
            full,
            dma_sems(4),
            dma_sems(steps),
            dma_sems(steps),
            dma_sems(7),
            dma_sems(steps),
            dma_sems(steps),
        ],
        flops=4 * rows * width * hidden + 2 * rows * width * width,
        moved=4 * width * hidden + 2 * width * width + 8 * rows * hidden,
        after=after,
    )


def scale_branch(info, owner, number, relay, vec, earlier, after=()):
    rows, width = relay.shape

    def kernel(s, g, v, gb_out, g_v, gb_v, sems):
        @pl.when(s[ACTIVE + owner] == 1)
        def _():
            begin(g, g_v, sems.at[0]).wait()
            gb_v[...] = (v[SMLP : SMLP + 1] * g_v[...].astype(F32)).astype(BF16)
            begin(gb_v, gb_out.at[number], sems.at[1]).wait()

    return manual(
        kernel,
        info,
        [(relay, False), (vec, True)],
        [((MICRO, rows, width), BF16, False, earlier)],
        [pltpu.VMEM((rows, width), BF16), pltpu.VMEM((rows, width), BF16), dma_sems(2)],
        moved=4 * rows * width,
        after=after,
    )[0]


def mlp_backward(info, owner, number, source, tokens, vec, wo_own, wo_oth, wu_own, wu_oth, wd_own, wd_oth, kept, grads, scaled, after):
    count = len(tokens)
    _, rows, width = kept["x"].shape
    side_hidden = wu_own.shape[1]
    hidden = 2 * side_hidden
    half = width // 2
    steps = hidden // CHUNK
    split = steps // 2

    def kernel(s, *refs):
        work(s, refs[:count], *refs[count:])

    def work(
        s, token_refs, branch, slope, res, att, v, woo, wot, wuo, wut, wdo, wdt,
        gb_out, before_out, ga_out, gm_out, gr_out, small_out, shift_out,
        g_v, branch_v, slope_v, res_v, att_v, wo_v, wu_v, wd_v, gb_v, d_v, before_v, ga_v, gm_v,
        gr_v, acc, sums, tok_sems, in_sems, slope_sems, wu_sems, wd_sems, out_sems, before_sems,
    ):
        @pl.when(s[ACTIVE + owner] == 0)
        def _():
            small_out[...] = jnp.zeros_like(small_out)
            shift_out[...] = jnp.zeros_like(shift_out)

        @pl.when(s[ACTIVE + owner] == 1)
        def _():
            slot = number
            arriving = token_copies(s, source, number, token_refs, g_v, tok_sems)
            ups, downs, slopes = [], [], []

            def prefetch(i):
                if i < steps:
                    part = pl.ds((i % split) * CHUNK, CHUNK)
                    up, down = (wuo, wdo) if i < split else (wut, wdt)
                    here = pl.ds(i * CHUNK, CHUNK)
                    downs.append(begin(down.at[part], wd_v.at[i], wd_sems.at[i]))
                    slopes.append(begin(slope.at[slot, :, here], slope_v.at[i], slope_sems.at[i]))
                    ups.append(begin(up.at[:, part], wu_v.at[i], wu_sems.at[i]))

            prefetch(0)
            branch_in = begin(branch.at[slot], branch_v, in_sems.at[0])
            prefetch(1)
            last = []
            for copy in arriving:
                copy.wait()
            for t in tiles(rows):
                gb_v[t] = (v[SMLP : SMLP + 1] * g_v[t].astype(F32)).astype(BF16)
            outs = []
            if not scaled:
                outs.append(begin(gb_v, gb_out.at[slot], out_sems.at[0]))

            def down_product(i):
                downs[i].wait()
                d_v[i % 2] = dot_nt(gb_v[...], wd_v[i])

            down_product(0)
            branch_in.wait()
            sums[...] = jnp.zeros_like(sums)
            for t in tiles(rows):
                sums[0] += eights(g_v[t].astype(F32) * branch_v[t].astype(F32))
                sums[1] += eights(gb_v[t].astype(F32))

            def up_product(i):
                ups[i].wait()
                part = pl.ds(i * CHUNK, CHUNK)
                outs.append(begin(before_v.at[i], before_out.at[slot, :, part], before_sems.at[i]))
                product = dot_nt(before_v[i], wu_v[i])
                acc[...] = product if i == 0 else acc[...] + product

            for i in range(steps):
                prefetch(i + 2)
                if i == steps - 2:
                    last = [
                        begin(res.at[slot], res_v, in_sems.at[1]),
                        begin(att.at[slot], att_v, in_sems.at[2]),
                        begin(woo, wo_v.at[0], in_sems.at[3]),
                        begin(wot, wo_v.at[1], in_sems.at[4]),
                    ]
                slopes[i].wait()
                if i > 0:
                    up_product(i - 1)
                if i + 1 < steps:
                    down_product(i + 1)
                total = jnp.zeros((8, CHUNK), F32)
                for t in tiles(rows):
                    grad_before = (d_v[i % 2, t] * slope_v[i, t].astype(F32)).astype(BF16)
                    before_v[i, t] = grad_before
                    total = total + eights(grad_before.astype(F32))
                shift_out[i : i + 1] = col_sum(total)
            up_product(steps - 1)
            for copy in last:
                copy.wait()
            for t in tiles(rows):
                hat, scale = norm_stats(res_v[t])
                error = acc[t]
                sums[2] += eights(error * hat)
                sums[3] += eights(error)
                grad = g_v[t].astype(F32) + norm_backward(hat, scale, v[LN2G : LN2G + 1], error)
                gr_v[t] = grad
                sums[4] += eights(grad * att_v[t].astype(F32))
                ga = (v[SATT : SATT + 1] * grad).astype(BF16)
                ga_v[t] = ga
                sums[5] += eights(ga.astype(F32))
            outs.append(begin(ga_v, ga_out.at[slot], out_sems.at[1]))
            outs.append(begin(gr_v, gr_out, out_sems.at[3]))
            gm_v[:, :half] = dot_nt(ga_v[...], wo_v[0]).astype(BF16)
            gm_v[:, half:] = dot_nt(ga_v[...], wo_v[1]).astype(BF16)
            outs.append(begin(gm_v, gm_out, out_sems.at[2]))
            small_out[...] = jnp.zeros_like(small_out)
            for row in range(6):
                small_out[row : row + 1] = col_sum(sums[row])
            for copy in outs:
                copy.wait()

    stack = (MICRO, rows, width)
    plain = pltpu.VMEM((rows, width), BF16)
    full = pltpu.VMEM((rows, width), F32)
    chunks = pltpu.VMEM((steps, rows, CHUNK), BF16)
    return manual(
        kernel,
        info,
        [(array, False) for array in tokens]
        + [
            (kept["branch"], False),
            (kept["slope"], False),
            (kept["residual"], False),
            (kept["attended"], False),
            (vec, True),
            (wo_own, False),
            (wo_oth, False),
            (wu_own, False),
            (wu_oth, False),
            (wd_own, False),
            (wd_oth, False),
        ],
        [
            (stack, BF16, False, None if scaled else grads.get("branch")),
            ((MICRO, rows, hidden), BF16, False, grads.get("before")),
            (stack, BF16, False, grads.get("attended")),
            ((rows, width), BF16, False, None),
            ((rows, width), F32, False, None),
            ((8, width), F32, True, None),
            ((steps, CHUNK), F32, True, None),
        ],
        [
            plain,
            plain,
            chunks,
            full,
            plain,
            pltpu.VMEM((2, half, width), BF16),
            pltpu.VMEM((steps, width, CHUNK), BF16),
            pltpu.VMEM((steps, CHUNK, width), BF16),
            plain,
            pltpu.VMEM((2, rows, CHUNK), F32),
            chunks,
            plain,
            plain,
            full,
            full,
            pltpu.VMEM((6, 8, width), F32),
            dma_sems(2),
            dma_sems(5),
            dma_sems(steps),
            dma_sems(steps),
            dma_sems(steps),
            dma_sems(4),
            dma_sems(steps),
        ],
        flops=4 * rows * width * hidden + 2 * rows * width * width,
        moved=4 * width * hidden + 2 * width * width + 8 * rows * hidden,
        after=after,
    )


def attend_backward(info, owner, number, grad_mixed, kept, after=()):
    _, rows, width = kept["q"].shape
    heads = width // HEAD_DIM
    lanes = 2 * HEAD_DIM
    block = 2 * lanes
    steps = width // block
    score_scale = HEAD_DIM**-0.5

    def kernel(s, *refs):
        @pl.when(s[ACTIVE + owner] == 1)
        def _():
            compute(*refs)

    def compute(gm, q_ref, kv, grown, full, inv, dq_out, here_out, there_out, *scratch):
        probs, scores = scratch[:4], scratch[4:8]
        own_v, centre_v = scratch[8:]
        first_q = lax.broadcasted_iota(jnp.int32, (rows, lanes), 1) < HEAD_DIM
        first_t = lax.broadcasted_iota(jnp.int32, (TILE, lanes), 1) < HEAD_DIM

        def columns(head):
            return slice(head // 2 * lanes, (head // 2 + 1) * lanes)

        for pair in range(2):
            place = columns(2 * pair)
            for t in tiles(rows):
                scaled = (gm[t, place].astype(F32) * inv[0, t, place]).astype(BF16)
                product = scaled.astype(F32) * full[0, t, place]
                for side in range(2):
                    mine = first_t if side == 0 else ~first_t
                    own_v[2 * pair + side, t] = jnp.where(mine, scaled, 0)
                    centre_v[2 * pair + side, t] = jnp.sum(
                        jnp.where(mine, product, 0.0), axis=-1, keepdims=True
                    )

        def prob(head):
            probs[head][...] = dot_nt(own_v[head], kv[0, 1, :, columns(head)])

        prob(0)
        grad_q, grad_k, grad_v = [], [], []
        for head in range(4):
            if head < 3:
                prob(head + 1)
            for t in tiles(rows):
                weight = grown[0, head, t].astype(F32)
                scores[head][t] = (weight * (probs[head][t] - centre_v[head, t])).astype(BF16)
            mine = first_q if head % 2 == 0 else ~first_q
            grad_v.append(dot_tn(grown[0, head], own_v[head]))
            grad_q.append(dot(scores[head][...], kv[0, 0, :, columns(head)]))
            masked = jnp.where(mine, q_ref[0, :, columns(head)], 0)
            grad_k.append(dot_tn(scores[head][...], masked))
            if head % 2 == 1:
                place = columns(head)
                dq = jnp.where(first_q, grad_q[head - 1], grad_q[head]) * score_scale
                dq_out[:, place] = dq.astype(BF16)
                dk = ((grad_k[head - 1] + grad_k[head]) * score_scale).astype(BF16)
                dv = (grad_v[head - 1] + grad_v[head]).astype(BF16)
                here_out[0, :, place] = dk[:rows]
                here_out[1, :, place] = dv[:rows]
                there_out[0, :, place] = dk[rows:]
                there_out[1, :, place] = dv[rows:]

    def on(s):
        return s[ACTIVE + owner]

    def slot(s):
        return jnp.where(on(s) == 1, number, SPARE)

    column = lambda i, s: (slot(s), 0, i * on(s))
    plain = lambda i, s: (0, i * on(s))
    return call(
        kernel,
        info,
        (steps,),
        [
            (grad_mixed, (rows, block), plain),
            (kept["q"], (1, rows, block), lambda i, s: (number, 0, i * on(s))),
            (kept["kv"], (1, 2, 2 * rows, block), lambda i, s: (slot(s), 0, 0, i * on(s))),
            (kept["grown"], (1, 4, rows, 2 * rows), lambda i, s: (slot(s), i * on(s), 0, 0)),
            (kept["mixed_full"], (1, rows, block), column),
            (kept["inverse"], (1, rows, block), column),
        ],
        [
            ((rows, width), BF16, (rows, block), plain, None),
            ((2, rows, width), BF16, (2, rows, block), lambda i, s: (0, 0, i * on(s)), None),
            ((2, rows, width), BF16, (2, rows, block), lambda i, s: (0, 0, i * on(s)), None),
        ],
        [pltpu.VMEM((rows, 2 * rows), F32)] * 4
        + [pltpu.VMEM((rows, 2 * rows), BF16)] * 4
        + [pltpu.VMEM((4, rows, lanes), BF16), pltpu.VMEM((4, rows, 1), F32)],
        flops=16 * rows * rows * width,
        moved=4 * heads * rows * rows + 30 * rows * width,
        after=after,
    )


def qkv_backward(info, owner, number, dq, dkv_here, dkv_there, w_own, w_oth, grad_res, vec, kept, grads, after=()):
    _, rows, width = kept["x"].shape
    half = width // 2

    def kernel(s, dq_ref, here, there, own, oth, gr, x_ref, v, packed_out, gx_out, relay_out,
               small_out, shift_out, a_v, b_v, p_v, w_v, gr_v, x_v, gx_v, acc, sums,
               a_sems, b_sems, w_sems, in_sems, packed_sems, out_sems):
        @pl.when(s[ACTIVE + owner] == 0)
        def _():
            small_out[...] = jnp.zeros_like(small_out)
            shift_out[...] = jnp.zeros_like(shift_out)

        @pl.when(s[ACTIVE + owner] == 1)
        def _():
            slot = number
            loads = []
            for part in range(6):
                kind, side = part % 3, part // 3
                columns = pl.ds(side * half, half)
                if kind == 0:
                    copies = [begin(dq_ref.at[:, columns], a_v.at[part], a_sems.at[part])]
                else:
                    turned = pl.ds((1 - side) * half, half)
                    copies = [
                        begin(here.at[kind - 1, :, columns], a_v.at[part], a_sems.at[part]),
                        begin(there.at[kind - 1, :, turned], b_v.at[part], b_sems.at[part]),
                    ]
                weight = own if side == 0 else oth
                copies.append(begin(weight.at[kind], w_v.at[part], w_sems.at[part]))
                loads.append(copies)
            last = [
                begin(x_ref.at[slot], x_v, in_sems.at[0]),
                begin(gr, gr_v, in_sems.at[1]),
            ]
            outs = []
            for part in range(6):
                for copy in loads[part]:
                    copy.wait()
                total = jnp.zeros((8, half), F32)
                for t in tiles(rows):
                    packed = a_v[part, t]
                    if part % 3 > 0:
                        packed = (packed.astype(F32) + b_v[part, t].astype(F32)).astype(BF16)
                    p_v[part, t] = packed
                    total = total + eights(packed.astype(F32))
                shift_out[part : part + 1] = col_sum(total)
                outs.append(
                    begin(
                        p_v.at[part],
                        packed_out.at[slot, :, pl.ds(part * half, half)],
                        packed_sems.at[part],
                    )
                )
                product = dot_nt(p_v[part], w_v[part])
                acc[...] = product if part == 0 else acc[...] + product
            for copy in last:
                copy.wait()
            sums[...] = jnp.zeros_like(sums)
            for t in tiles(rows):
                hat, scale = norm_stats(x_v[t].astype(F32))
                error = acc[t]
                grad = gr_v[t] + norm_backward(hat, scale, v[LN1G : LN1G + 1], error)
                gx_v[t] = grad.astype(BF16)
                sums[0] += eights(error * hat)
                sums[1] += eights(error)
            outs.append(begin(gx_v, relay_out, out_sems.at[0]))
            outs.append(begin(gx_v, gx_out.at[slot], out_sems.at[1]))
            small_out[...] = jnp.zeros_like(small_out)
            for row in range(2):
                small_out[row : row + 1] = col_sum(sums[row])
            for copy in outs:
                copy.wait()

    stack = (MICRO, rows, width)
    parts = pltpu.VMEM((6, rows, half), BF16)
    return manual(
        kernel,
        info,
        [
            (dq, False),
            (dkv_here, False),
            (dkv_there, False),
            (w_own, False),
            (w_oth, False),
            (grad_res, False),
            (kept["x"], False),
            (vec, True),
        ],
        [
            ((MICRO, rows, 3 * width), BF16, False, grads.get("packed")),
            (stack, BF16, False, grads.get("input")),
            ((rows, width), BF16, False, None),
            ((8, width), F32, True, None),
            ((8, half), F32, True, None),
        ],
        [
            parts,
            parts,
            parts,
            pltpu.VMEM((6, width, half), BF16),
            pltpu.VMEM((rows, width), F32),
            pltpu.VMEM((rows, width), BF16),
            pltpu.VMEM((rows, width), BF16),
            pltpu.VMEM((rows, width), F32),
            pltpu.VMEM((2, 8, width), F32),
            dma_sems(6),
            dma_sems(6),
            dma_sems(6),
            dma_sems(2),
            dma_sems(6),
            dma_sems(2),
        ],
        flops=6 * rows * width * width,
        moved=6 * width * width + 16 * rows * width,
        after=after,
    )


def swap(block):
    return lax.ppermute(block, "tensor", [(0, 1), (1, 0)])


def ring_order(count):
    return list(range(0, count, 2)) + list(range(count - 1, 0, -2))


def tied(value, *others):
    return lax.optimization_barrier((value, *others))[0]


class Ring:
    def __init__(self, info, parts, shapes, places):
        self.info, self.parts, self.shapes, self.places = info, parts, shapes, places
        self.count = lax.axis_size("dp")
        order = ring_order(self.count)
        n = self.count
        self.chunk = parts[0][0].shape[0] // (2 * n)
        self.widths = [pair[0].shape[1] for pair in parts]
        self.signs = (1, -1)
        self.routes = [[(order[i], order[(i + s) % n]) for i in range(n)] for s in self.signs]
        self.step = 0
        self.steps = 2 * (n - 1)
        self.totals = [None] * len(shapes)
        self.moving = self.add([0, 0], None)

    def unit(self, way, ahead):
        return UNITS + way * self.count + ahead % self.count

    def add(self, ahead, arrived, after=()):
        chunk, width, parts = self.chunk, sum(self.widths), len(self.parts)
        units = [self.unit(w, ahead[w]) for w in range(2)]
        terms = 2 if arrived is None else 3

        def kernel(s, *refs):
            halves = refs[: 2 * parts]
            refs = refs[2 * parts :]
            if terms == 3:
                arrivals, refs = refs[:2], refs[2:]
            outs, (held, sems) = refs[:2], refs[2:]
            copies = []
            for w in range(2):
                rows = pl.ds(pl.multiple_of(s[units[w]] * chunk, chunk), chunk)
                base = 0
                for number, columns in enumerate(self.widths):
                    for term in range(2):
                        copies.append(
                            begin(
                                halves[2 * number + term].at[rows],
                                held.at[w, term, :, pl.ds(base, columns)],
                                sems.at[w, term, number],
                            )
                        )
                    base += columns
                if terms == 3:
                    copies.append(begin(arrivals[w], held.at[w, 2], sems.at[w, 2, 0]))
            for copy in copies:
                copy.wait()
            for w in range(2):
                for t in tiles(chunk):
                    for first in range(0, width, 512):
                        c = slice(first, min(first + 512, width))
                        total = held[w, 0, t, c].astype(F32) + held[w, 1, t, c].astype(F32)
                        if terms == 3:
                            total = total + held[w, 2, t, c].astype(F32)
                        outs[w][t, c] = total.astype(BF16)

        arrays = [(term, False) for pair in self.parts for term in pair]
        if arrived is not None:
            arrays += [(block, False) for block in arrived]
        return manual(
            kernel,
            self.info,
            arrays,
            [((chunk, width), BF16, True, None)] * 2,
            [pltpu.VMEM((2, terms, chunk, width), BF16), pltpu.SemaphoreType.DMA((2, 3, parts))],
            moved=2 * (terms + 1) * 2 * chunk * width,
            vmem=RING_MIB,
            after=after,
        )

    def put(self, ahead, blocks, after=()):
        chunk, width = self.chunk, sum(self.widths)
        units = [self.unit(w, pair[w]) for pair in ahead for w in range(2)]
        size = len(units)
        count = len(self.shapes)
        pieces = sum(len(self.places.columns(c)) for c in range(count))

        def kernel(s, *refs):
            sources, outs = refs[:size], refs[size : size + count]
            held, wide, in_sems, out_sems = refs[size + count + 2 :]
            loads = [begin(sources[w], held.at[w], in_sems.at[w]) for w in range(size)]
            copies = []
            for w in range(size):
                loads[w].wait()
                for t in tiles(chunk):
                    for first in range(0, width, 512):
                        c = slice(first, min(first + 512, width))
                        wide[w, t, c] = held[w, t, c].astype(F32)
                number = 0
                for target in range(count):
                    for first, columns in self.places.columns(target):
                        ref = self.places.ref(
                            outs[target], target, first, columns, s[units[w]], chunk
                        )
                        copies.append(
                            begin(
                                wide.at[w, :, pl.ds(first, columns)],
                                ref,
                                out_sems.at[w, number],
                            )
                        )
                        number += 1
            for copy in copies:
                copy.wait()

        results = manual(
            kernel,
            self.info,
            [(block, False) for block in blocks[:-2]] + [(block, False) for block in blocks[-2:]],
            [(shape, F32, False, old) for shape, old in zip(self.shapes, self.totals)]
            + [((chunk, width), BF16, False, None)] * 2,
            [
                pltpu.VMEM((size, chunk, width), BF16),
                pltpu.VMEM((size, chunk, width), F32),
                dma_sems(size),
                pltpu.SemaphoreType.DMA((size, pieces)),
            ],
            moved=2 * 6 * chunk * width,
            vmem=RING_MIB,
            after=after,
            same={size - 2: count, size - 1: count + 1},
        )
        self.totals = list(results[:count])
        return list(results[count:])

    def advance(self, *after):
        arrived = [lax.ppermute(self.moving[w], "dp", self.routes[w]) for w in range(2)]
        if after:
            arrived = list(lax.optimization_barrier((*arrived, *after))[:2])
        step = self.step
        if step < self.count - 1:
            self.moving = self.add([-s * (step + 1) for s in self.signs], arrived)
        else:
            ahead = [[-s * (step - self.count + 1) for s in self.signs]]
            blocks = arrived
            if step == self.count - 1:
                ahead.insert(0, self.signs)
                blocks = list(self.moving) + arrived
            self.moving = self.put(ahead, blocks)
        self.step += 1

    def done(self):
        return self.step == self.steps

    def finish(self):
        while not self.done():
            self.advance()
        return self.totals


class WholeRows:
    def __init__(self, width):
        self.width = width

    def columns(self, target):
        return [(0, self.width)]

    def ref(self, out, target, first, columns, unit, chunk):
        return out.at[pl.ds(pl.multiple_of(unit * chunk, chunk), chunk)]


class TailPlaces:
    def __init__(self, half, lanes):
        self.half, self.lanes = half, lanes

    def columns(self, target):
        half = self.half
        if target == 0:
            return [(j * half, half) for j in range(3)]
        return [(3 * half, half)] if target == 1 else [(4 * half, self.lanes)]

    def ref(self, out, target, first, columns, unit, chunk):
        rows = pl.ds(pl.multiple_of(unit * chunk, chunk), chunk)
        if target == 0:
            return out.at[first // self.half, rows]
        if target == 2:
            return out.at[rows]
        each = self.half // chunk
        return out.at[
            pl.ds(pl.multiple_of(lax.rem(unit, each) * chunk, chunk), chunk),
            pl.ds(pl.multiple_of(lax.div(unit, each) * self.half, self.half), self.half),
        ]


def partner_tokens(info, block, numbers):
    _, _, seq, half = block.shape
    rows = seq // 2

    def kernel(s, ref, out, sems):
        start = pl.multiple_of((1 - s[RANK]) * rows, rows)
        copies = [
            begin(ref.at[number, 0, pl.ds(start, rows)], out.at[place], sems.at[place])
            for place, number in enumerate(numbers)
        ]
        for copy in copies:
            copy.wait()

    return manual(
        kernel,
        info,
        [(block, False)],
        [((len(numbers), rows, half), BF16, True, None)],
        [dma_sems(len(numbers))],
        vmem=8,
    )[0]


def partner_features(info, block):
    micro, rows, width = block.shape
    half = width // 2

    def kernel(s, ref, out, sems):
        start = pl.multiple_of((1 - s[RANK]) * half, half)
        copies = [
            begin(ref.at[m, :, pl.ds(start, half)], out.at[m], sems.at[m]) for m in range(micro)
        ]
        for copy in copies:
            copy.wait()

    return manual(
        kernel,
        info,
        [(block, False)],
        [((micro, rows, half), BF16, True, None)],
        [dma_sems(micro)],
        vmem=8,
    )[0]


def join_tokens(info, block, received):
    micro, rows, width = block.shape
    half = width // 2

    def kernel(s, ref, other, out, sems):
        rank = s[RANK]
        features = pl.ds(pl.multiple_of(rank * half, half), half)
        here = pl.ds(pl.multiple_of(rank * rows, rows), rows)
        there = pl.ds(pl.multiple_of((1 - rank) * rows, rows), rows)
        copies = []
        for m in range(micro):
            copies.append(begin(ref.at[m, :, features], out.at[0, m, 0, here], sems.at[0, m]))
            copies.append(begin(other.at[m], out.at[0, m, 0, there], sems.at[1, m]))
        for copy in copies:
            copy.wait()

    return manual(
        kernel,
        info,
        [(block, False), (received, False)],
        [((1, micro, 1, 2 * rows, half), BF16, True, None)],
        [pltpu.SemaphoreType.DMA((2, micro))],
        vmem=8,
    )[0]


LANES = 128


def gather_vectors(info, sums, rows_out):
    calls = len(sums)
    width = sums[0][0].shape[1]
    half = width // 2

    def kernel(s, *refs):
        own, oth = refs[4 * calls :]
        low = s[RANK] == 0

        def total(kind):
            blocks = [refs[4 * c + kind][...] for c in range(calls)]
            return sum(blocks[1:], blocks[0])

        two, up, one, qkv = [total(kind) for kind in range(4)]
        own[...] = jnp.zeros_like(own)
        oth[...] = jnp.zeros_like(oth)
        place = 0

        def write(first, second):
            nonlocal place
            for c in range(0, half, LANES):
                own[place : place + 1] = first[:, c : c + LANES].astype(BF16)
                oth[place : place + 1] = second[:, c : c + LANES].astype(BF16)
                place += 1

        for block, count in ((one, 2), (two, 6)):
            for row in range(count):
                line = block[row : row + 1]
                left, right = line[:, :half], line[:, half:]
                write(jnp.where(low, left, right), jnp.where(low, right, left))
        for row in range(3):
            write(qkv[row : row + 1], qkv[3 + row : 4 + row])
        hidden_rows = up.shape[0] // 2
        for row in range(hidden_rows):
            write(up[row : row + 1], up[hidden_rows + row : hidden_rows + row + 1])

    vmem = pl.BlockSpec(memory_space=pltpu.VMEM)
    return pl.pallas_call(
        kernel,
        in_specs=[pl.BlockSpec(memory_space=pltpu.SMEM)] + [vmem] * (4 * calls),
        out_specs=[vmem] * 2,
        out_shape=[jax.ShapeDtypeStruct((rows_out, LANES), BF16)] * 2,
    )(info, *[block for group in sums for block in group])


def spread_vectors(sums, half, hidden_half):
    def kernel(ref, *outs):
        def line(number, out, row=0, columns=half, first=0):
            for c in range(0, columns, LANES):
                place = (number * half + c) // LANES
                out[row : row + 1, first + c : first + c + LANES] = ref[place : place + 1]

        for number in range(8):
            line(number, outs[number])
        line(8, outs[8])
        line(10, outs[8], row=1)
        line(11, outs[9], columns=hidden_half)

    vmem = pl.BlockSpec(memory_space=pltpu.VMEM)
    shapes = [(1, half)] * 8 + [(2, half), (1, hidden_half)]
    return pl.pallas_call(
        kernel,
        in_specs=[vmem],
        out_specs=[vmem] * 10,
        out_shape=[jax.ShapeDtypeStruct(shape, F32) for shape in shapes],
    )(sums)


def pack_vectors(blocks, hidden_bias):
    half = blocks[0].shape[1]
    hidden_rows = hidden_bias.shape[1] // half
    filled = sum(b.shape[0] for b in blocks)

    def kernel(*refs):
        out = refs[-1]
        place = 0
        for ref in refs[: len(blocks)]:
            for row in range(ref.shape[0]):
                out[place : place + 1] = ref[row : row + 1].astype(F32)
                place += 1
        for row in range(hidden_rows):
            columns = slice(row * half, (row + 1) * half)
            out[place : place + 1] = refs[len(blocks)][:, columns].astype(F32)
            place += 1

    return pl.pallas_call(
        kernel, out_shape=jax.ShapeDtypeStruct((filled + hidden_rows, half), F32)
    )(*blocks, hidden_bias)


def join_vectors(scalars, own, oth, hidden_rows):
    half = own.shape[1]

    def kernel(s, own_ref, oth_ref, vec, bias_q, bias_v, bias_up):
        low = s[RANK] == 0
        vec[:, :half] = jnp.where(low, own_ref[:8], oth_ref[:8])
        vec[:, half:] = jnp.where(low, oth_ref[:8], own_ref[:8])
        for row, out in ((8, bias_q), (9, bias_v)):
            out[:, :half] = own_ref[row : row + 1]
            out[:, half:] = oth_ref[row : row + 1]
        bias_up[:hidden_rows] = own_ref[10 : 10 + hidden_rows]
        bias_up[hidden_rows:] = oth_ref[10 : 10 + hidden_rows]

    vmem = pl.BlockSpec(memory_space=pltpu.VMEM)
    return pl.pallas_call(
        kernel,
        in_specs=[pl.BlockSpec(memory_space=pltpu.SMEM), vmem, vmem],
        out_specs=[vmem] * 4,
        out_shape=[
            jax.ShapeDtypeStruct((8, 2 * half), F32),
            jax.ShapeDtypeStruct((1, 2 * half), F32),
            jax.ShapeDtypeStruct((1, 2 * half), F32),
            jax.ShapeDtypeStruct((2 * hidden_rows, half), F32),
        ],
    )(scalars, own, oth)


def shards(
    inputs,
    cotangent,
    ln1_gain,
    ln1_bias,
    qkv_weight,
    qv_bias,
    out_weight,
    out_bias,
    scale_attn,
    ln2_gain,
    ln2_bias,
    fc1_weight,
    fc1_bias,
    fc2_weight,
    fc2_bias,
    scale_mlp,
):
    micro, images, seq_len, half = inputs.shape
    assert micro == MICRO and images == 1
    width = 2 * half
    hidden_half = fc1_weight.shape[2]

    count = lax.axis_size("dp")
    order = ring_order(count)
    table = [
        [rank, int(section == 0), int(section == 1)]
        + [way * count + (order.index(i) + ahead) % count for way in range(2) for ahead in range(count)]
        for section in range(2)
        for rank in range(2)
        for i in range(count)
    ]
    info = lax.dynamic_slice(
        jnp.asarray(table, jnp.int32),
        (lax.axis_index(("section", "tensor", "dp")), 0),
        (1, len(table[0])),
        allow_negative_indices=False,
    ).reshape(-1)

    first_oth = swap(partner_tokens(info, inputs, (0,))[0])
    vectors = pack_vectors(
        [
            ln1_gain, ln1_bias, out_bias, scale_attn, ln2_gain, ln2_bias, fc2_bias, scale_mlp,
            qv_bias[0],
        ],
        fc1_bias,
    )
    vectors_oth = swap(vectors)
    wq_own = jnp.transpose(qkv_weight[0], (1, 0, 2))
    wq_oth = swap(tied(wq_own, vectors))
    vec, bias_q, bias_v, b_up = join_vectors(info, vectors, vectors_oth, hidden_half // half)
    b_up = b_up.reshape(2 * hidden_half // CHUNK, CHUNK)
    wo_own, wu_own, wd_own = out_weight[0], fc1_weight[0], fc2_weight[0]
    wo_oth = swap(tied(wo_own, first_oth, vectors_oth))
    wu_oth = swap(tied(wu_own, first_oth, vectors_oth))
    wd_oth = swap(tied(wd_own, first_oth, vectors_oth))
    second_oth = swap(partner_tokens(info, tied(inputs, wd_oth), (1,))[0])
    cot_oth = swap(partner_tokens(info, tied(cotangent, wd_oth), (0, 1)))

    kept = {}

    def forward(owner, number, source, tokens, after=(), late=()):
        kept["x"], kept["normed1"], kv_here = norm_kv(
            info, owner, number, source, tokens, vec, wq_own, wq_oth, bias_v, kept, after
        )
        kv_there = swap(kv_here)
        kept["q"] = project_q(info, owner, number, kept["normed1"], wq_own, wq_oth, bias_q, kept)
        kept["grown"], kept["mixed_full"], mixed, kept["inverse"], kept["kv"] = attend(
            info, owner, number, kept["q"], kv_here, kv_there, kept
        )
        (
            kept["attended"],
            kept["residual"],
            kept["normed2"],
            kept["active"],
            kept["slope"],
            kept["branch"],
            kept["output"],
            relayed,
            kept["mixed"],
        ) = mlp_forward(
            info, owner, number, mixed, kept["x"], vec, wo_own, wo_oth, wu_own, wu_oth, wd_own,
            wd_oth, b_up, kept, late,
        )
        return relayed

    grads = {}
    sums = []

    def backward_mlp(owner, number, source, tokens, after, scaled=False):
        (
            branch,
            grads["before"],
            grads["attended"],
            grad_mixed,
            grad_res,
            small,
            shift,
        ) = mlp_backward(
            info, owner, number, source, tokens, vec, wo_own, wo_oth, wu_own, wu_oth, wd_own,
            wd_oth, kept, grads, scaled, after,
        )
        if not scaled:
            grads["branch"] = branch
        return grad_mixed, grad_res, small, shift

    def backward_attention(owner, number, grad_mixed, after=()):
        dq, dkv_here, dkv_send = attend_backward(info, owner, number, grad_mixed, kept, after)
        return dq, dkv_here, swap(dkv_send)

    def backward_qkv(owner, number, dq, dkv_here, dkv_there, grad_res, small, shift, after=()):
        grads["packed"], grads["input"], relayed, small_one, shift_qkv = qkv_backward(
            info, owner, number, dq, dkv_here, dkv_there, wq_own, wq_oth, grad_res, vec, kept,
            grads, after,
        )
        sums.append((small, shift, small_one, shift_qkv))
        return relayed

    def backward(owner, number, source, tokens, after):
        grad_mixed, grad_res, small, shift = backward_mlp(owner, number, source, tokens, after)
        flows = backward_attention(owner, number, grad_mixed)
        return backward_qkv(owner, number, *flows, grad_res, small, shift)

    relayed = forward(0, 0, "argument", (inputs, first_oth))
    first = lax.ppermute(relayed, "section", [(0, 1)])
    relayed = forward(0, 1, "argument", (inputs, second_oth), [relayed])
    second = lax.ppermute(relayed, "section", [(0, 1)])
    relayed = forward(1, 0, "relay", (first,), [relayed])
    relayed = backward(1, 0, "argument", (cotangent, cot_oth[0]), [relayed, second])
    first = lax.ppermute(relayed, "section", [(1, 0)])
    relayed = forward(1, 1, "relay", (second,), [relayed], [first])
    relayed = backward(1, 1, "argument", (cotangent, cot_oth[1]), [relayed])
    second = lax.ppermute(relayed, "section", [(1, 0)])
    relayed = backward(0, 0, "relay", (first,), [relayed])

    def weight_grad(left, right):
        return lax.dot_general(
            left, right, (((0, 1), (0, 1)), ((), ())), preferred_element_type=F32
        ).astype(BF16)

    grads["branch"] = scale_branch(info, 0, 1, second, vec, grads["branch"], [relayed])
    active, g_branch = kept["active"], grads["branch"]
    down_oth = weight_grad(active[:, :, hidden_half:], g_branch)
    down_sent = swap(down_oth)
    down_own = weight_grad(active[:, :, :hidden_half], g_branch)
    ring_down = Ring(info, [(down_own, down_sent)], [down_own.shape], WholeRows(width))
    second = tied(second, *ring_down.moving)
    grad_mixed, grad_res, small, shift = backward_mlp(
        0, 1, "relay", (second,), list(ring_down.moving), scaled=True
    )
    ring_down.advance(grad_mixed)
    normed2 = tied(kept["normed2"], *ring_down.moving)
    before = grads["before"]
    up_oth = weight_grad(normed2, before[:, :, hidden_half:])
    up_sent = swap(up_oth)
    ring_down.advance(up_oth)
    normed2 = tied(normed2, *ring_down.moving)
    up_own = weight_grad(normed2, before[:, :, :hidden_half])
    ring_down.advance(up_own)
    ring_up = Ring(info, [(up_own, up_sent)], [up_own.shape], WholeRows(hidden_half))
    grad_mixed = tied(grad_mixed, *ring_down.moving, *ring_up.moving)
    flows = backward_attention(0, 1, grad_mixed)
    ring_down.advance(flows[0])
    ring_up.advance(flows[0])
    grad_res = tied(grad_res, *ring_down.moving, *ring_up.moving)
    backward_qkv(0, 1, *flows, grad_res, small, shift)
    packed = grads["packed"]
    ring_down.advance(packed)
    ring_up.advance(packed)
    normed1 = tied(kept["normed1"], *ring_down.moving, *ring_up.moving)
    vectors = gather_vectors(info, sums, width)

    def tail(index):
        columns = packed[:, :, index * 3 * half : (index + 1) * 3 * half]
        mixed = kept["mixed"][:, :, index * half : (index + 1) * half]
        g_att = grads["attended"]
        outs = [weight_grad(mixed, g_att[:, :, half * j : half * (j + 1)]) for j in range(2)]
        return [weight_grad(normed1, columns), jnp.concatenate(outs, axis=0), vectors[index]]

    tail_oth = tail(1)
    tail_sent = [swap(block) for block in tail_oth]
    ring_down.advance(tail_oth[0])
    ring_up.advance(tail_oth[0])
    normed1 = tied(normed1, *ring_down.moving, *ring_up.moving)
    tail_own = tail(0)
    ring_down.advance(tail_own[0])
    ring_up.advance(tail_own[0])
    ring_tail = Ring(
        info,
        list(zip(tail_own, tail_sent)),
        [(3, width, half), (half, width), (width, LANES)],
        TailPlaces(half, LANES),
    )
    rings = [ring_down, ring_up, ring_tail]
    before_it = ring_tail
    while not all(ring.done() for ring in rings):
        for ring in rings:
            if not ring.done():
                ring.advance(*before_it.moving)
                before_it = ring
    (total_down,) = ring_down.finish()
    (total_up,) = ring_up.finish()
    total_qkv, total_out, total_vectors = ring_tail.finish()
    block_outputs = join_tokens(info, kept["output"], swap(partner_features(info, kept["output"])))
    input_grads = join_tokens(info, grads["input"], swap(partner_features(info, grads["input"])))
    rows = spread_vectors(total_vectors, half, hidden_half)
    return (
        block_outputs,
        input_grads,
        rows[0],
        rows[1],
        jnp.transpose(total_qkv, (1, 0, 2))[None],
        rows[8][None],
        total_out[None],
        rows[7],
        rows[6],
        rows[4],
        rows[5],
        total_up[None],
        rows[9],
        total_down[None],
        rows[3],
        rows[2],
    )


def solution(mesh):
    placed = (
        P(None, "dp", None, "tensor"),
        P(None, "dp", None, "tensor"),
        P("section", "tensor"),
        P("section", "tensor"),
        P("section", None, None, "tensor"),
        P("section", None, "tensor"),
        P("section", "tensor", None),
        P("section", "tensor"),
        P("section", "tensor"),
        P("section", "tensor"),
        P("section", "tensor"),
        P("section", None, "tensor"),
        P("section", "tensor"),
        P("section", "tensor", None),
        P("section", "tensor"),
        P("section", "tensor"),
    )
    return jax.shard_map(
        shards,
        mesh=mesh,
        in_specs=placed,
        out_specs=(
            P("section", None, "dp", None, "tensor"),
            P("section", None, "dp", None, "tensor"),
            P("section", "tensor"),
            P("section", "tensor"),
            P("section", None, None, "tensor"),
            P("section", None, "tensor"),
            P("section", "tensor", None),
            P("section", "tensor"),
            P("section", "tensor"),
            P("section", "tensor"),
            P("section", "tensor"),
            P("section", None, "tensor"),
            P("section", "tensor"),
            P("section", "tensor", None),
            P("section", "tensor"),
            P("section", "tensor"),
        ),
        check_vma=False,
    )
```

```python
import math

import jax
import jax.numpy as jnp
from jax import lax
from jax.experimental import pallas as pl
from jax.experimental.pallas import tpu as pltpu
from jax.sharding import PartitionSpec as P

HEAD_DIM = 64
EPSILON = 1e-06
F32 = jnp.float32
BF16 = jnp.bfloat16
MIB = 1 << 20
VMEM_MIB = 62
RING_MIB = 61
TILE = 16
MICRO = 2
SPARE = MICRO
RANK, ACTIVE, UNITS = 0, 1, 3
LN1G, LN1B, OUTB, SATT, LN2G, LN2B, FC2B, SMLP = range(8)


def dot(left, right):
    return jnp.dot(left, right, preferred_element_type=F32)


def dot_nt(left, right):
    return lax.dot_general(left, right, (((1,), (1,)), ((), ())), preferred_element_type=F32)


def dot_tn(left, right):
    return lax.dot_general(left, right, (((0,), (0,)), ((), ())), preferred_element_type=F32)


def norm_stats(values):
    centre = jnp.mean(values, axis=-1, keepdims=True)
    centred = values - centre
    spread = jnp.mean(centred * centred, axis=-1, keepdims=True)
    scale = lax.rsqrt(spread + EPSILON)
    return centred * scale, scale


def tiles(rows):
    return [slice(r, r + TILE) for r in range(0, rows, TILE)]


def each_tile(rows, body):
    def step(i, carry):
        body(pl.ds(pl.multiple_of(i * TILE, TILE), TILE))
        return carry

    lax.fori_loop(0, rows // TILE, step, 0, unroll=2)


def eights(values):
    total = values[:8]
    for r in range(8, values.shape[0], 8):
        total = total + values[r : r + 8]
    return total


def norm_backward(hat, scale, gain, error):
    weighted = error * gain
    mean_one = jnp.mean(weighted, axis=-1, keepdims=True)
    mean_two = jnp.mean(weighted * hat, axis=-1, keepdims=True)
    return scale * (weighted - mean_one - hat * mean_two)


def col_sum(values):
    return jnp.sum(values, axis=0, keepdims=True)


def call(kernel, scalars, grid, ins, outs, scratch=(), flops=0, moved=0, after=()):
    arrays = [a for a, _, _ in ins]
    in_specs = [pl.BlockSpec(b, m) for _, b, m in ins]
    aliases = {}
    for number, out in enumerate(outs):
        if out[4] is not None:
            aliases[1 + len(arrays)] = number
            arrays.append(out[4])
            in_specs.append(pl.BlockSpec(memory_space=pl.ANY))
    arrays += after
    in_specs += [pl.BlockSpec(memory_space=pl.ANY)] * len(after)
    extra = len(aliases) + len(after)
    in_count = len(ins)

    def body(*refs):
        kernel(*refs[: 1 + in_count], *refs[1 + in_count + extra :])

    return pl.pallas_call(
        body,
        out_shape=[jax.ShapeDtypeStruct(s, d) for s, d, _, _, _ in outs],
        grid_spec=pltpu.PrefetchScalarGridSpec(
            num_scalar_prefetch=1,
            grid=grid,
            in_specs=in_specs,
            out_specs=[pl.BlockSpec(b, m) for _, _, b, m, _ in outs],
            scratch_shapes=list(scratch),
        ),
        input_output_aliases=aliases,
        compiler_params=pltpu.CompilerParams(
            dimension_semantics=("arbitrary",) * len(grid), vmem_limit_bytes=VMEM_MIB * MIB
        ),
        cost_estimate=pl.CostEstimate(
            flops=int(flops), bytes_accessed=int(moved), transcendentals=0
        ),
    )(scalars, *arrays)


def manual(kernel, scalars, ins, outs, scratch, flops=0, moved=0, vmem=VMEM_MIB, after=(), same=None):
    any_space = pl.BlockSpec(memory_space=pl.ANY)
    vmem_space = pl.BlockSpec(memory_space=pltpu.VMEM)
    arrays = [a for a, _ in ins]
    in_specs = [vmem_space if inside else any_space for _, inside in ins]
    aliases = {1 + i: o for i, o in (same or {}).items()}
    before = len(arrays)
    for number, out in enumerate(outs):
        if out[3] is not None:
            aliases[1 + len(arrays)] = number
            arrays.append(out[3])
            in_specs.append(any_space)
    arrays += after
    in_specs += [any_space] * len(after)
    extra = len(arrays) - before
    in_count = len(ins)

    def body(*refs):
        kernel(*refs[: 1 + in_count], *refs[1 + in_count + extra :])

    return pl.pallas_call(
        body,
        out_shape=[jax.ShapeDtypeStruct(s, d) for s, d, _, _ in outs],
        in_specs=[pl.BlockSpec(memory_space=pltpu.SMEM)] + in_specs,
        out_specs=[vmem_space if inside else any_space for _, _, inside, _ in outs],
        scratch_shapes=list(scratch),
        input_output_aliases=aliases,
        compiler_params=pltpu.CompilerParams(vmem_limit_bytes=vmem * MIB),
        cost_estimate=pl.CostEstimate(
            flops=int(flops), bytes_accessed=int(moved), transcendentals=0
        ),
    )(scalars, *arrays)


def begin(src, dst, sem):
    copy = pltpu.make_async_copy(src, dst, sem)
    copy.start()
    return copy


def dma_sems(count):
    return pltpu.SemaphoreType.DMA((count,))


def whole2(i, s):
    return (0, 0)


def slot3(i, s):
    return (s[0], 0, 0)


def token_copies(s, source, number, refs, target, sems):
    rows, width = target.shape
    half = width // 2
    rank = s[RANK]
    if source == "relay":
        return [begin(refs[0], target, sems.at[0])]
    first = pl.multiple_of(rank * half, half)
    second = pl.multiple_of((1 - rank) * half, half)
    whole, other = refs
    return [
        begin(
            whole.at[number, 0, pl.ds(pl.multiple_of(rank * rows, rows), rows)],
            target.at[:, pl.ds(first, half)],
            sems.at[0],
        ),
        begin(other, target.at[:, pl.ds(second, half)], sems.at[1]),
    ]


def norm_kv(info, owner, number, source, tokens, vec, w_own, w_oth, bias_v, kept, after=()):
    rows, width = tokens[-1].shape[0], vec.shape[1]
    half = width // 2
    count = len(tokens)

    def kernel(s, *refs):
        token_refs = refs[:count]
        (v, own, oth, bv, x_out, n_out, kv_out, x_v, n_v, w_v, kv_v, tok_sems, w_sems,
         out_sems) = refs[count:]

        @pl.when(s[ACTIVE + owner] == 1)
        def _():
            arriving = token_copies(s, source, number, token_refs, x_v, tok_sems)
            for part in range(4):
                ref = own if part < 2 else oth
                begin(ref.at[1 + part % 2], w_v.at[part], w_sems.at[part])
            for copy in arriving:
                copy.wait()
            outs = [begin(x_v, x_out.at[number], out_sems.at[0])]

            def norm(t):
                hat, _ = norm_stats(x_v[t].astype(F32))
                n_v[t] = (hat * v[LN1G : LN1G + 1] + v[LN1B : LN1B + 1]).astype(BF16)

            each_tile(rows, norm)
            outs.append(begin(n_v, n_out.at[number], out_sems.at[1]))

            def out_copy(part):
                columns = pl.ds(pl.multiple_of(part // 2 * half, half), half)
                return pltpu.make_async_copy(
                    kv_v.at[part], kv_out.at[part % 2, :, columns], out_sems.at[2 + part]
                )

            def project(part, carry):
                pltpu.make_async_copy(own.at[0], w_v.at[part], w_sems.at[part]).wait()
                columns = pl.ds(pl.multiple_of(part // 2 * half, half), half)
                shift = bv[:, columns] * (part % 2).astype(F32)
                kv_v[part] = (dot(n_v[...], w_v[part]) + shift).astype(BF16)
                out_copy(part).start()
                return carry

            lax.fori_loop(0, 4, project, 0)
            for copy in outs:
                copy.wait()
            for part in range(4):
                out_copy(part).wait()

    stack = (MICRO, rows, width)
    return manual(
        kernel,
        info,
        [(array, False) for array in tokens]
        + [(vec, True), (w_own, False), (w_oth, False), (bias_v, True)],
        [
            (stack, BF16, False, kept.get("x")),
            (stack, BF16, False, kept.get("normed1")),
            ((2, rows, width), BF16, False, None),
        ],
        [
            pltpu.VMEM((rows, width), BF16),
            pltpu.VMEM((rows, width), BF16),
            pltpu.VMEM((4, width, half), BF16),
            pltpu.VMEM((4, rows, half), BF16),
            dma_sems(2),
            dma_sems(4),
            dma_sems(6),
        ],
        flops=2 * rows * width * 2 * width,
        moved=4 * width * width + 10 * rows * width,
        after=after,
    )


def project_q(info, owner, number, normed, w_own, w_oth, bias_q, kept):
    _, rows, width = normed.shape
    half = width // 2

    def kernel(s, n, own, oth, bq, q_out, n_v, w_v, q_v, in_sems, out_sems):
        @pl.when(s[ACTIVE + owner] == 1)
        def _():
            load = begin(n.at[number], n_v, in_sems.at[0])
            loads = [
                begin(own.at[0], w_v.at[0], in_sems.at[1]),
                begin(oth.at[0], w_v.at[1], in_sems.at[2]),
            ]
            load.wait()
            outs = []
            for side in range(2):
                loads[side].wait()
                columns = slice(side * half, (side + 1) * half)
                q_v[side] = (dot(n_v[...], w_v[side]) + bq[:, columns]).astype(BF16)
                outs.append(
                    begin(
                        q_v.at[side],
                        q_out.at[number, :, pl.ds(side * half, half)],
                        out_sems.at[side],
                    )
                )
            for copy in outs:
                copy.wait()

    return manual(
        kernel,
        info,
        [(normed, False), (w_own, False), (w_oth, False), (bias_q, True)],
        [((MICRO, rows, width), BF16, False, kept.get("q"))],
        [
            pltpu.VMEM((rows, width), BF16),
            pltpu.VMEM((2, width, half), BF16),
            pltpu.VMEM((2, rows, half), BF16),
            dma_sems(3),
            dma_sems(2),
        ],
        flops=2 * rows * width * width,
        moved=2 * width * width + 4 * rows * width,
    )[0]


def attend(info, owner, number, q, kv_here, kv_there, kept):
    _, rows, width = q.shape
    heads = width // HEAD_DIM
    factor = HEAD_DIM**-0.5 * math.log2(math.e)
    lanes = 2 * HEAD_DIM
    block = 2 * lanes
    steps = width // block

    def kernel(s, *refs):
        @pl.when(s[ACTIVE + owner] == 1)
        def _():
            compute(*refs)

    def compute(q_ref, here, there, e_out, o_out, mixed_out, inv_out, kv_out, *scratch):
        scores, results = scratch[:4], scratch[4:]
        kv_out[0, :, :rows] = here[...]
        kv_out[0, :, rows:] = there[...]
        first_q = lax.broadcasted_iota(jnp.int32, (rows, lanes), 1) < HEAD_DIM
        first_k = lax.broadcasted_iota(jnp.int32, (2 * rows, lanes), 1) < HEAD_DIM
        first_t = lax.broadcasted_iota(jnp.int32, (TILE, lanes), 1) < HEAD_DIM

        def columns(head):
            return slice(head // 2 * lanes, (head // 2 + 1) * lanes)

        def score(head):
            mine = first_q if head % 2 == 0 else ~first_q
            masked = jnp.where(mine, q_ref[0, :, columns(head)], 0)
            scores[head][...] = dot_nt(masked, kv_out[0, 0, :, columns(head)])

        score(0)
        for head in range(4):
            if head < 3:
                score(head + 1)
            for t in tiles(rows):
                tile = scores[head][t]
                top = jnp.max(tile, axis=-1, keepdims=True)
                e_out[0, head, t] = jnp.exp2((tile - top) * factor).astype(BF16)
            mine = first_k if head % 2 == 0 else ~first_k
            values = jnp.where(mine, kv_out[0, 1, :, columns(head)], 1)
            results[head][...] = dot(e_out[0, head], values)
        for pair in range(2):
            place = slice(pair * lanes, (pair + 1) * lanes)
            for t in tiles(rows):
                one, two = results[2 * pair][t], results[2 * pair + 1][t]
                total = jnp.where(
                    first_t, pltpu.roll(one, HEAD_DIM, 1), pltpu.roll(two, HEAD_DIM, 1)
                )
                inverse = 1.0 / total
                mixed = jnp.where(first_t, one, two) * inverse
                o_out[0, t, place] = mixed
                mixed_out[t, place] = mixed.astype(BF16)
                inv_out[0, t, place] = inverse

    def on(s):
        return s[ACTIVE + owner]

    def slot(s):
        return jnp.where(on(s) == 1, number, SPARE)

    column = lambda i, s: (slot(s), 0, i * on(s))
    spare = MICRO + 1
    return call(
        kernel,
        info,
        (steps,),
        [
            (q, (1, rows, block), lambda i, s: (number, 0, i * on(s))),
            (kv_here, (2, rows, block), lambda i, s: (0, 0, i * on(s))),
            (
                kv_there,
                (2, rows, block),
                lambda i, s: (0, 0, lax.rem(i + steps // 2, steps) * on(s)),
            ),
        ],
        [
            (
                (spare, heads, rows, 2 * rows),
                BF16,
                (1, 4, rows, 2 * rows),
                lambda i, s: (slot(s), i * on(s), 0, 0),
                kept.get("grown"),
            ),
            ((spare, rows, width), F32, (1, rows, block), column, kept.get("mixed_full")),
            ((rows, width), BF16, (rows, block), lambda i, s: (0, i * on(s)), None),
            ((spare, rows, width), F32, (1, rows, block), column, kept.get("inverse")),
            (
                (spare, 2, 2 * rows, width),
                BF16,
                (1, 2, 2 * rows, block),
                lambda i, s: (slot(s), 0, 0, i * on(s)),
                kept.get("kv"),
            ),
        ],
        [pltpu.VMEM((rows, 2 * rows), F32)] * 4 + [pltpu.VMEM((rows, lanes), F32)] * 4,
        flops=8 * rows * rows * width,
        moved=4 * heads * rows * rows + 30 * rows * width,
    )


def gelu_parts(x):
    size = jnp.abs(x)
    base = 1.0 + (0.3275911 * math.sqrt(0.5)) * size
    t = pl.reciprocal(base, approx=True)
    t = t * (2.0 - base * t)
    grown = jnp.exp2(x * x * (-0.5 * math.log2(math.e)))
    poly = 0.5 * 1.061405429
    for factor in (-1.453152027, 1.421413741, -0.284496736, 0.254829592):
        poly = poly * t + 0.5 * factor
    tail = poly * t * grown
    below = jnp.where(x < 0.0, tail, 1.0 - tail)
    return x * below, below + x * grown * (1.0 / math.sqrt(2.0 * math.pi))


CHUNK = 512


def mlp_forward(info, owner, number, mixed, x, vec, wo_own, wo_oth, wu_own, wu_oth, wd_own, wd_oth, b_up, kept, after=()):
    _, rows, width = x.shape
    side_hidden = wu_own.shape[1]
    hidden = 2 * side_hidden
    half = width // 2
    steps = hidden // CHUNK
    split = steps // 2

    def kernel(
        s, m, x_ref, v, woo, wot, wuo, wut, wdo, wdt, bu,
        att_out, res_out, n_out, act_out, slope_out, branch_out, y_out, relay_out, m_out,
        m_v, x_v, wo_v, wu_v, wd_v, att_v, res_v, n_v, h_one, h_two, act_v, slope_v, branch_v, y_v,
        acc,
        in_sems, wu_sems, wd_sems, out_sems, act_sems, slope_sems,
    ):
        @pl.when(s[ACTIVE + owner] == 1)
        def _():
            slot = number
            first = [
                begin(m, m_v, in_sems.at[0]),
                begin(woo, wo_v.at[0], in_sems.at[1]),
                begin(wot, wo_v.at[1], in_sems.at[2]),
                begin(x_ref.at[slot], x_v, in_sems.at[3]),
            ]
            for i in range(steps):
                part = pl.ds((i % split) * CHUNK, CHUNK)
                up, down = (wuo, wdo) if i < split else (wut, wdt)
                begin(up.at[:, part], wu_v.at[i], wu_sems.at[i])
                begin(down.at[part], wd_v.at[i], wd_sems.at[i])
            for copy in first:
                copy.wait()
            acc[...] = dot(m_v[:, :half], wo_v[0]) + dot(m_v[:, half:], wo_v[1])

            def first_norm(t):
                attended = acc[t] + v[OUTB : OUTB + 1]
                att_v[t] = attended.astype(BF16)
                residual = x_v[t].astype(F32) + v[SATT : SATT + 1] * attended
                res_v[t] = residual
                hat, _ = norm_stats(residual)
                n_v[t] = (hat * v[LN2G : LN2G + 1] + v[LN2B : LN2B + 1]).astype(BF16)

            each_tile(rows, first_norm)
            outs = [
                begin(att_v, att_out.at[slot], out_sems.at[0]),
                begin(res_v, res_out.at[slot], out_sems.at[1]),
                begin(n_v, n_out.at[slot], out_sems.at[2]),
                begin(m_v, m_out.at[slot], out_sems.at[6]),
            ]

            def up_product(i, target):
                target[...] = dot(n_v[...], wu_v[i])

            def up_wait(i):
                pltpu.make_async_copy(
                    wuo.at[:, pl.ds(0, CHUNK)], wu_v.at[i], wu_sems.at[i]
                ).wait()

            def down_wait(i):
                pltpu.make_async_copy(wdo.at[pl.ds(0, CHUNK)], wd_v.at[i], wd_sems.at[i]).wait()

            def copies(i, side):
                part = pl.ds(pl.multiple_of(i * CHUNK, CHUNK), CHUNK)
                return [
                    pltpu.make_async_copy(
                        act_v.at[side], act_out.at[slot, :, part], act_sems.at[side]
                    ),
                    pltpu.make_async_copy(
                        slope_v.at[side], slope_out.at[slot, :, part], slope_sems.at[side]
                    ),
                ]

            def activate(i, source, side):
                shift = bu[pl.ds(i, 1), :]
                for t in tiles(rows):
                    active, slope = gelu_parts(source[t] + shift)
                    act_v[side, t] = active.astype(BF16)
                    slope_v[side, t] = slope.astype(BF16)

            def pair(j, carry):
                i = 2 * j
                up_wait(i + 1)

                @pl.when(j > 0)
                def _():
                    for copy in copies(i - 2, 0) + copies(i - 1, 1):
                        copy.wait()

                up_product(i + 1, h_two)
                activate(i, h_one, 0)
                for copy in copies(i, 0):
                    copy.start()
                down_wait(i)

                @pl.when(i + 2 < steps)
                def _():
                    up_wait(i + 2)

                up_product(jnp.minimum(i + 2, steps - 1), h_one)
                acc[...] += dot(act_v[0], wd_v[i])
                activate(i + 1, h_two, 1)
                for copy in copies(i + 1, 1):
                    copy.start()
                down_wait(i + 1)
                acc[...] += dot(act_v[1], wd_v[i + 1])
                return carry

            acc[...] = jnp.zeros_like(acc)
            up_wait(0)
            up_product(0, h_one)
            lax.fori_loop(0, steps // 2, pair, 0)

            def finish(t):
                branch = acc[t] + v[FC2B : FC2B + 1]
                y_v[t] = (res_v[t] + v[SMLP : SMLP + 1] * branch).astype(BF16)
                branch_v[t] = branch.astype(BF16)

            each_tile(rows, finish)
            outs += copies(steps - 2, 0) + copies(steps - 1, 1)
            outs.append(begin(y_v, relay_out, out_sems.at[3]))
            outs.append(begin(y_v, y_out.at[slot], out_sems.at[4]))
            outs.append(begin(branch_v, branch_out.at[slot], out_sems.at[5]))
            for copy in outs:
                copy.wait()

    stack = (MICRO, rows, width)
    tall = (MICRO, rows, hidden)
    plain = pltpu.VMEM((rows, width), BF16)
    full = pltpu.VMEM((rows, width), F32)
    chunks = pltpu.VMEM((2, rows, CHUNK), BF16)
    return manual(
        kernel,
        info,
        [
            (mixed, False),
            (x, False),
            (vec, True),
            (wo_own, False),
            (wo_oth, False),
            (wu_own, False),
            (wu_oth, False),
            (wd_own, False),
            (wd_oth, False),
            (b_up, True),
        ],
        [
            (stack, BF16, False, kept.get("attended")),
            (stack, F32, False, kept.get("residual")),
            (stack, BF16, False, kept.get("normed2")),
            (tall, BF16, False, kept.get("active")),
            (tall, BF16, False, kept.get("slope")),
            (stack, BF16, False, kept.get("branch")),
            (stack, BF16, False, kept.get("output")),
            ((rows, width), BF16, False, None),
            (stack, BF16, False, kept.get("mixed")),
        ],
        [
            plain,
            plain,
            pltpu.VMEM((2, half, width), BF16),
            pltpu.VMEM((steps, width, CHUNK), BF16),
            pltpu.VMEM((steps, CHUNK, width), BF16),
            plain,
            full,
            plain,
            pltpu.VMEM((rows, CHUNK), F32),
            pltpu.VMEM((rows, CHUNK), F32),
            chunks,
            chunks,
            plain,
            plain,
            full,
            dma_sems(4),
            dma_sems(steps),
            dma_sems(steps),
            dma_sems(7),
            dma_sems(2),
            dma_sems(2),
        ],
        flops=4 * rows * width * hidden + 2 * rows * width * width,
        moved=4 * width * hidden + 2 * width * width + 8 * rows * hidden,
        after=after,
    )


def scale_branch(info, owner, number, relay, vec, earlier, after=()):
    rows, width = relay.shape

    def kernel(s, g, v, gb_out, g_v, gb_v, sems):
        @pl.when(s[ACTIVE + owner] == 1)
        def _():
            begin(g, g_v, sems.at[0]).wait()
            gb_v[...] = (v[SMLP : SMLP + 1] * g_v[...].astype(F32)).astype(BF16)
            begin(gb_v, gb_out.at[number], sems.at[1]).wait()

    return manual(
        kernel,
        info,
        [(relay, False), (vec, True)],
        [((MICRO, rows, width), BF16, False, earlier)],
        [pltpu.VMEM((rows, width), BF16), pltpu.VMEM((rows, width), BF16), dma_sems(2)],
        moved=4 * rows * width,
        after=after,
    )[0]


def mlp_backward(info, owner, number, source, tokens, vec, wo_own, wo_oth, wu_own, wu_oth, wd_own, wd_oth, kept, grads, scaled, after):
    count = len(tokens)
    _, rows, width = kept["x"].shape
    side_hidden = wu_own.shape[1]
    hidden = 2 * side_hidden
    half = width // 2
    steps = hidden // CHUNK
    split = steps // 2

    def kernel(s, *refs):
        work(s, refs[:count], *refs[count:])

    def work(
        s, token_refs, branch, slope, res, att, v, woo, wot, wuo, wut, wdo, wdt,
        gb_out, before_out, ga_out, gm_out, gr_out, small_out, shift_out,
        g_v, branch_v, slope_v, res_v, att_v, wo_v, wu_v, wd_v, gb_v, d_one, d_two, before_v, ga_v, gm_v,
        gr_v, acc, sums, tok_sems, in_sems, slope_sems, wu_sems, wd_sems, out_sems, before_sems,
    ):
        @pl.when(s[ACTIVE + owner] == 0)
        def _():
            small_out[...] = jnp.zeros_like(small_out)
            shift_out[...] = jnp.zeros_like(shift_out)

        @pl.when(s[ACTIVE + owner] == 1)
        def _():
            slot = number
            arriving = token_copies(s, source, number, token_refs, g_v, tok_sems)
            branch_in = begin(branch.at[slot], branch_v, in_sems.at[0])
            for i in range(steps):
                part = pl.ds((i % split) * CHUNK, CHUNK)
                up, down = (wuo, wdo) if i < split else (wut, wdt)
                here = pl.ds(i * CHUNK, CHUNK)
                begin(down.at[part], wd_v.at[i], wd_sems.at[i])
                begin(slope.at[slot, :, here], slope_v.at[i], slope_sems.at[i])
                begin(up.at[:, part], wu_v.at[i], wu_sems.at[i])
            last = [
                begin(res.at[slot], res_v, in_sems.at[1]),
                begin(att.at[slot], att_v, in_sems.at[2]),
                begin(woo, wo_v.at[0], in_sems.at[3]),
                begin(wot, wo_v.at[1], in_sems.at[4]),
            ]
            for copy in arriving:
                copy.wait()

            def scale(t):
                gb_v[t] = (v[SMLP : SMLP + 1] * g_v[t].astype(F32)).astype(BF16)

            each_tile(rows, scale)
            outs = []
            if not scaled:
                outs.append(begin(gb_v, gb_out.at[slot], out_sems.at[0]))

            def down_product(i, target):
                target[...] = dot_nt(gb_v[...], wd_v[i])

            def down_wait(i):
                pltpu.make_async_copy(wdo.at[pl.ds(0, CHUNK)], wd_v.at[i], wd_sems.at[i]).wait()

            def up_wait(i):
                pltpu.make_async_copy(
                    wuo.at[:, pl.ds(0, CHUNK)], wu_v.at[i], wu_sems.at[i]
                ).wait()

            def slope_wait(i):
                pltpu.make_async_copy(
                    slope.at[slot, :, pl.ds(0, CHUNK)], slope_v.at[i], slope_sems.at[i]
                ).wait()

            def copy_out(i, side):
                part = pl.ds(pl.multiple_of(i * CHUNK, CHUNK), CHUNK)
                return pltpu.make_async_copy(
                    before_v.at[side], before_out.at[slot, :, part], before_sems.at[side]
                )

            def differentiate(i, source, side):
                total = jnp.zeros((8, CHUNK), F32)
                for t in tiles(rows):
                    grad_before = (source[t] * slope_v[i, t].astype(F32)).astype(BF16)
                    before_v[side, t] = grad_before
                    total = total + eights(grad_before.astype(F32))
                shift_out[pl.ds(i, 1), :] = col_sum(total)

            def pair(j, carry):
                i = 2 * j
                slope_wait(i)
                down_wait(i + 1)

                @pl.when(j > 0)
                def _():
                    copy_out(i - 2, 0).wait()
                    copy_out(i - 1, 1).wait()

                down_product(i + 1, d_two)
                differentiate(i, d_one, 0)
                copy_out(i, 0).start()
                slope_wait(i + 1)
                up_wait(i)

                @pl.when(i + 2 < steps)
                def _():
                    down_wait(i + 2)

                down_product(jnp.minimum(i + 2, steps - 1), d_one)
                acc[...] += dot_nt(before_v[0], wu_v[i])
                differentiate(i + 1, d_two, 1)
                copy_out(i + 1, 1).start()
                up_wait(i + 1)
                acc[...] += dot_nt(before_v[1], wu_v[i + 1])
                return carry

            acc[...] = jnp.zeros_like(acc)
            down_wait(0)
            down_product(0, d_one)
            branch_in.wait()
            sums[...] = jnp.zeros_like(sums)

            def branch_sums(t):
                sums[0] += eights(g_v[t].astype(F32) * branch_v[t].astype(F32))
                sums[1] += eights(gb_v[t].astype(F32))

            each_tile(rows, branch_sums)
            lax.fori_loop(0, steps // 2, pair, 0)
            outs += [copy_out(steps - 2, 0), copy_out(steps - 1, 1)]
            for copy in last:
                copy.wait()

            def last_norm(t):
                hat, scale = norm_stats(res_v[t])
                error = acc[t]
                sums[2] += eights(error * hat)
                sums[3] += eights(error)
                grad = g_v[t].astype(F32) + norm_backward(hat, scale, v[LN2G : LN2G + 1], error)
                gr_v[t] = grad
                sums[4] += eights(grad * att_v[t].astype(F32))
                ga = (v[SATT : SATT + 1] * grad).astype(BF16)
                ga_v[t] = ga
                sums[5] += eights(ga.astype(F32))

            each_tile(rows, last_norm)
            outs.append(begin(ga_v, ga_out.at[slot], out_sems.at[1]))
            outs.append(begin(gr_v, gr_out, out_sems.at[3]))
            gm_v[:, :half] = dot_nt(ga_v[...], wo_v[0]).astype(BF16)
            gm_v[:, half:] = dot_nt(ga_v[...], wo_v[1]).astype(BF16)
            outs.append(begin(gm_v, gm_out, out_sems.at[2]))
            small_out[...] = jnp.zeros_like(small_out)
            for row in range(6):
                small_out[row : row + 1] = col_sum(sums[row])
            for copy in outs:
                copy.wait()

    stack = (MICRO, rows, width)
    plain = pltpu.VMEM((rows, width), BF16)
    full = pltpu.VMEM((rows, width), F32)
    chunks = pltpu.VMEM((steps, rows, CHUNK), BF16)
    return manual(
        kernel,
        info,
        [(array, False) for array in tokens]
        + [
            (kept["branch"], False),
            (kept["slope"], False),
            (kept["residual"], False),
            (kept["attended"], False),
            (vec, True),
            (wo_own, False),
            (wo_oth, False),
            (wu_own, False),
            (wu_oth, False),
            (wd_own, False),
            (wd_oth, False),
        ],
        [
            (stack, BF16, False, None if scaled else grads.get("branch")),
            ((MICRO, rows, hidden), BF16, False, grads.get("before")),
            (stack, BF16, False, grads.get("attended")),
            ((rows, width), BF16, False, None),
            ((rows, width), F32, False, None),
            ((8, width), F32, True, None),
            ((steps, CHUNK), F32, True, None),
        ],
        [
            plain,
            plain,
            chunks,
            full,
            plain,
            pltpu.VMEM((2, half, width), BF16),
            pltpu.VMEM((steps, width, CHUNK), BF16),
            pltpu.VMEM((steps, CHUNK, width), BF16),
            plain,
            pltpu.VMEM((rows, CHUNK), F32),
            pltpu.VMEM((rows, CHUNK), F32),
            pltpu.VMEM((2, rows, CHUNK), BF16),
            plain,
            plain,
            full,
            full,
            pltpu.VMEM((6, 8, width), F32),
            dma_sems(2),
            dma_sems(5),
            dma_sems(steps),
            dma_sems(steps),
            dma_sems(steps),
            dma_sems(4),
            dma_sems(2),
        ],
        flops=4 * rows * width * hidden + 2 * rows * width * width,
        moved=4 * width * hidden + 2 * width * width + 8 * rows * hidden,
        after=after,
    )


def attend_backward(info, owner, number, grad_mixed, kept, after=()):
    _, rows, width = kept["q"].shape
    heads = width // HEAD_DIM
    lanes = 2 * HEAD_DIM
    block = 2 * lanes
    steps = width // block
    score_scale = HEAD_DIM**-0.5

    def kernel(s, *refs):
        @pl.when(s[ACTIVE + owner] == 1)
        def _():
            compute(*refs)

    def compute(gm, q_ref, kv, grown, full, inv, dq_out, here_out, there_out, *scratch):
        probs, scores = scratch[:4], scratch[4:8]
        own_v, centre_v = scratch[8:]
        first_q = lax.broadcasted_iota(jnp.int32, (rows, lanes), 1) < HEAD_DIM
        first_t = lax.broadcasted_iota(jnp.int32, (TILE, lanes), 1) < HEAD_DIM

        def columns(head):
            return slice(head // 2 * lanes, (head // 2 + 1) * lanes)

        for pair in range(2):
            place = columns(2 * pair)
            for t in tiles(rows):
                scaled = (gm[t, place].astype(F32) * inv[0, t, place]).astype(BF16)
                product = scaled.astype(F32) * full[0, t, place]
                for side in range(2):
                    mine = first_t if side == 0 else ~first_t
                    own_v[2 * pair + side, t] = jnp.where(mine, scaled, 0)
                    centre_v[2 * pair + side, t] = jnp.sum(
                        jnp.where(mine, product, 0.0), axis=-1, keepdims=True
                    )

        def prob(head):
            probs[head][...] = dot_nt(own_v[head], kv[0, 1, :, columns(head)])

        prob(0)
        grad_q, grad_k, grad_v = [], [], []
        for head in range(4):
            if head < 3:
                prob(head + 1)
            for t in tiles(rows):
                weight = grown[0, head, t].astype(F32)
                scores[head][t] = (weight * (probs[head][t] - centre_v[head, t])).astype(BF16)
            mine = first_q if head % 2 == 0 else ~first_q
            grad_v.append(dot_tn(grown[0, head], own_v[head]))
            grad_q.append(dot(scores[head][...], kv[0, 0, :, columns(head)]))
            masked = jnp.where(mine, q_ref[0, :, columns(head)], 0)
            grad_k.append(dot_tn(scores[head][...], masked))
            if head % 2 == 1:
                place = columns(head)
                dq = jnp.where(first_q, grad_q[head - 1], grad_q[head]) * score_scale
                dq_out[:, place] = dq.astype(BF16)
                dk = ((grad_k[head - 1] + grad_k[head]) * score_scale).astype(BF16)
                dv = (grad_v[head - 1] + grad_v[head]).astype(BF16)
                here_out[0, :, place] = dk[:rows]
                here_out[1, :, place] = dv[:rows]
                there_out[0, :, place] = dk[rows:]
                there_out[1, :, place] = dv[rows:]

    def on(s):
        return s[ACTIVE + owner]

    def slot(s):
        return jnp.where(on(s) == 1, number, SPARE)

    column = lambda i, s: (slot(s), 0, i * on(s))
    plain = lambda i, s: (0, i * on(s))
    return call(
        kernel,
        info,
        (steps,),
        [
            (grad_mixed, (rows, block), plain),
            (kept["q"], (1, rows, block), lambda i, s: (number, 0, i * on(s))),
            (kept["kv"], (1, 2, 2 * rows, block), lambda i, s: (slot(s), 0, 0, i * on(s))),
            (kept["grown"], (1, 4, rows, 2 * rows), lambda i, s: (slot(s), i * on(s), 0, 0)),
            (kept["mixed_full"], (1, rows, block), column),
            (kept["inverse"], (1, rows, block), column),
        ],
        [
            ((rows, width), BF16, (rows, block), plain, None),
            ((2, rows, width), BF16, (2, rows, block), lambda i, s: (0, 0, i * on(s)), None),
            ((2, rows, width), BF16, (2, rows, block), lambda i, s: (0, 0, i * on(s)), None),
        ],
        [pltpu.VMEM((rows, 2 * rows), F32)] * 4
        + [pltpu.VMEM((rows, 2 * rows), BF16)] * 4
        + [pltpu.VMEM((4, rows, lanes), BF16), pltpu.VMEM((4, rows, 1), F32)],
        flops=16 * rows * rows * width,
        moved=4 * heads * rows * rows + 30 * rows * width,
        after=after,
    )


def qkv_backward(info, owner, number, dq, dkv_here, dkv_there, w_own, w_oth, grad_res, vec, kept, grads, after=()):
    _, rows, width = kept["x"].shape
    half = width // 2

    def kernel(s, dq_ref, here, there, own, oth, gr, x_ref, v, packed_out, gx_out, relay_out,
               small_out, shift_out, a_v, b_v, p_v, w_v, gr_v, x_v, gx_v, acc, sums,
               a_sems, b_sems, w_sems, in_sems, packed_sems, out_sems):
        @pl.when(s[ACTIVE + owner] == 0)
        def _():
            small_out[...] = jnp.zeros_like(small_out)
            shift_out[...] = jnp.zeros_like(shift_out)

        @pl.when(s[ACTIVE + owner] == 1)
        def _():
            slot = number
            for part in range(6):
                kind, side = part % 3, part // 3
                columns = pl.ds(side * half, half)
                if kind == 0:
                    begin(dq_ref.at[:, columns], a_v.at[part], a_sems.at[part])
                else:
                    turned = pl.ds((1 - side) * half, half)
                    begin(here.at[kind - 1, :, columns], a_v.at[part], a_sems.at[part])
                    begin(there.at[kind - 1, :, turned], b_v.at[part], b_sems.at[part])
                weight = own if side == 0 else oth
                begin(weight.at[kind], w_v.at[part], w_sems.at[part])
            last = [
                begin(x_ref.at[slot], x_v, in_sems.at[0]),
                begin(gr, gr_v, in_sems.at[1]),
            ]

            def out_copy(part):
                columns = pl.ds(pl.multiple_of(part * half, half), half)
                return pltpu.make_async_copy(
                    p_v.at[part], packed_out.at[slot, :, columns], packed_sems.at[part]
                )

            def project(part, carry):
                first = dq_ref.at[:, pl.ds(0, half)]
                pltpu.make_async_copy(first, a_v.at[part], a_sems.at[part]).wait()

                @pl.when(part % 3 > 0)
                def _():
                    pltpu.make_async_copy(first, b_v.at[part], b_sems.at[part]).wait()

                total = jnp.zeros((8, half), F32)
                both = part % 3 > 0
                for t in tiles(rows):
                    added = jnp.where(both, b_v[part, t].astype(F32), 0.0)
                    packed = (a_v[part, t].astype(F32) + added).astype(BF16)
                    p_v[part, t] = packed
                    total = total + eights(packed.astype(F32))
                shift_out[pl.ds(part, 1), :] = col_sum(total)
                out_copy(part).start()
                pltpu.make_async_copy(own.at[0], w_v.at[part], w_sems.at[part]).wait()
                acc[...] += dot_nt(p_v[part], w_v[part])
                return carry

            acc[...] = jnp.zeros_like(acc)
            lax.fori_loop(0, 6, project, 0)
            outs = [out_copy(part) for part in range(6)]
            for copy in last:
                copy.wait()
            sums[...] = jnp.zeros_like(sums)

            def norm(t):
                hat, scale = norm_stats(x_v[t].astype(F32))
                error = acc[t]
                grad = gr_v[t] + norm_backward(hat, scale, v[LN1G : LN1G + 1], error)
                gx_v[t] = grad.astype(BF16)
                sums[0] += eights(error * hat)
                sums[1] += eights(error)

            each_tile(rows, norm)
            outs.append(begin(gx_v, relay_out, out_sems.at[0]))
            outs.append(begin(gx_v, gx_out.at[slot], out_sems.at[1]))
            small_out[...] = jnp.zeros_like(small_out)
            for row in range(2):
                small_out[row : row + 1] = col_sum(sums[row])
            for copy in outs:
                copy.wait()

    stack = (MICRO, rows, width)
    parts = pltpu.VMEM((6, rows, half), BF16)
    return manual(
        kernel,
        info,
        [
            (dq, False),
            (dkv_here, False),
            (dkv_there, False),
            (w_own, False),
            (w_oth, False),
            (grad_res, False),
            (kept["x"], False),
            (vec, True),
        ],
        [
            ((MICRO, rows, 3 * width), BF16, False, grads.get("packed")),
            (stack, BF16, False, grads.get("input")),
            ((rows, width), BF16, False, None),
            ((8, width), F32, True, None),
            ((8, half), F32, True, None),
        ],
        [
            parts,
            parts,
            parts,
            pltpu.VMEM((6, width, half), BF16),
            pltpu.VMEM((rows, width), F32),
            pltpu.VMEM((rows, width), BF16),
            pltpu.VMEM((rows, width), BF16),
            pltpu.VMEM((rows, width), F32),
            pltpu.VMEM((2, 8, width), F32),
            dma_sems(6),
            dma_sems(6),
            dma_sems(6),
            dma_sems(2),
            dma_sems(6),
            dma_sems(2),
        ],
        flops=6 * rows * width * width,
        moved=6 * width * width + 16 * rows * width,
        after=after,
    )


def swap(block):
    return lax.ppermute(block, "tensor", [(0, 1), (1, 0)])


def ring_order(count):
    return list(range(0, count, 2)) + list(range(count - 1, 0, -2))


def tied(value, *others):
    return lax.optimization_barrier((value, *others))[0]


class Ring:
    def __init__(self, info, parts, shapes, places):
        self.info, self.parts, self.shapes, self.places = info, parts, shapes, places
        self.count = lax.axis_size("dp")
        order = ring_order(self.count)
        n = self.count
        self.chunk = parts[0][0].shape[0] // (2 * n)
        self.widths = [pair[0].shape[1] for pair in parts]
        self.signs = (1, -1)
        self.routes = [[(order[i], order[(i + s) % n]) for i in range(n)] for s in self.signs]
        self.step = 0
        self.steps = 2 * (n - 1)
        self.vmem = RING_MIB
        self.totals = [None] * len(shapes)
        self.moving = self.add([0, 0], None)

    def unit(self, way, ahead):
        return UNITS + way * self.count + ahead % self.count

    def add(self, ahead, arrived, after=()):
        chunk, width, parts = self.chunk, sum(self.widths), len(self.parts)
        units = [self.unit(w, ahead[w]) for w in range(2)]
        terms = 2 if arrived is None else 3

        def kernel(s, *refs):
            halves = refs[: 2 * parts]
            refs = refs[2 * parts :]
            if terms == 3:
                arrivals, refs = refs[:2], refs[2:]
            outs, (held, sems) = refs[:2], refs[2:]
            copies = []
            for w in range(2):
                rows = pl.ds(pl.multiple_of(s[units[w]] * chunk, chunk), chunk)
                base = 0
                for number, columns in enumerate(self.widths):
                    for term in range(2):
                        copies.append(
                            begin(
                                halves[2 * number + term].at[rows],
                                held.at[w, term, :, pl.ds(base, columns)],
                                sems.at[w, term, number],
                            )
                        )
                    base += columns
                if terms == 3:
                    copies.append(begin(arrivals[w], held.at[w, 2], sems.at[w, 2, 0]))
            for copy in copies:
                copy.wait()
            for w in range(2):
                for t in tiles(chunk):
                    for first in range(0, width, 512):
                        c = slice(first, min(first + 512, width))
                        total = held[w, 0, t, c].astype(F32) + held[w, 1, t, c].astype(F32)
                        if terms == 3:
                            total = total + held[w, 2, t, c].astype(F32)
                        outs[w][t, c] = total.astype(BF16)

        arrays = [(term, False) for pair in self.parts for term in pair]
        if arrived is not None:
            arrays += [(block, False) for block in arrived]
        return manual(
            kernel,
            self.info,
            arrays,
            [((chunk, width), BF16, True, None)] * 2,
            [pltpu.VMEM((2, terms, chunk, width), BF16), pltpu.SemaphoreType.DMA((2, 3, parts))],
            moved=2 * (terms + 1) * 2 * chunk * width,
            vmem=self.vmem,
            after=after,
        )

    def put(self, ahead, blocks, after=()):
        chunk, width = self.chunk, sum(self.widths)
        units = [self.unit(w, pair[w]) for pair in ahead for w in range(2)]
        size = len(units)
        count = len(self.shapes)
        pieces = sum(len(self.places.columns(c)) for c in range(count))

        def kernel(s, *refs):
            sources, outs = refs[:size], refs[size : size + count]
            held, wide, in_sems, out_sems = refs[size + count + 2 :]
            loads = [begin(sources[w], held.at[w], in_sems.at[w]) for w in range(size)]
            copies = []
            for w in range(size):
                loads[w].wait()
                for t in tiles(chunk):
                    for first in range(0, width, 512):
                        c = slice(first, min(first + 512, width))
                        wide[w, t, c] = held[w, t, c].astype(F32)
                number = 0
                for target in range(count):
                    for first, columns in self.places.columns(target):
                        ref = self.places.ref(
                            outs[target], target, first, columns, s[units[w]], chunk
                        )
                        copies.append(
                            begin(
                                wide.at[w, :, pl.ds(first, columns)],
                                ref,
                                out_sems.at[w, number],
                            )
                        )
                        number += 1
            for copy in copies:
                copy.wait()

        results = manual(
            kernel,
            self.info,
            [(block, False) for block in blocks[:-2]] + [(block, False) for block in blocks[-2:]],
            [(shape, F32, False, old) for shape, old in zip(self.shapes, self.totals)]
            + [((chunk, width), BF16, False, None)] * 2,
            [
                pltpu.VMEM((size, chunk, width), BF16),
                pltpu.VMEM((size, chunk, width), F32),
                dma_sems(size),
                pltpu.SemaphoreType.DMA((size, pieces)),
            ],
            moved=2 * 6 * chunk * width,
            vmem=self.vmem,
            after=after,
            same={size - 2: count, size - 1: count + 1},
        )
        self.totals = list(results[:count])
        return list(results[count:])

    def advance(self, *after):
        arrived = [lax.ppermute(self.moving[w], "dp", self.routes[w]) for w in range(2)]
        if after:
            arrived = list(lax.optimization_barrier((*arrived, *after))[:2])
        step = self.step
        if step < self.count - 1:
            self.moving = self.add([-s * (step + 1) for s in self.signs], arrived)
        else:
            ahead = [[-s * (step - self.count + 1) for s in self.signs]]
            blocks = arrived
            if step == self.count - 1:
                ahead.insert(0, self.signs)
                blocks = list(self.moving) + arrived
            self.moving = self.put(ahead, blocks)
        self.step += 1

    def done(self):
        return self.step == self.steps

    def finish(self):
        while not self.done():
            self.advance()
        return self.totals


class WholeRows:
    def __init__(self, width):
        self.width = width

    def columns(self, target):
        return [(0, self.width)]

    def ref(self, out, target, first, columns, unit, chunk):
        return out.at[pl.ds(pl.multiple_of(unit * chunk, chunk), chunk)]


class TailPlaces:
    def __init__(self, half, lanes):
        self.half, self.lanes = half, lanes

    def columns(self, target):
        half = self.half
        if target == 0:
            return [(j * half, half) for j in range(3)]
        return [(3 * half, half)] if target == 1 else [(4 * half, self.lanes)]

    def ref(self, out, target, first, columns, unit, chunk):
        rows = pl.ds(pl.multiple_of(unit * chunk, chunk), chunk)
        if target == 0:
            return out.at[first // self.half, rows]
        if target == 2:
            return out.at[rows]
        each = self.half // chunk
        return out.at[
            pl.ds(pl.multiple_of(lax.rem(unit, each) * chunk, chunk), chunk),
            pl.ds(pl.multiple_of(lax.div(unit, each) * self.half, self.half), self.half),
        ]


def partner_tokens(info, block, numbers):
    _, _, seq, half = block.shape
    rows = seq // 2

    def kernel(s, ref, out, sems):
        start = pl.multiple_of((1 - s[RANK]) * rows, rows)
        copies = [
            begin(ref.at[number, 0, pl.ds(start, rows)], out.at[place], sems.at[place])
            for place, number in enumerate(numbers)
        ]
        for copy in copies:
            copy.wait()

    return manual(
        kernel,
        info,
        [(block, False)],
        [((len(numbers), rows, half), BF16, True, None)],
        [dma_sems(len(numbers))],
        vmem=8,
    )[0]


def partner_features(info, block):
    micro, rows, width = block.shape
    half = width // 2

    def kernel(s, ref, out, sems):
        start = pl.multiple_of((1 - s[RANK]) * half, half)
        copies = [
            begin(ref.at[m, :, pl.ds(start, half)], out.at[m], sems.at[m]) for m in range(micro)
        ]
        for copy in copies:
            copy.wait()

    return manual(
        kernel,
        info,
        [(block, False)],
        [((micro, rows, half), BF16, True, None)],
        [dma_sems(micro)],
        vmem=8,
    )[0]


def join_tokens(info, block, received):
    micro, rows, width = block.shape
    half = width // 2

    def kernel(s, ref, other, out, sems):
        rank = s[RANK]
        features = pl.ds(pl.multiple_of(rank * half, half), half)
        here = pl.ds(pl.multiple_of(rank * rows, rows), rows)
        there = pl.ds(pl.multiple_of((1 - rank) * rows, rows), rows)
        copies = []
        for m in range(micro):
            copies.append(begin(ref.at[m, :, features], out.at[0, m, 0, here], sems.at[0, m]))
            copies.append(begin(other.at[m], out.at[0, m, 0, there], sems.at[1, m]))
        for copy in copies:
            copy.wait()

    return manual(
        kernel,
        info,
        [(block, False), (received, False)],
        [((1, micro, 1, 2 * rows, half), BF16, True, None)],
        [pltpu.SemaphoreType.DMA((2, micro))],
        vmem=8,
    )[0]


LANES = 128


def gather_vectors(info, sums, rows_out):
    calls = len(sums)
    width = sums[0][0].shape[1]
    half = width // 2

    def kernel(s, *refs):
        own, oth = refs[4 * calls :]
        low = s[RANK] == 0

        def total(kind):
            blocks = [refs[4 * c + kind][...] for c in range(calls)]
            return sum(blocks[1:], blocks[0])

        two, up, one, qkv = [total(kind) for kind in range(4)]
        own[...] = jnp.zeros_like(own)
        oth[...] = jnp.zeros_like(oth)
        place = 0

        def write(first, second):
            nonlocal place
            for c in range(0, half, LANES):
                own[place : place + 1] = first[:, c : c + LANES].astype(BF16)
                oth[place : place + 1] = second[:, c : c + LANES].astype(BF16)
                place += 1

        for block, count in ((one, 2), (two, 6)):
            for row in range(count):
                line = block[row : row + 1]
                left, right = line[:, :half], line[:, half:]
                write(jnp.where(low, left, right), jnp.where(low, right, left))
        for row in range(3):
            write(qkv[row : row + 1], qkv[3 + row : 4 + row])
        hidden_rows = up.shape[0] // 2
        for row in range(hidden_rows):
            write(up[row : row + 1], up[hidden_rows + row : hidden_rows + row + 1])

    vmem = pl.BlockSpec(memory_space=pltpu.VMEM)
    return pl.pallas_call(
        kernel,
        in_specs=[pl.BlockSpec(memory_space=pltpu.SMEM)] + [vmem] * (4 * calls),
        out_specs=[vmem] * 2,
        out_shape=[jax.ShapeDtypeStruct((rows_out, LANES), BF16)] * 2,
    )(info, *[block for group in sums for block in group])


def spread_vectors(sums, half, hidden_half):
    def kernel(ref, *outs):
        def line(number, out, row=0, columns=half, first=0):
            for c in range(0, columns, LANES):
                place = (number * half + c) // LANES
                out[row : row + 1, first + c : first + c + LANES] = ref[place : place + 1]

        for number in range(8):
            line(number, outs[number])
        line(8, outs[8])
        line(10, outs[8], row=1)
        line(11, outs[9], columns=hidden_half)

    vmem = pl.BlockSpec(memory_space=pltpu.VMEM)
    shapes = [(1, half)] * 8 + [(2, half), (1, hidden_half)]
    return pl.pallas_call(
        kernel,
        in_specs=[vmem],
        out_specs=[vmem] * 10,
        out_shape=[jax.ShapeDtypeStruct(shape, F32) for shape in shapes],
    )(sums)


def pack_vectors(blocks, hidden_bias):
    half = blocks[0].shape[1]
    hidden_rows = hidden_bias.shape[1] // half
    filled = sum(b.shape[0] for b in blocks)

    def kernel(*refs):
        out = refs[-1]
        place = 0
        for ref in refs[: len(blocks)]:
            for row in range(ref.shape[0]):
                out[place : place + 1] = ref[row : row + 1].astype(F32)
                place += 1
        for row in range(hidden_rows):
            columns = slice(row * half, (row + 1) * half)
            out[place : place + 1] = refs[len(blocks)][:, columns].astype(F32)
            place += 1

    return pl.pallas_call(
        kernel, out_shape=jax.ShapeDtypeStruct((filled + hidden_rows, half), F32)
    )(*blocks, hidden_bias)


def join_vectors(scalars, own, oth, hidden_rows):
    half = own.shape[1]

    def kernel(s, own_ref, oth_ref, vec, bias_q, bias_v, bias_up):
        low = s[RANK] == 0
        vec[:, :half] = jnp.where(low, own_ref[:8], oth_ref[:8])
        vec[:, half:] = jnp.where(low, oth_ref[:8], own_ref[:8])
        for row, out in ((8, bias_q), (9, bias_v)):
            out[:, :half] = own_ref[row : row + 1]
            out[:, half:] = oth_ref[row : row + 1]
        bias_up[:hidden_rows] = own_ref[10 : 10 + hidden_rows]
        bias_up[hidden_rows:] = oth_ref[10 : 10 + hidden_rows]

    vmem = pl.BlockSpec(memory_space=pltpu.VMEM)
    return pl.pallas_call(
        kernel,
        in_specs=[pl.BlockSpec(memory_space=pltpu.SMEM), vmem, vmem],
        out_specs=[vmem] * 4,
        out_shape=[
            jax.ShapeDtypeStruct((8, 2 * half), F32),
            jax.ShapeDtypeStruct((1, 2 * half), F32),
            jax.ShapeDtypeStruct((1, 2 * half), F32),
            jax.ShapeDtypeStruct((2 * hidden_rows, half), F32),
        ],
    )(scalars, own, oth)


def shards(
    inputs,
    cotangent,
    ln1_gain,
    ln1_bias,
    qkv_weight,
    qv_bias,
    out_weight,
    out_bias,
    scale_attn,
    ln2_gain,
    ln2_bias,
    fc1_weight,
    fc1_bias,
    fc2_weight,
    fc2_bias,
    scale_mlp,
):
    micro, images, seq_len, half = inputs.shape
    assert micro == MICRO and images == 1
    width = 2 * half
    hidden_half = fc1_weight.shape[2]

    count = lax.axis_size("dp")
    order = ring_order(count)
    table = [
        [rank, int(section == 0), int(section == 1)]
        + [way * count + (order.index(i) + ahead) % count for way in range(2) for ahead in range(count)]
        for section in range(2)
        for rank in range(2)
        for i in range(count)
    ]
    info = lax.dynamic_slice(
        jnp.asarray(table, jnp.int32),
        (lax.axis_index(("section", "tensor", "dp")), 0),
        (1, len(table[0])),
        allow_negative_indices=False,
    ).reshape(-1)

    first_oth = swap(partner_tokens(info, inputs, (0,))[0])
    vectors = pack_vectors(
        [
            ln1_gain, ln1_bias, out_bias, scale_attn, ln2_gain, ln2_bias, fc2_bias, scale_mlp,
            qv_bias[0],
        ],
        fc1_bias,
    )
    vectors_oth = swap(vectors)
    wq_own = jnp.transpose(qkv_weight[0], (1, 0, 2))
    wq_oth = swap(tied(wq_own, vectors))
    vec, bias_q, bias_v, b_up = join_vectors(info, vectors, vectors_oth, hidden_half // half)
    b_up = b_up.reshape(2 * hidden_half // CHUNK, CHUNK)
    wo_own, wu_own, wd_own = out_weight[0], fc1_weight[0], fc2_weight[0]
    wo_oth = swap(tied(wo_own, first_oth, vectors_oth))
    wu_oth = swap(tied(wu_own, first_oth, vectors_oth))
    wd_oth = swap(tied(wd_own, first_oth, vectors_oth))
    second_oth = swap(partner_tokens(info, tied(inputs, wd_oth), (1,))[0])
    cot_oth = swap(partner_tokens(info, tied(cotangent, wd_oth), (0, 1)))

    kept = {}

    def forward(owner, number, source, tokens, after=(), late=()):
        kept["x"], kept["normed1"], kv_here = norm_kv(
            info, owner, number, source, tokens, vec, wq_own, wq_oth, bias_v, kept, after
        )
        kv_there = swap(kv_here)
        kept["q"] = project_q(info, owner, number, kept["normed1"], wq_own, wq_oth, bias_q, kept)
        kept["grown"], kept["mixed_full"], mixed, kept["inverse"], kept["kv"] = attend(
            info, owner, number, kept["q"], kv_here, kv_there, kept
        )
        (
            kept["attended"],
            kept["residual"],
            kept["normed2"],
            kept["active"],
            kept["slope"],
            kept["branch"],
            kept["output"],
            relayed,
            kept["mixed"],
        ) = mlp_forward(
            info, owner, number, mixed, kept["x"], vec, wo_own, wo_oth, wu_own, wu_oth, wd_own,
            wd_oth, b_up, kept, late,
        )
        return relayed

    grads = {}
    sums = []

    def backward_mlp(owner, number, source, tokens, after, scaled=False):
        (
            branch,
            grads["before"],
            grads["attended"],
            grad_mixed,
            grad_res,
            small,
            shift,
        ) = mlp_backward(
            info, owner, number, source, tokens, vec, wo_own, wo_oth, wu_own, wu_oth, wd_own,
            wd_oth, kept, grads, scaled, after,
        )
        if not scaled:
            grads["branch"] = branch
        return grad_mixed, grad_res, small, shift

    def backward_attention(owner, number, grad_mixed, after=()):
        dq, dkv_here, dkv_send = attend_backward(info, owner, number, grad_mixed, kept, after)
        return dq, dkv_here, swap(dkv_send)

    def backward_qkv(owner, number, dq, dkv_here, dkv_there, grad_res, small, shift, after=()):
        grads["packed"], grads["input"], relayed, small_one, shift_qkv = qkv_backward(
            info, owner, number, dq, dkv_here, dkv_there, wq_own, wq_oth, grad_res, vec, kept,
            grads, after,
        )
        sums.append((small, shift, small_one, shift_qkv))
        return relayed

    def backward(owner, number, source, tokens, after, late=()):
        grad_mixed, grad_res, small, shift = backward_mlp(owner, number, source, tokens, after)
        flows = backward_attention(owner, number, grad_mixed, late)
        return backward_qkv(owner, number, *flows, grad_res, small, shift)

    relayed = forward(0, 0, "argument", (inputs, first_oth))
    first = lax.ppermute(relayed, "section", [(0, 1)])
    relayed = forward(0, 1, "argument", (inputs, second_oth), [relayed])
    second = lax.ppermute(relayed, "section", [(0, 1)])
    relayed = forward(1, 0, "relay", (first,), [relayed])
    relayed = backward(1, 0, "argument", (cotangent, cot_oth[0]), [relayed], [second])
    first = lax.ppermute(relayed, "section", [(1, 0)])
    relayed = forward(1, 1, "relay", (second,), [relayed], [first])
    relayed = backward(1, 1, "argument", (cotangent, cot_oth[1]), [relayed])
    second = lax.ppermute(relayed, "section", [(1, 0)])
    relayed = backward(0, 0, "relay", (first,), [relayed])

    def weight_grad(left, right):
        return lax.dot_general(
            left, right, (((0, 1), (0, 1)), ((), ())), preferred_element_type=F32
        ).astype(BF16)

    grads["branch"] = scale_branch(info, 0, 1, second, vec, grads["branch"], [relayed])
    active, g_branch = kept["active"], grads["branch"]
    down_oth = weight_grad(active[:, :, hidden_half:], g_branch)
    down_sent = swap(down_oth)
    down_own = weight_grad(active[:, :, :hidden_half], g_branch)
    ring_down = Ring(info, [(down_own, down_sent)], [down_own.shape], WholeRows(width))
    second = tied(second, *ring_down.moving)
    grad_mixed, grad_res, small, shift = backward_mlp(
        0, 1, "relay", (second,), list(ring_down.moving), scaled=True
    )
    ring_down.advance(grad_mixed)
    normed2 = tied(kept["normed2"], *ring_down.moving)
    before = grads["before"]
    up_oth = weight_grad(normed2, before[:, :, hidden_half:])
    up_sent = swap(up_oth)
    ring_down.advance(up_oth)
    normed2 = tied(normed2, *ring_down.moving)
    up_own = weight_grad(normed2, before[:, :, :hidden_half])
    ring_down.advance(up_own)
    ring_up = Ring(info, [(up_own, up_sent)], [up_own.shape], WholeRows(hidden_half))
    grad_mixed = tied(grad_mixed, *ring_down.moving, *ring_up.moving)
    flows = backward_attention(0, 1, grad_mixed)
    ring_down.advance(flows[0])
    ring_up.advance(flows[0])
    grad_res = tied(grad_res, *ring_down.moving, *ring_up.moving)
    backward_qkv(0, 1, *flows, grad_res, small, shift)
    packed = grads["packed"]
    ring_down.advance(packed)
    ring_up.advance(packed)
    normed1 = tied(kept["normed1"], *ring_down.moving, *ring_up.moving)
    vectors = gather_vectors(info, sums, width)

    def tail(index):
        columns = packed[:, :, index * 3 * half : (index + 1) * 3 * half]
        mixed = kept["mixed"][:, :, index * half : (index + 1) * half]
        g_att = grads["attended"]
        outs = [weight_grad(mixed, g_att[:, :, half * j : half * (j + 1)]) for j in range(2)]
        return [weight_grad(normed1, columns), jnp.concatenate(outs, axis=0), vectors[index]]

    tail_oth = tail(1)
    tail_sent = [swap(block) for block in tail_oth]
    ring_down.advance(tail_oth[0])
    ring_up.advance(tail_oth[0])
    normed1 = tied(normed1, *ring_down.moving, *ring_up.moving)
    tail_own = tail(0)
    ring_down.advance(tail_own[0])
    ring_up.advance(tail_own[0])
    ring_tail = Ring(
        info,
        list(zip(tail_own, tail_sent)),
        [(3, width, half), (half, width), (width, LANES)],
        TailPlaces(half, LANES),
    )
    rings = [ring_down, ring_up, ring_tail]
    for ring in rings:
        ring.vmem = 16
    before_it = ring_tail
    while not all(ring.done() for ring in rings):
        for ring in rings:
            if not ring.done():
                ring.advance(*before_it.moving)
                before_it = ring
    (total_down,) = ring_down.finish()
    (total_up,) = ring_up.finish()
    total_qkv, total_out, total_vectors = ring_tail.finish()
    block_outputs = join_tokens(info, kept["output"], swap(partner_features(info, kept["output"])))
    input_grads = join_tokens(info, grads["input"], swap(partner_features(info, grads["input"])))
    rows = spread_vectors(total_vectors, half, hidden_half)
    return (
        block_outputs,
        input_grads,
        rows[0],
        rows[1],
        jnp.transpose(total_qkv, (1, 0, 2))[None],
        rows[8][None],
        total_out[None],
        rows[7],
        rows[6],
        rows[4],
        rows[5],
        total_up[None],
        rows[9],
        total_down[None],
        rows[3],
        rows[2],
    )


def solution(mesh):
    placed = (
        P(None, "dp", None, "tensor"),
        P(None, "dp", None, "tensor"),
        P("section", "tensor"),
        P("section", "tensor"),
        P("section", None, None, "tensor"),
        P("section", None, "tensor"),
        P("section", "tensor", None),
        P("section", "tensor"),
        P("section", "tensor"),
        P("section", "tensor"),
        P("section", "tensor"),
        P("section", None, "tensor"),
        P("section", "tensor"),
        P("section", "tensor", None),
        P("section", "tensor"),
        P("section", "tensor"),
    )
    return jax.shard_map(
        shards,
        mesh=mesh,
        in_specs=placed,
        out_specs=(
            P("section", None, "dp", None, "tensor"),
            P("section", None, "dp", None, "tensor"),
            P("section", "tensor"),
            P("section", "tensor"),
            P("section", None, None, "tensor"),
            P("section", None, "tensor"),
            P("section", "tensor", None),
            P("section", "tensor"),
            P("section", "tensor"),
            P("section", "tensor"),
            P("section", "tensor"),
            P("section", None, "tensor"),
            P("section", "tensor"),
            P("section", "tensor", None),
            P("section", "tensor"),
            P("section", "tensor"),
        ),
        check_vma=False,
    )
```

```python
import math

import jax
import jax.numpy as jnp
from jax import lax
from jax.experimental import pallas as pl
from jax.experimental.pallas import tpu as pltpu
from jax.sharding import PartitionSpec as P

HEAD_DIM = 64
EPSILON = 1e-06
F32 = jnp.float32
BF16 = jnp.bfloat16
MIB = 1 << 20
VMEM_MIB = 62
RING_MIB = 61
TILE = 16
MICRO = 2
SPARE = MICRO
RANK, ACTIVE, UNITS = 0, 1, 3
LN1G, LN1B, OUTB, SATT, LN2G, LN2B, FC2B, SMLP = range(8)


def dot(left, right):
    return jnp.dot(left, right, preferred_element_type=F32)


def dot_nt(left, right):
    return lax.dot_general(left, right, (((1,), (1,)), ((), ())), preferred_element_type=F32)


def dot_tn(left, right):
    return lax.dot_general(left, right, (((0,), (0,)), ((), ())), preferred_element_type=F32)


def norm_stats(values):
    centre = jnp.mean(values, axis=-1, keepdims=True)
    centred = values - centre
    spread = jnp.mean(centred * centred, axis=-1, keepdims=True)
    scale = lax.rsqrt(spread + EPSILON)
    return centred * scale, scale


def tiles(rows):
    return [slice(r, r + TILE) for r in range(0, rows, TILE)]


def eights(values):
    total = values[:8]
    for r in range(8, values.shape[0], 8):
        total = total + values[r : r + 8]
    return total


def norm_backward(hat, scale, gain, error):
    weighted = error * gain
    mean_one = jnp.mean(weighted, axis=-1, keepdims=True)
    mean_two = jnp.mean(weighted * hat, axis=-1, keepdims=True)
    return scale * (weighted - mean_one - hat * mean_two)


def col_sum(values):
    return jnp.sum(values, axis=0, keepdims=True)


def call(kernel, scalars, grid, ins, outs, scratch=(), flops=0, moved=0, after=()):
    arrays = [a for a, _, _ in ins]
    in_specs = [pl.BlockSpec(b, m) for _, b, m in ins]
    aliases = {}
    for number, out in enumerate(outs):
        if out[4] is not None:
            aliases[1 + len(arrays)] = number
            arrays.append(out[4])
            in_specs.append(pl.BlockSpec(memory_space=pl.ANY))
    arrays += after
    in_specs += [pl.BlockSpec(memory_space=pl.ANY)] * len(after)
    extra = len(aliases) + len(after)
    in_count = len(ins)

    def body(*refs):
        kernel(*refs[: 1 + in_count], *refs[1 + in_count + extra :])

    return pl.pallas_call(
        body,
        out_shape=[jax.ShapeDtypeStruct(s, d) for s, d, _, _, _ in outs],
        grid_spec=pltpu.PrefetchScalarGridSpec(
            num_scalar_prefetch=1,
            grid=grid,
            in_specs=in_specs,
            out_specs=[pl.BlockSpec(b, m) for _, _, b, m, _ in outs],
            scratch_shapes=list(scratch),
        ),
        input_output_aliases=aliases,
        compiler_params=pltpu.CompilerParams(
            dimension_semantics=("arbitrary",) * len(grid), vmem_limit_bytes=VMEM_MIB * MIB
        ),
        cost_estimate=pl.CostEstimate(
            flops=int(flops), bytes_accessed=int(moved), transcendentals=0
        ),
    )(scalars, *arrays)


def manual(kernel, scalars, ins, outs, scratch, flops=0, moved=0, vmem=VMEM_MIB, after=(), same=None):
    any_space = pl.BlockSpec(memory_space=pl.ANY)
    vmem_space = pl.BlockSpec(memory_space=pltpu.VMEM)
    arrays = [a for a, _ in ins]
    in_specs = [vmem_space if inside else any_space for _, inside in ins]
    aliases = {1 + i: o for i, o in (same or {}).items()}
    before = len(arrays)
    for number, out in enumerate(outs):
        if out[3] is not None:
            aliases[1 + len(arrays)] = number
            arrays.append(out[3])
            in_specs.append(any_space)
    arrays += after
    in_specs += [any_space] * len(after)
    extra = len(arrays) - before
    in_count = len(ins)

    def body(*refs):
        kernel(*refs[: 1 + in_count], *refs[1 + in_count + extra :])

    return pl.pallas_call(
        body,
        out_shape=[jax.ShapeDtypeStruct(s, d) for s, d, _, _ in outs],
        in_specs=[pl.BlockSpec(memory_space=pltpu.SMEM)] + in_specs,
        out_specs=[vmem_space if inside else any_space for _, _, inside, _ in outs],
        scratch_shapes=list(scratch),
        input_output_aliases=aliases,
        compiler_params=pltpu.CompilerParams(vmem_limit_bytes=vmem * MIB),
        cost_estimate=pl.CostEstimate(
            flops=int(flops), bytes_accessed=int(moved), transcendentals=0
        ),
    )(scalars, *arrays)


def begin(src, dst, sem):
    copy = pltpu.make_async_copy(src, dst, sem)
    copy.start()
    return copy


def dma_sems(count):
    return pltpu.SemaphoreType.DMA((count,))


def whole2(i, s):
    return (0, 0)


def slot3(i, s):
    return (s[0], 0, 0)


def token_copies(s, source, number, refs, target, sems):
    rows, width = target.shape
    half = width // 2
    rank = s[RANK]
    if source == "relay":
        return [begin(refs[0], target, sems.at[0])]
    first = pl.multiple_of(rank * half, half)
    second = pl.multiple_of((1 - rank) * half, half)
    whole, other = refs
    return [
        begin(
            whole.at[number, 0, pl.ds(pl.multiple_of(rank * rows, rows), rows)],
            target.at[:, pl.ds(first, half)],
            sems.at[0],
        ),
        begin(other, target.at[:, pl.ds(second, half)], sems.at[1]),
    ]


def norm_kv(info, owner, number, source, tokens, vec, w_own, w_oth, bias_v, kept, after=()):
    rows, width = tokens[-1].shape[0], vec.shape[1]
    half = width // 2
    count = len(tokens)

    def kernel(s, *refs):
        token_refs = refs[:count]
        (v, own, oth, bv, x_out, n_out, kv_out, x_v, n_v, w_v, kv_v, tok_sems, w_sems,
         out_sems) = refs[count:]

        @pl.when(s[ACTIVE + owner] == 1)
        def _():
            arriving = token_copies(s, source, number, token_refs, x_v, tok_sems)
            loads = []
            for part in range(4):
                ref = own if part < 2 else oth
                loads.append(begin(ref.at[1 + part % 2], w_v.at[part], w_sems.at[part]))
            for copy in arriving:
                copy.wait()
            outs = [begin(x_v, x_out.at[number], out_sems.at[0])]
            for t in tiles(rows):
                hat, _ = norm_stats(x_v[t].astype(F32))
                n_v[t] = (hat * v[LN1G : LN1G + 1] + v[LN1B : LN1B + 1]).astype(BF16)
            outs.append(begin(n_v, n_out.at[number], out_sems.at[1]))
            for part in range(4):
                loads[part].wait()
                result = dot(n_v[...], w_v[part])
                kind, side = part % 2, part // 2
                columns = slice(side * half, (side + 1) * half)
                if kind == 1:
                    result = result + bv[:, columns]
                kv_v[part] = result.astype(BF16)
                outs.append(
                    begin(
                        kv_v.at[part],
                        kv_out.at[kind, :, pl.ds(side * half, half)],
                        out_sems.at[2 + part],
                    )
                )
            for copy in outs:
                copy.wait()

    stack = (MICRO, rows, width)
    return manual(
        kernel,
        info,
        [(array, False) for array in tokens]
        + [(vec, True), (w_own, False), (w_oth, False), (bias_v, True)],
        [
            (stack, BF16, False, kept.get("x")),
            (stack, BF16, False, kept.get("normed1")),
            ((2, rows, width), BF16, False, None),
        ],
        [
            pltpu.VMEM((rows, width), BF16),
            pltpu.VMEM((rows, width), BF16),
            pltpu.VMEM((4, width, half), BF16),
            pltpu.VMEM((4, rows, half), BF16),
            dma_sems(2),
            dma_sems(4),
            dma_sems(6),
        ],
        flops=2 * rows * width * 2 * width,
        moved=4 * width * width + 10 * rows * width,
        after=after,
    )


def project_q(info, owner, number, normed, w_own, w_oth, bias_q, kept):
    _, rows, width = normed.shape
    half = width // 2

    def kernel(s, n, own, oth, bq, q_out, n_v, w_v, q_v, in_sems, out_sems):
        @pl.when(s[ACTIVE + owner] == 1)
        def _():
            load = begin(n.at[number], n_v, in_sems.at[0])
            loads = [
                begin(own.at[0], w_v.at[0], in_sems.at[1]),
                begin(oth.at[0], w_v.at[1], in_sems.at[2]),
            ]
            load.wait()
            outs = []
            for side in range(2):
                loads[side].wait()
                columns = slice(side * half, (side + 1) * half)
                q_v[side] = (dot(n_v[...], w_v[side]) + bq[:, columns]).astype(BF16)
                outs.append(
                    begin(
                        q_v.at[side],
                        q_out.at[number, :, pl.ds(side * half, half)],
                        out_sems.at[side],
                    )
                )
            for copy in outs:
                copy.wait()

    return manual(
        kernel,
        info,
        [(normed, False), (w_own, False), (w_oth, False), (bias_q, True)],
        [((MICRO, rows, width), BF16, False, kept.get("q"))],
        [
            pltpu.VMEM((rows, width), BF16),
            pltpu.VMEM((2, width, half), BF16),
            pltpu.VMEM((2, rows, half), BF16),
            dma_sems(3),
            dma_sems(2),
        ],
        flops=2 * rows * width * width,
        moved=2 * width * width + 4 * rows * width,
    )[0]


def attend(info, owner, number, q, kv_here, kv_there, kept):
    _, rows, width = q.shape
    heads = width // HEAD_DIM
    factor = HEAD_DIM**-0.5 * math.log2(math.e)
    lanes = 2 * HEAD_DIM
    block = 2 * lanes
    steps = width // block

    def kernel(s, *refs):
        @pl.when(s[ACTIVE + owner] == 1)
        def _():
            compute(*refs)

    def compute(q_ref, here, there, e_out, o_out, mixed_out, inv_out, kv_out, *scratch):
        scores, results = scratch[:4], scratch[4:]
        kv_out[0, :, :rows] = here[...]
        kv_out[0, :, rows:] = there[...]
        first_q = lax.broadcasted_iota(jnp.int32, (rows, lanes), 1) < HEAD_DIM
        first_k = lax.broadcasted_iota(jnp.int32, (2 * rows, lanes), 1) < HEAD_DIM
        first_t = lax.broadcasted_iota(jnp.int32, (TILE, lanes), 1) < HEAD_DIM

        def columns(head):
            return slice(head // 2 * lanes, (head // 2 + 1) * lanes)

        def score(head):
            mine = first_q if head % 2 == 0 else ~first_q
            masked = jnp.where(mine, q_ref[0, :, columns(head)], 0)
            scores[head][...] = dot_nt(masked, kv_out[0, 0, :, columns(head)])

        score(0)
        for head in range(4):
            if head < 3:
                score(head + 1)
            for t in tiles(rows):
                tile = scores[head][t]
                top = jnp.max(tile, axis=-1, keepdims=True)
                e_out[0, head, t] = jnp.exp2((tile - top) * factor).astype(BF16)
            mine = first_k if head % 2 == 0 else ~first_k
            values = jnp.where(mine, kv_out[0, 1, :, columns(head)], 1)
            results[head][...] = dot(e_out[0, head], values)
        for pair in range(2):
            place = slice(pair * lanes, (pair + 1) * lanes)
            for t in tiles(rows):
                one, two = results[2 * pair][t], results[2 * pair + 1][t]
                total = jnp.where(
                    first_t, pltpu.roll(one, HEAD_DIM, 1), pltpu.roll(two, HEAD_DIM, 1)
                )
                inverse = 1.0 / total
                mixed = jnp.where(first_t, one, two) * inverse
                o_out[0, t, place] = mixed
                mixed_out[t, place] = mixed.astype(BF16)
                inv_out[0, t, place] = inverse

    def on(s):
        return s[ACTIVE + owner]

    def slot(s):
        return jnp.where(on(s) == 1, number, SPARE)

    column = lambda i, s: (slot(s), 0, i * on(s))
    spare = MICRO + 1
    return call(
        kernel,
        info,
        (steps,),
        [
            (q, (1, rows, block), lambda i, s: (number, 0, i * on(s))),
            (kv_here, (2, rows, block), lambda i, s: (0, 0, i * on(s))),
            (
                kv_there,
                (2, rows, block),
                lambda i, s: (0, 0, lax.rem(i + steps // 2, steps) * on(s)),
            ),
        ],
        [
            (
                (spare, heads, rows, 2 * rows),
                BF16,
                (1, 4, rows, 2 * rows),
                lambda i, s: (slot(s), i * on(s), 0, 0),
                kept.get("grown"),
            ),
            ((spare, rows, width), F32, (1, rows, block), column, kept.get("mixed_full")),
            ((rows, width), BF16, (rows, block), lambda i, s: (0, i * on(s)), None),
            ((spare, rows, width), F32, (1, rows, block), column, kept.get("inverse")),
            (
                (spare, 2, 2 * rows, width),
                BF16,
                (1, 2, 2 * rows, block),
                lambda i, s: (slot(s), 0, 0, i * on(s)),
                kept.get("kv"),
            ),
        ],
        [pltpu.VMEM((rows, 2 * rows), F32)] * 4 + [pltpu.VMEM((rows, lanes), F32)] * 4,
        flops=8 * rows * rows * width,
        moved=4 * heads * rows * rows + 30 * rows * width,
    )


def gelu_parts(x):
    size = jnp.abs(x)
    base = 1.0 + (0.3275911 * math.sqrt(0.5)) * size
    t = pl.reciprocal(base, approx=True)
    t = t * (2.0 - base * t)
    grown = jnp.exp2(x * x * (-0.5 * math.log2(math.e)))
    poly = 0.5 * 1.061405429
    for factor in (-1.453152027, 1.421413741, -0.284496736, 0.254829592):
        poly = poly * t + 0.5 * factor
    tail = poly * t * grown
    below = jnp.where(x < 0.0, tail, 1.0 - tail)
    return x * below, below + x * grown * (1.0 / math.sqrt(2.0 * math.pi))


CHUNK = 512


def mlp_forward(info, owner, number, mixed, x, vec, wo_own, wo_oth, wu_own, wu_oth, wd_own, wd_oth, b_up, kept, after=()):
    _, rows, width = x.shape
    side_hidden = wu_own.shape[1]
    hidden = 2 * side_hidden
    half = width // 2
    steps = hidden // CHUNK
    split = steps // 2

    def kernel(
        s, m, x_ref, v, woo, wot, wuo, wut, wdo, wdt, bu,
        att_out, res_out, n_out, act_out, slope_out, branch_out, y_out, relay_out, m_out,
        m_v, x_v, wo_v, wu_v, wd_v, att_v, res_v, n_v, h_v, act_v, slope_v, branch_v, y_v, acc,
        in_sems, wu_sems, wd_sems, out_sems, act_sems, slope_sems,
    ):
        @pl.when(s[ACTIVE + owner] == 1)
        def _():
            slot = number
            first = [
                begin(m, m_v, in_sems.at[0]),
                begin(woo, wo_v.at[0], in_sems.at[1]),
                begin(wot, wo_v.at[1], in_sems.at[2]),
                begin(x_ref.at[slot], x_v, in_sems.at[3]),
            ]
            ups, downs = [], []

            def prefetch(i):
                if i < steps:
                    part = pl.ds((i % split) * CHUNK, CHUNK)
                    up, down = (wuo, wdo) if i < split else (wut, wdt)
                    ups.append(begin(up.at[:, part], wu_v.at[i], wu_sems.at[i]))
                    downs.append(begin(down.at[part], wd_v.at[i], wd_sems.at[i]))

            prefetch(0)
            prefetch(1)
            for copy in first:
                copy.wait()
            acc[...] = dot(m_v[:, :half], wo_v[0]) + dot(m_v[:, half:], wo_v[1])
            for t in tiles(rows):
                attended = acc[t] + v[OUTB : OUTB + 1]
                att_v[t] = attended.astype(BF16)
                residual = x_v[t].astype(F32) + v[SATT : SATT + 1] * attended
                res_v[t] = residual
                hat, _ = norm_stats(residual)
                n_v[t] = (hat * v[LN2G : LN2G + 1] + v[LN2B : LN2B + 1]).astype(BF16)
            outs = [
                begin(att_v, att_out.at[slot], out_sems.at[0]),
                begin(res_v, res_out.at[slot], out_sems.at[1]),
                begin(n_v, n_out.at[slot], out_sems.at[2]),
                begin(m_v, m_out.at[slot], out_sems.at[6]),
            ]

            def up_product(i):
                ups[i].wait()
                h_v[i % 2] = dot(n_v[...], wu_v[i])

            def down_product(i):
                downs[i].wait()
                part = pl.ds(i * CHUNK, CHUNK)
                outs.append(begin(act_v.at[i], act_out.at[slot, :, part], act_sems.at[i]))
                outs.append(begin(slope_v.at[i], slope_out.at[slot, :, part], slope_sems.at[i]))
                product = dot(act_v[i], wd_v[i])
                acc[...] = product if i == 0 else acc[...] + product

            up_product(0)
            for i in range(steps):
                prefetch(i + 2)
                if i > 0:
                    down_product(i - 1)
                if i + 1 < steps:
                    up_product(i + 1)
                for t in tiles(rows):
                    active, slope = gelu_parts(h_v[i % 2, t] + bu[i : i + 1])
                    act_v[i, t] = active.astype(BF16)
                    slope_v[i, t] = slope.astype(BF16)
            down_product(steps - 1)
            for t in tiles(rows):
                branch = acc[t] + v[FC2B : FC2B + 1]
                y_v[t] = (res_v[t] + v[SMLP : SMLP + 1] * branch).astype(BF16)
                branch_v[t] = branch.astype(BF16)
            outs.append(begin(y_v, relay_out, out_sems.at[3]))
            outs.append(begin(y_v, y_out.at[slot], out_sems.at[4]))
            outs.append(begin(branch_v, branch_out.at[slot], out_sems.at[5]))
            for copy in outs:
                copy.wait()

    stack = (MICRO, rows, width)
    tall = (MICRO, rows, hidden)
    plain = pltpu.VMEM((rows, width), BF16)
    full = pltpu.VMEM((rows, width), F32)
    chunks = pltpu.VMEM((steps, rows, CHUNK), BF16)
    return manual(
        kernel,
        info,
        [
            (mixed, False),
            (x, False),
            (vec, True),
            (wo_own, False),
            (wo_oth, False),
            (wu_own, False),
            (wu_oth, False),
            (wd_own, False),
            (wd_oth, False),
            (b_up, True),
        ],
        [
            (stack, BF16, False, kept.get("attended")),
            (stack, F32, False, kept.get("residual")),
            (stack, BF16, False, kept.get("normed2")),
            (tall, BF16, False, kept.get("active")),
            (tall, BF16, False, kept.get("slope")),
            (stack, BF16, False, kept.get("branch")),
            (stack, BF16, False, kept.get("output")),
            ((rows, width), BF16, False, None),
            (stack, BF16, False, kept.get("mixed")),
        ],
        [
            plain,
            plain,
            pltpu.VMEM((2, half, width), BF16),
            pltpu.VMEM((steps, width, CHUNK), BF16),
            pltpu.VMEM((steps, CHUNK, width), BF16),
            plain,
            full,
            plain,
            pltpu.VMEM((2, rows, CHUNK), F32),
            chunks,
            chunks,
            plain,
            plain,
            full,
            dma_sems(4),
            dma_sems(steps),
            dma_sems(steps),
            dma_sems(7),
            dma_sems(steps),
            dma_sems(steps),
        ],
        flops=4 * rows * width * hidden + 2 * rows * width * width,
        moved=4 * width * hidden + 2 * width * width + 8 * rows * hidden,
        after=after,
    )


def scale_branch(info, owner, number, relay, vec, earlier, after=()):
    rows, width = relay.shape

    def kernel(s, g, v, gb_out, g_v, gb_v, sems):
        @pl.when(s[ACTIVE + owner] == 1)
        def _():
            begin(g, g_v, sems.at[0]).wait()
            gb_v[...] = (v[SMLP : SMLP + 1] * g_v[...].astype(F32)).astype(BF16)
            begin(gb_v, gb_out.at[number], sems.at[1]).wait()

    return manual(
        kernel,
        info,
        [(relay, False), (vec, True)],
        [((MICRO, rows, width), BF16, False, earlier)],
        [pltpu.VMEM((rows, width), BF16), pltpu.VMEM((rows, width), BF16), dma_sems(2)],
        moved=4 * rows * width,
        after=after,
    )[0]


def mlp_backward(info, owner, number, source, tokens, vec, wo_own, wo_oth, wu_own, wu_oth, wd_own, wd_oth, kept, grads, scaled, after):
    count = len(tokens)
    _, rows, width = kept["x"].shape
    side_hidden = wu_own.shape[1]
    hidden = 2 * side_hidden
    half = width // 2
    steps = hidden // CHUNK
    split = steps // 2

    def kernel(s, *refs):
        work(s, refs[:count], *refs[count:])

    def work(
        s, token_refs, branch, slope, res, att, v, woo, wot, wuo, wut, wdo, wdt,
        gb_out, before_out, ga_out, gm_out, gr_out, small_out, shift_out,
        g_v, branch_v, slope_v, res_v, att_v, wo_v, wu_v, wd_v, gb_v, d_v, before_v, ga_v, gm_v,
        gr_v, acc, sums, tok_sems, in_sems, slope_sems, wu_sems, wd_sems, out_sems, before_sems,
    ):
        @pl.when(s[ACTIVE + owner] == 0)
        def _():
            small_out[...] = jnp.zeros_like(small_out)
            shift_out[...] = jnp.zeros_like(shift_out)

        @pl.when(s[ACTIVE + owner] == 1)
        def _():
            slot = number
            arriving = token_copies(s, source, number, token_refs, g_v, tok_sems)
            ups, downs, slopes = [], [], []

            def prefetch(i):
                if i < steps:
                    part = pl.ds((i % split) * CHUNK, CHUNK)
                    up, down = (wuo, wdo) if i < split else (wut, wdt)
                    here = pl.ds(i * CHUNK, CHUNK)
                    downs.append(begin(down.at[part], wd_v.at[i], wd_sems.at[i]))
                    slopes.append(begin(slope.at[slot, :, here], slope_v.at[i], slope_sems.at[i]))
                    ups.append(begin(up.at[:, part], wu_v.at[i], wu_sems.at[i]))

            prefetch(0)
            branch_in = begin(branch.at[slot], branch_v, in_sems.at[0])
            prefetch(1)
            last = []
            for copy in arriving:
                copy.wait()
            for t in tiles(rows):
                gb_v[t] = (v[SMLP : SMLP + 1] * g_v[t].astype(F32)).astype(BF16)
            outs = []
            if not scaled:
                outs.append(begin(gb_v, gb_out.at[slot], out_sems.at[0]))

            def down_product(i):
                downs[i].wait()
                d_v[i % 2] = dot_nt(gb_v[...], wd_v[i])

            down_product(0)
            branch_in.wait()
            sums[...] = jnp.zeros_like(sums)
            for t in tiles(rows):
                sums[0] += eights(g_v[t].astype(F32) * branch_v[t].astype(F32))
                sums[1] += eights(gb_v[t].astype(F32))

            def up_product(i):
                ups[i].wait()
                part = pl.ds(i * CHUNK, CHUNK)
                outs.append(begin(before_v.at[i], before_out.at[slot, :, part], before_sems.at[i]))
                product = dot_nt(before_v[i], wu_v[i])
                acc[...] = product if i == 0 else acc[...] + product

            for i in range(steps):
                prefetch(i + 2)
                if i == steps - 2:
                    last = [
                        begin(res.at[slot], res_v, in_sems.at[1]),
                        begin(att.at[slot], att_v, in_sems.at[2]),
                        begin(woo, wo_v.at[0], in_sems.at[3]),
                        begin(wot, wo_v.at[1], in_sems.at[4]),
                    ]
                slopes[i].wait()
                if i > 0:
                    up_product(i - 1)
                if i + 1 < steps:
                    down_product(i + 1)
                total = jnp.zeros((8, CHUNK), F32)
                for t in tiles(rows):
                    grad_before = (d_v[i % 2, t] * slope_v[i, t].astype(F32)).astype(BF16)
                    before_v[i, t] = grad_before
                    total = total + eights(grad_before.astype(F32))
                shift_out[i : i + 1] = col_sum(total)
            up_product(steps - 1)
            for copy in last:
                copy.wait()
            for t in tiles(rows):
                hat, scale = norm_stats(res_v[t])
                error = acc[t]
                sums[2] += eights(error * hat)
                sums[3] += eights(error)
                grad = g_v[t].astype(F32) + norm_backward(hat, scale, v[LN2G : LN2G + 1], error)
                gr_v[t] = grad
                sums[4] += eights(grad * att_v[t].astype(F32))
                ga = (v[SATT : SATT + 1] * grad).astype(BF16)
                ga_v[t] = ga
                sums[5] += eights(ga.astype(F32))
            outs.append(begin(ga_v, ga_out.at[slot], out_sems.at[1]))
            outs.append(begin(gr_v, gr_out, out_sems.at[3]))
            gm_v[:, :half] = dot_nt(ga_v[...], wo_v[0]).astype(BF16)
            gm_v[:, half:] = dot_nt(ga_v[...], wo_v[1]).astype(BF16)
            outs.append(begin(gm_v, gm_out, out_sems.at[2]))
            small_out[...] = jnp.zeros_like(small_out)
            for row in range(6):
                small_out[row : row + 1] = col_sum(sums[row])
            for copy in outs:
                copy.wait()

    stack = (MICRO, rows, width)
    plain = pltpu.VMEM((rows, width), BF16)
    full = pltpu.VMEM((rows, width), F32)
    chunks = pltpu.VMEM((steps, rows, CHUNK), BF16)
    return manual(
        kernel,
        info,
        [(array, False) for array in tokens]
        + [
            (kept["branch"], False),
            (kept["slope"], False),
            (kept["residual"], False),
            (kept["attended"], False),
            (vec, True),
            (wo_own, False),
            (wo_oth, False),
            (wu_own, False),
            (wu_oth, False),
            (wd_own, False),
            (wd_oth, False),
        ],
        [
            (stack, BF16, False, None if scaled else grads.get("branch")),
            ((MICRO, rows, hidden), BF16, False, grads.get("before")),
            (stack, BF16, False, grads.get("attended")),
            ((rows, width), BF16, False, None),
            ((rows, width), F32, False, None),
            ((8, width), F32, True, None),
            ((steps, CHUNK), F32, True, None),
        ],
        [
            plain,
            plain,
            chunks,
            full,
            plain,
            pltpu.VMEM((2, half, width), BF16),
            pltpu.VMEM((steps, width, CHUNK), BF16),
            pltpu.VMEM((steps, CHUNK, width), BF16),
            plain,
            pltpu.VMEM((2, rows, CHUNK), F32),
            chunks,
            plain,
            plain,
            full,
            full,
            pltpu.VMEM((6, 8, width), F32),
            dma_sems(2),
            dma_sems(5),
            dma_sems(steps),
            dma_sems(steps),
            dma_sems(steps),
            dma_sems(4),
            dma_sems(steps),
        ],
        flops=4 * rows * width * hidden + 2 * rows * width * width,
        moved=4 * width * hidden + 2 * width * width + 8 * rows * hidden,
        after=after,
    )


def attend_backward(info, owner, number, grad_mixed, kept, after=()):
    _, rows, width = kept["q"].shape
    heads = width // HEAD_DIM
    lanes = 2 * HEAD_DIM
    block = 2 * lanes
    steps = width // block
    score_scale = HEAD_DIM**-0.5

    def kernel(s, *refs):
        @pl.when(s[ACTIVE + owner] == 1)
        def _():
            compute(*refs)

    def compute(gm, q_ref, kv, grown, full, inv, dq_out, here_out, there_out, *scratch):
        probs, scores = scratch[:4], scratch[4:8]
        own_v, centre_v = scratch[8:]
        first_q = lax.broadcasted_iota(jnp.int32, (rows, lanes), 1) < HEAD_DIM
        first_t = lax.broadcasted_iota(jnp.int32, (TILE, lanes), 1) < HEAD_DIM

        def columns(head):
            return slice(head // 2 * lanes, (head // 2 + 1) * lanes)

        for pair in range(2):
            place = columns(2 * pair)
            for t in tiles(rows):
                scaled = (gm[t, place].astype(F32) * inv[0, t, place]).astype(BF16)
                product = scaled.astype(F32) * full[0, t, place]
                for side in range(2):
                    mine = first_t if side == 0 else ~first_t
                    own_v[2 * pair + side, t] = jnp.where(mine, scaled, 0)
                    centre_v[2 * pair + side, t] = jnp.sum(
                        jnp.where(mine, product, 0.0), axis=-1, keepdims=True
                    )

        def prob(head):
            probs[head][...] = dot_nt(own_v[head], kv[0, 1, :, columns(head)])

        prob(0)
        grad_q, grad_k, grad_v = [], [], []
        for head in range(4):
            if head < 3:
                prob(head + 1)
            for t in tiles(rows):
                weight = grown[0, head, t].astype(F32)
                scores[head][t] = (weight * (probs[head][t] - centre_v[head, t])).astype(BF16)
            mine = first_q if head % 2 == 0 else ~first_q
            grad_v.append(dot_tn(grown[0, head], own_v[head]))
            grad_q.append(dot(scores[head][...], kv[0, 0, :, columns(head)]))
            masked = jnp.where(mine, q_ref[0, :, columns(head)], 0)
            grad_k.append(dot_tn(scores[head][...], masked))
            if head % 2 == 1:
                place = columns(head)
                dq = jnp.where(first_q, grad_q[head - 1], grad_q[head]) * score_scale
                dq_out[:, place] = dq.astype(BF16)
                dk = ((grad_k[head - 1] + grad_k[head]) * score_scale).astype(BF16)
                dv = (grad_v[head - 1] + grad_v[head]).astype(BF16)
                here_out[0, :, place] = dk[:rows]
                here_out[1, :, place] = dv[:rows]
                there_out[0, :, place] = dk[rows:]
                there_out[1, :, place] = dv[rows:]

    def on(s):
        return s[ACTIVE + owner]

    def slot(s):
        return jnp.where(on(s) == 1, number, SPARE)

    column = lambda i, s: (slot(s), 0, i * on(s))
    plain = lambda i, s: (0, i * on(s))
    return call(
        kernel,
        info,
        (steps,),
        [
            (grad_mixed, (rows, block), plain),
            (kept["q"], (1, rows, block), lambda i, s: (number, 0, i * on(s))),
            (kept["kv"], (1, 2, 2 * rows, block), lambda i, s: (slot(s), 0, 0, i * on(s))),
            (kept["grown"], (1, 4, rows, 2 * rows), lambda i, s: (slot(s), i * on(s), 0, 0)),
            (kept["mixed_full"], (1, rows, block), column),
            (kept["inverse"], (1, rows, block), column),
        ],
        [
            ((rows, width), BF16, (rows, block), plain, None),
            ((2, rows, width), BF16, (2, rows, block), lambda i, s: (0, 0, i * on(s)), None),
            ((2, rows, width), BF16, (2, rows, block), lambda i, s: (0, 0, i * on(s)), None),
        ],
        [pltpu.VMEM((rows, 2 * rows), F32)] * 4
        + [pltpu.VMEM((rows, 2 * rows), BF16)] * 4
        + [pltpu.VMEM((4, rows, lanes), BF16), pltpu.VMEM((4, rows, 1), F32)],
        flops=16 * rows * rows * width,
        moved=4 * heads * rows * rows + 30 * rows * width,
        after=after,
    )


def qkv_backward(info, owner, number, dq, dkv_here, dkv_there, w_own, w_oth, grad_res, vec, kept, grads, after=()):
    _, rows, width = kept["x"].shape
    half = width // 2

    def kernel(s, dq_ref, here, there, own, oth, gr, x_ref, v, packed_out, gx_out, relay_out,
               small_out, shift_out, a_v, b_v, p_v, w_v, gr_v, x_v, gx_v, acc, sums,
               a_sems, b_sems, w_sems, in_sems, packed_sems, out_sems):
        @pl.when(s[ACTIVE + owner] == 0)
        def _():
            small_out[...] = jnp.zeros_like(small_out)
            shift_out[...] = jnp.zeros_like(shift_out)

        @pl.when(s[ACTIVE + owner] == 1)
        def _():
            slot = number
            loads = []
            for part in range(6):
                kind, side = part % 3, part // 3
                columns = pl.ds(side * half, half)
                if kind == 0:
                    copies = [begin(dq_ref.at[:, columns], a_v.at[part], a_sems.at[part])]
                else:
                    turned = pl.ds((1 - side) * half, half)
                    copies = [
                        begin(here.at[kind - 1, :, columns], a_v.at[part], a_sems.at[part]),
                        begin(there.at[kind - 1, :, turned], b_v.at[part], b_sems.at[part]),
                    ]
                weight = own if side == 0 else oth
                copies.append(begin(weight.at[kind], w_v.at[part], w_sems.at[part]))
                loads.append(copies)
            last = [
                begin(x_ref.at[slot], x_v, in_sems.at[0]),
                begin(gr, gr_v, in_sems.at[1]),
            ]
            outs = []
            for part in range(6):
                for copy in loads[part]:
                    copy.wait()
                total = jnp.zeros((8, half), F32)
                for t in tiles(rows):
                    packed = a_v[part, t]
                    if part % 3 > 0:
                        packed = (packed.astype(F32) + b_v[part, t].astype(F32)).astype(BF16)
                    p_v[part, t] = packed
                    total = total + eights(packed.astype(F32))
                shift_out[part : part + 1] = col_sum(total)
                outs.append(
                    begin(
                        p_v.at[part],
                        packed_out.at[slot, :, pl.ds(part * half, half)],
                        packed_sems.at[part],
                    )
                )
                product = dot_nt(p_v[part], w_v[part])
                acc[...] = product if part == 0 else acc[...] + product
            for copy in last:
                copy.wait()
            sums[...] = jnp.zeros_like(sums)
            for t in tiles(rows):
                hat, scale = norm_stats(x_v[t].astype(F32))
                error = acc[t]
                grad = gr_v[t] + norm_backward(hat, scale, v[LN1G : LN1G + 1], error)
                gx_v[t] = grad.astype(BF16)
                sums[0] += eights(error * hat)
                sums[1] += eights(error)
            outs.append(begin(gx_v, relay_out, out_sems.at[0]))
            outs.append(begin(gx_v, gx_out.at[slot], out_sems.at[1]))
            small_out[...] = jnp.zeros_like(small_out)
            for row in range(2):
                small_out[row : row + 1] = col_sum(sums[row])
            for copy in outs:
                copy.wait()

    stack = (MICRO, rows, width)
    parts = pltpu.VMEM((6, rows, half), BF16)
    return manual(
        kernel,
        info,
        [
            (dq, False),
            (dkv_here, False),
            (dkv_there, False),
            (w_own, False),
            (w_oth, False),
            (grad_res, False),
            (kept["x"], False),
            (vec, True),
        ],
        [
            ((MICRO, rows, 3 * width), BF16, False, grads.get("packed")),
            (stack, BF16, False, grads.get("input")),
            ((rows, width), BF16, False, None),
            ((8, width), F32, True, None),
            ((8, half), F32, True, None),
        ],
        [
            parts,
            parts,
            parts,
            pltpu.VMEM((6, width, half), BF16),
            pltpu.VMEM((rows, width), F32),
            pltpu.VMEM((rows, width), BF16),
            pltpu.VMEM((rows, width), BF16),
            pltpu.VMEM((rows, width), F32),
            pltpu.VMEM((2, 8, width), F32),
            dma_sems(6),
            dma_sems(6),
            dma_sems(6),
            dma_sems(2),
            dma_sems(6),
            dma_sems(2),
        ],
        flops=6 * rows * width * width,
        moved=6 * width * width + 16 * rows * width,
        after=after,
    )


def swap(block):
    return lax.ppermute(block, "tensor", [(0, 1), (1, 0)])


def ring_order(count):
    return list(range(0, count, 2)) + list(range(count - 1, 0, -2))


def tied(value, *others):
    return lax.optimization_barrier((value, *others))[0]


class Ring:
    def __init__(self, info, parts, shapes, places):
        self.info, self.parts, self.shapes, self.places = info, parts, shapes, places
        self.count = lax.axis_size("dp")
        order = ring_order(self.count)
        n = self.count
        self.chunk = parts[0][0].shape[0] // (2 * n)
        self.widths = [pair[0].shape[1] for pair in parts]
        self.signs = (1, -1)
        self.routes = [[(order[i], order[(i + s) % n]) for i in range(n)] for s in self.signs]
        self.step = 0
        self.steps = 2 * (n - 1)
        self.totals = [None] * len(shapes)
        self.vmem = RING_MIB
        self.moving = self.add([0, 0], None)
        self.vmem = 16

    def unit(self, way, ahead):
        return UNITS + way * self.count + ahead % self.count

    def add(self, ahead, arrived, after=()):
        chunk, width, parts = self.chunk, sum(self.widths), len(self.parts)
        units = [self.unit(w, ahead[w]) for w in range(2)]
        terms = 2 if arrived is None else 3

        def kernel(s, *refs):
            halves = refs[: 2 * parts]
            refs = refs[2 * parts :]
            if terms == 3:
                arrivals, refs = refs[:2], refs[2:]
            outs, (held, sems) = refs[:2], refs[2:]
            copies = []
            for w in range(2):
                rows = pl.ds(pl.multiple_of(s[units[w]] * chunk, chunk), chunk)
                base = 0
                for number, columns in enumerate(self.widths):
                    for term in range(2):
                        copies.append(
                            begin(
                                halves[2 * number + term].at[rows],
                                held.at[w, term, :, pl.ds(base, columns)],
                                sems.at[w, term, number],
                            )
                        )
                    base += columns
                if terms == 3:
                    copies.append(begin(arrivals[w], held.at[w, 2], sems.at[w, 2, 0]))
            for copy in copies:
                copy.wait()
            for w in range(2):
                for t in tiles(chunk):
                    for first in range(0, width, 512):
                        c = slice(first, min(first + 512, width))
                        total = held[w, 0, t, c].astype(F32) + held[w, 1, t, c].astype(F32)
                        if terms == 3:
                            total = total + held[w, 2, t, c].astype(F32)
                        outs[w][t, c] = total.astype(BF16)

        arrays = [(term, False) for pair in self.parts for term in pair]
        if arrived is not None:
            arrays += [(block, False) for block in arrived]
        return manual(
            kernel,
            self.info,
            arrays,
            [((chunk, width), BF16, True, None)] * 2,
            [pltpu.VMEM((2, terms, chunk, width), BF16), pltpu.SemaphoreType.DMA((2, 3, parts))],
            moved=2 * (terms + 1) * 2 * chunk * width,
            vmem=self.vmem,
            after=after,
        )

    def put(self, ahead, blocks, after=()):
        chunk, width = self.chunk, sum(self.widths)
        units = [self.unit(w, pair[w]) for pair in ahead for w in range(2)]
        size = len(units)
        count = len(self.shapes)
        pieces = sum(len(self.places.columns(c)) for c in range(count))

        def kernel(s, *refs):
            sources, outs = refs[:size], refs[size : size + count]
            held, wide, in_sems, out_sems = refs[size + count + 2 :]
            loads = [begin(sources[w], held.at[w], in_sems.at[w]) for w in range(size)]
            copies = []
            for w in range(size):
                loads[w].wait()
                for t in tiles(chunk):
                    for first in range(0, width, 512):
                        c = slice(first, min(first + 512, width))
                        wide[w, t, c] = held[w, t, c].astype(F32)
                number = 0
                for target in range(count):
                    for first, columns in self.places.columns(target):
                        ref = self.places.ref(
                            outs[target], target, first, columns, s[units[w]], chunk
                        )
                        copies.append(
                            begin(
                                wide.at[w, :, pl.ds(first, columns)],
                                ref,
                                out_sems.at[w, number],
                            )
                        )
                        number += 1
            for copy in copies:
                copy.wait()

        results = manual(
            kernel,
            self.info,
            [(block, False) for block in blocks[:-2]] + [(block, False) for block in blocks[-2:]],
            [(shape, F32, False, old) for shape, old in zip(self.shapes, self.totals)]
            + [((chunk, width), BF16, False, None)] * 2,
            [
                pltpu.VMEM((size, chunk, width), BF16),
                pltpu.VMEM((size, chunk, width), F32),
                dma_sems(size),
                pltpu.SemaphoreType.DMA((size, pieces)),
            ],
            moved=2 * 6 * chunk * width,
            vmem=self.vmem,
            after=after,
            same={size - 2: count, size - 1: count + 1},
        )
        self.totals = list(results[:count])
        return list(results[count:])

    def advance(self, *after):
        arrived = [lax.ppermute(self.moving[w], "dp", self.routes[w]) for w in range(2)]
        if after:
            arrived = list(lax.optimization_barrier((*arrived, *after))[:2])
        step = self.step
        if step < self.count - 1:
            self.moving = self.add([-s * (step + 1) for s in self.signs], arrived)
        else:
            ahead = [[-s * (step - self.count + 1) for s in self.signs]]
            blocks = arrived
            if step == self.count - 1:
                ahead.insert(0, self.signs)
                blocks = list(self.moving) + arrived
            self.moving = self.put(ahead, blocks)
        self.step += 1

    def done(self):
        return self.step == self.steps

    def finish(self):
        while not self.done():
            self.advance()
        return self.totals


class MlpPlaces:
    def __init__(self, width, second, rows):
        self.width, self.second, self.rows = width, second, rows

    def columns(self, target):
        if target == 0:
            return [(0, self.width)]
        return [(self.width, self.second), (self.width + self.second, self.second)]

    def ref(self, out, target, first, columns, unit, chunk):
        base = self.rows if first > self.width else 0
        return out.at[pl.ds(pl.multiple_of(base + unit * chunk, chunk), chunk)]


class TailPlaces:
    def __init__(self, half, lanes):
        self.half, self.lanes = half, lanes

    def columns(self, target):
        half = self.half
        if target == 0:
            return [(j * half, half) for j in range(3)]
        return [(3 * half, half)] if target == 1 else [(4 * half, self.lanes)]

    def ref(self, out, target, first, columns, unit, chunk):
        rows = pl.ds(pl.multiple_of(unit * chunk, chunk), chunk)
        if target == 0:
            return out.at[first // self.half, rows]
        if target == 2:
            return out.at[rows]
        each = self.half // chunk
        return out.at[
            pl.ds(pl.multiple_of(lax.rem(unit, each) * chunk, chunk), chunk),
            pl.ds(pl.multiple_of(lax.div(unit, each) * self.half, self.half), self.half),
        ]


def partner_tokens(info, block, numbers):
    _, _, seq, half = block.shape
    rows = seq // 2

    def kernel(s, ref, out, sems):
        start = pl.multiple_of((1 - s[RANK]) * rows, rows)
        copies = [
            begin(ref.at[number, 0, pl.ds(start, rows)], out.at[place], sems.at[place])
            for place, number in enumerate(numbers)
        ]
        for copy in copies:
            copy.wait()

    return manual(
        kernel,
        info,
        [(block, False)],
        [((len(numbers), rows, half), BF16, True, None)],
        [dma_sems(len(numbers))],
        vmem=8,
    )[0]


def partner_features(info, block):
    micro, rows, width = block.shape
    half = width // 2

    def kernel(s, ref, out, sems):
        start = pl.multiple_of((1 - s[RANK]) * half, half)
        copies = [
            begin(ref.at[m, :, pl.ds(start, half)], out.at[m], sems.at[m]) for m in range(micro)
        ]
        for copy in copies:
            copy.wait()

    return manual(
        kernel,
        info,
        [(block, False)],
        [((micro, rows, half), BF16, True, None)],
        [dma_sems(micro)],
        vmem=8,
    )[0]


def join_tokens(info, block, received):
    micro, rows, width = block.shape
    half = width // 2

    def kernel(s, ref, other, out, sems):
        rank = s[RANK]
        features = pl.ds(pl.multiple_of(rank * half, half), half)
        here = pl.ds(pl.multiple_of(rank * rows, rows), rows)
        there = pl.ds(pl.multiple_of((1 - rank) * rows, rows), rows)
        copies = []
        for m in range(micro):
            copies.append(begin(ref.at[m, :, features], out.at[0, m, 0, here], sems.at[0, m]))
            copies.append(begin(other.at[m], out.at[0, m, 0, there], sems.at[1, m]))
        for copy in copies:
            copy.wait()

    return manual(
        kernel,
        info,
        [(block, False), (received, False)],
        [((1, micro, 1, 2 * rows, half), BF16, True, None)],
        [pltpu.SemaphoreType.DMA((2, micro))],
        vmem=8,
    )[0]


LANES = 128


def gather_vectors(info, sums, rows_out):
    calls = len(sums)
    width = sums[0][0].shape[1]
    half = width // 2

    def kernel(s, *refs):
        own, oth = refs[4 * calls :]
        low = s[RANK] == 0

        def total(kind):
            blocks = [refs[4 * c + kind][...] for c in range(calls)]
            return sum(blocks[1:], blocks[0])

        two, up, one, qkv = [total(kind) for kind in range(4)]
        own[...] = jnp.zeros_like(own)
        oth[...] = jnp.zeros_like(oth)
        place = 0

        def write(first, second):
            nonlocal place
            for c in range(0, half, LANES):
                own[place : place + 1] = first[:, c : c + LANES].astype(BF16)
                oth[place : place + 1] = second[:, c : c + LANES].astype(BF16)
                place += 1

        for block, count in ((one, 2), (two, 6)):
            for row in range(count):
                line = block[row : row + 1]
                left, right = line[:, :half], line[:, half:]
                write(jnp.where(low, left, right), jnp.where(low, right, left))
        for row in range(3):
            write(qkv[row : row + 1], qkv[3 + row : 4 + row])
        hidden_rows = up.shape[0] // 2
        for row in range(hidden_rows):
            write(up[row : row + 1], up[hidden_rows + row : hidden_rows + row + 1])

    vmem = pl.BlockSpec(memory_space=pltpu.VMEM)
    return pl.pallas_call(
        kernel,
        in_specs=[pl.BlockSpec(memory_space=pltpu.SMEM)] + [vmem] * (4 * calls),
        out_specs=[vmem] * 2,
        out_shape=[jax.ShapeDtypeStruct((rows_out, LANES), BF16)] * 2,
    )(info, *[block for group in sums for block in group])


def spread_vectors(sums, half, hidden_half):
    def kernel(ref, *outs):
        def line(number, out, row=0, columns=half, first=0):
            for c in range(0, columns, LANES):
                place = (number * half + c) // LANES
                out[row : row + 1, first + c : first + c + LANES] = ref[place : place + 1]

        for number in range(8):
            line(number, outs[number])
        line(8, outs[8])
        line(10, outs[8], row=1)
        line(11, outs[9], columns=hidden_half)

    vmem = pl.BlockSpec(memory_space=pltpu.VMEM)
    shapes = [(1, half)] * 8 + [(2, half), (1, hidden_half)]
    return pl.pallas_call(
        kernel,
        in_specs=[vmem],
        out_specs=[vmem] * 10,
        out_shape=[jax.ShapeDtypeStruct(shape, F32) for shape in shapes],
    )(sums)


def pack_vectors(blocks, hidden_bias):
    half = blocks[0].shape[1]
    hidden_rows = hidden_bias.shape[1] // half
    filled = sum(b.shape[0] for b in blocks)

    def kernel(*refs):
        out = refs[-1]
        place = 0
        for ref in refs[: len(blocks)]:
            for row in range(ref.shape[0]):
                out[place : place + 1] = ref[row : row + 1].astype(F32)
                place += 1
        for row in range(hidden_rows):
            columns = slice(row * half, (row + 1) * half)
            out[place : place + 1] = refs[len(blocks)][:, columns].astype(F32)
            place += 1

    return pl.pallas_call(
        kernel, out_shape=jax.ShapeDtypeStruct((filled + hidden_rows, half), F32)
    )(*blocks, hidden_bias)


def join_vectors(scalars, own, oth, hidden_rows):
    half = own.shape[1]

    def kernel(s, own_ref, oth_ref, vec, bias_q, bias_v, bias_up):
        low = s[RANK] == 0
        vec[:, :half] = jnp.where(low, own_ref[:8], oth_ref[:8])
        vec[:, half:] = jnp.where(low, oth_ref[:8], own_ref[:8])
        for row, out in ((8, bias_q), (9, bias_v)):
            out[:, :half] = own_ref[row : row + 1]
            out[:, half:] = oth_ref[row : row + 1]
        bias_up[:hidden_rows] = own_ref[10 : 10 + hidden_rows]
        bias_up[hidden_rows:] = oth_ref[10 : 10 + hidden_rows]

    vmem = pl.BlockSpec(memory_space=pltpu.VMEM)
    return pl.pallas_call(
        kernel,
        in_specs=[pl.BlockSpec(memory_space=pltpu.SMEM), vmem, vmem],
        out_specs=[vmem] * 4,
        out_shape=[
            jax.ShapeDtypeStruct((8, 2 * half), F32),
            jax.ShapeDtypeStruct((1, 2 * half), F32),
            jax.ShapeDtypeStruct((1, 2 * half), F32),
            jax.ShapeDtypeStruct((2 * hidden_rows, half), F32),
        ],
    )(scalars, own, oth)


def shards(
    inputs,
    cotangent,
    ln1_gain,
    ln1_bias,
    qkv_weight,
    qv_bias,
    out_weight,
    out_bias,
    scale_attn,
    ln2_gain,
    ln2_bias,
    fc1_weight,
    fc1_bias,
    fc2_weight,
    fc2_bias,
    scale_mlp,
):
    micro, images, seq_len, half = inputs.shape
    assert micro == MICRO and images == 1
    width = 2 * half
    hidden_half = fc1_weight.shape[2]

    count = lax.axis_size("dp")
    order = ring_order(count)
    table = [
        [rank, int(section == 0), int(section == 1)]
        + [way * count + (order.index(i) + ahead) % count for way in range(2) for ahead in range(count)]
        for section in range(2)
        for rank in range(2)
        for i in range(count)
    ]
    info = lax.dynamic_slice(
        jnp.asarray(table, jnp.int32),
        (lax.axis_index(("section", "tensor", "dp")), 0),
        (1, len(table[0])),
        allow_negative_indices=False,
    ).reshape(-1)

    first_oth = swap(partner_tokens(info, inputs, (0,))[0])
    vectors = pack_vectors(
        [
            ln1_gain, ln1_bias, out_bias, scale_attn, ln2_gain, ln2_bias, fc2_bias, scale_mlp,
            qv_bias[0],
        ],
        fc1_bias,
    )
    vectors_oth = swap(vectors)
    wq_own = jnp.transpose(qkv_weight[0], (1, 0, 2))
    wq_oth = swap(tied(wq_own, vectors))
    vec, bias_q, bias_v, b_up = join_vectors(info, vectors, vectors_oth, hidden_half // half)
    b_up = b_up.reshape(2 * hidden_half // CHUNK, CHUNK)
    wo_own, wu_own, wd_own = out_weight[0], fc1_weight[0], fc2_weight[0]
    wo_oth = swap(tied(wo_own, first_oth, vectors_oth))
    wu_oth = swap(tied(wu_own, first_oth, vectors_oth))
    wd_oth = swap(tied(wd_own, first_oth, vectors_oth))
    second_oth = swap(partner_tokens(info, tied(inputs, wd_oth), (1,))[0])
    cot_oth = swap(partner_tokens(info, tied(cotangent, wd_oth), (0, 1)))

    kept = {}

    def forward(owner, number, source, tokens, after=(), late=()):
        kept["x"], kept["normed1"], kv_here = norm_kv(
            info, owner, number, source, tokens, vec, wq_own, wq_oth, bias_v, kept, after
        )
        kv_there = swap(kv_here)
        kept["q"] = project_q(info, owner, number, kept["normed1"], wq_own, wq_oth, bias_q, kept)
        kept["grown"], kept["mixed_full"], mixed, kept["inverse"], kept["kv"] = attend(
            info, owner, number, kept["q"], kv_here, kv_there, kept
        )
        (
            kept["attended"],
            kept["residual"],
            kept["normed2"],
            kept["active"],
            kept["slope"],
            kept["branch"],
            kept["output"],
            relayed,
            kept["mixed"],
        ) = mlp_forward(
            info, owner, number, mixed, kept["x"], vec, wo_own, wo_oth, wu_own, wu_oth, wd_own,
            wd_oth, b_up, kept, late,
        )
        return relayed

    grads = {}
    sums = []

    def backward_mlp(owner, number, source, tokens, after, scaled=False):
        (
            branch,
            grads["before"],
            grads["attended"],
            grad_mixed,
            grad_res,
            small,
            shift,
        ) = mlp_backward(
            info, owner, number, source, tokens, vec, wo_own, wo_oth, wu_own, wu_oth, wd_own,
            wd_oth, kept, grads, scaled, after,
        )
        if not scaled:
            grads["branch"] = branch
        return grad_mixed, grad_res, small, shift

    def backward_attention(owner, number, grad_mixed, after=()):
        dq, dkv_here, dkv_send = attend_backward(info, owner, number, grad_mixed, kept, after)
        return dq, dkv_here, swap(dkv_send)

    def backward_qkv(owner, number, dq, dkv_here, dkv_there, grad_res, small, shift, after=()):
        grads["packed"], grads["input"], relayed, small_one, shift_qkv = qkv_backward(
            info, owner, number, dq, dkv_here, dkv_there, wq_own, wq_oth, grad_res, vec, kept,
            grads, after,
        )
        sums.append((small, shift, small_one, shift_qkv))
        return relayed

    def backward(owner, number, source, tokens, after):
        grad_mixed, grad_res, small, shift = backward_mlp(owner, number, source, tokens, after)
        flows = backward_attention(owner, number, grad_mixed)
        return backward_qkv(owner, number, *flows, grad_res, small, shift)

    relayed = forward(0, 0, "argument", (inputs, first_oth))
    first = lax.ppermute(relayed, "section", [(0, 1)])
    relayed = forward(0, 1, "argument", (inputs, second_oth), [relayed])
    second = lax.ppermute(relayed, "section", [(0, 1)])
    relayed = forward(1, 0, "relay", (first,), [relayed])
    relayed = backward(1, 0, "argument", (cotangent, cot_oth[0]), [relayed, second])
    first = lax.ppermute(relayed, "section", [(1, 0)])
    relayed = forward(1, 1, "relay", (second,), [relayed], [first])
    relayed = backward(1, 1, "argument", (cotangent, cot_oth[1]), [relayed])
    second = lax.ppermute(relayed, "section", [(1, 0)])
    relayed = backward(0, 0, "relay", (first,), [relayed])

    def weight_grad(left, right):
        return lax.dot_general(
            left, right, (((0, 1), (0, 1)), ((), ())), preferred_element_type=F32
        ).astype(BF16)

    grads["branch"] = scale_branch(info, 0, 1, second, vec, grads["branch"], [relayed])
    active, g_branch = kept["active"], grads["branch"]
    split = hidden_half // 2
    assert split == width

    def down_grad(start):
        return weight_grad(active[:, :, start : start + split], g_branch)

    down = []
    for start in (0, split):
        sent = swap(down_grad(hidden_half + start))
        down.append((down_grad(start), sent))
    grad_mixed, grad_res, small, shift = backward_mlp(
        0, 1, "relay", (second,), [pair[0] for pair in down], scaled=True
    )
    normed2, before = kept["normed2"], grads["before"]
    up_sent = swap(weight_grad(normed2, before[:, :, hidden_half:]))
    up_own = weight_grad(normed2, before[:, :, :hidden_half])
    ring_mlp = Ring(
        info,
        [(up_own, up_sent), *down],
        [up_own.shape, (hidden_half, width)],
        MlpPlaces(hidden_half, width, split),
    )
    flows = backward_attention(0, 1, grad_mixed, list(ring_mlp.moving))
    ring_mlp.advance(flows[0])
    grad_res = tied(grad_res, *ring_mlp.moving)
    backward_qkv(0, 1, *flows, grad_res, small, shift)
    packed = grads["packed"]
    ring_mlp.advance(packed)
    normed1 = tied(kept["normed1"], *ring_mlp.moving)
    vectors = gather_vectors(info, sums, width)

    def tail(index):
        columns = packed[:, :, index * 3 * half : (index + 1) * 3 * half]
        mixed = kept["mixed"][:, :, index * half : (index + 1) * half]
        g_att = grads["attended"]
        outs = [weight_grad(mixed, g_att[:, :, half * j : half * (j + 1)]) for j in range(2)]
        return [weight_grad(normed1, columns), jnp.concatenate(outs, axis=0), vectors[index]]

    tail_oth = tail(1)
    tail_sent = [swap(block) for block in tail_oth]
    tail_own = tail(0)
    ring_mlp.advance(tail_own[0])
    ring_tail = Ring(
        info,
        list(zip(tail_own, tail_sent)),
        [(3, width, half), (half, width), (width, LANES)],
        TailPlaces(half, LANES),
    )
    rings = [ring_mlp, ring_tail]
    before_it = ring_tail
    while not all(ring.done() for ring in rings):
        for ring in rings:
            if not ring.done():
                ring.advance(*before_it.moving)
                before_it = ring
    total_up, total_down = ring_mlp.finish()
    total_qkv, total_out, total_vectors = ring_tail.finish()
    block_outputs = join_tokens(info, kept["output"], swap(partner_features(info, kept["output"])))
    input_grads = join_tokens(info, grads["input"], swap(partner_features(info, grads["input"])))
    rows = spread_vectors(total_vectors, half, hidden_half)
    return (
        block_outputs,
        input_grads,
        rows[0],
        rows[1],
        jnp.transpose(total_qkv, (1, 0, 2))[None],
        rows[8][None],
        total_out[None],
        rows[7],
        rows[6],
        rows[4],
        rows[5],
        total_up[None],
        rows[9],
        total_down[None],
        rows[3],
        rows[2],
    )


def solution(mesh):
    placed = (
        P(None, "dp", None, "tensor"),
        P(None, "dp", None, "tensor"),
        P("section", "tensor"),
        P("section", "tensor"),
        P("section", None, None, "tensor"),
        P("section", None, "tensor"),
        P("section", "tensor", None),
        P("section", "tensor"),
        P("section", "tensor"),
        P("section", "tensor"),
        P("section", "tensor"),
        P("section", None, "tensor"),
        P("section", "tensor"),
        P("section", "tensor", None),
        P("section", "tensor"),
        P("section", "tensor"),
    )
    return jax.shard_map(
        shards,
        mesh=mesh,
        in_specs=placed,
        out_specs=(
            P("section", None, "dp", None, "tensor"),
            P("section", None, "dp", None, "tensor"),
            P("section", "tensor"),
            P("section", "tensor"),
            P("section", None, None, "tensor"),
            P("section", None, "tensor"),
            P("section", "tensor", None),
            P("section", "tensor"),
            P("section", "tensor"),
            P("section", "tensor"),
            P("section", "tensor"),
            P("section", None, "tensor"),
            P("section", "tensor"),
            P("section", "tensor", None),
            P("section", "tensor"),
            P("section", "tensor"),
        ),
        check_vma=False,
    )
```

```python
import math

import jax
import jax.numpy as jnp
from jax import lax
from jax.experimental import pallas as pl
from jax.experimental.pallas import tpu as pltpu
from jax.sharding import PartitionSpec as P

HEAD_DIM = 64
EPSILON = 1e-06
F32 = jnp.float32
BF16 = jnp.bfloat16
MIB = 1 << 20
VMEM_MIB = 62
RING_MIB = 61
TILE = 16
MICRO = 2
SPARE = MICRO
RANK, ACTIVE, UNITS = 0, 1, 3
LN1G, LN1B, OUTB, SATT, LN2G, LN2B, FC2B, SMLP = range(8)


def dot(left, right):
    return jnp.dot(left, right, preferred_element_type=F32)


def dot_nt(left, right):
    return lax.dot_general(left, right, (((1,), (1,)), ((), ())), preferred_element_type=F32)


def dot_tn(left, right):
    return lax.dot_general(left, right, (((0,), (0,)), ((), ())), preferred_element_type=F32)


def norm_stats(values):
    centre = jnp.mean(values, axis=-1, keepdims=True)
    centred = values - centre
    spread = jnp.mean(centred * centred, axis=-1, keepdims=True)
    scale = lax.rsqrt(spread + EPSILON)
    return centred * scale, scale


def tiles(rows):
    return [slice(r, r + TILE) for r in range(0, rows, TILE)]


def each_tile(rows, body):
    def step(i, carry):
        body(pl.ds(pl.multiple_of(i * TILE, TILE), TILE))
        return carry

    lax.fori_loop(0, rows // TILE, step, 0, unroll=8)


def eights(values):
    total = values[:8]
    for r in range(8, values.shape[0], 8):
        total = total + values[r : r + 8]
    return total


def norm_backward(hat, scale, gain, error):
    weighted = error * gain
    mean_one = jnp.mean(weighted, axis=-1, keepdims=True)
    mean_two = jnp.mean(weighted * hat, axis=-1, keepdims=True)
    return scale * (weighted - mean_one - hat * mean_two)


def col_sum(values):
    return jnp.sum(values, axis=0, keepdims=True)


def call(kernel, scalars, grid, ins, outs, scratch=(), flops=0, moved=0, after=()):
    arrays = [a for a, _, _ in ins]
    in_specs = [pl.BlockSpec(b, m) for _, b, m in ins]
    aliases = {}
    for number, out in enumerate(outs):
        if out[4] is not None:
            aliases[1 + len(arrays)] = number
            arrays.append(out[4])
            in_specs.append(pl.BlockSpec(memory_space=pl.ANY))
    arrays += after
    in_specs += [pl.BlockSpec(memory_space=pl.ANY)] * len(after)
    extra = len(aliases) + len(after)
    in_count = len(ins)

    def body(*refs):
        kernel(*refs[: 1 + in_count], *refs[1 + in_count + extra :])

    return pl.pallas_call(
        body,
        out_shape=[jax.ShapeDtypeStruct(s, d) for s, d, _, _, _ in outs],
        grid_spec=pltpu.PrefetchScalarGridSpec(
            num_scalar_prefetch=1,
            grid=grid,
            in_specs=in_specs,
            out_specs=[pl.BlockSpec(b, m) for _, _, b, m, _ in outs],
            scratch_shapes=list(scratch),
        ),
        input_output_aliases=aliases,
        compiler_params=pltpu.CompilerParams(
            dimension_semantics=("arbitrary",) * len(grid), vmem_limit_bytes=VMEM_MIB * MIB
        ),
        cost_estimate=pl.CostEstimate(
            flops=int(flops), bytes_accessed=int(moved), transcendentals=0
        ),
    )(scalars, *arrays)


def manual(kernel, scalars, ins, outs, scratch, flops=0, moved=0, vmem=VMEM_MIB, after=(), same=None):
    any_space = pl.BlockSpec(memory_space=pl.ANY)
    vmem_space = pl.BlockSpec(memory_space=pltpu.VMEM)
    arrays = [a for a, _ in ins]
    in_specs = [vmem_space if inside else any_space for _, inside in ins]
    aliases = {1 + i: o for i, o in (same or {}).items()}
    before = len(arrays)
    for number, out in enumerate(outs):
        if out[3] is not None:
            aliases[1 + len(arrays)] = number
            arrays.append(out[3])
            in_specs.append(any_space)
    arrays += after
    in_specs += [any_space] * len(after)
    extra = len(arrays) - before
    in_count = len(ins)

    def body(*refs):
        kernel(*refs[: 1 + in_count], *refs[1 + in_count + extra :])

    return pl.pallas_call(
        body,
        out_shape=[jax.ShapeDtypeStruct(s, d) for s, d, _, _ in outs],
        in_specs=[pl.BlockSpec(memory_space=pltpu.SMEM)] + in_specs,
        out_specs=[vmem_space if inside else any_space for _, _, inside, _ in outs],
        scratch_shapes=list(scratch),
        input_output_aliases=aliases,
        compiler_params=pltpu.CompilerParams(vmem_limit_bytes=vmem * MIB),
        cost_estimate=pl.CostEstimate(
            flops=int(flops), bytes_accessed=int(moved), transcendentals=0
        ),
    )(scalars, *arrays)


def begin(src, dst, sem):
    copy = pltpu.make_async_copy(src, dst, sem)
    copy.start()
    return copy


def dma_sems(count):
    return pltpu.SemaphoreType.DMA((count,))


def whole2(i, s):
    return (0, 0)


def slot3(i, s):
    return (s[0], 0, 0)


def token_copies(s, source, number, refs, target, sems):
    rows, width = target.shape
    half = width // 2
    rank = s[RANK]
    if source == "relay":
        return [begin(refs[0], target, sems.at[0])]
    first = pl.multiple_of(rank * half, half)
    second = pl.multiple_of((1 - rank) * half, half)
    whole, other = refs
    return [
        begin(
            whole.at[number, 0, pl.ds(pl.multiple_of(rank * rows, rows), rows)],
            target.at[:, pl.ds(first, half)],
            sems.at[0],
        ),
        begin(other, target.at[:, pl.ds(second, half)], sems.at[1]),
    ]


def norm_kv(info, owner, number, source, tokens, vec, w_own, w_oth, bias_v, kept, after=()):
    rows, width = tokens[-1].shape[0], vec.shape[1]
    half = width // 2
    count = len(tokens)

    def kernel(s, *refs):
        token_refs = refs[:count]
        (v, own, oth, bv, x_out, n_out, kv_out, x_v, n_v, w_v, kv_v, tok_sems, w_sems,
         out_sems) = refs[count:]

        @pl.when(s[ACTIVE + owner] == 1)
        def _():
            arriving = token_copies(s, source, number, token_refs, x_v, tok_sems)
            loads = []
            for part in range(4):
                ref = own if part < 2 else oth
                loads.append(begin(ref.at[1 + part % 2], w_v.at[part], w_sems.at[part]))
            for copy in arriving:
                copy.wait()
            outs = [begin(x_v, x_out.at[number], out_sems.at[0])]
            for t in tiles(rows):
                hat, _ = norm_stats(x_v[t].astype(F32))
                n_v[t] = (hat * v[LN1G : LN1G + 1] + v[LN1B : LN1B + 1]).astype(BF16)
            outs.append(begin(n_v, n_out.at[number], out_sems.at[1]))
            for part in range(4):
                loads[part].wait()
                result = dot(n_v[...], w_v[part])
                kind, side = part % 2, part // 2
                columns = slice(side * half, (side + 1) * half)
                if kind == 1:
                    result = result + bv[:, columns]
                kv_v[part] = result.astype(BF16)
                outs.append(
                    begin(
                        kv_v.at[part],
                        kv_out.at[kind, :, pl.ds(side * half, half)],
                        out_sems.at[2 + part],
                    )
                )
            for copy in outs:
                copy.wait()

    stack = (MICRO, rows, width)
    return manual(
        kernel,
        info,
        [(array, False) for array in tokens]
        + [(vec, True), (w_own, False), (w_oth, False), (bias_v, True)],
        [
            (stack, BF16, False, kept.get("x")),
            (stack, BF16, False, kept.get("normed1")),
            ((2, rows, width), BF16, False, None),
        ],
        [
            pltpu.VMEM((rows, width), BF16),
            pltpu.VMEM((rows, width), BF16),
            pltpu.VMEM((4, width, half), BF16),
            pltpu.VMEM((4, rows, half), BF16),
            dma_sems(2),
            dma_sems(4),
            dma_sems(6),
        ],
        flops=2 * rows * width * 2 * width,
        moved=4 * width * width + 10 * rows * width,
        after=after,
    )


def project_q(info, owner, number, normed, w_own, w_oth, bias_q, kept):
    _, rows, width = normed.shape
    half = width // 2

    def kernel(s, n, own, oth, bq, q_out, n_v, w_v, q_v, in_sems, out_sems):
        @pl.when(s[ACTIVE + owner] == 1)
        def _():
            load = begin(n.at[number], n_v, in_sems.at[0])
            loads = [
                begin(own.at[0], w_v.at[0], in_sems.at[1]),
                begin(oth.at[0], w_v.at[1], in_sems.at[2]),
            ]
            load.wait()
            outs = []
            for side in range(2):
                loads[side].wait()
                columns = slice(side * half, (side + 1) * half)
                q_v[side] = (dot(n_v[...], w_v[side]) + bq[:, columns]).astype(BF16)
                outs.append(
                    begin(
                        q_v.at[side],
                        q_out.at[number, :, pl.ds(side * half, half)],
                        out_sems.at[side],
                    )
                )
            for copy in outs:
                copy.wait()

    return manual(
        kernel,
        info,
        [(normed, False), (w_own, False), (w_oth, False), (bias_q, True)],
        [((MICRO, rows, width), BF16, False, kept.get("q"))],
        [
            pltpu.VMEM((rows, width), BF16),
            pltpu.VMEM((2, width, half), BF16),
            pltpu.VMEM((2, rows, half), BF16),
            dma_sems(3),
            dma_sems(2),
        ],
        flops=2 * rows * width * width,
        moved=2 * width * width + 4 * rows * width,
    )[0]


def attend(info, owner, number, q, kv_here, kv_there, kept):
    _, rows, width = q.shape
    heads = width // HEAD_DIM
    factor = HEAD_DIM**-0.5 * math.log2(math.e)
    lanes = 2 * HEAD_DIM
    block = 2 * lanes
    steps = width // block

    def kernel(s, *refs):
        @pl.when(s[ACTIVE + owner] == 1)
        def _():
            compute(*refs)

    def compute(q_ref, here, there, e_out, o_out, mixed_out, inv_out, kv_out, *scratch):
        scores, results = scratch[:4], scratch[4:]
        kv_out[0, :, :rows] = here[...]
        kv_out[0, :, rows:] = there[...]
        first_q = lax.broadcasted_iota(jnp.int32, (rows, lanes), 1) < HEAD_DIM
        first_k = lax.broadcasted_iota(jnp.int32, (2 * rows, lanes), 1) < HEAD_DIM
        first_t = lax.broadcasted_iota(jnp.int32, (TILE, lanes), 1) < HEAD_DIM

        def columns(head):
            return slice(head // 2 * lanes, (head // 2 + 1) * lanes)

        def score(head):
            mine = first_q if head % 2 == 0 else ~first_q
            masked = jnp.where(mine, q_ref[0, :, columns(head)], 0)
            scores[head][...] = dot_nt(masked, kv_out[0, 0, :, columns(head)])

        score(0)
        for head in range(4):
            if head < 3:
                score(head + 1)
            for t in tiles(rows):
                tile = scores[head][t]
                top = jnp.max(tile, axis=-1, keepdims=True)
                e_out[0, head, t] = jnp.exp2((tile - top) * factor).astype(BF16)
            mine = first_k if head % 2 == 0 else ~first_k
            values = jnp.where(mine, kv_out[0, 1, :, columns(head)], 1)
            results[head][...] = dot(e_out[0, head], values)
        for pair in range(2):
            place = slice(pair * lanes, (pair + 1) * lanes)
            for t in tiles(rows):
                one, two = results[2 * pair][t], results[2 * pair + 1][t]
                total = jnp.where(
                    first_t, pltpu.roll(one, HEAD_DIM, 1), pltpu.roll(two, HEAD_DIM, 1)
                )
                inverse = 1.0 / total
                mixed = jnp.where(first_t, one, two) * inverse
                o_out[0, t, place] = mixed
                mixed_out[t, place] = mixed.astype(BF16)
                inv_out[0, t, place] = inverse

    def on(s):
        return s[ACTIVE + owner]

    def slot(s):
        return jnp.where(on(s) == 1, number, SPARE)

    column = lambda i, s: (slot(s), 0, i * on(s))
    spare = MICRO + 1
    return call(
        kernel,
        info,
        (steps,),
        [
            (q, (1, rows, block), lambda i, s: (number, 0, i * on(s))),
            (kv_here, (2, rows, block), lambda i, s: (0, 0, i * on(s))),
            (
                kv_there,
                (2, rows, block),
                lambda i, s: (0, 0, lax.rem(i + steps // 2, steps) * on(s)),
            ),
        ],
        [
            (
                (spare, heads, rows, 2 * rows),
                BF16,
                (1, 4, rows, 2 * rows),
                lambda i, s: (slot(s), i * on(s), 0, 0),
                kept.get("grown"),
            ),
            ((spare, rows, width), F32, (1, rows, block), column, kept.get("mixed_full")),
            ((rows, width), BF16, (rows, block), lambda i, s: (0, i * on(s)), None),
            ((spare, rows, width), F32, (1, rows, block), column, kept.get("inverse")),
            (
                (spare, 2, 2 * rows, width),
                BF16,
                (1, 2, 2 * rows, block),
                lambda i, s: (slot(s), 0, 0, i * on(s)),
                kept.get("kv"),
            ),
        ],
        [pltpu.VMEM((rows, 2 * rows), F32)] * 4 + [pltpu.VMEM((rows, lanes), F32)] * 4,
        flops=8 * rows * rows * width,
        moved=4 * heads * rows * rows + 30 * rows * width,
    )


def gelu_parts(x):
    size = jnp.abs(x)
    base = 1.0 + (0.3275911 * math.sqrt(0.5)) * size
    t = pl.reciprocal(base, approx=True)
    t = t * (2.0 - base * t)
    grown = jnp.exp2(x * x * (-0.5 * math.log2(math.e)))
    poly = 0.5 * 1.061405429
    for factor in (-1.453152027, 1.421413741, -0.284496736, 0.254829592):
        poly = poly * t + 0.5 * factor
    tail = poly * t * grown
    below = jnp.where(x < 0.0, tail, 1.0 - tail)
    return x * below, below + x * grown * (1.0 / math.sqrt(2.0 * math.pi))


CHUNK = 512


def mlp_forward(info, owner, number, mixed, x, vec, wo_own, wo_oth, wu_own, wu_oth, wd_own, wd_oth, b_up, kept, after=()):
    _, rows, width = x.shape
    side_hidden = wu_own.shape[1]
    hidden = 2 * side_hidden
    half = width // 2
    steps = hidden // CHUNK
    split = steps // 2

    def kernel(
        s, m, x_ref, v, woo, wot, wuo, wut, wdo, wdt, bu,
        att_out, res_out, n_out, act_out, slope_out, branch_out, y_out, relay_out, m_out,
        m_v, x_v, wo_v, wu_v, wd_v, att_v, res_v, n_v, h_one, h_two, a_one, a_two, d_one, d_two,
        branch_v, y_v, acc,
        in_sems, wu_sems, wd_sems, out_sems, act_sems, slope_sems,
    ):
        @pl.when(s[ACTIVE + owner] == 1)
        def _():
            slot = number
            first = [
                begin(m, m_v, in_sems.at[0]),
                begin(woo, wo_v.at[0], in_sems.at[1]),
                begin(wot, wo_v.at[1], in_sems.at[2]),
                begin(x_ref.at[slot], x_v, in_sems.at[3]),
            ]
            for i in range(steps):
                part = pl.ds((i % split) * CHUNK, CHUNK)
                up, down = (wuo, wdo) if i < split else (wut, wdt)
                begin(up.at[:, part], wu_v.at[i], wu_sems.at[i])
                begin(down.at[part], wd_v.at[i], wd_sems.at[i])
            for copy in first:
                copy.wait()
            acc[...] = dot(m_v[:, :half], wo_v[0]) + dot(m_v[:, half:], wo_v[1])

            def first_norm(t):
                attended = acc[t] + v[OUTB : OUTB + 1]
                att_v[t] = attended.astype(BF16)
                residual = x_v[t].astype(F32) + v[SATT : SATT + 1] * attended
                res_v[t] = residual
                hat, _ = norm_stats(residual)
                n_v[t] = (hat * v[LN2G : LN2G + 1] + v[LN2B : LN2B + 1]).astype(BF16)

            each_tile(rows, first_norm)
            outs = [
                begin(att_v, att_out.at[slot], out_sems.at[0]),
                begin(res_v, res_out.at[slot], out_sems.at[1]),
                begin(n_v, n_out.at[slot], out_sems.at[2]),
                begin(m_v, m_out.at[slot], out_sems.at[6]),
            ]

            def up_product(i, target):
                target[...] = dot(n_v[...], wu_v[i])

            def up_wait(i):
                pltpu.make_async_copy(
                    wuo.at[:, pl.ds(0, CHUNK)], wu_v.at[i], wu_sems.at[i]
                ).wait()

            def down_wait(i):
                pltpu.make_async_copy(wdo.at[pl.ds(0, CHUNK)], wd_v.at[i], wd_sems.at[i]).wait()

            def copies(i, active, slope, side):
                part = pl.ds(pl.multiple_of(i * CHUNK, CHUNK), CHUNK)
                return [
                    pltpu.make_async_copy(active, act_out.at[slot, :, part], act_sems.at[side]),
                    pltpu.make_async_copy(
                        slope, slope_out.at[slot, :, part], slope_sems.at[side]
                    ),
                ]

            def activate(i, source, active_to, slope_to):
                shift = bu[pl.ds(i, 1), :]
                for t in tiles(rows):
                    active, slope = gelu_parts(source[t] + shift)
                    active_to[t] = active.astype(BF16)
                    slope_to[t] = slope.astype(BF16)

            def pair(j, carry):
                i = 2 * j
                before = jnp.maximum(i - 1, 0)
                up_wait(i + 1)

                @pl.when(j > 0)
                def _():
                    for copy in copies(i - 2, a_one, d_one, 0):
                        copy.wait()
                    down_wait(i - 1)

                acc[...] += dot(a_two[...], wd_v[before])
                up_product(i + 1, h_two)
                activate(i, h_one, a_one, d_one)
                for copy in copies(i, a_one, d_one, 0):
                    copy.start()

                @pl.when(j > 0)
                def _():
                    down_wait(i)
                    for copy in copies(i - 1, a_two, d_two, 1):
                        copy.wait()

                @pl.when(i + 2 < steps)
                def _():
                    up_wait(i + 2)

                acc[...] += dot(a_one[...], wd_v[i])
                up_product(jnp.minimum(i + 2, steps - 1), h_one)
                activate(i + 1, h_two, a_two, d_two)
                for copy in copies(i + 1, a_two, d_two, 1):
                    copy.start()
                return carry

            acc[...] = jnp.zeros_like(acc)
            a_two[...] = jnp.zeros_like(a_two)
            up_wait(0)
            down_wait(0)
            up_product(0, h_one)
            lax.fori_loop(0, steps // 2, pair, 0)
            down_wait(steps - 1)
            acc[...] += dot(a_two[...], wd_v[steps - 1])

            def finish(t):
                branch = acc[t] + v[FC2B : FC2B + 1]
                y_v[t] = (res_v[t] + v[SMLP : SMLP + 1] * branch).astype(BF16)
                branch_v[t] = branch.astype(BF16)

            each_tile(rows, finish)
            outs += copies(steps - 2, a_one, d_one, 0) + copies(steps - 1, a_two, d_two, 1)
            outs.append(begin(y_v, relay_out, out_sems.at[3]))
            outs.append(begin(y_v, y_out.at[slot], out_sems.at[4]))
            outs.append(begin(branch_v, branch_out.at[slot], out_sems.at[5]))
            for copy in outs:
                copy.wait()

    stack = (MICRO, rows, width)
    tall = (MICRO, rows, hidden)
    plain = pltpu.VMEM((rows, width), BF16)
    full = pltpu.VMEM((rows, width), F32)
    chunk = pltpu.VMEM((rows, CHUNK), BF16)
    wide = pltpu.VMEM((rows, CHUNK), F32)
    return manual(
        kernel,
        info,
        [
            (mixed, False),
            (x, False),
            (vec, True),
            (wo_own, False),
            (wo_oth, False),
            (wu_own, False),
            (wu_oth, False),
            (wd_own, False),
            (wd_oth, False),
            (b_up, True),
        ],
        [
            (stack, BF16, False, kept.get("attended")),
            (stack, F32, False, kept.get("residual")),
            (stack, BF16, False, kept.get("normed2")),
            (tall, BF16, False, kept.get("active")),
            (tall, BF16, False, kept.get("slope")),
            (stack, BF16, False, kept.get("branch")),
            (stack, BF16, False, kept.get("output")),
            ((rows, width), BF16, False, None),
            (stack, BF16, False, kept.get("mixed")),
        ],
        [
            plain,
            plain,
            pltpu.VMEM((2, half, width), BF16),
            pltpu.VMEM((steps, width, CHUNK), BF16),
            pltpu.VMEM((steps, CHUNK, width), BF16),
            plain,
            full,
            plain,
            wide,
            wide,
            chunk,
            chunk,
            chunk,
            chunk,
            plain,
            plain,
            full,
            dma_sems(4),
            dma_sems(steps),
            dma_sems(steps),
            dma_sems(7),
            dma_sems(2),
            dma_sems(2),
        ],
        flops=4 * rows * width * hidden + 2 * rows * width * width,
        moved=4 * width * hidden + 2 * width * width + 8 * rows * hidden,
        after=after,
    )


def scale_branch(info, owner, number, relay, vec, earlier, after=()):
    rows, width = relay.shape

    def kernel(s, g, v, gb_out, g_v, gb_v, sems):
        @pl.when(s[ACTIVE + owner] == 1)
        def _():
            begin(g, g_v, sems.at[0]).wait()
            gb_v[...] = (v[SMLP : SMLP + 1] * g_v[...].astype(F32)).astype(BF16)
            begin(gb_v, gb_out.at[number], sems.at[1]).wait()

    return manual(
        kernel,
        info,
        [(relay, False), (vec, True)],
        [((MICRO, rows, width), BF16, False, earlier)],
        [pltpu.VMEM((rows, width), BF16), pltpu.VMEM((rows, width), BF16), dma_sems(2)],
        moved=4 * rows * width,
        after=after,
    )[0]


def mlp_backward(info, owner, number, source, tokens, vec, wo_own, wo_oth, wu_own, wu_oth, wd_own, wd_oth, kept, grads, scaled, after):
    count = len(tokens)
    _, rows, width = kept["x"].shape
    side_hidden = wu_own.shape[1]
    hidden = 2 * side_hidden
    half = width // 2
    steps = hidden // CHUNK
    split = steps // 2

    def kernel(s, *refs):
        work(s, refs[:count], *refs[count:])

    def work(
        s, token_refs, branch, slope, res, att, v, woo, wot, wuo, wut, wdo, wdt,
        gb_out, before_out, ga_out, gm_out, gr_out, small_out, shift_out,
        g_v, branch_v, slope_v, res_v, att_v, wo_v, wu_v, wd_v, gb_v, d_one, d_two, b_one, b_two, ga_v, gm_v,
        gr_v, acc, sums, tok_sems, in_sems, slope_sems, wu_sems, wd_sems, out_sems, before_sems,
    ):
        @pl.when(s[ACTIVE + owner] == 0)
        def _():
            small_out[...] = jnp.zeros_like(small_out)
            shift_out[...] = jnp.zeros_like(shift_out)

        @pl.when(s[ACTIVE + owner] == 1)
        def _():
            slot = number
            arriving = token_copies(s, source, number, token_refs, g_v, tok_sems)
            branch_in = begin(branch.at[slot], branch_v, in_sems.at[0])
            for i in range(steps):
                part = pl.ds((i % split) * CHUNK, CHUNK)
                up, down = (wuo, wdo) if i < split else (wut, wdt)
                here = pl.ds(i * CHUNK, CHUNK)
                begin(down.at[part], wd_v.at[i], wd_sems.at[i])
                begin(slope.at[slot, :, here], slope_v.at[i], slope_sems.at[i])
                begin(up.at[:, part], wu_v.at[i], wu_sems.at[i])
            last = [
                begin(res.at[slot], res_v, in_sems.at[1]),
                begin(att.at[slot], att_v, in_sems.at[2]),
                begin(woo, wo_v.at[0], in_sems.at[3]),
                begin(wot, wo_v.at[1], in_sems.at[4]),
            ]
            for copy in arriving:
                copy.wait()

            def scale(t):
                gb_v[t] = (v[SMLP : SMLP + 1] * g_v[t].astype(F32)).astype(BF16)

            each_tile(rows, scale)
            outs = []
            if not scaled:
                outs.append(begin(gb_v, gb_out.at[slot], out_sems.at[0]))

            def down_product(i, target):
                target[...] = dot_nt(gb_v[...], wd_v[i])

            def down_wait(i):
                pltpu.make_async_copy(wdo.at[pl.ds(0, CHUNK)], wd_v.at[i], wd_sems.at[i]).wait()

            def up_wait(i):
                pltpu.make_async_copy(
                    wuo.at[:, pl.ds(0, CHUNK)], wu_v.at[i], wu_sems.at[i]
                ).wait()

            def slope_wait(i):
                pltpu.make_async_copy(
                    slope.at[slot, :, pl.ds(0, CHUNK)], slope_v.at[i], slope_sems.at[i]
                ).wait()

            def copy_out(i, held, side):
                part = pl.ds(pl.multiple_of(i * CHUNK, CHUNK), CHUNK)
                return pltpu.make_async_copy(
                    held, before_out.at[slot, :, part], before_sems.at[side]
                )

            def differentiate(i, source, target):
                total = jnp.zeros((8, CHUNK), F32)
                for t in tiles(rows):
                    grad_before = (source[t] * slope_v[i, t].astype(F32)).astype(BF16)
                    target[t] = grad_before
                    total = total + eights(grad_before.astype(F32))
                shift_out[pl.ds(i, 1), :] = col_sum(total)

            def pair(j, carry):
                i = 2 * j
                before = jnp.maximum(i - 1, 0)
                slope_wait(i)
                down_wait(i + 1)

                @pl.when(j > 0)
                def _():
                    copy_out(i - 2, b_one, 0).wait()
                    up_wait(i - 1)

                acc[...] += dot_nt(b_two[...], wu_v[before])
                down_product(i + 1, d_two)
                differentiate(i, d_one, b_one)
                copy_out(i, b_one, 0).start()
                slope_wait(i + 1)

                @pl.when(j > 0)
                def _():
                    up_wait(i)
                    copy_out(i - 1, b_two, 1).wait()

                @pl.when(i + 2 < steps)
                def _():
                    down_wait(i + 2)

                acc[...] += dot_nt(b_one[...], wu_v[i])
                down_product(jnp.minimum(i + 2, steps - 1), d_one)
                differentiate(i + 1, d_two, b_two)
                copy_out(i + 1, b_two, 1).start()
                return carry

            acc[...] = jnp.zeros_like(acc)
            b_two[...] = jnp.zeros_like(b_two)
            down_wait(0)
            down_product(0, d_one)
            branch_in.wait()
            sums[...] = jnp.zeros_like(sums)

            def branch_sums(t):
                sums[0] += eights(g_v[t].astype(F32) * branch_v[t].astype(F32))
                sums[1] += eights(gb_v[t].astype(F32))

            each_tile(rows, branch_sums)
            up_wait(0)
            lax.fori_loop(0, steps // 2, pair, 0)
            up_wait(steps - 1)
            acc[...] += dot_nt(b_two[...], wu_v[steps - 1])
            outs += [copy_out(steps - 2, b_one, 0), copy_out(steps - 1, b_two, 1)]
            for copy in last:
                copy.wait()

            def last_norm(t):
                hat, scale = norm_stats(res_v[t])
                error = acc[t]
                sums[2] += eights(error * hat)
                sums[3] += eights(error)
                grad = g_v[t].astype(F32) + norm_backward(hat, scale, v[LN2G : LN2G + 1], error)
                gr_v[t] = grad
                sums[4] += eights(grad * att_v[t].astype(F32))
                ga = (v[SATT : SATT + 1] * grad).astype(BF16)
                ga_v[t] = ga
                sums[5] += eights(ga.astype(F32))

            each_tile(rows, last_norm)
            outs.append(begin(ga_v, ga_out.at[slot], out_sems.at[1]))
            outs.append(begin(gr_v, gr_out, out_sems.at[3]))
            gm_v[:, :half] = dot_nt(ga_v[...], wo_v[0]).astype(BF16)
            gm_v[:, half:] = dot_nt(ga_v[...], wo_v[1]).astype(BF16)
            outs.append(begin(gm_v, gm_out, out_sems.at[2]))
            small_out[...] = jnp.zeros_like(small_out)
            for row in range(6):
                small_out[row : row + 1] = col_sum(sums[row])
            for copy in outs:
                copy.wait()

    stack = (MICRO, rows, width)
    plain = pltpu.VMEM((rows, width), BF16)
    full = pltpu.VMEM((rows, width), F32)
    chunks = pltpu.VMEM((steps, rows, CHUNK), BF16)
    return manual(
        kernel,
        info,
        [(array, False) for array in tokens]
        + [
            (kept["branch"], False),
            (kept["slope"], False),
            (kept["residual"], False),
            (kept["attended"], False),
            (vec, True),
            (wo_own, False),
            (wo_oth, False),
            (wu_own, False),
            (wu_oth, False),
            (wd_own, False),
            (wd_oth, False),
        ],
        [
            (stack, BF16, False, None if scaled else grads.get("branch")),
            ((MICRO, rows, hidden), BF16, False, grads.get("before")),
            (stack, BF16, False, grads.get("attended")),
            ((rows, width), BF16, False, None),
            ((rows, width), F32, False, None),
            ((8, width), F32, True, None),
            ((steps, CHUNK), F32, True, None),
        ],
        [
            plain,
            plain,
            chunks,
            full,
            plain,
            pltpu.VMEM((2, half, width), BF16),
            pltpu.VMEM((steps, width, CHUNK), BF16),
            pltpu.VMEM((steps, CHUNK, width), BF16),
            plain,
            pltpu.VMEM((rows, CHUNK), F32),
            pltpu.VMEM((rows, CHUNK), F32),
            pltpu.VMEM((rows, CHUNK), BF16),
            pltpu.VMEM((rows, CHUNK), BF16),
            plain,
            plain,
            full,
            full,
            pltpu.VMEM((6, 8, width), F32),
            dma_sems(2),
            dma_sems(5),
            dma_sems(steps),
            dma_sems(steps),
            dma_sems(steps),
            dma_sems(4),
            dma_sems(2),
        ],
        flops=4 * rows * width * hidden + 2 * rows * width * width,
        moved=4 * width * hidden + 2 * width * width + 8 * rows * hidden,
        after=after,
    )


def attend_backward(info, owner, number, grad_mixed, kept, after=()):
    _, rows, width = kept["q"].shape
    heads = width // HEAD_DIM
    lanes = 2 * HEAD_DIM
    block = 2 * lanes
    steps = width // block
    score_scale = HEAD_DIM**-0.5

    def kernel(s, *refs):
        @pl.when(s[ACTIVE + owner] == 1)
        def _():
            compute(*refs)

    def compute(gm, q_ref, kv, grown, full, inv, dq_out, here_out, there_out, *scratch):
        probs, scores = scratch[:4], scratch[4:8]
        own_v, centre_v = scratch[8:]
        first_q = lax.broadcasted_iota(jnp.int32, (rows, lanes), 1) < HEAD_DIM
        first_t = lax.broadcasted_iota(jnp.int32, (TILE, lanes), 1) < HEAD_DIM

        def columns(head):
            return slice(head // 2 * lanes, (head // 2 + 1) * lanes)

        for pair in range(2):
            place = columns(2 * pair)
            for t in tiles(rows):
                scaled = (gm[t, place].astype(F32) * inv[0, t, place]).astype(BF16)
                product = scaled.astype(F32) * full[0, t, place]
                for side in range(2):
                    mine = first_t if side == 0 else ~first_t
                    own_v[2 * pair + side, t] = jnp.where(mine, scaled, 0)
                    centre_v[2 * pair + side, t] = jnp.sum(
                        jnp.where(mine, product, 0.0), axis=-1, keepdims=True
                    )

        def prob(head):
            probs[head][...] = dot_nt(own_v[head], kv[0, 1, :, columns(head)])

        prob(0)
        grad_q, grad_k, grad_v = [], [], []
        for head in range(4):
            if head < 3:
                prob(head + 1)
            for t in tiles(rows):
                weight = grown[0, head, t].astype(F32)
                scores[head][t] = (weight * (probs[head][t] - centre_v[head, t])).astype(BF16)
            mine = first_q if head % 2 == 0 else ~first_q
            grad_v.append(dot_tn(grown[0, head], own_v[head]))
            grad_q.append(dot(scores[head][...], kv[0, 0, :, columns(head)]))
            masked = jnp.where(mine, q_ref[0, :, columns(head)], 0)
            grad_k.append(dot_tn(scores[head][...], masked))
            if head % 2 == 1:
                place = columns(head)
                dq = jnp.where(first_q, grad_q[head - 1], grad_q[head]) * score_scale
                dq_out[:, place] = dq.astype(BF16)
                dk = ((grad_k[head - 1] + grad_k[head]) * score_scale).astype(BF16)
                dv = (grad_v[head - 1] + grad_v[head]).astype(BF16)
                here_out[0, :, place] = dk[:rows]
                here_out[1, :, place] = dv[:rows]
                there_out[0, :, place] = dk[rows:]
                there_out[1, :, place] = dv[rows:]

    def on(s):
        return s[ACTIVE + owner]

    def slot(s):
        return jnp.where(on(s) == 1, number, SPARE)

    column = lambda i, s: (slot(s), 0, i * on(s))
    plain = lambda i, s: (0, i * on(s))
    return call(
        kernel,
        info,
        (steps,),
        [
            (grad_mixed, (rows, block), plain),
            (kept["q"], (1, rows, block), lambda i, s: (number, 0, i * on(s))),
            (kept["kv"], (1, 2, 2 * rows, block), lambda i, s: (slot(s), 0, 0, i * on(s))),
            (kept["grown"], (1, 4, rows, 2 * rows), lambda i, s: (slot(s), i * on(s), 0, 0)),
            (kept["mixed_full"], (1, rows, block), column),
            (kept["inverse"], (1, rows, block), column),
        ],
        [
            ((rows, width), BF16, (rows, block), plain, None),
            ((2, rows, width), BF16, (2, rows, block), lambda i, s: (0, 0, i * on(s)), None),
            ((2, rows, width), BF16, (2, rows, block), lambda i, s: (0, 0, i * on(s)), None),
        ],
        [pltpu.VMEM((rows, 2 * rows), F32)] * 4
        + [pltpu.VMEM((rows, 2 * rows), BF16)] * 4
        + [pltpu.VMEM((4, rows, lanes), BF16), pltpu.VMEM((4, rows, 1), F32)],
        flops=16 * rows * rows * width,
        moved=4 * heads * rows * rows + 30 * rows * width,
        after=after,
    )


def qkv_backward(info, owner, number, dq, dkv_here, dkv_there, w_own, w_oth, grad_res, vec, kept, grads, after=()):
    _, rows, width = kept["x"].shape
    half = width // 2

    def kernel(s, dq_ref, here, there, own, oth, gr, x_ref, v, packed_out, gx_out, relay_out,
               small_out, shift_out, a_v, b_v, p_v, w_v, gr_v, x_v, gx_v, acc, sums,
               a_sems, b_sems, w_sems, in_sems, packed_sems, out_sems):
        @pl.when(s[ACTIVE + owner] == 0)
        def _():
            small_out[...] = jnp.zeros_like(small_out)
            shift_out[...] = jnp.zeros_like(shift_out)

        @pl.when(s[ACTIVE + owner] == 1)
        def _():
            slot = number
            loads = []
            for part in range(6):
                kind, side = part % 3, part // 3
                columns = pl.ds(side * half, half)
                if kind == 0:
                    copies = [begin(dq_ref.at[:, columns], a_v.at[part], a_sems.at[part])]
                else:
                    turned = pl.ds((1 - side) * half, half)
                    copies = [
                        begin(here.at[kind - 1, :, columns], a_v.at[part], a_sems.at[part]),
                        begin(there.at[kind - 1, :, turned], b_v.at[part], b_sems.at[part]),
                    ]
                weight = own if side == 0 else oth
                copies.append(begin(weight.at[kind], w_v.at[part], w_sems.at[part]))
                loads.append(copies)
            last = [
                begin(x_ref.at[slot], x_v, in_sems.at[0]),
                begin(gr, gr_v, in_sems.at[1]),
            ]
            outs = []
            for part in range(6):
                for copy in loads[part]:
                    copy.wait()
                total = jnp.zeros((8, half), F32)
                for t in tiles(rows):
                    packed = a_v[part, t]
                    if part % 3 > 0:
                        packed = (packed.astype(F32) + b_v[part, t].astype(F32)).astype(BF16)
                    p_v[part, t] = packed
                    total = total + eights(packed.astype(F32))
                shift_out[part : part + 1] = col_sum(total)
                outs.append(
                    begin(
                        p_v.at[part],
                        packed_out.at[slot, :, pl.ds(part * half, half)],
                        packed_sems.at[part],
                    )
                )
                product = dot_nt(p_v[part], w_v[part])
                acc[...] = product if part == 0 else acc[...] + product
            for copy in last:
                copy.wait()
            sums[...] = jnp.zeros_like(sums)
            for t in tiles(rows):
                hat, scale = norm_stats(x_v[t].astype(F32))
                error = acc[t]
                grad = gr_v[t] + norm_backward(hat, scale, v[LN1G : LN1G + 1], error)
                gx_v[t] = grad.astype(BF16)
                sums[0] += eights(error * hat)
                sums[1] += eights(error)
            outs.append(begin(gx_v, relay_out, out_sems.at[0]))
            outs.append(begin(gx_v, gx_out.at[slot], out_sems.at[1]))
            small_out[...] = jnp.zeros_like(small_out)
            for row in range(2):
                small_out[row : row + 1] = col_sum(sums[row])
            for copy in outs:
                copy.wait()

    stack = (MICRO, rows, width)
    parts = pltpu.VMEM((6, rows, half), BF16)
    return manual(
        kernel,
        info,
        [
            (dq, False),
            (dkv_here, False),
            (dkv_there, False),
            (w_own, False),
            (w_oth, False),
            (grad_res, False),
            (kept["x"], False),
            (vec, True),
        ],
        [
            ((MICRO, rows, 3 * width), BF16, False, grads.get("packed")),
            (stack, BF16, False, grads.get("input")),
            ((rows, width), BF16, False, None),
            ((8, width), F32, True, None),
            ((8, half), F32, True, None),
        ],
        [
            parts,
            parts,
            parts,
            pltpu.VMEM((6, width, half), BF16),
            pltpu.VMEM((rows, width), F32),
            pltpu.VMEM((rows, width), BF16),
            pltpu.VMEM((rows, width), BF16),
            pltpu.VMEM((rows, width), F32),
            pltpu.VMEM((2, 8, width), F32),
            dma_sems(6),
            dma_sems(6),
            dma_sems(6),
            dma_sems(2),
            dma_sems(6),
            dma_sems(2),
        ],
        flops=6 * rows * width * width,
        moved=6 * width * width + 16 * rows * width,
        after=after,
    )


def swap(block):
    return lax.ppermute(block, "tensor", [(0, 1), (1, 0)])


def ring_order(count):
    return list(range(0, count, 2)) + list(range(count - 1, 0, -2))


def tied(value, *others):
    return lax.optimization_barrier((value, *others))[0]


class Ring:
    def __init__(self, info, parts, shapes, places):
        self.info, self.parts, self.shapes, self.places = info, parts, shapes, places
        self.count = lax.axis_size("dp")
        order = ring_order(self.count)
        n = self.count
        self.chunk = parts[0][0].shape[0] // (2 * n)
        self.widths = [pair[0].shape[1] for pair in parts]
        self.signs = (1, -1)
        self.routes = [[(order[i], order[(i + s) % n]) for i in range(n)] for s in self.signs]
        self.step = 0
        self.steps = 2 * (n - 1)
        self.totals = [None] * len(shapes)
        self.vmem = RING_MIB
        self.moving = self.add([0, 0], None)

    def unit(self, way, ahead):
        return UNITS + way * self.count + ahead % self.count

    def add(self, ahead, arrived, after=()):
        chunk, width, parts = self.chunk, sum(self.widths), len(self.parts)
        units = [self.unit(w, ahead[w]) for w in range(2)]
        terms = 2 if arrived is None else 3

        def kernel(s, *refs):
            halves = refs[: 2 * parts]
            refs = refs[2 * parts :]
            if terms == 3:
                arrivals, refs = refs[:2], refs[2:]
            outs, (held, sems) = refs[:2], refs[2:]
            copies = []
            for w in range(2):
                rows = pl.ds(pl.multiple_of(s[units[w]] * chunk, chunk), chunk)
                base = 0
                for number, columns in enumerate(self.widths):
                    for term in range(2):
                        copies.append(
                            begin(
                                halves[2 * number + term].at[rows],
                                held.at[w, term, :, pl.ds(base, columns)],
                                sems.at[w, term, number],
                            )
                        )
                    base += columns
                if terms == 3:
                    copies.append(begin(arrivals[w], held.at[w, 2], sems.at[w, 2, 0]))
            for copy in copies:
                copy.wait()
            for w in range(2):
                for t in tiles(chunk):
                    for first in range(0, width, 512):
                        c = slice(first, min(first + 512, width))
                        total = held[w, 0, t, c].astype(F32) + held[w, 1, t, c].astype(F32)
                        if terms == 3:
                            total = total + held[w, 2, t, c].astype(F32)
                        outs[w][t, c] = total.astype(BF16)

        arrays = [(term, False) for pair in self.parts for term in pair]
        if arrived is not None:
            arrays += [(block, False) for block in arrived]
        return manual(
            kernel,
            self.info,
            arrays,
            [((chunk, width), BF16, True, None)] * 2,
            [pltpu.VMEM((2, terms, chunk, width), BF16), pltpu.SemaphoreType.DMA((2, 3, parts))],
            moved=2 * (terms + 1) * 2 * chunk * width,
            vmem=self.vmem,
            after=after,
        )

    def put(self, ahead, blocks, after=()):
        chunk, width = self.chunk, sum(self.widths)
        units = [self.unit(w, pair[w]) for pair in ahead for w in range(2)]
        size = len(units)
        count = len(self.shapes)
        pieces = sum(len(self.places.columns(c)) for c in range(count))

        def kernel(s, *refs):
            sources, outs = refs[:size], refs[size : size + count]
            held, wide, in_sems, out_sems = refs[size + count + 2 :]
            loads = [begin(sources[w], held.at[w], in_sems.at[w]) for w in range(size)]
            copies = []
            for w in range(size):
                loads[w].wait()
                for t in tiles(chunk):
                    for first in range(0, width, 512):
                        c = slice(first, min(first + 512, width))
                        wide[w, t, c] = held[w, t, c].astype(F32)
                number = 0
                for target in range(count):
                    for first, columns in self.places.columns(target):
                        ref = self.places.ref(
                            outs[target], target, first, columns, s[units[w]], chunk
                        )
                        copies.append(
                            begin(
                                wide.at[w, :, pl.ds(first, columns)],
                                ref,
                                out_sems.at[w, number],
                            )
                        )
                        number += 1
            for copy in copies:
                copy.wait()

        results = manual(
            kernel,
            self.info,
            [(block, False) for block in blocks[:-2]] + [(block, False) for block in blocks[-2:]],
            [(shape, F32, False, old) for shape, old in zip(self.shapes, self.totals)]
            + [((chunk, width), BF16, False, None)] * 2,
            [
                pltpu.VMEM((size, chunk, width), BF16),
                pltpu.VMEM((size, chunk, width), F32),
                dma_sems(size),
                pltpu.SemaphoreType.DMA((size, pieces)),
            ],
            moved=2 * 6 * chunk * width,
            vmem=self.vmem,
            after=after,
            same={size - 2: count, size - 1: count + 1},
        )
        self.totals = list(results[:count])
        return list(results[count:])

    def advance(self, *after):
        arrived = [lax.ppermute(self.moving[w], "dp", self.routes[w]) for w in range(2)]
        if after:
            arrived = list(lax.optimization_barrier((*arrived, *after))[:2])
        step = self.step
        if step < self.count - 1:
            self.moving = self.add([-s * (step + 1) for s in self.signs], arrived)
        else:
            ahead = [[-s * (step - self.count + 1) for s in self.signs]]
            blocks = arrived
            if step == self.count - 1:
                ahead.insert(0, self.signs)
                blocks = list(self.moving) + arrived
            self.moving = self.put(ahead, blocks)
        self.step += 1

    def done(self):
        return self.step == self.steps

    def finish(self):
        while not self.done():
            self.advance()
        return self.totals


class MlpPlaces:
    def __init__(self, width, second, rows):
        self.width, self.second, self.rows = width, second, rows

    def columns(self, target):
        if target == 0:
            return [(0, self.width)]
        return [(self.width, self.second), (self.width + self.second, self.second)]

    def ref(self, out, target, first, columns, unit, chunk):
        base = self.rows if first > self.width else 0
        return out.at[pl.ds(pl.multiple_of(base + unit * chunk, chunk), chunk)]


class TailPlaces:
    def __init__(self, half, lanes):
        self.half, self.lanes = half, lanes

    def columns(self, target):
        half = self.half
        if target == 0:
            return [(j * half, half) for j in range(3)]
        return [(3 * half, half)] if target == 1 else [(4 * half, self.lanes)]

    def ref(self, out, target, first, columns, unit, chunk):
        rows = pl.ds(pl.multiple_of(unit * chunk, chunk), chunk)
        if target == 0:
            return out.at[first // self.half, rows]
        if target == 2:
            return out.at[rows]
        each = self.half // chunk
        return out.at[
            pl.ds(pl.multiple_of(lax.rem(unit, each) * chunk, chunk), chunk),
            pl.ds(pl.multiple_of(lax.div(unit, each) * self.half, self.half), self.half),
        ]


def partner_tokens(info, block, numbers):
    _, _, seq, half = block.shape
    rows = seq // 2

    def kernel(s, ref, out, sems):
        start = pl.multiple_of((1 - s[RANK]) * rows, rows)
        copies = [
            begin(ref.at[number, 0, pl.ds(start, rows)], out.at[place], sems.at[place])
            for place, number in enumerate(numbers)
        ]
        for copy in copies:
            copy.wait()

    return manual(
        kernel,
        info,
        [(block, False)],
        [((len(numbers), rows, half), BF16, True, None)],
        [dma_sems(len(numbers))],
        vmem=8,
    )[0]


def partner_features(info, block):
    micro, rows, width = block.shape
    half = width // 2

    def kernel(s, ref, out, sems):
        start = pl.multiple_of((1 - s[RANK]) * half, half)
        copies = [
            begin(ref.at[m, :, pl.ds(start, half)], out.at[m], sems.at[m]) for m in range(micro)
        ]
        for copy in copies:
            copy.wait()

    return manual(
        kernel,
        info,
        [(block, False)],
        [((micro, rows, half), BF16, True, None)],
        [dma_sems(micro)],
        vmem=8,
    )[0]


def join_tokens(info, block, received):
    micro, rows, width = block.shape
    half = width // 2

    def kernel(s, ref, other, out, sems):
        rank = s[RANK]
        features = pl.ds(pl.multiple_of(rank * half, half), half)
        here = pl.ds(pl.multiple_of(rank * rows, rows), rows)
        there = pl.ds(pl.multiple_of((1 - rank) * rows, rows), rows)
        copies = []
        for m in range(micro):
            copies.append(begin(ref.at[m, :, features], out.at[0, m, 0, here], sems.at[0, m]))
            copies.append(begin(other.at[m], out.at[0, m, 0, there], sems.at[1, m]))
        for copy in copies:
            copy.wait()

    return manual(
        kernel,
        info,
        [(block, False), (received, False)],
        [((1, micro, 1, 2 * rows, half), BF16, True, None)],
        [pltpu.SemaphoreType.DMA((2, micro))],
        vmem=8,
    )[0]


LANES = 128


def gather_vectors(info, sums, rows_out):
    calls = len(sums)
    width = sums[0][0].shape[1]
    half = width // 2

    def kernel(s, *refs):
        own, oth = refs[4 * calls :]
        low = s[RANK] == 0

        def total(kind):
            blocks = [refs[4 * c + kind][...] for c in range(calls)]
            return sum(blocks[1:], blocks[0])

        two, up, one, qkv = [total(kind) for kind in range(4)]
        own[...] = jnp.zeros_like(own)
        oth[...] = jnp.zeros_like(oth)
        place = 0

        def write(first, second):
            nonlocal place
            for c in range(0, half, LANES):
                own[place : place + 1] = first[:, c : c + LANES].astype(BF16)
                oth[place : place + 1] = second[:, c : c + LANES].astype(BF16)
                place += 1

        for block, count in ((one, 2), (two, 6)):
            for row in range(count):
                line = block[row : row + 1]
                left, right = line[:, :half], line[:, half:]
                write(jnp.where(low, left, right), jnp.where(low, right, left))
        for row in range(3):
            write(qkv[row : row + 1], qkv[3 + row : 4 + row])
        hidden_rows = up.shape[0] // 2
        for row in range(hidden_rows):
            write(up[row : row + 1], up[hidden_rows + row : hidden_rows + row + 1])

    vmem = pl.BlockSpec(memory_space=pltpu.VMEM)
    return pl.pallas_call(
        kernel,
        in_specs=[pl.BlockSpec(memory_space=pltpu.SMEM)] + [vmem] * (4 * calls),
        out_specs=[vmem] * 2,
        out_shape=[jax.ShapeDtypeStruct((rows_out, LANES), BF16)] * 2,
    )(info, *[block for group in sums for block in group])


def spread_vectors(sums, half, hidden_half):
    def kernel(ref, *outs):
        def line(number, out, row=0, columns=half, first=0):
            for c in range(0, columns, LANES):
                place = (number * half + c) // LANES
                out[row : row + 1, first + c : first + c + LANES] = ref[place : place + 1]

        for number in range(8):
            line(number, outs[number])
        line(8, outs[8])
        line(10, outs[8], row=1)
        line(11, outs[9], columns=hidden_half)

    vmem = pl.BlockSpec(memory_space=pltpu.VMEM)
    shapes = [(1, half)] * 8 + [(2, half), (1, hidden_half)]
    return pl.pallas_call(
        kernel,
        in_specs=[vmem],
        out_specs=[vmem] * 10,
        out_shape=[jax.ShapeDtypeStruct(shape, F32) for shape in shapes],
    )(sums)


def pack_vectors(blocks, hidden_bias):
    half = blocks[0].shape[1]
    hidden_rows = hidden_bias.shape[1] // half
    filled = sum(b.shape[0] for b in blocks)

    def kernel(*refs):
        out = refs[-1]
        place = 0
        for ref in refs[: len(blocks)]:
            for row in range(ref.shape[0]):
                out[place : place + 1] = ref[row : row + 1].astype(F32)
                place += 1
        for row in range(hidden_rows):
            columns = slice(row * half, (row + 1) * half)
            out[place : place + 1] = refs[len(blocks)][:, columns].astype(F32)
            place += 1

    return pl.pallas_call(
        kernel, out_shape=jax.ShapeDtypeStruct((filled + hidden_rows, half), F32)
    )(*blocks, hidden_bias)


def join_vectors(scalars, own, oth, hidden_rows):
    half = own.shape[1]

    def kernel(s, own_ref, oth_ref, vec, bias_q, bias_v, bias_up):
        low = s[RANK] == 0
        vec[:, :half] = jnp.where(low, own_ref[:8], oth_ref[:8])
        vec[:, half:] = jnp.where(low, oth_ref[:8], own_ref[:8])
        for row, out in ((8, bias_q), (9, bias_v)):
            out[:, :half] = own_ref[row : row + 1]
            out[:, half:] = oth_ref[row : row + 1]
        bias_up[:hidden_rows] = own_ref[10 : 10 + hidden_rows]
        bias_up[hidden_rows:] = oth_ref[10 : 10 + hidden_rows]

    vmem = pl.BlockSpec(memory_space=pltpu.VMEM)
    return pl.pallas_call(
        kernel,
        in_specs=[pl.BlockSpec(memory_space=pltpu.SMEM), vmem, vmem],
        out_specs=[vmem] * 4,
        out_shape=[
            jax.ShapeDtypeStruct((8, 2 * half), F32),
            jax.ShapeDtypeStruct((1, 2 * half), F32),
            jax.ShapeDtypeStruct((1, 2 * half), F32),
            jax.ShapeDtypeStruct((2 * hidden_rows, half), F32),
        ],
    )(scalars, own, oth)


def shards(
    inputs,
    cotangent,
    ln1_gain,
    ln1_bias,
    qkv_weight,
    qv_bias,
    out_weight,
    out_bias,
    scale_attn,
    ln2_gain,
    ln2_bias,
    fc1_weight,
    fc1_bias,
    fc2_weight,
    fc2_bias,
    scale_mlp,
):
    micro, images, seq_len, half = inputs.shape
    assert micro == MICRO and images == 1
    width = 2 * half
    hidden_half = fc1_weight.shape[2]

    count = lax.axis_size("dp")
    order = ring_order(count)
    table = [
        [rank, int(section == 0), int(section == 1)]
        + [way * count + (order.index(i) + ahead) % count for way in range(2) for ahead in range(count)]
        for section in range(2)
        for rank in range(2)
        for i in range(count)
    ]
    info = lax.dynamic_slice(
        jnp.asarray(table, jnp.int32),
        (lax.axis_index(("section", "tensor", "dp")), 0),
        (1, len(table[0])),
        allow_negative_indices=False,
    ).reshape(-1)

    first_oth = swap(partner_tokens(info, inputs, (0,))[0])
    vectors = pack_vectors(
        [
            ln1_gain, ln1_bias, out_bias, scale_attn, ln2_gain, ln2_bias, fc2_bias, scale_mlp,
            qv_bias[0],
        ],
        fc1_bias,
    )
    vectors_oth = swap(vectors)
    wq_own = jnp.transpose(qkv_weight[0], (1, 0, 2))
    wq_oth = swap(tied(wq_own, vectors))
    vec, bias_q, bias_v, b_up = join_vectors(info, vectors, vectors_oth, hidden_half // half)
    b_up = b_up.reshape(2 * hidden_half // CHUNK, CHUNK)
    wo_own, wu_own, wd_own = out_weight[0], fc1_weight[0], fc2_weight[0]
    wo_oth = swap(tied(wo_own, first_oth, vectors_oth))
    wu_oth = swap(tied(wu_own, first_oth, vectors_oth))
    wd_oth = swap(tied(wd_own, first_oth, vectors_oth))
    second_oth = swap(partner_tokens(info, tied(inputs, wd_oth), (1,))[0])
    cot_oth = swap(partner_tokens(info, tied(cotangent, wd_oth), (0, 1)))

    kept = {}

    def forward(owner, number, source, tokens, after=(), late=()):
        kept["x"], kept["normed1"], kv_here = norm_kv(
            info, owner, number, source, tokens, vec, wq_own, wq_oth, bias_v, kept, after
        )
        kv_there = swap(kv_here)
        kept["q"] = project_q(info, owner, number, kept["normed1"], wq_own, wq_oth, bias_q, kept)
        kept["grown"], kept["mixed_full"], mixed, kept["inverse"], kept["kv"] = attend(
            info, owner, number, kept["q"], kv_here, kv_there, kept
        )
        (
            kept["attended"],
            kept["residual"],
            kept["normed2"],
            kept["active"],
            kept["slope"],
            kept["branch"],
            kept["output"],
            relayed,
            kept["mixed"],
        ) = mlp_forward(
            info, owner, number, mixed, kept["x"], vec, wo_own, wo_oth, wu_own, wu_oth, wd_own,
            wd_oth, b_up, kept, late,
        )
        return relayed

    grads = {}
    sums = []

    def backward_mlp(owner, number, source, tokens, after, scaled=False):
        (
            branch,
            grads["before"],
            grads["attended"],
            grad_mixed,
            grad_res,
            small,
            shift,
        ) = mlp_backward(
            info, owner, number, source, tokens, vec, wo_own, wo_oth, wu_own, wu_oth, wd_own,
            wd_oth, kept, grads, scaled, after,
        )
        if not scaled:
            grads["branch"] = branch
        return grad_mixed, grad_res, small, shift

    def backward_attention(owner, number, grad_mixed, after=()):
        dq, dkv_here, dkv_send = attend_backward(info, owner, number, grad_mixed, kept, after)
        return dq, dkv_here, swap(dkv_send)

    def backward_qkv(owner, number, dq, dkv_here, dkv_there, grad_res, small, shift, after=()):
        grads["packed"], grads["input"], relayed, small_one, shift_qkv = qkv_backward(
            info, owner, number, dq, dkv_here, dkv_there, wq_own, wq_oth, grad_res, vec, kept,
            grads, after,
        )
        sums.append((small, shift, small_one, shift_qkv))
        return relayed

    def backward(owner, number, source, tokens, after):
        grad_mixed, grad_res, small, shift = backward_mlp(owner, number, source, tokens, after)
        flows = backward_attention(owner, number, grad_mixed)
        return backward_qkv(owner, number, *flows, grad_res, small, shift)

    relayed = forward(0, 0, "argument", (inputs, first_oth))
    first = lax.ppermute(relayed, "section", [(0, 1)])
    relayed = forward(0, 1, "argument", (inputs, second_oth), [relayed])
    second = lax.ppermute(relayed, "section", [(0, 1)])
    relayed = forward(1, 0, "relay", (first,), [relayed])
    relayed = backward(1, 0, "argument", (cotangent, cot_oth[0]), [relayed, second])
    first = lax.ppermute(relayed, "section", [(1, 0)])
    relayed = forward(1, 1, "relay", (second,), [relayed], [first])
    relayed = backward(1, 1, "argument", (cotangent, cot_oth[1]), [relayed])
    second = lax.ppermute(relayed, "section", [(1, 0)])
    relayed = backward(0, 0, "relay", (first,), [relayed])

    def weight_grad(left, right):
        return lax.dot_general(
            left, right, (((0, 1), (0, 1)), ((), ())), preferred_element_type=F32
        ).astype(BF16)

    grads["branch"] = scale_branch(info, 0, 1, second, vec, grads["branch"], [relayed])
    active, g_branch = kept["active"], grads["branch"]
    split = hidden_half // 2
    assert split == width

    def down_grad(start):
        return weight_grad(active[:, :, start : start + split], g_branch)

    down = []
    for start in (0, split):
        sent = swap(down_grad(hidden_half + start))
        down.append((down_grad(start), sent))
    grad_mixed, grad_res, small, shift = backward_mlp(
        0, 1, "relay", (second,), [pair[0] for pair in down], scaled=True
    )
    normed2, before = kept["normed2"], grads["before"]
    up_sent = swap(weight_grad(normed2, before[:, :, hidden_half:]))
    up_own = weight_grad(normed2, before[:, :, :hidden_half])
    ring_mlp = Ring(
        info,
        [(up_own, up_sent), *down],
        [up_own.shape, (hidden_half, width)],
        MlpPlaces(hidden_half, width, split),
    )
    flows = backward_attention(0, 1, grad_mixed, list(ring_mlp.moving))
    ring_mlp.advance(flows[0])
    grad_res = tied(grad_res, *ring_mlp.moving)
    backward_qkv(0, 1, *flows, grad_res, small, shift)
    packed = grads["packed"]
    ring_mlp.advance(packed)
    normed1 = tied(kept["normed1"], *ring_mlp.moving)
    vectors = gather_vectors(info, sums, width)

    def tail(index):
        columns = packed[:, :, index * 3 * half : (index + 1) * 3 * half]
        mixed = kept["mixed"][:, :, index * half : (index + 1) * half]
        g_att = grads["attended"]
        outs = [weight_grad(mixed, g_att[:, :, half * j : half * (j + 1)]) for j in range(2)]
        return [weight_grad(normed1, columns), jnp.concatenate(outs, axis=0), vectors[index]]

    tail_oth = tail(1)
    tail_sent = [swap(block) for block in tail_oth]
    tail_own = tail(0)
    ring_mlp.advance(tail_own[0])
    ring_tail = Ring(
        info,
        list(zip(tail_own, tail_sent)),
        [(3, width, half), (half, width), (width, LANES)],
        TailPlaces(half, LANES),
    )
    rings = [ring_mlp, ring_tail]
    for ring in rings:
        ring.vmem = 16
    before_it = ring_tail
    while not all(ring.done() for ring in rings):
        for ring in rings:
            if not ring.done():
                ring.advance(*before_it.moving)
                before_it = ring
    total_up, total_down = ring_mlp.finish()
    total_qkv, total_out, total_vectors = ring_tail.finish()
    block_outputs = join_tokens(info, kept["output"], swap(partner_features(info, kept["output"])))
    input_grads = join_tokens(info, grads["input"], swap(partner_features(info, grads["input"])))
    rows = spread_vectors(total_vectors, half, hidden_half)
    return (
        block_outputs,
        input_grads,
        rows[0],
        rows[1],
        jnp.transpose(total_qkv, (1, 0, 2))[None],
        rows[8][None],
        total_out[None],
        rows[7],
        rows[6],
        rows[4],
        rows[5],
        total_up[None],
        rows[9],
        total_down[None],
        rows[3],
        rows[2],
    )


def solution(mesh):
    placed = (
        P(None, "dp", None, "tensor"),
        P(None, "dp", None, "tensor"),
        P("section", "tensor"),
        P("section", "tensor"),
        P("section", None, None, "tensor"),
        P("section", None, "tensor"),
        P("section", "tensor", None),
        P("section", "tensor"),
        P("section", "tensor"),
        P("section", "tensor"),
        P("section", "tensor"),
        P("section", None, "tensor"),
        P("section", "tensor"),
        P("section", "tensor", None),
        P("section", "tensor"),
        P("section", "tensor"),
    )
    return jax.shard_map(
        shards,
        mesh=mesh,
        in_specs=placed,
        out_specs=(
            P("section", None, "dp", None, "tensor"),
            P("section", None, "dp", None, "tensor"),
            P("section", "tensor"),
            P("section", "tensor"),
            P("section", None, None, "tensor"),
            P("section", None, "tensor"),
            P("section", "tensor", None),
            P("section", "tensor"),
            P("section", "tensor"),
            P("section", "tensor"),
            P("section", "tensor"),
            P("section", None, "tensor"),
            P("section", "tensor"),
            P("section", "tensor", None),
            P("section", "tensor"),
            P("section", "tensor"),
        ),
        check_vma=False,
    )
```

```python
import math

import jax
import jax.numpy as jnp
from jax import lax
from jax.experimental import pallas as pl
from jax.experimental.pallas import tpu as pltpu
from jax.sharding import PartitionSpec as P

HEAD_DIM = 64
EPSILON = 1e-06
F32 = jnp.float32
BF16 = jnp.bfloat16
MIB = 1 << 20
VMEM_MIB = 62
RING_MIB = 61
TILE = 16
MICRO = 2
SPARE = MICRO
RANK, ACTIVE, UNITS = 0, 1, 3
LN1G, LN1B, OUTB, SATT, LN2G, LN2B, FC2B, SMLP = range(8)


def dot(left, right):
    return jnp.dot(left, right, preferred_element_type=F32)


def dot_nt(left, right):
    return lax.dot_general(left, right, (((1,), (1,)), ((), ())), preferred_element_type=F32)


def dot_tn(left, right):
    return lax.dot_general(left, right, (((0,), (0,)), ((), ())), preferred_element_type=F32)


def norm_stats(values):
    centre = jnp.mean(values, axis=-1, keepdims=True)
    centred = values - centre
    spread = jnp.mean(centred * centred, axis=-1, keepdims=True)
    scale = lax.rsqrt(spread + EPSILON)
    return centred * scale, scale


def tiles(rows):
    return [slice(r, r + TILE) for r in range(0, rows, TILE)]


def eights(values):
    total = values[:8]
    for r in range(8, values.shape[0], 8):
        total = total + values[r : r + 8]
    return total


def norm_backward(hat, scale, gain, error):
    weighted = error * gain
    mean_one = jnp.mean(weighted, axis=-1, keepdims=True)
    mean_two = jnp.mean(weighted * hat, axis=-1, keepdims=True)
    return scale * (weighted - mean_one - hat * mean_two)


def col_sum(values):
    return jnp.sum(values, axis=0, keepdims=True)


def call(kernel, scalars, grid, ins, outs, scratch=(), flops=0, moved=0, after=()):
    arrays = [a for a, _, _ in ins]
    in_specs = [pl.BlockSpec(b, m) for _, b, m in ins]
    aliases = {}
    for number, out in enumerate(outs):
        if out[4] is not None:
            aliases[1 + len(arrays)] = number
            arrays.append(out[4])
            in_specs.append(pl.BlockSpec(memory_space=pl.ANY))
    arrays += after
    in_specs += [pl.BlockSpec(memory_space=pl.ANY)] * len(after)
    extra = len(aliases) + len(after)
    in_count = len(ins)

    def body(*refs):
        kernel(*refs[: 1 + in_count], *refs[1 + in_count + extra :])

    return pl.pallas_call(
        body,
        out_shape=[jax.ShapeDtypeStruct(s, d) for s, d, _, _, _ in outs],
        grid_spec=pltpu.PrefetchScalarGridSpec(
            num_scalar_prefetch=1,
            grid=grid,
            in_specs=in_specs,
            out_specs=[pl.BlockSpec(b, m) for _, _, b, m, _ in outs],
            scratch_shapes=list(scratch),
        ),
        input_output_aliases=aliases,
        compiler_params=pltpu.CompilerParams(
            dimension_semantics=("arbitrary",) * len(grid), vmem_limit_bytes=VMEM_MIB * MIB
        ),
        cost_estimate=pl.CostEstimate(
            flops=int(flops), bytes_accessed=int(moved), transcendentals=0
        ),
    )(scalars, *arrays)


def manual(kernel, scalars, ins, outs, scratch, flops=0, moved=0, vmem=VMEM_MIB, after=(), same=None):
    any_space = pl.BlockSpec(memory_space=pl.ANY)
    vmem_space = pl.BlockSpec(memory_space=pltpu.VMEM)
    arrays = [a for a, _ in ins]
    in_specs = [vmem_space if inside else any_space for _, inside in ins]
    aliases = {1 + i: o for i, o in (same or {}).items()}
    before = len(arrays)
    for number, out in enumerate(outs):
        if out[3] is not None:
            aliases[1 + len(arrays)] = number
            arrays.append(out[3])
            in_specs.append(any_space)
    arrays += after
    in_specs += [any_space] * len(after)
    extra = len(arrays) - before
    in_count = len(ins)

    def body(*refs):
        kernel(*refs[: 1 + in_count], *refs[1 + in_count + extra :])

    return pl.pallas_call(
        body,
        out_shape=[jax.ShapeDtypeStruct(s, d) for s, d, _, _ in outs],
        in_specs=[pl.BlockSpec(memory_space=pltpu.SMEM)] + in_specs,
        out_specs=[vmem_space if inside else any_space for _, _, inside, _ in outs],
        scratch_shapes=list(scratch),
        input_output_aliases=aliases,
        compiler_params=pltpu.CompilerParams(vmem_limit_bytes=vmem * MIB),
        cost_estimate=pl.CostEstimate(
            flops=int(flops), bytes_accessed=int(moved), transcendentals=0
        ),
    )(scalars, *arrays)


def begin(src, dst, sem):
    copy = pltpu.make_async_copy(src, dst, sem)
    copy.start()
    return copy


def dma_sems(count):
    return pltpu.SemaphoreType.DMA((count,))


def whole2(i, s):
    return (0, 0)


def slot3(i, s):
    return (s[0], 0, 0)


def token_copies(s, source, number, refs, target, sems):
    rows, width = target.shape
    half = width // 2
    rank = s[RANK]
    if source == "relay":
        return [begin(refs[0], target, sems.at[0])]
    first = pl.multiple_of(rank * half, half)
    second = pl.multiple_of((1 - rank) * half, half)
    whole, other = refs
    return [
        begin(
            whole.at[number, 0, pl.ds(pl.multiple_of(rank * rows, rows), rows)],
            target.at[:, pl.ds(first, half)],
            sems.at[0],
        ),
        begin(other, target.at[:, pl.ds(second, half)], sems.at[1]),
    ]


def norm_kv(info, owner, number, source, tokens, vec, w_own, w_oth, bias_v, kept, after=()):
    rows, width = tokens[-1].shape[0], vec.shape[1]
    half = width // 2
    count = len(tokens)

    def kernel(s, *refs):
        token_refs = refs[:count]
        (v, own, oth, bv, x_out, n_out, kv_out, x_v, n_v, w_v, kv_v, tok_sems, w_sems,
         out_sems) = refs[count:]

        @pl.when(s[ACTIVE + owner] == 1)
        def _():
            arriving = token_copies(s, source, number, token_refs, x_v, tok_sems)
            loads = []
            for part in range(4):
                ref = own if part < 2 else oth
                loads.append(begin(ref.at[1 + part % 2], w_v.at[part], w_sems.at[part]))
            for copy in arriving:
                copy.wait()
            outs = [begin(x_v, x_out.at[number], out_sems.at[0])]
            for t in tiles(rows):
                hat, _ = norm_stats(x_v[t].astype(F32))
                n_v[t] = (hat * v[LN1G : LN1G + 1] + v[LN1B : LN1B + 1]).astype(BF16)
            outs.append(begin(n_v, n_out.at[number], out_sems.at[1]))
            for part in range(4):
                loads[part].wait()
                result = dot(n_v[...], w_v[part])
                kind, side = part % 2, part // 2
                columns = slice(side * half, (side + 1) * half)
                if kind == 1:
                    result = result + bv[:, columns]
                kv_v[part] = result.astype(BF16)
                outs.append(
                    begin(
                        kv_v.at[part],
                        kv_out.at[kind, :, pl.ds(side * half, half)],
                        out_sems.at[2 + part],
                    )
                )
            for copy in outs:
                copy.wait()

    stack = (MICRO, rows, width)
    return manual(
        kernel,
        info,
        [(array, False) for array in tokens]
        + [(vec, True), (w_own, False), (w_oth, False), (bias_v, True)],
        [
            (stack, BF16, False, kept.get("x")),
            (stack, BF16, False, kept.get("normed1")),
            ((2, rows, width), BF16, False, None),
        ],
        [
            pltpu.VMEM((rows, width), BF16),
            pltpu.VMEM((rows, width), BF16),
            pltpu.VMEM((4, width, half), BF16),
            pltpu.VMEM((4, rows, half), BF16),
            dma_sems(2),
            dma_sems(4),
            dma_sems(6),
        ],
        flops=2 * rows * width * 2 * width,
        moved=4 * width * width + 10 * rows * width,
        after=after,
    )


def project_q(info, owner, number, normed, w_own, w_oth, bias_q, kept):
    _, rows, width = normed.shape
    half = width // 2

    def kernel(s, n, own, oth, bq, q_out, n_v, w_v, q_v, in_sems, out_sems):
        @pl.when(s[ACTIVE + owner] == 1)
        def _():
            load = begin(n.at[number], n_v, in_sems.at[0])
            loads = [
                begin(own.at[0], w_v.at[0], in_sems.at[1]),
                begin(oth.at[0], w_v.at[1], in_sems.at[2]),
            ]
            load.wait()
            outs = []
            for side in range(2):
                loads[side].wait()
                columns = slice(side * half, (side + 1) * half)
                q_v[side] = (dot(n_v[...], w_v[side]) + bq[:, columns]).astype(BF16)
                outs.append(
                    begin(
                        q_v.at[side],
                        q_out.at[number, :, pl.ds(side * half, half)],
                        out_sems.at[side],
                    )
                )
            for copy in outs:
                copy.wait()

    return manual(
        kernel,
        info,
        [(normed, False), (w_own, False), (w_oth, False), (bias_q, True)],
        [((MICRO, rows, width), BF16, False, kept.get("q"))],
        [
            pltpu.VMEM((rows, width), BF16),
            pltpu.VMEM((2, width, half), BF16),
            pltpu.VMEM((2, rows, half), BF16),
            dma_sems(3),
            dma_sems(2),
        ],
        flops=2 * rows * width * width,
        moved=2 * width * width + 4 * rows * width,
    )[0]


def attend(info, owner, number, q, kv_here, kv_there, kept):
    _, rows, width = q.shape
    heads = width // HEAD_DIM
    factor = HEAD_DIM**-0.5 * math.log2(math.e)
    lanes = 2 * HEAD_DIM
    block = 2 * lanes
    steps = width // block

    def kernel(s, *refs):
        @pl.when(s[ACTIVE + owner] == 1)
        def _():
            compute(*refs)

    def compute(q_ref, here, there, e_out, o_out, mixed_out, inv_out, kv_out, *scratch):
        scores, results = scratch[:4], scratch[4:]
        kv_out[0, :, :rows] = here[...]
        kv_out[0, :, rows:] = there[...]
        first_q = lax.broadcasted_iota(jnp.int32, (rows, lanes), 1) < HEAD_DIM
        first_k = lax.broadcasted_iota(jnp.int32, (2 * rows, lanes), 1) < HEAD_DIM
        first_t = lax.broadcasted_iota(jnp.int32, (TILE, lanes), 1) < HEAD_DIM

        def columns(head):
            return slice(head // 2 * lanes, (head // 2 + 1) * lanes)

        def score(head):
            mine = first_q if head % 2 == 0 else ~first_q
            masked = jnp.where(mine, q_ref[0, :, columns(head)], 0)
            scores[head][...] = dot_nt(masked, kv_out[0, 0, :, columns(head)])

        score(0)
        for head in range(4):
            if head < 3:
                score(head + 1)
            for t in tiles(rows):
                tile = scores[head][t]
                top = jnp.max(tile, axis=-1, keepdims=True)
                e_out[0, head, t] = jnp.exp2((tile - top) * factor).astype(BF16)
            mine = first_k if head % 2 == 0 else ~first_k
            values = jnp.where(mine, kv_out[0, 1, :, columns(head)], 1)
            results[head][...] = dot(e_out[0, head], values)
        for pair in range(2):
            place = slice(pair * lanes, (pair + 1) * lanes)
            for t in tiles(rows):
                one, two = results[2 * pair][t], results[2 * pair + 1][t]
                total = jnp.where(
                    first_t, pltpu.roll(one, HEAD_DIM, 1), pltpu.roll(two, HEAD_DIM, 1)
                )
                inverse = 1.0 / total
                mixed = jnp.where(first_t, one, two) * inverse
                o_out[0, t, place] = mixed
                mixed_out[t, place] = mixed.astype(BF16)
                inv_out[0, t, place] = inverse

    def on(s):
        return s[ACTIVE + owner]

    def slot(s):
        return jnp.where(on(s) == 1, number, SPARE)

    column = lambda i, s: (slot(s), 0, i * on(s))
    spare = MICRO + 1
    return call(
        kernel,
        info,
        (steps,),
        [
            (q, (1, rows, block), lambda i, s: (number, 0, i * on(s))),
            (kv_here, (2, rows, block), lambda i, s: (0, 0, i * on(s))),
            (
                kv_there,
                (2, rows, block),
                lambda i, s: (0, 0, lax.rem(i + steps // 2, steps) * on(s)),
            ),
        ],
        [
            (
                (spare, heads, rows, 2 * rows),
                BF16,
                (1, 4, rows, 2 * rows),
                lambda i, s: (slot(s), i * on(s), 0, 0),
                kept.get("grown"),
            ),
            ((spare, rows, width), F32, (1, rows, block), column, kept.get("mixed_full")),
            ((rows, width), BF16, (rows, block), lambda i, s: (0, i * on(s)), None),
            ((spare, rows, width), F32, (1, rows, block), column, kept.get("inverse")),
            (
                (spare, 2, 2 * rows, width),
                BF16,
                (1, 2, 2 * rows, block),
                lambda i, s: (slot(s), 0, 0, i * on(s)),
                kept.get("kv"),
            ),
        ],
        [pltpu.VMEM((rows, 2 * rows), F32)] * 4 + [pltpu.VMEM((rows, lanes), F32)] * 4,
        flops=8 * rows * rows * width,
        moved=4 * heads * rows * rows + 30 * rows * width,
    )


def gelu_parts(x):
    size = jnp.abs(x)
    base = 1.0 + (0.3275911 * math.sqrt(0.5)) * size
    t = pl.reciprocal(base, approx=True)
    t = t * (2.0 - base * t)
    grown = jnp.exp2(x * x * (-0.5 * math.log2(math.e)))
    poly = 0.5 * 1.061405429
    for factor in (-1.453152027, 1.421413741, -0.284496736, 0.254829592):
        poly = poly * t + 0.5 * factor
    tail = poly * t * grown
    below = jnp.where(x < 0.0, tail, 1.0 - tail)
    return x * below, below + x * grown * (1.0 / math.sqrt(2.0 * math.pi))


CHUNK = 512


def mlp_forward(info, owner, number, mixed, x, vec, wo_own, wo_oth, wu_own, wu_oth, wd_own, wd_oth, b_up, kept, after=()):
    _, rows, width = x.shape
    side_hidden = wu_own.shape[1]
    hidden = 2 * side_hidden
    half = width // 2
    steps = hidden // CHUNK
    split = steps // 2

    def kernel(
        s, m, x_ref, v, woo, wot, wuo, wut, wdo, wdt, bu,
        att_out, res_out, n_out, act_out, slope_out, branch_out, y_out, relay_out, m_out,
        m_v, x_v, wo_v, wu_v, wd_v, att_v, res_v, n_v, h_v, act_v, slope_v, branch_v, y_v, acc,
        in_sems, wu_sems, wd_sems, out_sems, act_sems, slope_sems,
    ):
        @pl.when(s[ACTIVE + owner] == 1)
        def _():
            slot = number
            first = [
                begin(m, m_v, in_sems.at[0]),
                begin(woo, wo_v.at[0], in_sems.at[1]),
                begin(wot, wo_v.at[1], in_sems.at[2]),
                begin(x_ref.at[slot], x_v, in_sems.at[3]),
            ]
            ups, downs = [], []

            def prefetch(i):
                if i < steps:
                    part = pl.ds((i % split) * CHUNK, CHUNK)
                    up, down = (wuo, wdo) if i < split else (wut, wdt)
                    ups.append(begin(up.at[:, part], wu_v.at[i], wu_sems.at[i]))
                    downs.append(begin(down.at[part], wd_v.at[i], wd_sems.at[i]))

            prefetch(0)
            prefetch(1)
            for copy in first:
                copy.wait()
            acc[...] = dot(m_v[:, :half], wo_v[0]) + dot(m_v[:, half:], wo_v[1])
            for t in tiles(rows):
                attended = acc[t] + v[OUTB : OUTB + 1]
                att_v[t] = attended.astype(BF16)
                residual = x_v[t].astype(F32) + v[SATT : SATT + 1] * attended
                res_v[t] = residual
                hat, _ = norm_stats(residual)
                n_v[t] = (hat * v[LN2G : LN2G + 1] + v[LN2B : LN2B + 1]).astype(BF16)
            outs = [
                begin(att_v, att_out.at[slot], out_sems.at[0]),
                begin(res_v, res_out.at[slot], out_sems.at[1]),
                begin(n_v, n_out.at[slot], out_sems.at[2]),
                begin(m_v, m_out.at[slot], out_sems.at[6]),
            ]

            def up_product(i):
                ups[i].wait()
                h_v[i % 2] = dot(n_v[...], wu_v[i])

            def down_product(i):
                downs[i].wait()
                part = pl.ds(i * CHUNK, CHUNK)
                outs.append(begin(act_v.at[i], act_out.at[slot, :, part], act_sems.at[i]))
                outs.append(begin(slope_v.at[i], slope_out.at[slot, :, part], slope_sems.at[i]))
                product = dot(act_v[i], wd_v[i])
                acc[...] = product if i == 0 else acc[...] + product

            up_product(0)
            for i in range(steps):
                prefetch(i + 2)
                if i > 0:
                    down_product(i - 1)
                if i + 1 < steps:
                    up_product(i + 1)
                for t in tiles(rows):
                    active, slope = gelu_parts(h_v[i % 2, t] + bu[i : i + 1])
                    act_v[i, t] = active.astype(BF16)
                    slope_v[i, t] = slope.astype(BF16)
            down_product(steps - 1)
            for t in tiles(rows):
                branch = acc[t] + v[FC2B : FC2B + 1]
                y_v[t] = (res_v[t] + v[SMLP : SMLP + 1] * branch).astype(BF16)
                branch_v[t] = branch.astype(BF16)
            outs.append(begin(y_v, relay_out, out_sems.at[3]))
            outs.append(begin(y_v, y_out.at[slot], out_sems.at[4]))
            outs.append(begin(branch_v, branch_out.at[slot], out_sems.at[5]))
            for copy in outs:
                copy.wait()

    stack = (MICRO, rows, width)
    tall = (MICRO, rows, hidden)
    plain = pltpu.VMEM((rows, width), BF16)
    full = pltpu.VMEM((rows, width), F32)
    chunks = pltpu.VMEM((steps, rows, CHUNK), BF16)
    return manual(
        kernel,
        info,
        [
            (mixed, False),
            (x, False),
            (vec, True),
            (wo_own, False),
            (wo_oth, False),
            (wu_own, False),
            (wu_oth, False),
            (wd_own, False),
            (wd_oth, False),
            (b_up, True),
        ],
        [
            (stack, BF16, False, kept.get("attended")),
            (stack, F32, False, kept.get("residual")),
            (stack, BF16, False, kept.get("normed2")),
            (tall, BF16, False, kept.get("active")),
            (tall, BF16, False, kept.get("slope")),
            (stack, BF16, False, kept.get("branch")),
            (stack, BF16, False, kept.get("output")),
            ((rows, width), BF16, False, None),
            (stack, BF16, False, kept.get("mixed")),
        ],
        [
            plain,
            plain,
            pltpu.VMEM((2, half, width), BF16),
            pltpu.VMEM((steps, width, CHUNK), BF16),
            pltpu.VMEM((steps, CHUNK, width), BF16),
            plain,
            full,
            plain,
            pltpu.VMEM((2, rows, CHUNK), F32),
            chunks,
            chunks,
            plain,
            plain,
            full,
            dma_sems(4),
            dma_sems(steps),
            dma_sems(steps),
            dma_sems(7),
            dma_sems(steps),
            dma_sems(steps),
        ],
        flops=4 * rows * width * hidden + 2 * rows * width * width,
        moved=4 * width * hidden + 2 * width * width + 8 * rows * hidden,
        after=after,
    )


def scale_branch(info, owner, number, relay, vec, earlier, after=()):
    rows, width = relay.shape

    def kernel(s, g, v, gb_out, g_v, gb_v, sems):
        @pl.when(s[ACTIVE + owner] == 1)
        def _():
            begin(g, g_v, sems.at[0]).wait()
            gb_v[...] = (v[SMLP : SMLP + 1] * g_v[...].astype(F32)).astype(BF16)
            begin(gb_v, gb_out.at[number], sems.at[1]).wait()

    return manual(
        kernel,
        info,
        [(relay, False), (vec, True)],
        [((MICRO, rows, width), BF16, False, earlier)],
        [pltpu.VMEM((rows, width), BF16), pltpu.VMEM((rows, width), BF16), dma_sems(2)],
        moved=4 * rows * width,
        after=after,
    )[0]


def mlp_backward(info, owner, number, source, tokens, vec, wo_own, wo_oth, wu_own, wu_oth, wd_own, wd_oth, kept, grads, scaled, after):
    count = len(tokens)
    _, rows, width = kept["x"].shape
    side_hidden = wu_own.shape[1]
    hidden = 2 * side_hidden
    half = width // 2
    steps = hidden // CHUNK
    split = steps // 2

    def kernel(s, *refs):
        work(s, refs[:count], *refs[count:])

    def work(
        s, token_refs, branch, slope, res, att, v, woo, wot, wuo, wut, wdo, wdt,
        gb_out, before_out, ga_out, gm_out, gr_out, small_out, shift_out,
        g_v, branch_v, slope_v, res_v, att_v, wo_v, wu_v, wd_v, gb_v, d_v, before_v, ga_v, gm_v,
        gr_v, acc, sums, tok_sems, in_sems, slope_sems, wu_sems, wd_sems, out_sems, before_sems,
    ):
        @pl.when(s[ACTIVE + owner] == 0)
        def _():
            small_out[...] = jnp.zeros_like(small_out)
            shift_out[...] = jnp.zeros_like(shift_out)

        @pl.when(s[ACTIVE + owner] == 1)
        def _():
            slot = number
            arriving = token_copies(s, source, number, token_refs, g_v, tok_sems)
            ups, downs, slopes = [], [], []

            def prefetch(i):
                if i < steps:
                    part = pl.ds((i % split) * CHUNK, CHUNK)
                    up, down = (wuo, wdo) if i < split else (wut, wdt)
                    here = pl.ds(i * CHUNK, CHUNK)
                    downs.append(begin(down.at[part], wd_v.at[i], wd_sems.at[i]))
                    slopes.append(begin(slope.at[slot, :, here], slope_v.at[i], slope_sems.at[i]))
                    ups.append(begin(up.at[:, part], wu_v.at[i], wu_sems.at[i]))

            prefetch(0)
            branch_in = begin(branch.at[slot], branch_v, in_sems.at[0])
            prefetch(1)
            last = []
            for copy in arriving:
                copy.wait()
            for t in tiles(rows):
                gb_v[t] = (v[SMLP : SMLP + 1] * g_v[t].astype(F32)).astype(BF16)
            outs = []
            if not scaled:
                outs.append(begin(gb_v, gb_out.at[slot], out_sems.at[0]))

            def down_product(i):
                downs[i].wait()
                d_v[i % 2] = dot_nt(gb_v[...], wd_v[i])

            down_product(0)
            branch_in.wait()
            sums[...] = jnp.zeros_like(sums)
            for t in tiles(rows):
                sums[0] += eights(g_v[t].astype(F32) * branch_v[t].astype(F32))
                sums[1] += eights(gb_v[t].astype(F32))

            def up_product(i):
                ups[i].wait()
                part = pl.ds(i * CHUNK, CHUNK)
                outs.append(begin(before_v.at[i], before_out.at[slot, :, part], before_sems.at[i]))
                product = dot_nt(before_v[i], wu_v[i])
                acc[...] = product if i == 0 else acc[...] + product

            for i in range(steps):
                prefetch(i + 2)
                if i == steps - 2:
                    last = [
                        begin(res.at[slot], res_v, in_sems.at[1]),
                        begin(att.at[slot], att_v, in_sems.at[2]),
                        begin(woo, wo_v.at[0], in_sems.at[3]),
                        begin(wot, wo_v.at[1], in_sems.at[4]),
                    ]
                slopes[i].wait()
                if i > 0:
                    up_product(i - 1)
                if i + 1 < steps:
                    down_product(i + 1)
                total = jnp.zeros((8, CHUNK), F32)
                for t in tiles(rows):
                    grad_before = (d_v[i % 2, t] * slope_v[i, t].astype(F32)).astype(BF16)
                    before_v[i, t] = grad_before
                    total = total + eights(grad_before.astype(F32))
                shift_out[i : i + 1] = col_sum(total)
            up_product(steps - 1)
            for copy in last:
                copy.wait()
            for t in tiles(rows):
                hat, scale = norm_stats(res_v[t])
                error = acc[t]
                sums[2] += eights(error * hat)
                sums[3] += eights(error)
                grad = g_v[t].astype(F32) + norm_backward(hat, scale, v[LN2G : LN2G + 1], error)
                gr_v[t] = grad
                sums[4] += eights(grad * att_v[t].astype(F32))
                ga = (v[SATT : SATT + 1] * grad).astype(BF16)
                ga_v[t] = ga
                sums[5] += eights(ga.astype(F32))
            outs.append(begin(ga_v, ga_out.at[slot], out_sems.at[1]))
            outs.append(begin(gr_v, gr_out, out_sems.at[3]))
            gm_v[:, :half] = dot_nt(ga_v[...], wo_v[0]).astype(BF16)
            gm_v[:, half:] = dot_nt(ga_v[...], wo_v[1]).astype(BF16)
            outs.append(begin(gm_v, gm_out, out_sems.at[2]))
            small_out[...] = jnp.zeros_like(small_out)
            for row in range(6):
                small_out[row : row + 1] = col_sum(sums[row])
            for copy in outs:
                copy.wait()

    stack = (MICRO, rows, width)
    plain = pltpu.VMEM((rows, width), BF16)
    full = pltpu.VMEM((rows, width), F32)
    chunks = pltpu.VMEM((steps, rows, CHUNK), BF16)
    return manual(
        kernel,
        info,
        [(array, False) for array in tokens]
        + [
            (kept["branch"], False),
            (kept["slope"], False),
            (kept["residual"], False),
            (kept["attended"], False),
            (vec, True),
            (wo_own, False),
            (wo_oth, False),
            (wu_own, False),
            (wu_oth, False),
            (wd_own, False),
            (wd_oth, False),
        ],
        [
            (stack, BF16, False, None if scaled else grads.get("branch")),
            ((MICRO, rows, hidden), BF16, False, grads.get("before")),
            (stack, BF16, False, grads.get("attended")),
            ((rows, width), BF16, False, None),
            ((rows, width), F32, False, None),
            ((8, width), F32, True, None),
            ((steps, CHUNK), F32, True, None),
        ],
        [
            plain,
            plain,
            chunks,
            full,
            plain,
            pltpu.VMEM((2, half, width), BF16),
            pltpu.VMEM((steps, width, CHUNK), BF16),
            pltpu.VMEM((steps, CHUNK, width), BF16),
            plain,
            pltpu.VMEM((2, rows, CHUNK), F32),
            chunks,
            plain,
            plain,
            full,
            full,
            pltpu.VMEM((6, 8, width), F32),
            dma_sems(2),
            dma_sems(5),
            dma_sems(steps),
            dma_sems(steps),
            dma_sems(steps),
            dma_sems(4),
            dma_sems(steps),
        ],
        flops=4 * rows * width * hidden + 2 * rows * width * width,
        moved=4 * width * hidden + 2 * width * width + 8 * rows * hidden,
        after=after,
    )


def attend_backward(info, owner, number, grad_mixed, kept, after=()):
    _, rows, width = kept["q"].shape
    heads = width // HEAD_DIM
    lanes = 2 * HEAD_DIM
    block = 2 * lanes
    steps = width // block
    score_scale = HEAD_DIM**-0.5

    def kernel(s, *refs):
        @pl.when(s[ACTIVE + owner] == 1)
        def _():
            compute(*refs)

    def compute(gm, q_ref, kv, grown, full, inv, dq_out, here_out, there_out, *scratch):
        probs, scores = scratch[:4], scratch[4:8]
        own_v, centre_v = scratch[8:]
        first_q = lax.broadcasted_iota(jnp.int32, (rows, lanes), 1) < HEAD_DIM
        first_t = lax.broadcasted_iota(jnp.int32, (TILE, lanes), 1) < HEAD_DIM

        def columns(head):
            return slice(head // 2 * lanes, (head // 2 + 1) * lanes)

        for pair in range(2):
            place = columns(2 * pair)
            for t in tiles(rows):
                scaled = (gm[t, place].astype(F32) * inv[0, t, place]).astype(BF16)
                product = scaled.astype(F32) * full[0, t, place]
                for side in range(2):
                    mine = first_t if side == 0 else ~first_t
                    own_v[2 * pair + side, t] = jnp.where(mine, scaled, 0)
                    centre_v[2 * pair + side, t] = jnp.sum(
                        jnp.where(mine, product, 0.0), axis=-1, keepdims=True
                    )

        def prob(head):
            probs[head][...] = dot_nt(own_v[head], kv[0, 1, :, columns(head)])

        prob(0)
        grad_q, grad_k, grad_v = [], [], []
        for head in range(4):
            if head < 3:
                prob(head + 1)
            for t in tiles(rows):
                weight = grown[0, head, t].astype(F32)
                scores[head][t] = (weight * (probs[head][t] - centre_v[head, t])).astype(BF16)
            mine = first_q if head % 2 == 0 else ~first_q
            grad_v.append(dot_tn(grown[0, head], own_v[head]))
            grad_q.append(dot(scores[head][...], kv[0, 0, :, columns(head)]))
            masked = jnp.where(mine, q_ref[0, :, columns(head)], 0)
            grad_k.append(dot_tn(scores[head][...], masked))
            if head % 2 == 1:
                place = columns(head)
                dq = jnp.where(first_q, grad_q[head - 1], grad_q[head]) * score_scale
                dq_out[:, place] = dq.astype(BF16)
                dk = ((grad_k[head - 1] + grad_k[head]) * score_scale).astype(BF16)
                dv = (grad_v[head - 1] + grad_v[head]).astype(BF16)
                here_out[0, :, place] = dk[:rows]
                here_out[1, :, place] = dv[:rows]
                there_out[0, :, place] = dk[rows:]
                there_out[1, :, place] = dv[rows:]

    def on(s):
        return s[ACTIVE + owner]

    def slot(s):
        return jnp.where(on(s) == 1, number, SPARE)

    column = lambda i, s: (slot(s), 0, i * on(s))
    plain = lambda i, s: (0, i * on(s))
    return call(
        kernel,
        info,
        (steps,),
        [
            (grad_mixed, (rows, block), plain),
            (kept["q"], (1, rows, block), lambda i, s: (number, 0, i * on(s))),
            (kept["kv"], (1, 2, 2 * rows, block), lambda i, s: (slot(s), 0, 0, i * on(s))),
            (kept["grown"], (1, 4, rows, 2 * rows), lambda i, s: (slot(s), i * on(s), 0, 0)),
            (kept["mixed_full"], (1, rows, block), column),
            (kept["inverse"], (1, rows, block), column),
        ],
        [
            ((rows, width), BF16, (rows, block), plain, None),
            ((2, rows, width), BF16, (2, rows, block), lambda i, s: (0, 0, i * on(s)), None),
            ((2, rows, width), BF16, (2, rows, block), lambda i, s: (0, 0, i * on(s)), None),
        ],
        [pltpu.VMEM((rows, 2 * rows), F32)] * 4
        + [pltpu.VMEM((rows, 2 * rows), BF16)] * 4
        + [pltpu.VMEM((4, rows, lanes), BF16), pltpu.VMEM((4, rows, 1), F32)],
        flops=16 * rows * rows * width,
        moved=4 * heads * rows * rows + 30 * rows * width,
        after=after,
    )


def qkv_backward(info, owner, number, dq, dkv_here, dkv_there, w_own, w_oth, grad_res, vec, kept, grads, after=()):
    _, rows, width = kept["x"].shape
    half = width // 2

    def kernel(s, dq_ref, here, there, own, oth, gr, x_ref, v, packed_out, gx_out, relay_out,
               small_out, shift_out, a_v, b_v, p_v, w_v, gr_v, x_v, gx_v, acc, sums,
               a_sems, b_sems, w_sems, in_sems, packed_sems, out_sems):
        @pl.when(s[ACTIVE + owner] == 0)
        def _():
            small_out[...] = jnp.zeros_like(small_out)
            shift_out[...] = jnp.zeros_like(shift_out)

        @pl.when(s[ACTIVE + owner] == 1)
        def _():
            slot = number
            loads = []
            for part in range(6):
                kind, side = part % 3, part // 3
                columns = pl.ds(side * half, half)
                if kind == 0:
                    copies = [begin(dq_ref.at[:, columns], a_v.at[part], a_sems.at[part])]
                else:
                    turned = pl.ds((1 - side) * half, half)
                    copies = [
                        begin(here.at[kind - 1, :, columns], a_v.at[part], a_sems.at[part]),
                        begin(there.at[kind - 1, :, turned], b_v.at[part], b_sems.at[part]),
                    ]
                weight = own if side == 0 else oth
                copies.append(begin(weight.at[kind], w_v.at[part], w_sems.at[part]))
                loads.append(copies)
            last = [
                begin(x_ref.at[slot], x_v, in_sems.at[0]),
                begin(gr, gr_v, in_sems.at[1]),
            ]
            outs = []
            for part in range(6):
                for copy in loads[part]:
                    copy.wait()
                total = jnp.zeros((8, half), F32)
                for t in tiles(rows):
                    packed = a_v[part, t]
                    if part % 3 > 0:
                        packed = (packed.astype(F32) + b_v[part, t].astype(F32)).astype(BF16)
                    p_v[part, t] = packed
                    total = total + eights(packed.astype(F32))
                shift_out[part : part + 1] = col_sum(total)
                outs.append(
                    begin(
                        p_v.at[part],
                        packed_out.at[slot, :, pl.ds(part * half, half)],
                        packed_sems.at[part],
                    )
                )
                product = dot_nt(p_v[part], w_v[part])
                acc[...] = product if part == 0 else acc[...] + product
            for copy in last:
                copy.wait()
            sums[...] = jnp.zeros_like(sums)
            for t in tiles(rows):
                hat, scale = norm_stats(x_v[t].astype(F32))
                error = acc[t]
                grad = gr_v[t] + norm_backward(hat, scale, v[LN1G : LN1G + 1], error)
                gx_v[t] = grad.astype(BF16)
                sums[0] += eights(error * hat)
                sums[1] += eights(error)
            outs.append(begin(gx_v, relay_out, out_sems.at[0]))
            outs.append(begin(gx_v, gx_out.at[slot], out_sems.at[1]))
            small_out[...] = jnp.zeros_like(small_out)
            for row in range(2):
                small_out[row : row + 1] = col_sum(sums[row])
            for copy in outs:
                copy.wait()

    stack = (MICRO, rows, width)
    parts = pltpu.VMEM((6, rows, half), BF16)
    return manual(
        kernel,
        info,
        [
            (dq, False),
            (dkv_here, False),
            (dkv_there, False),
            (w_own, False),
            (w_oth, False),
            (grad_res, False),
            (kept["x"], False),
            (vec, True),
        ],
        [
            ((MICRO, rows, 3 * width), BF16, False, grads.get("packed")),
            (stack, BF16, False, grads.get("input")),
            ((rows, width), BF16, False, None),
            ((8, width), F32, True, None),
            ((8, half), F32, True, None),
        ],
        [
            parts,
            parts,
            parts,
            pltpu.VMEM((6, width, half), BF16),
            pltpu.VMEM((rows, width), F32),
            pltpu.VMEM((rows, width), BF16),
            pltpu.VMEM((rows, width), BF16),
            pltpu.VMEM((rows, width), F32),
            pltpu.VMEM((2, 8, width), F32),
            dma_sems(6),
            dma_sems(6),
            dma_sems(6),
            dma_sems(2),
            dma_sems(6),
            dma_sems(2),
        ],
        flops=6 * rows * width * width,
        moved=6 * width * width + 16 * rows * width,
        after=after,
    )


def swap(block):
    return lax.ppermute(block, "tensor", [(0, 1), (1, 0)])


def ring_order(count):
    return list(range(0, count, 2)) + list(range(count - 1, 0, -2))


def tied(value, *others):
    return lax.optimization_barrier((value, *others))[0]


class Ring:
    def __init__(self, info, parts, shapes, places):
        self.info, self.parts, self.shapes, self.places = info, parts, shapes, places
        self.count = lax.axis_size("dp")
        order = ring_order(self.count)
        n = self.count
        self.chunk = parts[0][0].shape[0] // (2 * n)
        self.widths = [pair[0].shape[1] for pair in parts]
        self.signs = (1, -1)
        self.routes = [[(order[i], order[(i + s) % n]) for i in range(n)] for s in self.signs]
        self.step = 0
        self.steps = 2 * (n - 1)
        self.totals = [None] * len(shapes)
        self.vmem = RING_MIB
        self.moving = self.add([0, 0], None)

    def unit(self, way, ahead):
        return UNITS + way * self.count + ahead % self.count

    def add(self, ahead, arrived, after=()):
        chunk, width, parts = self.chunk, sum(self.widths), len(self.parts)
        units = [self.unit(w, ahead[w]) for w in range(2)]
        terms = 2 if arrived is None else 3

        def kernel(s, *refs):
            halves = refs[: 2 * parts]
            refs = refs[2 * parts :]
            if terms == 3:
                arrivals, refs = refs[:2], refs[2:]
            outs, (held, sems) = refs[:2], refs[2:]
            copies = []
            for w in range(2):
                rows = pl.ds(pl.multiple_of(s[units[w]] * chunk, chunk), chunk)
                base = 0
                for number, columns in enumerate(self.widths):
                    for term in range(2):
                        copies.append(
                            begin(
                                halves[2 * number + term].at[rows],
                                held.at[w, term, :, pl.ds(base, columns)],
                                sems.at[w, term, number],
                            )
                        )
                    base += columns
                if terms == 3:
                    copies.append(begin(arrivals[w], held.at[w, 2], sems.at[w, 2, 0]))
            for copy in copies:
                copy.wait()
            for w in range(2):
                for t in tiles(chunk):
                    for first in range(0, width, 512):
                        c = slice(first, min(first + 512, width))
                        total = held[w, 0, t, c].astype(F32) + held[w, 1, t, c].astype(F32)
                        if terms == 3:
                            total = total + held[w, 2, t, c].astype(F32)
                        outs[w][t, c] = total.astype(BF16)

        arrays = [(term, False) for pair in self.parts for term in pair]
        if arrived is not None:
            arrays += [(block, False) for block in arrived]
        return manual(
            kernel,
            self.info,
            arrays,
            [((chunk, width), BF16, True, None)] * 2,
            [pltpu.VMEM((2, terms, chunk, width), BF16), pltpu.SemaphoreType.DMA((2, 3, parts))],
            moved=2 * (terms + 1) * 2 * chunk * width,
            vmem=self.vmem,
            after=after,
        )

    def put(self, ahead, blocks, after=()):
        chunk, width = self.chunk, sum(self.widths)
        units = [self.unit(w, pair[w]) for pair in ahead for w in range(2)]
        size = len(units)
        count = len(self.shapes)
        pieces = sum(len(self.places.columns(c)) for c in range(count))

        def kernel(s, *refs):
            sources, outs = refs[:size], refs[size : size + count]
            held, wide, in_sems, out_sems = refs[size + count + 2 :]
            loads = [begin(sources[w], held.at[w], in_sems.at[w]) for w in range(size)]
            copies = []
            for w in range(size):
                loads[w].wait()
                for t in tiles(chunk):
                    for first in range(0, width, 512):
                        c = slice(first, min(first + 512, width))
                        wide[w, t, c] = held[w, t, c].astype(F32)
                number = 0
                for target in range(count):
                    for first, columns in self.places.columns(target):
                        ref = self.places.ref(
                            outs[target], target, first, columns, s[units[w]], chunk
                        )
                        copies.append(
                            begin(
                                wide.at[w, :, pl.ds(first, columns)],
                                ref,
                                out_sems.at[w, number],
                            )
                        )
                        number += 1
            for copy in copies:
                copy.wait()

        results = manual(
            kernel,
            self.info,
            [(block, False) for block in blocks[:-2]] + [(block, False) for block in blocks[-2:]],
            [(shape, F32, False, old) for shape, old in zip(self.shapes, self.totals)]
            + [((chunk, width), BF16, False, None)] * 2,
            [
                pltpu.VMEM((size, chunk, width), BF16),
                pltpu.VMEM((size, chunk, width), F32),
                dma_sems(size),
                pltpu.SemaphoreType.DMA((size, pieces)),
            ],
            moved=2 * 6 * chunk * width,
            vmem=self.vmem,
            after=after,
            same={size - 2: count, size - 1: count + 1},
        )
        self.totals = list(results[:count])
        return list(results[count:])

    def advance(self, *after):
        arrived = [lax.ppermute(self.moving[w], "dp", self.routes[w]) for w in range(2)]
        if after:
            arrived = list(lax.optimization_barrier((*arrived, *after))[:2])
        step = self.step
        if step < self.count - 1:
            self.moving = self.add([-s * (step + 1) for s in self.signs], arrived)
        else:
            ahead = [[-s * (step - self.count + 1) for s in self.signs]]
            blocks = arrived
            if step == self.count - 1:
                ahead.insert(0, self.signs)
                blocks = list(self.moving) + arrived
            self.moving = self.put(ahead, blocks)
        self.step += 1

    def done(self):
        return self.step == self.steps

    def finish(self):
        while not self.done():
            self.advance()
        return self.totals


class MlpPlaces:
    def __init__(self, width, second, rows):
        self.width, self.second, self.rows = width, second, rows

    def columns(self, target):
        if target == 0:
            return [(0, self.width)]
        return [(self.width, self.second), (self.width + self.second, self.second)]

    def ref(self, out, target, first, columns, unit, chunk):
        base = self.rows if first > self.width else 0
        return out.at[pl.ds(pl.multiple_of(base + unit * chunk, chunk), chunk)]


class TailPlaces:
    def __init__(self, half, lanes):
        self.half, self.lanes = half, lanes

    def columns(self, target):
        half = self.half
        if target == 0:
            return [(j * half, half) for j in range(3)]
        return [(3 * half, half)] if target == 1 else [(4 * half, self.lanes)]

    def ref(self, out, target, first, columns, unit, chunk):
        rows = pl.ds(pl.multiple_of(unit * chunk, chunk), chunk)
        if target == 0:
            return out.at[first // self.half, rows]
        if target == 2:
            return out.at[rows]
        each = self.half // chunk
        return out.at[
            pl.ds(pl.multiple_of(lax.rem(unit, each) * chunk, chunk), chunk),
            pl.ds(pl.multiple_of(lax.div(unit, each) * self.half, self.half), self.half),
        ]


def partner_tokens(info, block, numbers):
    _, _, seq, half = block.shape
    rows = seq // 2

    def kernel(s, ref, out, sems):
        start = pl.multiple_of((1 - s[RANK]) * rows, rows)
        copies = [
            begin(ref.at[number, 0, pl.ds(start, rows)], out.at[place], sems.at[place])
            for place, number in enumerate(numbers)
        ]
        for copy in copies:
            copy.wait()

    return manual(
        kernel,
        info,
        [(block, False)],
        [((len(numbers), rows, half), BF16, True, None)],
        [dma_sems(len(numbers))],
        vmem=8,
    )[0]


def partner_features(info, block):
    micro, rows, width = block.shape
    half = width // 2

    def kernel(s, ref, out, sems):
        start = pl.multiple_of((1 - s[RANK]) * half, half)
        copies = [
            begin(ref.at[m, :, pl.ds(start, half)], out.at[m], sems.at[m]) for m in range(micro)
        ]
        for copy in copies:
            copy.wait()

    return manual(
        kernel,
        info,
        [(block, False)],
        [((micro, rows, half), BF16, True, None)],
        [dma_sems(micro)],
        vmem=8,
    )[0]


def join_tokens(info, block, received):
    micro, rows, width = block.shape
    half = width // 2

    def kernel(s, ref, other, out, sems):
        rank = s[RANK]
        features = pl.ds(pl.multiple_of(rank * half, half), half)
        here = pl.ds(pl.multiple_of(rank * rows, rows), rows)
        there = pl.ds(pl.multiple_of((1 - rank) * rows, rows), rows)
        copies = []
        for m in range(micro):
            copies.append(begin(ref.at[m, :, features], out.at[0, m, 0, here], sems.at[0, m]))
            copies.append(begin(other.at[m], out.at[0, m, 0, there], sems.at[1, m]))
        for copy in copies:
            copy.wait()

    return manual(
        kernel,
        info,
        [(block, False), (received, False)],
        [((1, micro, 1, 2 * rows, half), BF16, True, None)],
        [pltpu.SemaphoreType.DMA((2, micro))],
        vmem=8,
    )[0]


LANES = 128


def gather_vectors(info, sums, rows_out):
    calls = len(sums)
    width = sums[0][0].shape[1]
    half = width // 2

    def kernel(s, *refs):
        own, oth = refs[4 * calls :]
        low = s[RANK] == 0

        def total(kind):
            blocks = [refs[4 * c + kind][...] for c in range(calls)]
            return sum(blocks[1:], blocks[0])

        two, up, one, qkv = [total(kind) for kind in range(4)]
        own[...] = jnp.zeros_like(own)
        oth[...] = jnp.zeros_like(oth)
        place = 0

        def write(first, second):
            nonlocal place
            for c in range(0, half, LANES):
                own[place : place + 1] = first[:, c : c + LANES].astype(BF16)
                oth[place : place + 1] = second[:, c : c + LANES].astype(BF16)
                place += 1

        for block, count in ((one, 2), (two, 6)):
            for row in range(count):
                line = block[row : row + 1]
                left, right = line[:, :half], line[:, half:]
                write(jnp.where(low, left, right), jnp.where(low, right, left))
        for row in range(3):
            write(qkv[row : row + 1], qkv[3 + row : 4 + row])
        hidden_rows = up.shape[0] // 2
        for row in range(hidden_rows):
            write(up[row : row + 1], up[hidden_rows + row : hidden_rows + row + 1])

    vmem = pl.BlockSpec(memory_space=pltpu.VMEM)
    return pl.pallas_call(
        kernel,
        in_specs=[pl.BlockSpec(memory_space=pltpu.SMEM)] + [vmem] * (4 * calls),
        out_specs=[vmem] * 2,
        out_shape=[jax.ShapeDtypeStruct((rows_out, LANES), BF16)] * 2,
    )(info, *[block for group in sums for block in group])


def spread_vectors(sums, half, hidden_half):
    def kernel(ref, *outs):
        def line(number, out, row=0, columns=half, first=0):
            for c in range(0, columns, LANES):
                place = (number * half + c) // LANES
                out[row : row + 1, first + c : first + c + LANES] = ref[place : place + 1]

        for number in range(8):
            line(number, outs[number])
        line(8, outs[8])
        line(10, outs[8], row=1)
        line(11, outs[9], columns=hidden_half)

    vmem = pl.BlockSpec(memory_space=pltpu.VMEM)
    shapes = [(1, half)] * 8 + [(2, half), (1, hidden_half)]
    return pl.pallas_call(
        kernel,
        in_specs=[vmem],
        out_specs=[vmem] * 10,
        out_shape=[jax.ShapeDtypeStruct(shape, F32) for shape in shapes],
    )(sums)


def pack_vectors(blocks, hidden_bias):
    half = blocks[0].shape[1]
    hidden_rows = hidden_bias.shape[1] // half
    filled = sum(b.shape[0] for b in blocks)

    def kernel(*refs):
        out = refs[-1]
        place = 0
        for ref in refs[: len(blocks)]:
            for row in range(ref.shape[0]):
                out[place : place + 1] = ref[row : row + 1].astype(F32)
                place += 1
        for row in range(hidden_rows):
            columns = slice(row * half, (row + 1) * half)
            out[place : place + 1] = refs[len(blocks)][:, columns].astype(F32)
            place += 1

    return pl.pallas_call(
        kernel, out_shape=jax.ShapeDtypeStruct((filled + hidden_rows, half), F32)
    )(*blocks, hidden_bias)


def join_vectors(scalars, own, oth, hidden_rows):
    half = own.shape[1]

    def kernel(s, own_ref, oth_ref, vec, bias_q, bias_v, bias_up):
        low = s[RANK] == 0
        vec[:, :half] = jnp.where(low, own_ref[:8], oth_ref[:8])
        vec[:, half:] = jnp.where(low, oth_ref[:8], own_ref[:8])
        for row, out in ((8, bias_q), (9, bias_v)):
            out[:, :half] = own_ref[row : row + 1]
            out[:, half:] = oth_ref[row : row + 1]
        bias_up[:hidden_rows] = own_ref[10 : 10 + hidden_rows]
        bias_up[hidden_rows:] = oth_ref[10 : 10 + hidden_rows]

    vmem = pl.BlockSpec(memory_space=pltpu.VMEM)
    return pl.pallas_call(
        kernel,
        in_specs=[pl.BlockSpec(memory_space=pltpu.SMEM), vmem, vmem],
        out_specs=[vmem] * 4,
        out_shape=[
            jax.ShapeDtypeStruct((8, 2 * half), F32),
            jax.ShapeDtypeStruct((1, 2 * half), F32),
            jax.ShapeDtypeStruct((1, 2 * half), F32),
            jax.ShapeDtypeStruct((2 * hidden_rows, half), F32),
        ],
    )(scalars, own, oth)


def shards(
    inputs,
    cotangent,
    ln1_gain,
    ln1_bias,
    qkv_weight,
    qv_bias,
    out_weight,
    out_bias,
    scale_attn,
    ln2_gain,
    ln2_bias,
    fc1_weight,
    fc1_bias,
    fc2_weight,
    fc2_bias,
    scale_mlp,
):
    micro, images, seq_len, half = inputs.shape
    assert micro == MICRO and images == 1
    width = 2 * half
    hidden_half = fc1_weight.shape[2]

    count = lax.axis_size("dp")
    order = ring_order(count)
    table = [
        [rank, int(section == 0), int(section == 1)]
        + [way * count + (order.index(i) + ahead) % count for way in range(2) for ahead in range(count)]
        for section in range(2)
        for rank in range(2)
        for i in range(count)
    ]
    info = lax.dynamic_slice(
        jnp.asarray(table, jnp.int32),
        (lax.axis_index(("section", "tensor", "dp")), 0),
        (1, len(table[0])),
        allow_negative_indices=False,
    ).reshape(-1)

    first_oth = swap(partner_tokens(info, inputs, (0,))[0])
    vectors = pack_vectors(
        [
            ln1_gain, ln1_bias, out_bias, scale_attn, ln2_gain, ln2_bias, fc2_bias, scale_mlp,
            qv_bias[0],
        ],
        fc1_bias,
    )
    vectors_oth = swap(vectors)
    wq_own = jnp.transpose(qkv_weight[0], (1, 0, 2))
    wq_oth = swap(tied(wq_own, vectors))
    vec, bias_q, bias_v, b_up = join_vectors(info, vectors, vectors_oth, hidden_half // half)
    b_up = b_up.reshape(2 * hidden_half // CHUNK, CHUNK)
    wo_own, wu_own, wd_own = out_weight[0], fc1_weight[0], fc2_weight[0]
    wo_oth = swap(tied(wo_own, first_oth, vectors_oth))
    wu_oth = swap(tied(wu_own, first_oth, vectors_oth))
    wd_oth = swap(tied(wd_own, first_oth, vectors_oth))
    second_oth = swap(partner_tokens(info, tied(inputs, wd_oth), (1,))[0])
    cot_oth = swap(partner_tokens(info, tied(cotangent, wd_oth), (0, 1)))

    kept = {}

    def enter(owner, number, source, tokens, after=()):
        kept["x"], kept["normed1"], kv_here = norm_kv(
            info, owner, number, source, tokens, vec, wq_own, wq_oth, bias_v, kept, after
        )
        return kv_here

    def forward(owner, number, kv_here, late=()):
        kv_there = swap(kv_here)
        kept["q"] = project_q(info, owner, number, kept["normed1"], wq_own, wq_oth, bias_q, kept)
        kept["grown"], kept["mixed_full"], mixed, kept["inverse"], kept["kv"] = attend(
            info, owner, number, kept["q"], kv_here, kv_there, kept
        )
        (
            kept["attended"],
            kept["residual"],
            kept["normed2"],
            kept["active"],
            kept["slope"],
            kept["branch"],
            kept["output"],
            relayed,
            kept["mixed"],
        ) = mlp_forward(
            info, owner, number, mixed, kept["x"], vec, wo_own, wo_oth, wu_own, wu_oth, wd_own,
            wd_oth, b_up, kept, late,
        )
        return relayed

    grads = {}
    sums = []

    def backward_mlp(owner, number, source, tokens, after, scaled=False):
        (
            branch,
            grads["before"],
            grads["attended"],
            grad_mixed,
            grad_res,
            small,
            shift,
        ) = mlp_backward(
            info, owner, number, source, tokens, vec, wo_own, wo_oth, wu_own, wu_oth, wd_own,
            wd_oth, kept, grads, scaled, after,
        )
        if not scaled:
            grads["branch"] = branch
        return grad_mixed, grad_res, small, shift

    def backward_attention(owner, number, grad_mixed, after=()):
        dq, dkv_here, dkv_send = attend_backward(info, owner, number, grad_mixed, kept, after)
        return dq, dkv_here, swap(dkv_send)

    def backward_qkv(owner, number, dq, dkv_here, dkv_there, grad_res, small, shift, after=()):
        grads["packed"], grads["input"], relayed, small_one, shift_qkv = qkv_backward(
            info, owner, number, dq, dkv_here, dkv_there, wq_own, wq_oth, grad_res, vec, kept,
            grads, after,
        )
        sums.append((small, shift, small_one, shift_qkv))
        return relayed

    def backward(owner, number, source, tokens, after):
        grad_mixed, grad_res, small, shift = backward_mlp(owner, number, source, tokens, after)
        flows = backward_attention(owner, number, grad_mixed)
        return backward_qkv(owner, number, *flows, grad_res, small, shift)

    kv_here = enter(0, 0, "argument", (inputs, first_oth))
    kv_next = enter(0, 1, "argument", (inputs, second_oth), [kv_here])
    relayed = forward(0, 0, kv_here, [kv_next])
    first = lax.ppermute(relayed, "section", [(0, 1)])
    relayed = forward(0, 1, kv_next, [relayed])
    second = lax.ppermute(relayed, "section", [(0, 1)])
    relayed = forward(1, 0, enter(1, 0, "relay", (first,), [relayed]))
    relayed = backward(1, 0, "argument", (cotangent, cot_oth[0]), [relayed, second])
    first = lax.ppermute(relayed, "section", [(1, 0)])
    relayed = forward(1, 1, enter(1, 1, "relay", (second,), [relayed]), [first])
    relayed = backward(1, 1, "argument", (cotangent, cot_oth[1]), [relayed])
    second = lax.ppermute(relayed, "section", [(1, 0)])
    relayed = backward(0, 0, "relay", (first,), [relayed])

    def weight_grad(left, right):
        return lax.dot_general(
            left, right, (((0, 1), (0, 1)), ((), ())), preferred_element_type=F32
        ).astype(BF16)

    grads["branch"] = scale_branch(info, 0, 1, second, vec, grads["branch"], [relayed])
    active, g_branch = kept["active"], grads["branch"]
    split = hidden_half // 2
    assert split == width

    def down_grad(start):
        return weight_grad(active[:, :, start : start + split], g_branch)

    down = []
    for start in (0, split):
        sent = swap(down_grad(hidden_half + start))
        down.append((down_grad(start), sent))
    grad_mixed, grad_res, small, shift = backward_mlp(
        0, 1, "relay", (second,), [pair[0] for pair in down], scaled=True
    )
    normed2, before = kept["normed2"], grads["before"]
    up_sent = swap(weight_grad(normed2, before[:, :, hidden_half:]))
    up_own = weight_grad(normed2, before[:, :, :hidden_half])
    ring_mlp = Ring(
        info,
        [(up_own, up_sent), *down],
        [up_own.shape, (hidden_half, width)],
        MlpPlaces(hidden_half, width, split),
    )
    flows = backward_attention(0, 1, grad_mixed, list(ring_mlp.moving))
    ring_mlp.advance(flows[0])
    grad_res = tied(grad_res, *ring_mlp.moving)
    backward_qkv(0, 1, *flows, grad_res, small, shift)
    packed = grads["packed"]
    ring_mlp.advance(packed)
    normed1 = tied(kept["normed1"], *ring_mlp.moving)
    vectors = gather_vectors(info, sums, width)

    def tail(index):
        columns = packed[:, :, index * 3 * half : (index + 1) * 3 * half]
        mixed = kept["mixed"][:, :, index * half : (index + 1) * half]
        g_att = grads["attended"]
        outs = [weight_grad(mixed, g_att[:, :, half * j : half * (j + 1)]) for j in range(2)]
        return [weight_grad(normed1, columns), jnp.concatenate(outs, axis=0), vectors[index]]

    tail_oth = tail(1)
    tail_sent = [swap(block) for block in tail_oth]
    tail_own = tail(0)
    ring_mlp.advance(tail_own[0])
    ring_tail = Ring(
        info,
        list(zip(tail_own, tail_sent)),
        [(3, width, half), (half, width), (width, LANES)],
        TailPlaces(half, LANES),
    )
    rings = [ring_mlp, ring_tail]
    for ring in rings:
        ring.vmem = 16
    before_it = ring_tail
    while not all(ring.done() for ring in rings):
        for ring in rings:
            if not ring.done():
                ring.advance(*before_it.moving)
                before_it = ring
    total_up, total_down = ring_mlp.finish()
    total_qkv, total_out, total_vectors = ring_tail.finish()
    block_outputs = join_tokens(info, kept["output"], swap(partner_features(info, kept["output"])))
    input_grads = join_tokens(info, grads["input"], swap(partner_features(info, grads["input"])))
    rows = spread_vectors(total_vectors, half, hidden_half)
    return (
        block_outputs,
        input_grads,
        rows[0],
        rows[1],
        jnp.transpose(total_qkv, (1, 0, 2))[None],
        rows[8][None],
        total_out[None],
        rows[7],
        rows[6],
        rows[4],
        rows[5],
        total_up[None],
        rows[9],
        total_down[None],
        rows[3],
        rows[2],
    )


def solution(mesh):
    placed = (
        P(None, "dp", None, "tensor"),
        P(None, "dp", None, "tensor"),
        P("section", "tensor"),
        P("section", "tensor"),
        P("section", None, None, "tensor"),
        P("section", None, "tensor"),
        P("section", "tensor", None),
        P("section", "tensor"),
        P("section", "tensor"),
        P("section", "tensor"),
        P("section", "tensor"),
        P("section", None, "tensor"),
        P("section", "tensor"),
        P("section", "tensor", None),
        P("section", "tensor"),
        P("section", "tensor"),
    )
    return jax.shard_map(
        shards,
        mesh=mesh,
        in_specs=placed,
        out_specs=(
            P("section", None, "dp", None, "tensor"),
            P("section", None, "dp", None, "tensor"),
            P("section", "tensor"),
            P("section", "tensor"),
            P("section", None, None, "tensor"),
            P("section", None, "tensor"),
            P("section", "tensor", None),
            P("section", "tensor"),
            P("section", "tensor"),
            P("section", "tensor"),
            P("section", "tensor"),
            P("section", None, "tensor"),
            P("section", "tensor"),
            P("section", "tensor", None),
            P("section", "tensor"),
            P("section", "tensor"),
        ),
        check_vma=False,
    )
```
